32 devices in a mesh: parts: 2 (over y), row: 4 (over z), col: 4 (over x, core).
Axes of the slice: x: 2, y: 2, z: 4, core: 2. Of those that a mesh axis runs over, the one named last changes fastest.
Arguments:
- amplitudes: bfloat16 [8, 100, 512, 512], P('parts', 'col', 'row'), parts along dimension 0, may hold values from -12 to 12
- integrals: bfloat16 [200, 512, 512], P(('parts', 'col'), 'row'), parts along dimension 0, may hold values from -0.109375 to 0.109375
- occ_irrep: int32 [200], P('parts'), parts along dimension 0, may hold values from 0 to 7, as said below
- vir_irrep: int32 [1024], P('parts'), parts along dimension 0, may hold values from 0 to 7, as said below
- screen: int32 [200, 8], P('parts'), parts along dimension 0, may hold values 0 or 1
- occ_energy: float32 [200], P('parts'), parts along dimension 0, may hold values from -1 to -0.3
- vir_energy: float32 [1024], P('parts'), parts along dimension 0, may hold values from 0.1 to 1
Outputs:
- update: float32 [512, 8, 512], P('row', 'parts', 'col'), parts along dimension 1
The draws below stay inside these ranges and needn't reach their ends.
There are 2 independent parts, one for each index of `parts`. The reference program is written for one: setup_inputs(seed, part) draws one part's arguments, and reference() takes and returns one part's arrays. A program takes and returns all parts, laid end to end along the dimension named above; each array names one. Nothing has to cross between parts.
Inputs may be any that keep to these rules, and one draw needn't show every extreme that they name: `occ_irrep`: the labels never fall from one orbital to the next; the first is 0 and the last is 7. `vir_irrep`: the labels never fall from one orbital to the next and every label from 0 to 7 occurs; exactly one label covers 256 virtual orbitals, every other label fewer.
All inputs are finite; a program needn't handle non-finite values.
Results may differ from the reference program's by a relative error of at most 0.0003.
Values may be sent and summed in bfloat16 or wider, within the bound.
No kernel may reach another device: no remote copies, remote signals or barrier semaphores. Data moves between devices by JAX's collectives and lax.ppermute only.
A program may use at most 128 MiB of HBM per device.

```python
import jax
import jax.numpy as jnp
from jax import lax

O = 100
V = 512
NI = 4
VMAX = 256


def sorted_labels(key, length):
    left_key, right_key = jax.random.split(key)
    smaller = jnp.minimum(jax.random.randint(left_key, (length - 2,), 0, 8), jax.random.randint(right_key, (length - 2,), 0, 8))
    bounds = jnp.array([0, 7], dtype=jnp.int32)
    return jnp.sort(jnp.concatenate([bounds, smaller.astype(jnp.int32)]))


def draw_occ_irrep(key, part):
    return sorted_labels(jax.random.fold_in(key, 11), O)


def draw_vir_irrep(key, part):
    label_key, spread_key = jax.random.split(jax.random.fold_in(key, 23))
    largest = jax.random.randint(label_key, (), 0, 8).astype(jnp.int32)
    spare_count = V - VMAX - 7
    picks = jax.random.randint(spread_key, (spare_count,), 0, 7).astype(jnp.int32)
    other_codes = jnp.arange(7, dtype=jnp.int32)
    other_counts = 1 + jnp.sum((picks[:, None] == other_codes[None, :]).astype(jnp.int32), axis=0)
    label_codes = jnp.arange(8, dtype=jnp.int32)
    other_index = label_codes - (label_codes > largest).astype(jnp.int32)
    other_index = jnp.minimum(other_index, 6)
    counts = jnp.where(label_codes == largest, jnp.int32(VMAX), other_counts[other_index])
    edges = jnp.cumsum(counts).astype(jnp.int32)
    positions = jnp.arange(V, dtype=jnp.int32)
    return jnp.sum((positions[:, None] >= edges[None, :]).astype(jnp.int32), axis=1).astype(jnp.int32)


def place_ends(values, own_key, smallest, high):
    place = [jax.random.randint(jax.random.fold_in(own_key, axis), (), 0, length) for axis, length in enumerate(values.shape)]
    widest = values.shape.index(max(values.shape))
    beside = place[:widest] + [(place[widest] + 1) % values.shape[widest]] + place[widest + 1:]
    return values.at[tuple(place)].set(smallest).at[tuple(beside)].set(high)


def spiked(values, rng, source, target, shards_of, factor):
    def block_of(axis_at):
        return (jnp.arange(values.shape[axis_at]) // (values.shape[axis_at] // shards_of)).reshape((-1,) + (1,) * (values.ndim - 1 - axis_at))

    near = jax.random.permutation(rng, shards_of)[block_of(target)]
    second = (block_of(target) + shards_of // 2) % shards_of
    return jnp.where((block_of(source) == near) | (block_of(source) == second), factor * values, values)


def steps_of(key, extent, pieces, smallest, high):
    level = 1.0
    for position, parts in pieces:
        steps = jax.random.uniform(jax.random.fold_in(jax.random.fold_in(key, 6), position), (parts,), jnp.float32, smallest / len(pieces), high / len(pieces))
        level = level * jnp.repeat(jnp.exp(steps), extent[position] // parts).reshape((-1,) + (1,) * (len(extent) - 1 - position))
    return level


def scatter_about(own_key, dims, width, bound, cuts=(), kind=jnp.bfloat16):
    values = width * jax.random.normal(own_key, dims, jnp.float32)
    if cuts:
        values = values * steps_of(own_key, dims, cuts, -0.22, 0.18)
    return jnp.clip(values, -bound, bound).astype(kind)


def heavy_noise(rng, dims, spread, bound, pieces, heavy, held_as=jnp.bfloat16):
    drawn = spread * jax.random.normal(rng, dims, jnp.float32)
    if pieces:
        drawn = drawn * steps_of(rng, dims, pieces, -0.22, 0.18)
    return jnp.clip(spiked(drawn, jax.random.fold_in(rng, 3), *heavy), -bound, bound).astype(held_as)


def setup_inputs(seed: int = 0, part: int = 0) -> dict:
    key_of = jax.random.split(jax.random.key(seed), 8)
    part_keys = jax.random.split(jax.random.fold_in(key_of[7], part), 8)
    amplitudes = scatter_about(part_keys[0], (NI, O, V, V), 2.0, 12.0, ((1, 4), (2, 4)))
    integrals = heavy_noise(part_keys[1], (O, V, V), (O * V // 8) ** -0.5, 0.109375, ((0, 4), (1, 4)), (1, 2, 4, 2.0))
    occ_irrep = draw_occ_irrep(jax.random.fold_in(jax.random.fold_in(key_of[7], part), 71), part)
    vir_irrep = draw_vir_irrep(jax.random.fold_in(jax.random.fold_in(key_of[7], part), 71), part)
    screen = place_ends((jax.random.randint(part_keys[4], (O, 8), 0, 4) < 3).astype(jnp.int32), jax.random.fold_in(part_keys[4], 1), 0, 1)
    occ_energy = jnp.clip(jax.random.uniform(part_keys[5], (O,), jnp.float32, -1.0, -0.3), -1.0, -0.3)
    vir_energy = jnp.clip(jax.random.uniform(part_keys[6], (V,), jnp.float32, 0.1, 1.0), 0.1, 1.0)
    return {"amplitudes": amplitudes, "integrals": integrals, "occ_irrep": occ_irrep, "vir_irrep": vir_irrep, "screen": screen, "occ_energy": occ_energy, "vir_energy": vir_energy}


def parity(first_label, second_label, third_label, fourth_label):
    return jnp.bitwise_xor(jnp.bitwise_xor(first_label, second_label), jnp.bitwise_xor(third_label, fourth_label))


def reference(amplitudes, integrals, occ_irrep, vir_irrep, screen, occ_energy, vir_energy):
    pair_label = occ_irrep[NI]
    irrep_codes = jnp.arange(8, dtype=jnp.int32)
    screen_cols = jnp.sum(screen[:, None, :] * (vir_irrep[None, :, None] == irrep_codes).astype(jnp.int32), axis=2)
    keep_int = (parity(occ_irrep[:, None, None], vir_irrep[None, :, None], pair_label, vir_irrep[None, None, :]) == 0) & (screen_cols[:, :, None] == 1)
    int_kept = jnp.where(keep_int, integrals, jnp.zeros_like(integrals))
    int_wide = int_kept.astype(jnp.float32)

    def one_orbital(inputs):
        amp_block, batch_label = inputs
        keep_amp = parity(batch_label, occ_irrep[:, None, None], vir_irrep[None, :, None], vir_irrep[None, None, :]) == 0
        amp_kept = jnp.where(keep_amp, amp_block, jnp.zeros_like(amp_block))
        return lax.dot_general(int_wide, amp_kept.astype(jnp.float32), (((0, 1), (0, 2)), ((), ())), precision=lax.Precision.HIGHEST)

    cycle_rows = lax.map(one_orbital, (amplitudes, occ_irrep[:NI]))
    cycle_all = jnp.transpose(cycle_rows, (1, 0, 2))
    denominator = occ_energy[:NI][None, :, None] + occ_energy[NI] - vir_energy[None, None, :] - vir_energy[:, None, None]
    return cycle_all / denominator
```

```python
import jax
import jax.numpy as jnp
from jax import lax
from jax.experimental import pallas as pl
from jax.experimental.pallas import tpu as pltpu
from jax.sharding import PartitionSpec as P

FOLD = 256
K_STEP = 5


def folded_integrals(integrals, occ_local, vir_local, vir_irrep, pair_label, screen_rows):
    irrep_codes = jnp.arange(8, dtype=jnp.int32)
    screen_local = jnp.sum(
        screen_rows[:, None, :] * (vir_local[None, :, None] == irrep_codes).astype(jnp.int32),
        axis=2,
    )
    target = jnp.bitwise_xor(
        jnp.bitwise_xor(occ_local[:, None], vir_local[None, :]), pair_label
    )
    target = jnp.where(screen_local == 1, target, -1)
    keep = target[:, :, None] == vir_irrep[None, None, :]
    kept = jnp.where(keep, integrals, jnp.zeros_like(integrals))
    return kept[:, :, :FOLD] + kept[:, :, FOLD:]


def shard_product_kernel(
    block_ref, label_ref, amp_ref, int_ref, left_ref, right_ref, total_in_ref, total_ref, mix_ref
):
    step = pl.program_id(0)

    @pl.when(step == 0)
    def _():
        total_ref[...] = total_in_ref[...]
        mixed = jnp.bitwise_xor(left_ref[...], right_ref[...])
        mix_ref[...] = mixed.astype(jnp.float32).astype(jnp.bfloat16)

    rows = amp_ref.shape[0] * amp_ref.shape[2]
    mixed = mix_ref[...]
    pieces = []
    for j in range(amp_ref.shape[1]):
        label = label_ref[step * amp_ref.shape[1] + j].astype(jnp.float32)
        tile = amp_ref[:, j].reshape(rows, amp_ref.shape[3])
        wanted = jnp.full(mixed.shape, label, jnp.float32).astype(jnp.bfloat16)
        pieces.append(jnp.where(mixed == wanted, tile, jnp.zeros_like(tile)))
    lhs = jnp.concatenate(pieces, axis=1)
    rhs = int_ref[...].reshape(-1, int_ref.shape[2])
    total_ref[...] += jnp.dot(lhs, rhs, preferred_element_type=jnp.float32)


def shard_product(total, amplitudes, fold, block, labels, k_start, row_labels, col_labels):
    batch, _, share, _ = amplitudes.shape
    k_count, depth, width = fold.shape
    first = k_start // K_STEP
    rows = batch * share
    return pl.pallas_call(
        shard_product_kernel,
        grid_spec=pltpu.PrefetchScalarGridSpec(
            num_scalar_prefetch=2,
            grid=(k_count // K_STEP,),
            in_specs=[
                pl.BlockSpec((batch, K_STEP, share, depth), lambda k, s, l: (0, first + k, 0, s[0])),
                pl.BlockSpec((K_STEP, depth, width), lambda k, s, l: (k, 0, 0)),
                pl.BlockSpec((rows, 1), lambda k, s, l: (0, 0)),
                pl.BlockSpec((1, depth), lambda k, s, l: (0, s[0])),
                pl.BlockSpec((rows, width), lambda k, s, l: (0, 0)),
            ],
            out_specs=pl.BlockSpec((rows, width), lambda k, s, l: (0, 0)),
            scratch_shapes=[pltpu.VMEM((rows, depth), jnp.bfloat16)],
        ),
        out_shape=jax.ShapeDtypeStruct((rows, width), jnp.float32),
        input_output_aliases={6: 0},
        compiler_params=pltpu.CompilerParams(vmem_limit_bytes=32 * 1024 * 1024),
    )(block, labels, amplitudes, fold, row_labels, col_labels, total)


def finish(cycle, occ_irrep, vir_irrep, occ_energy, vir_energy, a_start, a_size, b_start, b_size, batch):
    label_a = lax.dynamic_slice_in_dim(vir_irrep, a_start, a_size)
    label_b = lax.dynamic_slice_in_dim(vir_irrep, b_start, b_size)
    energy_a = lax.dynamic_slice_in_dim(vir_energy, a_start, a_size)
    energy_b = lax.dynamic_slice_in_dim(vir_energy, b_start, b_size)
    target = jnp.bitwise_xor(
        jnp.bitwise_xor(occ_irrep[:batch, None], occ_irrep[batch]), label_a[None, :]
    )
    keep = label_b[:, None, None] == target[None, :, :]
    denominator = (
        occ_energy[:batch][None, :, None]
        + occ_energy[batch]
        - energy_a[None, None, :]
        - energy_b[:, None, None]
    )
    swapped = jnp.transpose(cycle, (2, 0, 1))
    return jnp.where(keep, swapped, 0.0) / denominator


def on_square(amplitudes, fold, occ_irrep, occ_local, vir_local, vir_irrep):
    rows_n = lax.axis_size("row")
    batch, occ_share, share, _ = amplitudes.shape
    row = lax.axis_index("row")
    col = lax.axis_index("col")
    row_labels = jnp.bitwise_xor(occ_irrep[:batch, None], vir_local[None, :]).reshape(-1, 1)
    col_labels = vir_irrep[None, :]
    chunks = [(0, 15), (15, occ_share)]
    total = jnp.zeros((batch * share, FOLD), jnp.float32)

    def add(total, part, source, chunk):
        block = jnp.clip(source, 0, rows_n - 1).astype(jnp.int32).reshape(1)
        return shard_product(
            total, amplitudes, part, block, occ_local[chunk[0]:chunk[1]], chunk[0], row_labels, col_labels
        )

    own = [fold[lo:hi] for lo, hi in chunks]
    rightward = [(i, i + 1) for i in range(rows_n - 1)]
    leftward = [(i + 1, i) for i in range(rows_n - 1)]
    from_left, from_right = own, own
    for distance in range(rows_n):
        if distance:
            from_left = [lax.ppermute(v, "row", rightward) for v in from_left]
            from_right = [lax.ppermute(v, "row", leftward) for v in from_right]
        for n, chunk in enumerate(chunks):
            total = add(total, from_left[n], row - distance, chunk)
            if distance:
                total = add(total, from_right[n], row + distance, chunk)
    half = col % 2
    chip = col // 2
    width = FOLD // 2
    total = total.reshape(batch, share, FOLD)
    kept = lax.dynamic_slice_in_dim(total, half * width, width, 2)
    sent = lax.dynamic_slice_in_dim(total, (1 - half) * width, width, 2)
    kept = kept + lax.ppermute(sent, "col", [(q, q ^ 1) for q in range(4)])
    pair = batch // 2
    mine = lax.dynamic_slice_in_dim(kept, chip * pair, pair, 0)
    sent = lax.dynamic_slice_in_dim(kept, (1 - chip) * pair, pair, 0)
    mine = mine + lax.ppermute(sent, "col", [(q, q ^ 2) for q in range(4)])
    places = [(r, q) for r in range(4) for q in range(4)]
    same = lax.ppermute(mine, ("row", "col"), [(r * 4 + q, q * 4 + r) for r, q in places])
    other = lax.ppermute(mine, ("row", "col"), [(r * 4 + q, (q ^ 2) * 4 + r) for r, q in places])
    upper = row // 2 == 1
    low = jnp.where(upper, other, same)
    high = jnp.where(upper, same, other)
    return jnp.concatenate([low, high], axis=0)


def on_any(amplitudes, fold, occ_irrep, occ_local, vir_local, vir_irrep):
    batch, _, share, vir_total = amplitudes.shape
    keep = (
        jnp.bitwise_xor(occ_irrep[:batch, None], occ_local[None, :])[:, :, None, None]
        == jnp.bitwise_xor(vir_local[:, None], vir_irrep[None, :])[None, None]
    )
    kept = jnp.where(keep, amplitudes, jnp.zeros_like(amplitudes))
    whole = lax.all_gather(fold, "row", axis=1, tiled=True)
    cycle = lax.dot_general(
        kept, whole, (((1, 3), (0, 1)), ((), ())), preferred_element_type=jnp.float32
    )
    cycle = lax.psum(cycle, "col")
    cycle = jnp.concatenate([cycle] * (vir_total // FOLD), axis=2)
    cycle = lax.all_to_all(cycle, "row", split_axis=2, concat_axis=1, tiled=True)
    a_size = vir_total // lax.axis_size("col")
    return lax.dynamic_slice_in_dim(cycle, lax.axis_index("col") * a_size, a_size, 1)


def on_device(amplitudes, integrals, occ_irrep, vir_irrep, screen, occ_energy, vir_energy):
    batch, occ_share, vir_share, vir_total = amplitudes.shape
    row = lax.axis_index("row")
    col = lax.axis_index("col")
    occ_local = lax.dynamic_slice_in_dim(occ_irrep, col * occ_share, occ_share)
    vir_local = lax.dynamic_slice_in_dim(vir_irrep, row * vir_share, vir_share)
    screen_rows = lax.dynamic_slice_in_dim(screen, col * occ_share, occ_share, 0)
    fold = folded_integrals(
        integrals, occ_local, vir_local, vir_irrep, occ_irrep[batch], screen_rows
    )
    square = lax.axis_size("row") == 4 and lax.axis_size("col") == 4
    form = on_square if square else on_any
    cycle = form(amplitudes, fold, occ_irrep, occ_local, vir_local, vir_irrep)
    a_size = vir_total // lax.axis_size("col")
    return finish(
        cycle, occ_irrep, vir_irrep, occ_energy, vir_energy,
        col * a_size, a_size, row * vir_share, vir_share, batch,
    )


def solution(mesh):
    in_specs = (
        P("parts", "col", "row", None),
        P(("parts", "col"), "row", None),
        P("parts"),
        P("parts"),
        P("parts", None),
        P("parts"),
        P("parts"),
    )
    out_specs = P("row", "parts", "col")
    return jax.shard_map(
        on_device, mesh=mesh, in_specs=in_specs, out_specs=out_specs, check_vma=False
    )
```

```python
import jax
import jax.numpy as jnp
from jax import lax
from jax.experimental import pallas as pl
from jax.experimental.pallas import tpu as pltpu
from jax.sharding import PartitionSpec as P

FOLD = 256
K_STEP = 5


def folded_integrals(integrals, occ_local, vir_local, vir_irrep, pair_label, screen_rows):
    irrep_codes = jnp.arange(8, dtype=jnp.int32)
    screen_local = jnp.sum(
        screen_rows[:, None, :] * (vir_local[None, :, None] == irrep_codes).astype(jnp.int32),
        axis=2,
    )
    target = jnp.bitwise_xor(
        jnp.bitwise_xor(occ_local[:, None], vir_local[None, :]), pair_label
    )
    target = jnp.where(screen_local == 1, target, -1)
    keep = target[:, :, None] == vir_irrep[None, None, :]
    kept = jnp.where(keep, integrals, jnp.zeros_like(integrals))
    return kept[:, :, :FOLD] + kept[:, :, FOLD:]


def shard_product_kernel(block_ref, valid_ref, label_ref, amp_ref, *refs):
    sides = len(refs) - 5
    int_refs = refs[:sides]
    left_ref, right_ref, total_in_ref, total_ref, mix_ref = refs[sides:]
    step = pl.program_id(0)
    steps = pl.num_programs(0) // sides
    k_step = amp_ref.shape[1]
    rows = amp_ref.shape[0] * amp_ref.shape[2]

    @pl.when(step == 0)
    def _():
        total_ref[...] = total_in_ref[...]

    for side in range(sides):
        local = step - side * steps

        @pl.when((local == 0) & (valid_ref[side] == 1))
        def _():
            mixed = jnp.bitwise_xor(left_ref[...], right_ref[...])
            mix_ref[...] = mixed.astype(jnp.float32).astype(jnp.bfloat16)

        @pl.when((local >= 0) & (local < steps) & (valid_ref[side] == 1))
        def _(local=local, int_ref=int_refs[side]):
            mixed = mix_ref[...]
            pieces = []
            for j in range(k_step):
                label = label_ref[local * k_step + j].astype(jnp.float32)
                tile = amp_ref[:, j].reshape(rows, amp_ref.shape[3])
                wanted = jnp.full(mixed.shape, label, jnp.float32).astype(jnp.bfloat16)
                pieces.append(jnp.where(mixed == wanted, tile, jnp.zeros_like(tile)))
            lhs = jnp.concatenate(pieces, axis=1)
            rhs = int_ref[...].reshape(-1, int_ref.shape[2])
            total_ref[...] += jnp.dot(lhs, rhs, preferred_element_type=jnp.float32)


def shard_product(total, amplitudes, folds, sources, source_count, labels, k_start, row_labels, col_labels):
    batch, _, share, _ = amplitudes.shape
    k_count, depth, width = folds[0].shape
    first = k_start // K_STEP
    rows = batch * share
    steps = k_count // K_STEP
    sides = len(folds)
    sources = jnp.stack(sources).astype(jnp.int32)
    valid = ((sources >= 0) & (sources < source_count)).astype(jnp.int32)
    blocks = jnp.clip(sources, 0, source_count - 1)

    def amp_map(g, s, v, l):
        return (0, first + g % steps, 0, s[g // steps])

    def int_map(side):
        return lambda g, s, v, l: (jnp.clip(g - side * steps, 0, steps - 1), 0, 0)

    return pl.pallas_call(
        shard_product_kernel,
        grid_spec=pltpu.PrefetchScalarGridSpec(
            num_scalar_prefetch=3,
            grid=(sides * steps,),
            in_specs=[pl.BlockSpec((batch, K_STEP, share, depth), amp_map)]
            + [pl.BlockSpec((K_STEP, depth, width), int_map(side)) for side in range(sides)]
            + [
                pl.BlockSpec((rows, 1), lambda g, s, v, l: (0, 0)),
                pl.BlockSpec((1, depth), lambda g, s, v, l: (0, s[g // steps])),
                pl.BlockSpec((rows, width), lambda g, s, v, l: (0, 0)),
            ],
            out_specs=pl.BlockSpec((rows, width), lambda g, s, v, l: (0, 0)),
            scratch_shapes=[pltpu.VMEM((rows, depth), jnp.bfloat16)],
        ),
        out_shape=jax.ShapeDtypeStruct((rows, width), jnp.float32),
        input_output_aliases={6 + sides: 0},
        compiler_params=pltpu.CompilerParams(vmem_limit_bytes=32 * 1024 * 1024),
    )(blocks, valid, labels, amplitudes, *folds, row_labels, col_labels, total)


def finish(cycle, occ_irrep, vir_irrep, occ_energy, vir_energy, a_start, a_size, b_start, b_size, batch):
    label_a = lax.dynamic_slice_in_dim(vir_irrep, a_start, a_size)
    label_b = lax.dynamic_slice_in_dim(vir_irrep, b_start, b_size)
    energy_a = lax.dynamic_slice_in_dim(vir_energy, a_start, a_size)
    energy_b = lax.dynamic_slice_in_dim(vir_energy, b_start, b_size)
    target = jnp.bitwise_xor(
        jnp.bitwise_xor(occ_irrep[:batch, None], occ_irrep[batch]), label_a[None, :]
    )
    keep = label_b[:, None, None] == target[None, :, :]
    denominator = (
        occ_energy[:batch][None, :, None]
        + occ_energy[batch]
        - energy_a[None, None, :]
        - energy_b[:, None, None]
    )
    swapped = jnp.transpose(cycle, (2, 0, 1))
    return jnp.where(keep, swapped, 0.0) / denominator


def on_square(amplitudes, fold, occ_irrep, occ_local, vir_local, vir_irrep):
    rows_n = lax.axis_size("row")
    batch, occ_share, share, _ = amplitudes.shape
    row = lax.axis_index("row")
    col = lax.axis_index("col")
    row_labels = jnp.bitwise_xor(occ_irrep[:batch, None], vir_local[None, :]).reshape(-1, 1)
    col_labels = vir_irrep[None, :]
    chunks = [(0, 15), (15, occ_share)]
    total = jnp.zeros((batch * share, FOLD), jnp.float32)

    def add(total, parts, sources, chunk):
        return shard_product(
            total, amplitudes, parts, sources, rows_n, occ_local[chunk[0]:chunk[1]], chunk[0],
            row_labels, col_labels,
        )

    own = [fold[lo:hi] for lo, hi in chunks]
    rightward = [(i, i + 1) for i in range(rows_n - 1)]
    leftward = [(i + 1, i) for i in range(rows_n - 1)]
    held = [((v, v), (v,), (row,)) for v in own]
    for distance in range(1, rows_n + 1):
        for n, chunk in enumerate(chunks):
            (left, right), parts, sources = held[n]
            if distance < rows_n:
                left = lax.ppermute(left, "row", rightward)
                right = lax.ppermute(right, "row", leftward)
            total = add(total, parts, sources, chunk)
            if distance < rows_n:
                left, right, _ = lax.optimization_barrier((left, right, total))
            held[n] = ((left, right), (left, right), (row - distance, row + distance))
    half = col % 2
    chip = col // 2
    width = FOLD // 2
    total = total.reshape(batch, share, FOLD)
    kept = lax.dynamic_slice_in_dim(total, half * width, width, 2)
    sent = lax.dynamic_slice_in_dim(total, (1 - half) * width, width, 2)
    kept = kept + lax.ppermute(sent, "col", [(q, q ^ 1) for q in range(4)])
    pair = batch // 2
    mine = lax.dynamic_slice_in_dim(kept, chip * pair, pair, 0)
    sent = lax.dynamic_slice_in_dim(kept, (1 - chip) * pair, pair, 0)
    mine = mine + lax.ppermute(sent, "col", [(q, q ^ 2) for q in range(4)])
    places = [(r, q) for r in range(4) for q in range(4)]
    same = lax.ppermute(mine, ("row", "col"), [(r * 4 + q, q * 4 + r) for r, q in places])
    other = lax.ppermute(mine, ("row", "col"), [(r * 4 + q, (q ^ 2) * 4 + r) for r, q in places])
    upper = row // 2 == 1
    low = jnp.where(upper, other, same)
    high = jnp.where(upper, same, other)
    return jnp.concatenate([low, high], axis=0)


def on_any(amplitudes, fold, occ_irrep, occ_local, vir_local, vir_irrep):
    batch, _, share, vir_total = amplitudes.shape
    keep = (
        jnp.bitwise_xor(occ_irrep[:batch, None], occ_local[None, :])[:, :, None, None]
        == jnp.bitwise_xor(vir_local[:, None], vir_irrep[None, :])[None, None]
    )
    kept = jnp.where(keep, amplitudes, jnp.zeros_like(amplitudes))
    whole = lax.all_gather(fold, "row", axis=1, tiled=True)
    cycle = lax.dot_general(
        kept, whole, (((1, 3), (0, 1)), ((), ())), preferred_element_type=jnp.float32
    )
    cycle = lax.psum(cycle, "col")
    cycle = jnp.concatenate([cycle] * (vir_total // FOLD), axis=2)
    cycle = lax.all_to_all(cycle, "row", split_axis=2, concat_axis=1, tiled=True)
    a_size = vir_total // lax.axis_size("col")
    return lax.dynamic_slice_in_dim(cycle, lax.axis_index("col") * a_size, a_size, 1)


def on_device(amplitudes, integrals, occ_irrep, vir_irrep, screen, occ_energy, vir_energy):
    batch, occ_share, vir_share, vir_total = amplitudes.shape
    row = lax.axis_index("row")
    col = lax.axis_index("col")
    occ_local = lax.dynamic_slice_in_dim(occ_irrep, col * occ_share, occ_share)
    vir_local = lax.dynamic_slice_in_dim(vir_irrep, row * vir_share, vir_share)
    screen_rows = lax.dynamic_slice_in_dim(screen, col * occ_share, occ_share, 0)
    fold = folded_integrals(
        integrals, occ_local, vir_local, vir_irrep, occ_irrep[batch], screen_rows
    )
    square = lax.axis_size("row") == 4 and lax.axis_size("col") == 4
    form = on_square if square else on_any
    cycle = form(amplitudes, fold, occ_irrep, occ_local, vir_local, vir_irrep)
    a_size = vir_total // lax.axis_size("col")
    return finish(
        cycle, occ_irrep, vir_irrep, occ_energy, vir_energy,
        col * a_size, a_size, row * vir_share, vir_share, batch,
    )


def solution(mesh):
    in_specs = (
        P("parts", "col", "row", None),
        P(("parts", "col"), "row", None),
        P("parts"),
        P("parts"),
        P("parts", None),
        P("parts"),
        P("parts"),
    )
    out_specs = P("row", "parts", "col")
    return jax.shard_map(
        on_device, mesh=mesh, in_specs=in_specs, out_specs=out_specs, check_vma=False
    )
```

```python
import jax
import jax.numpy as jnp
from jax import lax
from jax.experimental import pallas as pl
from jax.experimental.pallas import tpu as pltpu
from jax.sharding import PartitionSpec as P

FOLD = 256
K_STEP = 5


def folded_integrals(integrals, occ_local, vir_local, vir_irrep, pair_label, screen_rows):
    irrep_codes = jnp.arange(8, dtype=jnp.int32)
    screen_local = jnp.sum(
        screen_rows[:, None, :] * (vir_local[None, :, None] == irrep_codes).astype(jnp.int32),
        axis=2,
    )
    target = jnp.bitwise_xor(
        jnp.bitwise_xor(occ_local[:, None], vir_local[None, :]), pair_label
    )
    target = jnp.where(screen_local == 1, target, -1)
    keep = target[:, :, None] == vir_irrep[None, None, :]
    kept = jnp.where(keep, integrals, jnp.zeros_like(integrals))
    return kept[:, :, :FOLD] + kept[:, :, FOLD:]


def shard_product_kernel(block_ref, valid_ref, label_ref, amp_ref, *refs):
    sides = len(refs) - 5
    int_refs = refs[:sides]
    left_ref, right_ref, total_in_ref, total_ref, mix_ref = refs[sides:]
    step = pl.program_id(0)
    steps = pl.num_programs(0) // sides
    k_step = amp_ref.shape[1]
    rows = amp_ref.shape[0] * amp_ref.shape[2]

    @pl.when(step == 0)
    def _():
        total_ref[...] = total_in_ref[...]

    for side in range(sides):
        local = step - side * steps

        @pl.when((local == 0) & (valid_ref[side] == 1))
        def _():
            mixed = jnp.bitwise_xor(left_ref[...], right_ref[...])
            mix_ref[...] = mixed.astype(jnp.float32).astype(jnp.bfloat16)

        @pl.when((local >= 0) & (local < steps) & (valid_ref[side] == 1))
        def _(local=local, int_ref=int_refs[side]):
            mixed = mix_ref[...]
            pieces = []
            for j in range(k_step):
                label = label_ref[local * k_step + j].astype(jnp.float32)
                tile = amp_ref[:, j].reshape(rows, amp_ref.shape[3])
                wanted = jnp.full(mixed.shape, label, jnp.float32).astype(jnp.bfloat16)
                pieces.append(jnp.where(mixed == wanted, tile, jnp.zeros_like(tile)))
            lhs = jnp.concatenate(pieces, axis=1)
            rhs = int_ref[...].reshape(-1, int_ref.shape[2])
            total_ref[...] += jnp.dot(lhs, rhs, preferred_element_type=jnp.float32)


def shard_product(total, amplitudes, folds, sources, source_count, labels, k_start, row_labels, col_labels):
    batch, _, share, _ = amplitudes.shape
    k_count, depth, width = folds[0].shape
    first = k_start // K_STEP
    rows = batch * share
    steps = k_count // K_STEP
    sides = len(folds)
    sources = jnp.stack(sources).astype(jnp.int32)
    valid = ((sources >= 0) & (sources < source_count)).astype(jnp.int32)
    blocks = jnp.clip(sources, 0, source_count - 1)

    def amp_map(g, s, v, l):
        return (0, first + g % steps, 0, s[g // steps])

    def int_map(side):
        return lambda g, s, v, l: (jnp.clip(g - side * steps, 0, steps - 1), 0, 0)

    return pl.pallas_call(
        shard_product_kernel,
        grid_spec=pltpu.PrefetchScalarGridSpec(
            num_scalar_prefetch=3,
            grid=(sides * steps,),
            in_specs=[pl.BlockSpec((batch, K_STEP, share, depth), amp_map)]
            + [pl.BlockSpec((K_STEP, depth, width), int_map(side)) for side in range(sides)]
            + [
                pl.BlockSpec((rows, 1), lambda g, s, v, l: (0, 0)),
                pl.BlockSpec((1, depth), lambda g, s, v, l: (0, s[g // steps])),
                pl.BlockSpec((rows, width), lambda g, s, v, l: (0, 0)),
            ],
            out_specs=pl.BlockSpec((rows, width), lambda g, s, v, l: (0, 0)),
            scratch_shapes=[pltpu.VMEM((rows, depth), jnp.bfloat16)],
        ),
        out_shape=jax.ShapeDtypeStruct((rows, width), jnp.float32),
        input_output_aliases={6 + sides: 0},
        compiler_params=pltpu.CompilerParams(vmem_limit_bytes=32 * 1024 * 1024),
    )(blocks, valid, labels, amplitudes, *folds, row_labels, col_labels, total)


NARROW = 64
CHUNKS = (10, 15)


def pack_kernel(
    x_ref, bits_ref, pos2_ref, pos3_ref, big_ref, int_ref, col_ref, row_ref,
    narrow_ref, m2a_ref, m2b_ref, m3a_ref, m3b_ref, mix_ref, spread_ref,
):
    step = pl.program_id(0)
    depth, total = mix_ref.shape
    half = depth // 2

    @pl.when(step == 0)
    def _():
        mixed = jnp.bitwise_xor(col_ref[...], row_ref[...])
        mix_ref[...] = mixed.astype(jnp.float32).astype(jnp.bfloat16)
        b = lax.broadcasted_iota(jnp.int32, spread_ref.shape, 0)
        lane = lax.broadcasted_iota(jnp.int32, spread_ref.shape, 1)
        lane_b = lane - 2 * NARROW
        is_big = jnp.transpose(jnp.broadcast_to(row_ref[...], (8, total)))[:, :1] == big_ref[0]
        narrow = (lane < 2 * NARROW) & (b % NARROW == lane % NARROW) & jnp.logical_not(is_big)
        wide = (lane >= 2 * NARROW) & (b % FOLD == lane_b) & is_big
        spread_ref[...] = jnp.where(narrow | wide, 1.0, 0.0).astype(jnp.bfloat16)

    lane = lax.broadcasted_iota(jnp.int32, (half, 2 * NARROW), 1)
    for j in range(int_ref.shape[0]):
        k = step * int_ref.shape[0] + j
        on = jnp.bitwise_and(lax.shift_right_logical(jnp.full((depth, 1), bits_ref[k]), col_ref[...]), 1)
        wanted = jnp.where(on == 1, x_ref[k], -1).astype(jnp.float32)
        wanted = jnp.broadcast_to(wanted, mix_ref.shape).astype(jnp.bfloat16)
        tile = int_ref[j]
        kept = jnp.where(mix_ref[...] == wanted, tile, jnp.zeros_like(tile))
        folded = jnp.dot(kept, spread_ref[...], preferred_element_type=jnp.float32)
        left, right = folded[:half, : 2 * NARROW], folded[half:, : 2 * NARROW]
        narrow_ref[j] = jnp.where(lane < NARROW, left, right).astype(jnp.bfloat16)
        wide = folded[:, 2 * NARROW:]
        pos2, pos3 = pos2_ref[k], pos3_ref[k]
        short = (wide[:half] + wide[half:]).astype(jnp.bfloat16)
        wide = wide.astype(jnp.bfloat16)

        @pl.when((pos2 >= 0) & (pos2 < CHUNKS[0]))
        def _():
            m2a_ref[pos2] = short

        @pl.when(pos2 >= CHUNKS[0])
        def _():
            m2b_ref[pos2 - CHUNKS[0]] = short

        @pl.when((pos3 >= 0) & (pos3 < CHUNKS[0]))
        def _():
            m3a_ref[pos3] = wide

        @pl.when(pos3 >= CHUNKS[0])
        def _():
            m3b_ref[pos3 - CHUNKS[0]] = wide


def pack(integrals, x, bits, pos2, pos3, big, vir_local, vir_irrep):
    occ_share, depth, total = integrals.shape
    short = [(n, depth // 2, FOLD) for n in CHUNKS]
    wide = [(n, depth, FOLD) for n in CHUNKS]
    shapes = [(occ_share, depth // 2, 2 * NARROW)] + short + wide
    fixed = lambda k, *_: (0, 0, 0)
    return pl.pallas_call(
        pack_kernel,
        grid_spec=pltpu.PrefetchScalarGridSpec(
            num_scalar_prefetch=5,
            grid=(occ_share // K_STEP,),
            in_specs=[
                pl.BlockSpec((K_STEP, depth, total), lambda k, *_: (k, 0, 0)),
                pl.BlockSpec((depth, 1), lambda k, *_: (0, 0)),
                pl.BlockSpec((1, total), lambda k, *_: (0, 0)),
            ],
            out_specs=[pl.BlockSpec((K_STEP, depth // 2, 2 * NARROW), lambda k, *_: (k, 0, 0))]
            + [pl.BlockSpec(v, fixed) for v in shapes[1:]],
            scratch_shapes=[
                pltpu.VMEM((depth, total), jnp.bfloat16),
                pltpu.VMEM((total, 2 * NARROW + FOLD), jnp.bfloat16),
            ],
        ),
        out_shape=[jax.ShapeDtypeStruct(v, jnp.bfloat16) for v in shapes],
        compiler_params=pltpu.CompilerParams(vmem_limit_bytes=32 * 1024 * 1024),
    )(x, bits, pos2, pos3, big, integrals, vir_local[:, None], vir_irrep[None, :])


def make_sparse_kernel(n2, n3):
    def kernel(label_ref, pos2_ref, pos3_ref, info_ref, amp_ref, row_ref, col_ref, big_ref, *refs):
        narrow_refs = refs[:6]
        m2_refs = refs[6:6 + n2]
        m3_refs = [refs[6 + n2 + 5 * n:11 + n2 + 5 * n] for n in range(n3)]
        out_ref, mix_ref, narrow_sum, wide_sum, buffer, sems = refs[6 + n2 + 5 * n3:]
        batch, k_all, share, total = amp_ref.shape
        rows = batch * share
        groups = k_all // K_STEP
        at_end = info_ref[0] == 1
        has_big, has_small = info_ref[1] == 1, info_ref[2] == 1

        def fetch(group, slot):
            return pltpu.make_async_copy(
                amp_ref.at[:, pl.ds(group * K_STEP, K_STEP)], buffer.at[slot], sems.at[slot]
            )

        fetch(0, 0).start()
        mixed = jnp.bitwise_xor(row_ref[...], col_ref[...])
        mix_ref[...] = mixed.astype(jnp.float32).astype(jnp.bfloat16)
        narrow_sum[...] = jnp.zeros(narrow_sum.shape, jnp.float32)
        wide_sum[...] = jnp.zeros(wide_sum.shape, jnp.float32)
        lane = lax.broadcasted_iota(jnp.int32, (share // 2, 2 * NARROW), 1)

        @pl.loop(0, groups)
        def _(group):
            slot = group % 2

            @pl.when(group + 1 < groups)
            def _():
                fetch(group + 1, 1 - slot).start()

            fetch(group, slot).wait()
            for j in range(K_STEP):
                k = group * K_STEP + j
                label = label_ref[k].astype(jnp.float32)
                pieces = []
                for s in range(4):
                    place = pl.ds(pl.multiple_of(info_ref[3 + s] * share, share), share)
                    tile = buffer[slot, :, j, :, place].reshape(rows, share)
                    wanted = jnp.full((rows, share), label, jnp.float32).astype(jnp.bfloat16)
                    pieces.append(jnp.where(mix_ref[:, place] == wanted, tile, jnp.zeros_like(tile)))
                lhs = jnp.concatenate(pieces, axis=1)

                @pl.when(has_small)
                def _():
                    own, e1, e2, e3, o1, o2 = [r[k] for r in narrow_refs]
                    blocks = (own, e1, jnp.where(at_end, e2, o1), jnp.where(at_end, e3, o2))
                    rhs = []
                    for block in blocks:
                        zero = jnp.zeros_like(block)
                        rhs += [jnp.where(lane < NARROW, block, zero), jnp.where(lane < NARROW, zero, block)]
                    narrow_sum[...] += jnp.dot(
                        lhs, jnp.concatenate(rhs, axis=0), preferred_element_type=jnp.float32
                    )

                pos2, pos3 = pos2_ref[k], pos3_ref[k]
                for n in range(n2):
                    first = CHUNKS[0] * n

                    @pl.when(has_big & (pos2 >= first) & (pos2 < first + CHUNKS[n]))
                    def _(n=n, first=first):
                        short = m2_refs[n][pos2 - first]
                        wide_sum[...] += jnp.dot(
                            pieces[0] + pieces[1] + pieces[2] + pieces[3],
                            jnp.concatenate([short, short], axis=0),
                            preferred_element_type=jnp.float32,
                        )

                for n in range(n3):
                    first = CHUNKS[0] * n

                    @pl.when(has_big & (pos3 >= first) & (pos3 < first + CHUNKS[n]))
                    def _(n=n, first=first):
                        own, e1, o1, e2, o2 = [r[pos3 - first] for r in m3_refs[n]]
                        blocks = [own, e1, jnp.where(at_end, e2, o1), jnp.where(at_end, jnp.zeros_like(o2), o2)]
                        wide_sum[...] += jnp.dot(
                            lhs, jnp.concatenate(blocks, axis=0), preferred_element_type=jnp.float32
                        )

        both = narrow_sum[...]
        both = both + pltpu.roll(both, NARROW, 1)
        out_ref[...] = jnp.where(
            big_ref[...] == 1, wide_sum[...], jnp.concatenate([both] * (FOLD // (2 * NARROW)), axis=1)
        )

    return kernel


def sparse_product(amplitudes, labels, pos2, pos3, info, row_labels, col_labels, row_big, narrow, m2, m3):
    batch, _, share, total = amplitudes.shape
    rows = batch * share
    vmem = pl.BlockSpec(memory_space=pltpu.VMEM)
    smem = pl.BlockSpec(memory_space=pltpu.SMEM)
    arrays = list(narrow) + list(m2) + [v for group in m3 for v in group]
    return pl.pallas_call(
        make_sparse_kernel(len(m2), len(m3)),
        in_specs=[smem] * 4 + [pl.BlockSpec(memory_space=pltpu.HBM)] + [vmem] * (3 + len(arrays)),
        out_specs=vmem,
        out_shape=jax.ShapeDtypeStruct((rows, FOLD), jnp.float32),
        scratch_shapes=[
            pltpu.VMEM((rows, total), jnp.bfloat16),
            pltpu.VMEM((rows, 2 * NARROW), jnp.float32),
            pltpu.VMEM((rows, FOLD), jnp.float32),
            pltpu.VMEM((2, batch, K_STEP, share, total), jnp.bfloat16),
            pltpu.SemaphoreType.DMA((2,)),
        ],
        compiler_params=pltpu.CompilerParams(vmem_limit_bytes=48 * 1024 * 1024),
    )(labels, pos2, pos3, info, amplitudes, row_labels, col_labels, row_big, *arrays)


def finish(cycle, occ_irrep, vir_irrep, occ_energy, vir_energy, a_start, a_size, b_start, b_size, batch):
    label_a = lax.dynamic_slice_in_dim(vir_irrep, a_start, a_size)
    label_b = lax.dynamic_slice_in_dim(vir_irrep, b_start, b_size)
    energy_a = lax.dynamic_slice_in_dim(vir_energy, a_start, a_size)
    energy_b = lax.dynamic_slice_in_dim(vir_energy, b_start, b_size)
    target = jnp.bitwise_xor(
        jnp.bitwise_xor(occ_irrep[:batch, None], occ_irrep[batch]), label_a[None, :]
    )
    keep = label_b[:, None, None] == target[None, :, :]
    denominator = (
        occ_energy[:batch][None, :, None]
        + occ_energy[batch]
        - energy_a[None, None, :]
        - energy_b[:, None, None]
    )
    swapped = jnp.transpose(cycle, (2, 0, 1))
    return jnp.where(keep, swapped, 0.0) / denominator


def dense_total(amplitudes, fold, occ_local, row_labels, col_labels, row):
    batch, occ_share, share, _ = amplitudes.shape
    rows_n = 4
    chunks = [(0, 15), (15, occ_share)]
    total = jnp.zeros((batch * share, FOLD), jnp.float32)

    def add(total, parts, sources, chunk):
        return shard_product(
            total, amplitudes, parts, sources, rows_n, occ_local[chunk[0]:chunk[1]], chunk[0],
            row_labels, col_labels,
        )

    own = [fold[lo:hi] for lo, hi in chunks]
    rightward = [(i, i + 1) for i in range(rows_n - 1)]
    leftward = [(i + 1, i) for i in range(rows_n - 1)]
    held = [((v, v), (v,), (row,)) for v in own]
    for distance in range(1, rows_n + 1):
        for n, chunk in enumerate(chunks):
            (left, right), parts, sources = held[n]
            if distance < rows_n:
                left = lax.ppermute(left, "row", rightward)
                right = lax.ppermute(right, "row", leftward)
            total = add(total, parts, sources, chunk)
            if distance < rows_n:
                left, right, _ = lax.optimization_barrier((left, right, total))
            held[n] = ((left, right), (left, right), (row - distance, row + distance))
    return total


def on_square(amplitudes, integrals, occ_irrep, occ_local, vir_local, vir_irrep, screen_rows):
    batch, occ_share, share, vir_total = amplitudes.shape
    row = lax.axis_index("row")
    col = lax.axis_index("col")
    pair_label = occ_irrep[batch]
    row_labels = jnp.bitwise_xor(occ_irrep[:batch, None], vir_local[None, :]).reshape(-1, 1)
    col_labels = vir_irrep[None, :]
    codes = jnp.arange(8, dtype=jnp.int32)
    counts = jnp.sum((vir_irrep[:, None] == codes).astype(jnp.int32), axis=0)
    big = jnp.sum(jnp.where(counts == FOLD, codes, 0))
    x = jnp.bitwise_xor(occ_local, pair_label)
    bits = jnp.sum(jnp.where(screen_rows == 1, jnp.left_shift(1, codes), 0), axis=1)
    on_big = jnp.bitwise_and(jnp.right_shift(bits, jnp.bitwise_xor(big, x)), 1) == 1
    active2 = (on_big & (x != 0)).astype(jnp.int32)
    active3 = (on_big & (x == 0)).astype(jnp.int32)
    earlier = jnp.arange(occ_share)[None, :] < jnp.arange(occ_share)[:, None]
    place2 = jnp.sum(jnp.where(earlier, active2[None, :], 0), axis=1)
    place3 = jnp.sum(jnp.where(earlier, active3[None, :], 0), axis=1)
    pos2 = jnp.where(active2 == 1, place2, -1)
    pos3 = jnp.where(active3 == 1, place3, -1)
    count2, count3 = jnp.sum(active2), jnp.sum(active3)
    narrow_ok = jnp.max(jnp.where(codes == big, 0, counts)) <= NARROW
    form = jnp.where(
        count3 == 0, 0, jnp.where(count3 <= CHUNKS[0], 1, jnp.where(count2 <= CHUNKS[0], 2, 3))
    )
    form = jnp.where(narrow_ok, form, 3)
    row_big = (jnp.bitwise_xor(row_labels, pair_label) == big).astype(jnp.int32)
    lower = row < 2
    info = jnp.stack([
        jnp.where((row == 0) | (row == 3), 1, 0),
        jnp.max(row_big),
        1 - jnp.min(row_big),
        row,
        jnp.bitwise_xor(row, 1),
        jnp.where(lower, 2, 1),
        jnp.where(lower, 3, 0),
    ]).astype(jnp.int32)
    narrow, m2a, m2b, m3a, m3b = pack(
        integrals, x, bits, pos2, pos3, big.reshape(1), vir_local, vir_irrep
    )
    outer = [(0, 1), (1, 0), (2, 3), (3, 2)]
    inner = [(1, 2), (2, 1), (0, 0), (3, 3)]

    def move(v, pairs):
        return lax.ppermute(v, "row", pairs)

    def summed(own):
        first = move(own, [(0, 1), (3, 2)])
        second = move(own + first, [(1, 2), (2, 1)])
        third = move(own + second, [(1, 0), (2, 3)])
        return own + first + second + third

    def spread(own):
        e1, o1 = move(own, outer), move(own, inner)
        return e1, o1, move(o1, outer), move(e1, inner)

    def sparse(m2, m3):
        def run(narrow, m2a, m2b, m3a, m3b):
            shorts = [m2a, m2b][:m2]
            wides = [m3a, m3b][:m3]
            e1, o1, e2, o2 = spread(narrow)
            e3 = move(o2, outer)
            wides = [(own,) + spread(own) for own in wides]
            shorts = [summed(own) for own in shorts]
            return sparse_product(
                amplitudes, occ_local, pos2, pos3, info, row_labels, col_labels, row_big,
                (narrow, e1, e2, e3, o1, o2), shorts, wides,
            )

        return run

    def dense(*_):
        fold = folded_integrals(integrals, occ_local, vir_local, vir_irrep, pair_label, screen_rows)
        return dense_total(amplitudes, fold, occ_local, row_labels, col_labels, row)

    total = lax.switch(
        form, [sparse(2, 0), sparse(2, 1), sparse(1, 2), dense], narrow, m2a, m2b, m3a, m3b
    )
    half = col % 2
    chip = col // 2
    width = FOLD // 2
    total = total.reshape(batch, share, FOLD)
    kept = lax.dynamic_slice_in_dim(total, half * width, width, 2)
    sent = lax.dynamic_slice_in_dim(total, (1 - half) * width, width, 2)
    kept = kept + lax.ppermute(sent, "col", [(q, q ^ 1) for q in range(4)])
    pair = batch // 2
    mine = lax.dynamic_slice_in_dim(kept, chip * pair, pair, 0)
    sent = lax.dynamic_slice_in_dim(kept, (1 - chip) * pair, pair, 0)
    mine = mine + lax.ppermute(sent, "col", [(q, q ^ 2) for q in range(4)])
    places = [(r, q) for r in range(4) for q in range(4)]
    same = lax.ppermute(mine, ("row", "col"), [(r * 4 + q, q * 4 + r) for r, q in places])
    other = lax.ppermute(mine, ("row", "col"), [(r * 4 + q, (q ^ 2) * 4 + r) for r, q in places])
    upper = row // 2 == 1
    low = jnp.where(upper, other, same)
    high = jnp.where(upper, same, other)
    return jnp.concatenate([low, high], axis=0)


def on_any(amplitudes, integrals, occ_irrep, occ_local, vir_local, vir_irrep, screen_rows):
    fold = folded_integrals(
        integrals, occ_local, vir_local, vir_irrep, occ_irrep[amplitudes.shape[0]], screen_rows
    )
    batch, _, share, vir_total = amplitudes.shape
    keep = (
        jnp.bitwise_xor(occ_irrep[:batch, None], occ_local[None, :])[:, :, None, None]
        == jnp.bitwise_xor(vir_local[:, None], vir_irrep[None, :])[None, None]
    )
    kept = jnp.where(keep, amplitudes, jnp.zeros_like(amplitudes))
    whole = lax.all_gather(fold, "row", axis=1, tiled=True)
    cycle = lax.dot_general(
        kept, whole, (((1, 3), (0, 1)), ((), ())), preferred_element_type=jnp.float32
    )
    cycle = lax.psum(cycle, "col")
    cycle = jnp.concatenate([cycle] * (vir_total // FOLD), axis=2)
    cycle = lax.all_to_all(cycle, "row", split_axis=2, concat_axis=1, tiled=True)
    a_size = vir_total // lax.axis_size("col")
    return lax.dynamic_slice_in_dim(cycle, lax.axis_index("col") * a_size, a_size, 1)


def on_device(amplitudes, integrals, occ_irrep, vir_irrep, screen, occ_energy, vir_energy):
    batch, occ_share, vir_share, vir_total = amplitudes.shape
    row = lax.axis_index("row")
    col = lax.axis_index("col")
    occ_local = lax.dynamic_slice_in_dim(occ_irrep, col * occ_share, occ_share)
    vir_local = lax.dynamic_slice_in_dim(vir_irrep, row * vir_share, vir_share)
    screen_rows = lax.dynamic_slice_in_dim(screen, col * occ_share, occ_share, 0)
    square = lax.axis_size("row") == 4 and lax.axis_size("col") == 4
    form = on_square if square else on_any
    cycle = form(amplitudes, integrals, occ_irrep, occ_local, vir_local, vir_irrep, screen_rows)
    a_size = vir_total // lax.axis_size("col")
    return finish(
        cycle, occ_irrep, vir_irrep, occ_energy, vir_energy,
        col * a_size, a_size, row * vir_share, vir_share, batch,
    )


def solution(mesh):
    in_specs = (
        P("parts", "col", "row", None),
        P(("parts", "col"), "row", None),
        P("parts"),
        P("parts"),
        P("parts", None),
        P("parts"),
        P("parts"),
    )
    out_specs = P("row", "parts", "col")
    return jax.shard_map(
        on_device, mesh=mesh, in_specs=in_specs, out_specs=out_specs, check_vma=False
    )
```

```python
import jax
import jax.numpy as jnp
from jax import lax
from jax.experimental import pallas as pl
from jax.experimental.pallas import tpu as pltpu
from jax.sharding import PartitionSpec as P

FOLD = 256
K_STEP = 5


def folded_integrals(integrals, occ_local, vir_local, vir_irrep, pair_label, screen_rows):
    irrep_codes = jnp.arange(8, dtype=jnp.int32)
    screen_local = jnp.sum(
        screen_rows[:, None, :] * (vir_local[None, :, None] == irrep_codes).astype(jnp.int32),
        axis=2,
    )
    target = jnp.bitwise_xor(
        jnp.bitwise_xor(occ_local[:, None], vir_local[None, :]), pair_label
    )
    target = jnp.where(screen_local == 1, target, -1)
    keep = target[:, :, None] == vir_irrep[None, None, :]
    kept = jnp.where(keep, integrals, jnp.zeros_like(integrals))
    return kept[:, :, :FOLD] + kept[:, :, FOLD:]


def shard_product_kernel(block_ref, valid_ref, label_ref, amp_ref, *refs):
    sides = len(refs) - 5
    int_refs = refs[:sides]
    left_ref, right_ref, total_in_ref, total_ref, mix_ref = refs[sides:]
    step = pl.program_id(0)
    steps = pl.num_programs(0) // sides
    k_step = amp_ref.shape[1]
    rows = amp_ref.shape[0] * amp_ref.shape[2]

    @pl.when(step == 0)
    def _():
        total_ref[...] = total_in_ref[...]

    for side in range(sides):
        local = step - side * steps

        @pl.when((local == 0) & (valid_ref[side] == 1))
        def _():
            mixed = jnp.bitwise_xor(left_ref[...], right_ref[...])
            mix_ref[...] = mixed.astype(jnp.float32).astype(jnp.bfloat16)

        @pl.when((local >= 0) & (local < steps) & (valid_ref[side] == 1))
        def _(local=local, int_ref=int_refs[side]):
            mixed = mix_ref[...]
            pieces = []
            for j in range(k_step):
                label = label_ref[local * k_step + j].astype(jnp.float32)
                tile = amp_ref[:, j].reshape(rows, amp_ref.shape[3])
                wanted = jnp.full(mixed.shape, label, jnp.float32).astype(jnp.bfloat16)
                pieces.append(jnp.where(mixed == wanted, tile, jnp.zeros_like(tile)))
            lhs = jnp.concatenate(pieces, axis=1)
            rhs = int_ref[...].reshape(-1, int_ref.shape[2])
            total_ref[...] += jnp.dot(lhs, rhs, preferred_element_type=jnp.float32)


def shard_product(total, amplitudes, folds, sources, source_count, labels, k_start, row_labels, col_labels):
    batch, _, share, _ = amplitudes.shape
    k_count, depth, width = folds[0].shape
    first = k_start // K_STEP
    rows = batch * share
    steps = k_count // K_STEP
    sides = len(folds)
    sources = jnp.stack(sources).astype(jnp.int32)
    valid = ((sources >= 0) & (sources < source_count)).astype(jnp.int32)
    blocks = jnp.clip(sources, 0, source_count - 1)

    def amp_map(g, s, v, l):
        return (0, first + g % steps, 0, s[g // steps])

    def int_map(side):
        return lambda g, s, v, l: (jnp.clip(g - side * steps, 0, steps - 1), 0, 0)

    return pl.pallas_call(
        shard_product_kernel,
        grid_spec=pltpu.PrefetchScalarGridSpec(
            num_scalar_prefetch=3,
            grid=(sides * steps,),
            in_specs=[pl.BlockSpec((batch, K_STEP, share, depth), amp_map)]
            + [pl.BlockSpec((K_STEP, depth, width), int_map(side)) for side in range(sides)]
            + [
                pl.BlockSpec((rows, 1), lambda g, s, v, l: (0, 0)),
                pl.BlockSpec((1, depth), lambda g, s, v, l: (0, s[g // steps])),
                pl.BlockSpec((rows, width), lambda g, s, v, l: (0, 0)),
            ],
            out_specs=pl.BlockSpec((rows, width), lambda g, s, v, l: (0, 0)),
            scratch_shapes=[pltpu.VMEM((rows, depth), jnp.bfloat16)],
        ),
        out_shape=jax.ShapeDtypeStruct((rows, width), jnp.float32),
        input_output_aliases={6 + sides: 0},
        compiler_params=pltpu.CompilerParams(vmem_limit_bytes=32 * 1024 * 1024),
    )(blocks, valid, labels, amplitudes, *folds, row_labels, col_labels, total)


NARROW = 64
CAPS = (20, 5)
FEW = 10


def label_columns(row_labels):
    return jnp.transpose(jnp.broadcast_to(row_labels, (8, row_labels.shape[1])))


def pack_kernel(
    occ_ref, vir_ref, screen_ref, place_ref, int_ref, row_ref,
    narrow_ref, m2a_ref, m2b_ref, m3a_ref, m3b_ref, pos2_ref, pos3_ref, form_ref,
    mix_ref, spread_ref, column_ref, counts_ref, pair_at,
):
    step = pl.program_id(0)
    k_step, depth, total = int_ref.shape
    half = depth // 2
    row, col = place_ref[0], place_ref[1]
    pair_label = occ_ref[pair_at]
    big = jnp.where(vir_ref[0] == vir_ref[FOLD - 1], vir_ref[0], vir_ref[FOLD])

    @pl.when(step == 0)
    def _():
        counts_ref[0] = 0
        counts_ref[1] = 0
        column_ref[...] = label_columns(row_ref[...])
        column = column_ref[pl.ds(pl.multiple_of(row * depth, depth), depth), :1]
        mix_ref[...] = jnp.bitwise_xor(column, row_ref[...]).astype(jnp.float32).astype(jnp.bfloat16)
        residue = lax.broadcasted_iota(jnp.int32, spread_ref.shape, 0)
        b = lax.broadcasted_iota(jnp.int32, spread_ref.shape, 1)
        narrow = (b % NARROW == residue) & (row_ref[...] != big)
        spread_ref[...] = jnp.where(narrow, 1.0, 0.0).astype(jnp.bfloat16)

    column = column_ref[pl.ds(pl.multiple_of(row * depth, depth), depth), :1]
    kept = []
    slots = []
    for j in range(k_step):
        k = step * k_step + j
        k_whole = col * (k_step * pl.num_programs(0)) + k
        x = jnp.bitwise_xor(occ_ref[k_whole], pair_label)
        bits = screen_ref[k_whole, 0]
        for g in range(1, 8):
            bits = bits + screen_ref[k_whole, g] * (1 << g)
        on = jnp.bitwise_and(lax.shift_right_logical(jnp.full((depth, 1), bits), column), 1)
        wanted = jnp.where(on == 1, x, -1).astype(jnp.float32)
        wanted = jnp.broadcast_to(wanted, mix_ref.shape).astype(jnp.bfloat16)
        tile = int_ref[j]
        kept.append(jnp.where(mix_ref[...] == wanted, tile, jnp.zeros_like(tile)))
        on_big = screen_ref[k_whole, jnp.bitwise_xor(big, x)] == 1
        active2, active3 = on_big & (x != 0), on_big & (x == 0)
        pos2 = jnp.where(active2, counts_ref[0], -1)
        pos3 = jnp.where(active3, counts_ref[1], -1)
        counts_ref[0] = counts_ref[0] + active2.astype(jnp.int32)
        counts_ref[1] = counts_ref[1] + active3.astype(jnp.int32)
        pos2_ref[k] = pos2
        pos3_ref[k] = pos3
        slots.append((pos2, pos3))
    kept = jnp.concatenate(kept, axis=0)
    narrow = lax.dot_general(
        spread_ref[...], kept, (((1,), (1,)), ((), ())), preferred_element_type=jnp.float32
    ).astype(jnp.bfloat16)
    wide = jnp.where(
        jnp.broadcast_to((row_ref[...] == big).astype(jnp.float32), kept.shape).astype(jnp.bfloat16) == 1,
        kept,
        jnp.zeros_like(kept),
    )
    wide = wide[:, :FOLD] + wide[:, FOLD:]
    for j in range(k_step):
        narrow_ref[j] = narrow[:, j * depth:(j + 1) * depth]
        whole = wide[j * depth:(j + 1) * depth]
        pos2, pos3 = slots[j]

        @pl.when((pos2 >= 0) & (pos2 < CAPS[0]))
        def _():
            m2a_ref[pos2] = whole[:half] + whole[half:]

        @pl.when(pos2 >= CAPS[0])
        def _():
            m2b_ref[pos2 - CAPS[0]] = whole[:half] + whole[half:]

        @pl.when((pos3 >= 0) & (pos3 < CAPS[0]))
        def _():
            m3a_ref[pos3] = whole

        @pl.when(pos3 >= CAPS[0])
        def _():
            m3b_ref[pos3 - CAPS[0]] = whole

    @pl.when(step == pl.num_programs(0) - 1)
    def _():
        labels = row_ref[...]
        lane = lax.broadcasted_iota(jnp.int32, labels.shape, 1)
        ahead = pltpu.roll(labels, total - NARROW, 1)
        long = (labels == ahead) & (lane < total - NARROW) & (labels != big)
        too_long = jnp.max(long.astype(jnp.int32)) == 1
        n2, n3 = counts_ref[0], counts_ref[1]
        form = jnp.where((n2 <= FEW) & (n3 <= CAPS[0]), 3, jnp.where(n2 <= FEW, 4, 5))
        form = jnp.where((n3 <= FEW) & (n2 <= CAPS[0]), 2, form)
        form = jnp.where(n3 == 0, jnp.where(n2 <= CAPS[0], 0, 1), form)
        form_ref[0] = jnp.where(too_long, 5, form)


def pack(integrals, occ_irrep, vir_irrep, screen, place, pair_at):
    occ_share, depth, total = integrals.shape
    shapes = [(occ_share, NARROW, depth)]
    shapes += [(n, depth // 2, FOLD) for n in CAPS] + [(n, depth, FOLD) for n in CAPS]
    fixed = lambda k, *_: (0, 0, 0)
    smem = pl.BlockSpec(memory_space=pltpu.SMEM)

    def kernel(*refs):
        pack_kernel(*refs, pair_at)

    return pl.pallas_call(
        kernel,
        grid_spec=pltpu.PrefetchScalarGridSpec(
            num_scalar_prefetch=4,
            grid=(occ_share // K_STEP,),
            in_specs=[
                pl.BlockSpec((K_STEP, depth, total), lambda k, *_: (k, 0, 0)),
                pl.BlockSpec((1, total), lambda k, *_: (0, 0)),
            ],
            out_specs=[pl.BlockSpec((K_STEP, NARROW, depth), lambda k, *_: (k, 0, 0))]
            + [pl.BlockSpec(v, fixed) for v in shapes[1:]]
            + [smem] * 3,
            scratch_shapes=[
                pltpu.VMEM((depth, total), jnp.bfloat16),
                pltpu.VMEM((NARROW, total), jnp.bfloat16),
                pltpu.VMEM((total, 8), jnp.int32),
                pltpu.SMEM((2,), jnp.int32),
            ],
        ),
        out_shape=[jax.ShapeDtypeStruct(v, jnp.bfloat16) for v in shapes]
        + [jax.ShapeDtypeStruct((n,), jnp.int32) for n in (occ_share, occ_share, 1)],
        compiler_params=pltpu.CompilerParams(vmem_limit_bytes=32 * 1024 * 1024),
    )(occ_irrep, vir_irrep, screen, place, integrals, vir_irrep[None, :])


def make_sparse_kernel(n2, n3, starts2, starts3):
    def kernel(occ_ref, vir_ref, pos2_ref, pos3_ref, place_ref, amp_ref, row_ref, *refs):
        narrow_refs = refs[:4]
        m2_refs = refs[4:4 + n2]
        m3_refs = [refs[4 + n2 + 5 * n:9 + n2 + 5 * n] for n in range(n3)]
        (
            out0, out1, out2, out3, mix_ref, column_ref, narrow_sum, wide_sum, lhs_ref, fold_ref, narrow_rhs,
            short_rhs, wide_rhs, buffer, sems,
        ) = refs[4 + n2 + 5 * n3:]
        batch, k_all, share, total = amp_ref.shape
        rows = batch * share
        groups = k_all // K_STEP
        row, col = place_ref[0], place_ref[1]
        at_end = (row == 0) | (row == 3)
        pair_label = occ_ref[batch]
        big = jnp.where(vir_ref[0] == vir_ref[FOLD - 1], vir_ref[0], vir_ref[FOLD])

        def fetch(group, slot):
            return pltpu.make_async_copy(
                amp_ref.at[:, pl.ds(group * K_STEP, K_STEP)], buffer.at[slot], sems.at[slot]
            )

        fetch(0, 0).start()
        column_ref[...] = label_columns(row_ref[...])
        column = column_ref[pl.ds(pl.multiple_of(row * share, share), share), :1]
        column = jnp.concatenate([jnp.bitwise_xor(column, occ_ref[i]) for i in range(batch)], axis=0)
        mix_ref[...] = jnp.bitwise_xor(column, row_ref[...]).astype(jnp.float32).astype(jnp.bfloat16)
        narrow_sum[...] = jnp.zeros(narrow_sum.shape, jnp.float32)
        wide_sum[...] = jnp.zeros(wide_sum.shape, jnp.float32)

        @pl.loop(0, groups)
        def _(group):
            slot = group % 2

            @pl.when(group + 1 < groups)
            def _():
                fetch(group + 1, 1 - slot).start()

            for j in range(K_STEP):
                k = group * K_STEP + j
                for s in range(4):
                    place = pl.ds((j * 4 + s) * share, share)
                    block = narrow_refs[s][k]
                    narrow_rhs[:NARROW, place] = block
                    narrow_rhs[NARROW:, place] = block
                pos2, pos3 = pos2_ref[k], pos3_ref[k]
                here = pl.ds(j * share, share)

                @pl.when(pos2 < 0)
                def _():
                    short_rhs[here] = jnp.zeros((share, FOLD), jnp.bfloat16)

                for n in range(n2):
                    inside = (pos2 >= starts2[n]) & (pos2 < starts2[n + 1])

                    @pl.when(inside)
                    def _(n=n):
                        short = m2_refs[n][pos2 - starts2[n]]
                        short_rhs[here] = jnp.concatenate([short, short], axis=0)

                if n3:
                    wide_here = pl.ds(j * 4 * share, 4 * share)

                    @pl.when(pos3 < 0)
                    def _():
                        wide_rhs[wide_here] = jnp.zeros((4 * share, FOLD), jnp.bfloat16)

                for n in range(n3):
                    inside = (pos3 >= starts3[n]) & (pos3 < starts3[n + 1])

                    @pl.when(inside)
                    def _(n=n):
                        own, e1, o1, e2, o2 = [r.at[pos3 - starts3[n]] for r in m3_refs[n]]
                        first = j * 4 * share
                        wide_rhs[pl.ds(first, share)] = own[...]
                        wide_rhs[pl.ds(first + share, share)] = e1[...]

                        @pl.when(at_end)
                        def _():
                            wide_rhs[pl.ds(first + 2 * share, share)] = e2[...]
                            wide_rhs[pl.ds(first + 3 * share, share)] = jnp.zeros((share, FOLD), jnp.bfloat16)

                        @pl.when(jnp.logical_not(at_end))
                        def _():
                            wide_rhs[pl.ds(first + 2 * share, share)] = o2[...]
                            wide_rhs[pl.ds(first + 3 * share, share)] = o1[...]

            fetch(group, slot).wait()
            for j in range(K_STEP):
                label = occ_ref[col * k_all + group * K_STEP + j].astype(jnp.float32)
                folded = None
                for s in range(4):
                    source = jnp.bitwise_xor(row, s)
                    place = pl.ds(pl.multiple_of(source * share, share), share)
                    tile = buffer[slot, :, j, :, place].reshape(rows, share)
                    wanted = jnp.full((rows, share), label, jnp.float32).astype(jnp.bfloat16)
                    piece = jnp.where(mix_ref[:, place] == wanted, tile, jnp.zeros_like(tile))
                    lhs_ref[:, pl.ds((j * 4 + s) * share, share)] = piece
                    folded = piece if folded is None else folded + piece
                fold_ref[:, pl.ds(j * share, share)] = folded
            narrow_sum[...] += lax.dot_general(
                lhs_ref[...], narrow_rhs[...], (((1,), (1,)), ((), ())), preferred_element_type=jnp.float32
            )
            wide = jnp.dot(fold_ref[...], short_rhs[...], preferred_element_type=jnp.float32)
            if n3:
                wide += jnp.dot(lhs_ref[...], wide_rhs[...], preferred_element_type=jnp.float32)
            wide_sum[...] += wide

        target = jnp.bitwise_xor(column, pair_label)
        both = jnp.concatenate([narrow_sum[...]] * (FOLD // (2 * NARROW)), axis=1)
        wide_sum[...] = jnp.where(target == big, wide_sum[...], both)
        for t, out_ref in enumerate((out0, out1, out2, out3)):
            goal = jnp.bitwise_xor(col, t)
            width, height = FOLD // 2, rows // 2
            lanes = pl.ds(pl.multiple_of((goal % 2) * width, width), width)
            lines = pl.ds(pl.multiple_of((goal // 2) * height, height), height)
            out_ref[...] = wide_sum[lines, lanes].reshape(out_ref.shape)

    return kernel


def sparse_product(amplitudes, occ_irrep, vir_irrep, pos2, pos3, place, narrow, m2, m3):
    batch, _, share, total = amplitudes.shape
    rows = batch * share
    vmem = pl.BlockSpec(memory_space=pltpu.VMEM)
    smem = pl.BlockSpec(memory_space=pltpu.SMEM)
    arrays = list(narrow) + list(m2) + [v for group in m3 for v in group]
    starts2, starts3 = [0], [0]
    for v in m2:
        starts2.append(starts2[-1] + v.shape[0])
    for v in m3:
        starts3.append(starts3[-1] + v[0].shape[0])
    depth = K_STEP * 4 * share
    wide_depth = depth if m3 else 16
    return pl.pallas_call(
        make_sparse_kernel(len(m2), len(m3), starts2, starts3),
        in_specs=[smem] * 5 + [pl.BlockSpec(memory_space=pltpu.HBM)] + [vmem] * (1 + len(arrays)),
        out_specs=[vmem] * 4,
        out_shape=[jax.ShapeDtypeStruct((batch // 2, share, FOLD // 2), jnp.float32)] * 4,
        scratch_shapes=[
            pltpu.VMEM((rows, total), jnp.bfloat16),
            pltpu.VMEM((total, 8), jnp.int32),
            pltpu.VMEM((rows, 2 * NARROW), jnp.float32),
            pltpu.VMEM((rows, FOLD), jnp.float32),
            pltpu.VMEM((rows, depth), jnp.bfloat16),
            pltpu.VMEM((rows, K_STEP * share), jnp.bfloat16),
            pltpu.VMEM((2 * NARROW, depth), jnp.bfloat16),
            pltpu.VMEM((K_STEP * share, FOLD), jnp.bfloat16),
            pltpu.VMEM((wide_depth, FOLD), jnp.bfloat16),
            pltpu.VMEM((2, batch, K_STEP, share, total), jnp.bfloat16),
            pltpu.SemaphoreType.DMA((2,)),
        ],
        compiler_params=pltpu.CompilerParams(vmem_limit_bytes=48 * 1024 * 1024),
    )(occ_irrep, vir_irrep, pos2, pos3, place, amplitudes, vir_irrep[None, :], *arrays)


def finish(cycle, occ_irrep, vir_irrep, occ_energy, vir_energy, a_start, a_size, b_start, b_size, batch):
    label_a = lax.dynamic_slice_in_dim(vir_irrep, a_start, a_size)
    label_b = lax.dynamic_slice_in_dim(vir_irrep, b_start, b_size)
    energy_a = lax.dynamic_slice_in_dim(vir_energy, a_start, a_size)
    energy_b = lax.dynamic_slice_in_dim(vir_energy, b_start, b_size)
    target = jnp.bitwise_xor(
        jnp.bitwise_xor(occ_irrep[:batch, None], occ_irrep[batch]), label_a[None, :]
    )
    keep = label_b[:, None, None] == target[None, :, :]
    denominator = (
        occ_energy[:batch][None, :, None]
        + occ_energy[batch]
        - energy_a[None, None, :]
        - energy_b[:, None, None]
    )
    swapped = jnp.transpose(cycle, (2, 0, 1))
    return jnp.where(keep, swapped, 0.0) / denominator


def dense_total(amplitudes, fold, occ_local, row_labels, col_labels, row):
    batch, occ_share, share, _ = amplitudes.shape
    rows_n = 4
    chunks = [(0, 15), (15, occ_share)]
    total = jnp.zeros((batch * share, FOLD), jnp.float32)

    def add(total, parts, sources, chunk):
        return shard_product(
            total, amplitudes, parts, sources, rows_n, occ_local[chunk[0]:chunk[1]], chunk[0],
            row_labels, col_labels,
        )

    own = [fold[lo:hi] for lo, hi in chunks]
    rightward = [(i, i + 1) for i in range(rows_n - 1)]
    leftward = [(i + 1, i) for i in range(rows_n - 1)]
    held = [((v, v), (v,), (row,)) for v in own]
    for distance in range(1, rows_n + 1):
        for n, chunk in enumerate(chunks):
            (left, right), parts, sources = held[n]
            if distance < rows_n:
                left = lax.ppermute(left, "row", rightward)
                right = lax.ppermute(right, "row", leftward)
            total = add(total, parts, sources, chunk)
            if distance < rows_n:
                left, right, _ = lax.optimization_barrier((left, right, total))
            held[n] = ((left, right), (left, right), (row - distance, row + distance))
    return total


def on_square(amplitudes, integrals, occ_irrep, vir_irrep, screen):
    batch, occ_share, share, vir_total = amplitudes.shape
    row = lax.axis_index("row")
    col = lax.axis_index("col")
    place = jnp.stack([row, col]).astype(jnp.int32)
    narrow, m2a, m2b, m3a, m3b, pos2, pos3, form = pack(
        integrals, occ_irrep, vir_irrep, screen, place, batch
    )
    outer = [(0, 1), (1, 0), (2, 3), (3, 2)]
    inner = [(1, 2), (2, 1)]
    outward = [(1, 0), (2, 3)]

    def move(v, pairs):
        return lax.ppermute(v, "row", pairs)

    def summed(own):
        first = move(own, [(0, 1), (3, 2)])
        second = move(own + first, inner)
        third = move(own + second, outward)
        return own + first + second + third

    def spread(own):
        e1, o1 = move(own, outer), move(own, inner)
        return own, e1, o1, move(o1, outward), move(e1, inner)

    def sparse(choose):
        def run(narrow, m2a, m2b, m3a, m3b):
            shorts, wides = choose(m2a, m2b, m3a, m3b)
            wides = [spread(own) for own in wides]
            shorts = [summed(own) for own in shorts]
            blocks = [narrow] + [move(narrow, [(r, r ^ s) for r in range(4)]) for s in (1, 2, 3)]
            return list(sparse_product(
                amplitudes, occ_irrep, vir_irrep, pos2, pos3, place, blocks, shorts, wides
            ))

        return run

    def dense(*_):
        occ_local = lax.dynamic_slice_in_dim(occ_irrep, col * occ_share, occ_share)
        vir_local = lax.dynamic_slice_in_dim(vir_irrep, row * share, share)
        screen_rows = lax.dynamic_slice_in_dim(screen, col * occ_share, occ_share, 0)
        fold = folded_integrals(
            integrals, occ_local, vir_local, vir_irrep, occ_irrep[batch], screen_rows
        )
        row_labels = jnp.bitwise_xor(occ_irrep[:batch, None], vir_local[None, :]).reshape(-1, 1)
        total = dense_total(amplitudes, fold, occ_local, row_labels, vir_irrep[None, :], row)
        total = total.reshape(batch, share, FOLD)
        quarter = (batch // 2, share, FOLD // 2)
        goals = [jnp.bitwise_xor(col, t) for t in range(4)]
        return [
            lax.dynamic_slice(total, (g // 2 * quarter[0], 0, g % 2 * quarter[2]), quarter) for g in goals
        ]

    branches = [
        sparse(lambda m2a, m2b, m3a, m3b: ([m2a], [])),
        sparse(lambda m2a, m2b, m3a, m3b: ([m2a, m2b], [])),
        sparse(lambda m2a, m2b, m3a, m3b: ([m2a], [m3a[:FEW]])),
        sparse(lambda m2a, m2b, m3a, m3b: ([m2a[:FEW]], [m3a])),
        sparse(lambda m2a, m2b, m3a, m3b: ([m2a[:FEW]], [m3a, m3b])),
        dense,
    ]
    quarters = lax.switch(form[0], branches, narrow, m2a, m2b, m3a, m3b)
    mine = quarters[0]
    for t in (1, 2, 3):
        mine = mine + lax.ppermute(quarters[t], "col", [(q, q ^ t) for q in range(4)])
    places = [(r, q) for r in range(4) for q in range(4)]
    same = lax.ppermute(mine, ("row", "col"), [(r * 4 + q, q * 4 + r) for r, q in places])
    other = lax.ppermute(mine, ("row", "col"), [(r * 4 + q, (q ^ 2) * 4 + r) for r, q in places])
    upper = row // 2 == 1
    low = jnp.where(upper, other, same)
    high = jnp.where(upper, same, other)
    return jnp.concatenate([low, high], axis=0)


def on_any(amplitudes, integrals, occ_irrep, vir_irrep, screen):
    batch, occ_share, share, vir_total = amplitudes.shape
    row = lax.axis_index("row")
    col = lax.axis_index("col")
    occ_local = lax.dynamic_slice_in_dim(occ_irrep, col * occ_share, occ_share)
    vir_local = lax.dynamic_slice_in_dim(vir_irrep, row * share, share)
    screen_rows = lax.dynamic_slice_in_dim(screen, col * occ_share, occ_share, 0)
    fold = folded_integrals(
        integrals, occ_local, vir_local, vir_irrep, occ_irrep[batch], screen_rows
    )
    keep = (
        jnp.bitwise_xor(occ_irrep[:batch, None], occ_local[None, :])[:, :, None, None]
        == jnp.bitwise_xor(vir_local[:, None], vir_irrep[None, :])[None, None]
    )
    kept = jnp.where(keep, amplitudes, jnp.zeros_like(amplitudes))
    whole = lax.all_gather(fold, "row", axis=1, tiled=True)
    cycle = lax.dot_general(
        kept, whole, (((1, 3), (0, 1)), ((), ())), preferred_element_type=jnp.float32
    )
    cycle = lax.psum(cycle, "col")
    cycle = jnp.concatenate([cycle] * (vir_total // FOLD), axis=2)
    cycle = lax.all_to_all(cycle, "row", split_axis=2, concat_axis=1, tiled=True)
    a_size = vir_total // lax.axis_size("col")
    return lax.dynamic_slice_in_dim(cycle, col * a_size, a_size, 1)


def on_device(amplitudes, integrals, occ_irrep, vir_irrep, screen, occ_energy, vir_energy):
    batch, _, vir_share, vir_total = amplitudes.shape
    square = lax.axis_size("row") == 4 and lax.axis_size("col") == 4
    form = on_square if square else on_any
    cycle = form(amplitudes, integrals, occ_irrep, vir_irrep, screen)
    a_size = vir_total // lax.axis_size("col")
    return finish(
        cycle, occ_irrep, vir_irrep, occ_energy, vir_energy,
        lax.axis_index("col") * a_size, a_size, lax.axis_index("row") * vir_share, vir_share, batch,
    )


def solution(mesh):
    in_specs = (
        P("parts", "col", "row", None),
        P(("parts", "col"), "row", None),
        P("parts"),
        P("parts"),
        P("parts", None),
        P("parts"),
        P("parts"),
    )
    out_specs = P("row", "parts", "col")
    return jax.shard_map(
        on_device, mesh=mesh, in_specs=in_specs, out_specs=out_specs, check_vma=False
    )
```

```python
import jax
import jax.numpy as jnp
from jax import lax
from jax.experimental import pallas as pl
from jax.experimental.pallas import tpu as pltpu
from jax.sharding import PartitionSpec as P

FOLD = 256
K_STEP = 5


def folded_integrals(integrals, occ_local, vir_local, vir_irrep, pair_label, screen_rows):
    irrep_codes = jnp.arange(8, dtype=jnp.int32)
    screen_local = jnp.sum(
        screen_rows[:, None, :] * (vir_local[None, :, None] == irrep_codes).astype(jnp.int32),
        axis=2,
    )
    target = jnp.bitwise_xor(
        jnp.bitwise_xor(occ_local[:, None], vir_local[None, :]), pair_label
    )
    target = jnp.where(screen_local == 1, target, -1)
    keep = target[:, :, None] == vir_irrep[None, None, :]
    kept = jnp.where(keep, integrals, jnp.zeros_like(integrals))
    return kept[:, :, :FOLD] + kept[:, :, FOLD:]


def shard_product_kernel(block_ref, valid_ref, label_ref, amp_ref, *refs):
    sides = len(refs) - 5
    int_refs = refs[:sides]
    left_ref, right_ref, total_in_ref, total_ref, mix_ref = refs[sides:]
    step = pl.program_id(0)
    steps = pl.num_programs(0) // sides
    k_step = amp_ref.shape[1]
    rows = amp_ref.shape[0] * amp_ref.shape[2]

    @pl.when(step == 0)
    def _():
        total_ref[...] = total_in_ref[...]

    for side in range(sides):
        local = step - side * steps

        @pl.when((local == 0) & (valid_ref[side] == 1))
        def _():
            mixed = jnp.bitwise_xor(left_ref[...], right_ref[...])
            mix_ref[...] = mixed.astype(jnp.float32).astype(jnp.bfloat16)

        @pl.when((local >= 0) & (local < steps) & (valid_ref[side] == 1))
        def _(local=local, int_ref=int_refs[side]):
            mixed = mix_ref[...]
            pieces = []
            for j in range(k_step):
                label = label_ref[local * k_step + j].astype(jnp.float32)
                tile = amp_ref[:, j].reshape(rows, amp_ref.shape[3])
                wanted = jnp.full(mixed.shape, label, jnp.float32).astype(jnp.bfloat16)
                pieces.append(jnp.where(mixed == wanted, tile, jnp.zeros_like(tile)))
            lhs = jnp.concatenate(pieces, axis=1)
            rhs = int_ref[...].reshape(-1, int_ref.shape[2])
            total_ref[...] += jnp.dot(lhs, rhs, preferred_element_type=jnp.float32)


def shard_product(total, amplitudes, folds, sources, source_count, labels, k_start, row_labels, col_labels):
    batch, _, share, _ = amplitudes.shape
    k_count, depth, width = folds[0].shape
    first = k_start // K_STEP
    rows = batch * share
    steps = k_count // K_STEP
    sides = len(folds)
    sources = jnp.stack(sources).astype(jnp.int32)
    valid = ((sources >= 0) & (sources < source_count)).astype(jnp.int32)
    blocks = jnp.clip(sources, 0, source_count - 1)

    def amp_map(g, s, v, l):
        return (0, first + g % steps, 0, s[g // steps])

    def int_map(side):
        return lambda g, s, v, l: (jnp.clip(g - side * steps, 0, steps - 1), 0, 0)

    return pl.pallas_call(
        shard_product_kernel,
        grid_spec=pltpu.PrefetchScalarGridSpec(
            num_scalar_prefetch=3,
            grid=(sides * steps,),
            in_specs=[pl.BlockSpec((batch, K_STEP, share, depth), amp_map)]
            + [pl.BlockSpec((K_STEP, depth, width), int_map(side)) for side in range(sides)]
            + [
                pl.BlockSpec((rows, 1), lambda g, s, v, l: (0, 0)),
                pl.BlockSpec((1, depth), lambda g, s, v, l: (0, s[g // steps])),
                pl.BlockSpec((rows, width), lambda g, s, v, l: (0, 0)),
            ],
            out_specs=pl.BlockSpec((rows, width), lambda g, s, v, l: (0, 0)),
            scratch_shapes=[pltpu.VMEM((rows, depth), jnp.bfloat16)],
        ),
        out_shape=jax.ShapeDtypeStruct((rows, width), jnp.float32),
        input_output_aliases={6 + sides: 0},
        compiler_params=pltpu.CompilerParams(vmem_limit_bytes=32 * 1024 * 1024),
    )(blocks, valid, labels, amplitudes, *folds, row_labels, col_labels, total)


NARROW = 64
CAPS = (20, 5)
FEW = 10
FEWER = 5


def label_columns(row_labels):
    return jnp.transpose(jnp.broadcast_to(row_labels, (8, row_labels.shape[1])))


def pack_kernel(
    occ_ref, vir_ref, screen_ref, place_ref, int_ref, row_ref,
    narrow_ref, m2a_ref, m2b_ref, m3a_ref, m3b_ref, pos2_ref, pos3_ref, form_ref,
    mix_ref, spread_ref, big_mask_ref, column_ref, counts_ref, pair_at,
):
    step = pl.program_id(0)
    k_step, depth, total = int_ref.shape
    half = depth // 2
    row, col = place_ref[0], place_ref[1]
    pair_label = occ_ref[pair_at]
    big = largest_irrep(vir_ref)

    @pl.when(step == 0)
    def _():
        counts_ref[0] = 0
        counts_ref[1] = 0
        column_ref[...] = label_columns(row_ref[...])
        column = column_ref[pl.ds(pl.multiple_of(row * depth, depth), depth), :1]
        mix_ref[...] = jnp.bitwise_xor(column, row_ref[...]).astype(jnp.float32).astype(jnp.bfloat16)
        residue = lax.broadcasted_iota(jnp.int32, spread_ref.shape, 0)
        b = lax.broadcasted_iota(jnp.int32, spread_ref.shape, 1)
        narrow = (b % NARROW == residue) & (row_ref[...] != big)
        spread_ref[...] = jnp.where(narrow, 1.0, 0.0).astype(jnp.bfloat16)
        is_big = jnp.where(row_ref[...] == big, 1.0, 0.0)
        big_mask_ref[...] = jnp.broadcast_to(is_big, big_mask_ref.shape).astype(jnp.bfloat16)

    local = row_ref[:, pl.ds(pl.multiple_of(row * depth, depth), depth)]
    kept, slots, open_rows = [], [], []
    for j in range(k_step):
        k = step * k_step + j
        k_whole = col * (k_step * pl.num_programs(0)) + k
        x = jnp.bitwise_xor(occ_ref[k_whole], pair_label)
        bits = screen_ref[k_whole, 0]
        for g in range(1, 8):
            bits = bits + screen_ref[k_whole, g] * (1 << g)
        open_rows.append(jnp.bitwise_and(lax.shift_right_logical(jnp.full(local.shape, bits), local), 1) == 1)
        wanted = jnp.full(mix_ref.shape, x.astype(jnp.float32)).astype(jnp.bfloat16)
        tile = int_ref[j]
        kept.append(jnp.where(mix_ref[...] == wanted, tile, jnp.zeros_like(tile)))
        on_big = screen_ref[k_whole, jnp.bitwise_xor(big, x)] == 1
        active2, active3 = on_big & (x != 0), on_big & (x == 0)
        pos2 = jnp.where(active2, counts_ref[0], -1)
        pos3 = jnp.where(active3, counts_ref[1], -1)
        counts_ref[0] = counts_ref[0] + active2.astype(jnp.int32)
        counts_ref[1] = counts_ref[1] + active3.astype(jnp.int32)
        pos2_ref[k] = pos2
        pos3_ref[k] = pos3
        slots.append((pos2, pos3))
    narrow = lax.dot_general(
        spread_ref[...], jnp.concatenate(kept, axis=0), (((1,), (1,)), ((), ())),
        preferred_element_type=jnp.float32,
    )
    for j in range(k_step):
        block = jnp.where(open_rows[j], narrow[:, j * depth:(j + 1) * depth], 0.0)
        narrow_ref[j] = block.astype(jnp.bfloat16)
        whole = kept[j] * big_mask_ref[...]
        whole = whole[:, :FOLD] + whole[:, FOLD:]
        pos2, pos3 = slots[j]

        @pl.when((pos2 >= 0) & (pos2 < CAPS[0]))
        def _():
            m2a_ref[pos2] = whole[:half] + whole[half:]

        @pl.when(pos2 >= CAPS[0])
        def _():
            m2b_ref[pos2 - CAPS[0]] = whole[:half] + whole[half:]

        @pl.when((pos3 >= 0) & (pos3 < CAPS[0]))
        def _():
            m3a_ref[pos3] = whole

        @pl.when(pos3 >= CAPS[0])
        def _():
            m3b_ref[pos3 - CAPS[0]] = whole

    @pl.when(step == pl.num_programs(0) - 1)
    def _():
        labels = row_ref[...]
        lane = lax.broadcasted_iota(jnp.int32, labels.shape, 1)
        ahead = pltpu.roll(labels, total - NARROW, 1)
        long = (labels == ahead) & (lane < total - NARROW) & (labels != big)
        too_long = jnp.max(long.astype(jnp.int32)) == 1
        n2, n3 = counts_ref[0], counts_ref[1]
        mixed = occ_ref[0] != pair_label
        form = jnp.where((n2 <= FEW) & (n3 <= CAPS[0]), 4, jnp.where(n2 <= FEW, 5, 6))
        form = jnp.where((n3 <= FEW) & (n2 <= CAPS[0]), 3, form)
        form = jnp.where((n3 <= FEWER) & (n2 <= CAPS[0]), 2, form)
        form = jnp.where(mixed, 6, form)
        form = jnp.where(n3 == 0, jnp.where(n2 <= CAPS[0], 0, 1), form)
        form_ref[0] = jnp.where(too_long, 6, form)


def pack(integrals, occ_irrep, vir_irrep, screen, place, pair_at):
    occ_share, depth, total = integrals.shape
    shapes = [(occ_share, NARROW, depth)]
    shapes += [(n, depth // 2, FOLD) for n in CAPS] + [(n, depth, FOLD) for n in CAPS]
    fixed = lambda k, *_: (0, 0, 0)
    smem = pl.BlockSpec(memory_space=pltpu.SMEM)

    def kernel(*refs):
        pack_kernel(*refs, pair_at)

    return pl.pallas_call(
        kernel,
        grid_spec=pltpu.PrefetchScalarGridSpec(
            num_scalar_prefetch=4,
            grid=(occ_share // K_STEP,),
            in_specs=[
                pl.BlockSpec((K_STEP, depth, total), lambda k, *_: (k, 0, 0)),
                pl.BlockSpec((1, total), lambda k, *_: (0, 0)),
            ],
            out_specs=[pl.BlockSpec((K_STEP, NARROW, depth), lambda k, *_: (k, 0, 0))]
            + [pl.BlockSpec(v, fixed) for v in shapes[1:]]
            + [smem] * 3,
            scratch_shapes=[
                pltpu.VMEM((depth, total), jnp.bfloat16),
                pltpu.VMEM((NARROW, total), jnp.bfloat16),
                pltpu.VMEM((depth, total), jnp.bfloat16),
                pltpu.VMEM((total, 8), jnp.int32),
                pltpu.SMEM((2,), jnp.int32),
            ],
        ),
        out_shape=[jax.ShapeDtypeStruct(v, jnp.bfloat16) for v in shapes]
        + [jax.ShapeDtypeStruct((n,), jnp.int32) for n in (occ_share, occ_share, 1)],
        compiler_params=pltpu.CompilerParams(vmem_limit_bytes=32 * 1024 * 1024),
    )(occ_irrep, vir_irrep, screen, place, integrals, vir_irrep[None, :])


SLOTS = (0, 1, 3, 2)


def largest_irrep(vir_ref):
    return jnp.where(vir_ref[0] == vir_ref[FOLD - 1], vir_ref[0], vir_ref[FOLD])


def amplitude_rows(column_ref, row_ref, occ_ref, row, batch, share):
    column_ref[...] = label_columns(row_ref[...])
    column = column_ref[pl.ds(pl.multiple_of(row * share, share), share), :1]
    return jnp.concatenate([jnp.bitwise_xor(column, occ_ref[i]) for i in range(batch)], axis=0)


def write_quarters(total_ref, col, outs):
    rows, fold = total_ref.shape
    width, height = fold // 2, rows // 2
    for t, out_ref in enumerate(outs):
        goal = jnp.bitwise_xor(col, t)
        lanes = pl.ds(pl.multiple_of((goal % 2) * width, width), width)
        lines = pl.ds(pl.multiple_of((goal // 2) * height, height), height)
        out_ref[...] = total_ref[lines, lanes].reshape(out_ref.shape)


def chosen(refs, starts, pos, pick):
    block = None
    for n, group in enumerate(refs):
        inside = (pos >= starts[n]) & (pos < starts[n + 1])
        at = jnp.clip(pos - starts[n], 0, starts[n + 1] - starts[n] - 1)
        found = pick(group, at)
        found = jnp.where(inside, found, jnp.zeros_like(found))
        block = found if block is None else block + found
    return block


def make_sparse_kernel(n2, n3, starts2, starts3):
    def kernel(occ_ref, vir_ref, pos2_ref, pos3_ref, place_ref, amp_ref, row_ref, *refs):
        narrow_refs = refs[:6]
        m2_refs = refs[6:6 + n2]
        m3_refs = [refs[6 + n2 + 3 * n:9 + n2 + 3 * n] for n in range(n3)]
        refs = refs[6 + n2 + 3 * n3:]
        outs, refs = (refs[:1], refs[1:]) if n3 else (refs[:4], refs[4:])
        (
            mix_ref, column_ref, narrow_sum, wide_sum, lhs_ref, fold_ref, narrow_rhs,
            short_rhs, wide_rhs, buffer, sems,
        ) = refs
        batch, k_all, share, total = amp_ref.shape
        rows = batch * share
        groups = k_all // K_STEP
        row, col = place_ref[0], place_ref[1]
        at_end = (row == 0) | (row == 3)
        big = largest_irrep(vir_ref)

        def fetch(group, slot):
            return pltpu.make_async_copy(
                amp_ref.at[:, pl.ds(group * K_STEP, K_STEP)], buffer.at[slot], sems.at[slot]
            )

        fetch(0, 0).start()
        column = amplitude_rows(column_ref, row_ref, occ_ref, row, batch, share)
        mix_ref[...] = jnp.bitwise_xor(column, row_ref[...]).astype(jnp.float32).astype(jnp.bfloat16)
        narrow_sum[...] = jnp.zeros(narrow_sum.shape, jnp.float32)
        wide_sum[...] = jnp.zeros(wide_sum.shape, jnp.float32)

        @pl.loop(0, groups)
        def _(group):
            slot = group % 2

            @pl.when(group + 1 < groups)
            def _():
                fetch(group + 1, 1 - slot).start()

            fetch(group, slot).wait()
            for j in range(K_STEP):
                k = group * K_STEP + j
                own, e1, e2, e3, o1, o2 = [ref[k] for ref in narrow_refs]
                blocks = (own, e1, jnp.where(at_end, e3, o1), jnp.where(at_end, e2, o2))
                for n, block in enumerate(blocks):
                    place = pl.ds((n * K_STEP + j) * share, share)
                    narrow_rhs[:NARROW, place] = block
                    narrow_rhs[NARROW:, place] = block
                short = chosen(m2_refs, starts2, pos2_ref[k], lambda ref, at: ref[at])
                short_rhs[pl.ds(j * share, share)] = jnp.concatenate([short, short], axis=0)
                if n3:
                    for n in range(3):
                        block = chosen(m3_refs, starts3, pos3_ref[k], lambda group, at, n=n: group[n][at])
                        if n == 2:
                            block = jnp.where(at_end, jnp.zeros_like(block), block)
                        wide_rhs[pl.ds((n * K_STEP + j) * share, share)] = block
                label = occ_ref[col * k_all + k].astype(jnp.float32)
                wanted = jnp.full((rows, share), label).astype(jnp.bfloat16)
                folded = None
                for n, s in enumerate(SLOTS):
                    source = jnp.bitwise_xor(row, s)
                    place = pl.ds(pl.multiple_of(source * share, share), share)
                    tile = buffer[slot, :, j, :, place].reshape(rows, share)
                    piece = jnp.where(mix_ref[:, place] == wanted, tile, jnp.zeros_like(tile))
                    lhs_ref[:, pl.ds((n * K_STEP + j) * share, share)] = piece
                    folded = piece if folded is None else folded + piece
                fold_ref[:, pl.ds(j * share, share)] = folded
            narrow_sum[...] += lax.dot_general(
                lhs_ref[...], narrow_rhs[...], (((1,), (1,)), ((), ())), preferred_element_type=jnp.float32
            )
            wide = jnp.dot(fold_ref[...], short_rhs[...], preferred_element_type=jnp.float32)
            if n3:
                lhs = lhs_ref[:, :3 * K_STEP * share]
                wide += jnp.dot(lhs, wide_rhs[...], preferred_element_type=jnp.float32)
            wide_sum[...] += wide

        target = jnp.bitwise_xor(column, occ_ref[batch])
        both = jnp.concatenate([narrow_sum[...]] * (FOLD // (2 * NARROW)), axis=1)
        combined = jnp.where(target == big, wide_sum[...], both)
        if n3:
            outs[0][...] = combined
        else:
            wide_sum[...] = combined
            write_quarters(wide_sum, col, outs)

    return kernel


def starts_of(arrays):
    starts = [0]
    for v in arrays:
        starts.append(starts[-1] + v.shape[0])
    return starts


def sparse_product(amplitudes, occ_irrep, vir_irrep, pos2, pos3, place, narrow, m2, m3):
    batch, _, share, total = amplitudes.shape
    rows = batch * share
    vmem = pl.BlockSpec(memory_space=pltpu.VMEM)
    smem = pl.BlockSpec(memory_space=pltpu.SMEM)
    arrays = list(narrow) + list(m2) + [v for group in m3 for v in group]
    depth = K_STEP * share
    if m3:
        out_shape = [jax.ShapeDtypeStruct((rows, FOLD), jnp.float32)]
    else:
        out_shape = [jax.ShapeDtypeStruct((batch // 2, share, FOLD // 2), jnp.float32)] * 4
    return pl.pallas_call(
        make_sparse_kernel(len(m2), len(m3), starts_of(m2), starts_of([v[0] for v in m3])),
        in_specs=[smem] * 5 + [pl.BlockSpec(memory_space=pltpu.HBM)] + [vmem] * (1 + len(arrays)),
        out_specs=[vmem] * len(out_shape),
        out_shape=out_shape,
        scratch_shapes=[
            pltpu.VMEM((rows, total), jnp.bfloat16),
            pltpu.VMEM((total, 8), jnp.int32),
            pltpu.VMEM((rows, 2 * NARROW), jnp.float32),
            pltpu.VMEM((rows, FOLD), jnp.float32),
            pltpu.VMEM((rows, 4 * depth), jnp.bfloat16),
            pltpu.VMEM((rows, depth), jnp.bfloat16),
            pltpu.VMEM((2 * NARROW, 4 * depth), jnp.bfloat16),
            pltpu.VMEM((depth, FOLD), jnp.bfloat16),
            pltpu.VMEM((3 * depth if m3 else 16, FOLD), jnp.bfloat16),
            pltpu.VMEM((2, batch, K_STEP, share, total), jnp.bfloat16),
            pltpu.SemaphoreType.DMA((2,)),
        ],
        compiler_params=pltpu.CompilerParams(vmem_limit_bytes=48 * 1024 * 1024),
    )(occ_irrep, vir_irrep, pos2, pos3, place, amplitudes, vir_irrep[None, :], *arrays)


def make_far_kernel(n3, starts3):
    def kernel(occ_ref, vir_ref, pos3_ref, place_ref, amp_ref, row_ref, total_in_ref, *refs):
        m3_refs = [refs[2 * n:2 * n + 2] for n in range(n3)]
        outs = refs[2 * n3:2 * n3 + 4]
        mix_ref, column_ref, total_ref, lhs_ref, rhs_ref, buffer, sems = refs[2 * n3 + 4:]
        batch, k_all, share, total = amp_ref.shape
        rows = batch * share
        groups = k_all // K_STEP
        row, col = place_ref[0], place_ref[1]
        at_end = (row == 0) | (row == 3)
        place = pl.ds(pl.multiple_of(jnp.bitwise_xor(row, 2) * share, share), share)

        def fetch(group):
            return pltpu.make_async_copy(
                amp_ref.at[:, pl.ds(group * K_STEP, K_STEP), :, place], buffer.at[group], sems.at[group]
            )

        for group in range(groups):
            fetch(group).start()
        column = amplitude_rows(column_ref, row_ref, occ_ref, row, batch, share)
        target = jnp.bitwise_xor(column, occ_ref[batch])
        mixed = jnp.bitwise_xor(column, row_ref[:, place])
        mixed = jnp.where(target == largest_irrep(vir_ref), mixed, -1)
        mix_ref[...] = mixed.astype(jnp.float32).astype(jnp.bfloat16)
        total_ref[...] = total_in_ref[...]
        for group in range(groups):
            fetch(group).wait()
            for j in range(K_STEP):
                k = group * K_STEP + j
                label = occ_ref[col * k_all + k].astype(jnp.float32)
                wanted = jnp.full((rows, share), label).astype(jnp.bfloat16)
                tile = buffer[group, :, j].reshape(rows, share)
                here = pl.ds(j * share, share)
                lhs_ref[:, here] = jnp.where(mix_ref[...] == wanted, tile, jnp.zeros_like(tile))
                rhs_ref[here] = chosen(
                    m3_refs, starts3, pos3_ref[k], lambda pair, at: jnp.where(at_end, pair[0][at], pair[1][at])
                )
            total_ref[...] += jnp.dot(lhs_ref[...], rhs_ref[...], preferred_element_type=jnp.float32)
        write_quarters(total_ref, col, outs)

    return kernel


def far_product(total, amplitudes, occ_irrep, vir_irrep, pos3, place, m3):
    batch, k_all, share, vir_total = amplitudes.shape
    rows = batch * share
    vmem = pl.BlockSpec(memory_space=pltpu.VMEM)
    smem = pl.BlockSpec(memory_space=pltpu.SMEM)
    groups = k_all // K_STEP
    return pl.pallas_call(
        make_far_kernel(len(m3), starts_of([v[0] for v in m3])),
        in_specs=[smem] * 4 + [pl.BlockSpec(memory_space=pltpu.HBM)] + [vmem] * (2 + 2 * len(m3)),
        out_specs=[vmem] * 4,
        out_shape=[jax.ShapeDtypeStruct((batch // 2, share, FOLD // 2), jnp.float32)] * 4,
        scratch_shapes=[
            pltpu.VMEM((rows, share), jnp.bfloat16),
            pltpu.VMEM((vir_total, 8), jnp.int32),
            pltpu.VMEM((rows, FOLD), jnp.float32),
            pltpu.VMEM((rows, K_STEP * share), jnp.bfloat16),
            pltpu.VMEM((K_STEP * share, FOLD), jnp.bfloat16),
            pltpu.VMEM((groups, batch, K_STEP, share, share), jnp.bfloat16),
            pltpu.SemaphoreType.DMA((groups,)),
        ],
        compiler_params=pltpu.CompilerParams(vmem_limit_bytes=48 * 1024 * 1024),
    )(occ_irrep, vir_irrep, pos3, place, amplitudes, vir_irrep[None, :], total, *[v for g in m3 for v in g])


def finish(cycle, occ_irrep, vir_irrep, occ_energy, vir_energy, a_start, a_size, b_start, b_size, batch):
    label_a = lax.dynamic_slice_in_dim(vir_irrep, a_start, a_size)
    label_b = lax.dynamic_slice_in_dim(vir_irrep, b_start, b_size)
    energy_a = lax.dynamic_slice_in_dim(vir_energy, a_start, a_size)
    energy_b = lax.dynamic_slice_in_dim(vir_energy, b_start, b_size)
    target = jnp.bitwise_xor(
        jnp.bitwise_xor(occ_irrep[:batch, None], occ_irrep[batch]), label_a[None, :]
    )
    keep = label_b[:, None, None] == target[None, :, :]
    denominator = (
        occ_energy[:batch][None, :, None]
        + occ_energy[batch]
        - energy_a[None, None, :]
        - energy_b[:, None, None]
    )
    swapped = jnp.transpose(cycle, (2, 0, 1))
    return jnp.where(keep, swapped, 0.0) / denominator


def dense_total(amplitudes, fold, occ_local, row_labels, col_labels, row):
    batch, occ_share, share, _ = amplitudes.shape
    rows_n = 4
    chunks = [(0, 15), (15, occ_share)]
    total = jnp.zeros((batch * share, FOLD), jnp.float32)

    def add(total, parts, sources, chunk):
        return shard_product(
            total, amplitudes, parts, sources, rows_n, occ_local[chunk[0]:chunk[1]], chunk[0],
            row_labels, col_labels,
        )

    own = [fold[lo:hi] for lo, hi in chunks]
    rightward = [(i, i + 1) for i in range(rows_n - 1)]
    leftward = [(i + 1, i) for i in range(rows_n - 1)]
    held = [((v, v), (v,), (row,)) for v in own]
    for distance in range(1, rows_n + 1):
        for n, chunk in enumerate(chunks):
            (left, right), parts, sources = held[n]
            if distance < rows_n:
                left = lax.ppermute(left, "row", rightward)
                right = lax.ppermute(right, "row", leftward)
            total = add(total, parts, sources, chunk)
            if distance < rows_n:
                left, right, _ = lax.optimization_barrier((left, right, total))
            held[n] = ((left, right), (left, right), (row - distance, row + distance))
    return total


def on_square(amplitudes, integrals, occ_irrep, vir_irrep, screen):
    batch, occ_share, share, vir_total = amplitudes.shape
    row = lax.axis_index("row")
    col = lax.axis_index("col")
    place = jnp.stack([row, col]).astype(jnp.int32)
    narrow, m2a, m2b, m3a, m3b, pos2, pos3, form = pack(
        integrals, occ_irrep, vir_irrep, screen, place, batch
    )
    outer = [(0, 1), (1, 0), (2, 3), (3, 2)]
    inner = [(1, 2), (2, 1)]
    outward = [(1, 0), (2, 3)]

    def move(v, pairs):
        return lax.ppermute(v, "row", pairs)

    def summed(own):
        first = move(own, [(0, 1), (3, 2)])
        second = move(own + first, inner)
        third = move(own + second, outward)
        return own + first + second + third

    def sparse(choose):
        def run(narrow, m2a, m2b, m3a, m3b):
            shorts, wides = choose(m2a, m2b, m3a, m3b)
            near = [(own, move(own, outer), move(own, inner)) for own in wides]
            far = [(move(o1, outward), move(e1, inner)) for _, e1, o1 in near]
            e1, o1 = move(narrow, outer), move(narrow, inner)
            e2, o2 = move(o1, outward), move(e1, inner)
            blocks = (narrow, e1, e2, move(o2, outward), o1, o2)
            shorts = [summed(own) for own in shorts]
            result = sparse_product(
                amplitudes, occ_irrep, vir_irrep, pos2, pos3, place, blocks, shorts, near
            )
            if far:
                result = far_product(result[0], amplitudes, occ_irrep, vir_irrep, pos3, place, far)
            return list(result)

        return run

    def dense(*_):
        occ_local = lax.dynamic_slice_in_dim(occ_irrep, col * occ_share, occ_share)
        vir_local = lax.dynamic_slice_in_dim(vir_irrep, row * share, share)
        screen_rows = lax.dynamic_slice_in_dim(screen, col * occ_share, occ_share, 0)
        fold = folded_integrals(
            integrals, occ_local, vir_local, vir_irrep, occ_irrep[batch], screen_rows
        )
        row_labels = jnp.bitwise_xor(occ_irrep[:batch, None], vir_local[None, :]).reshape(-1, 1)
        total = dense_total(amplitudes, fold, occ_local, row_labels, vir_irrep[None, :], row)
        total = total.reshape(batch, share, FOLD)
        quarter = (batch // 2, share, FOLD // 2)
        goals = [jnp.bitwise_xor(col, t) for t in range(4)]
        return [
            lax.dynamic_slice(total, (g // 2 * quarter[0], 0, g % 2 * quarter[2]), quarter) for g in goals
        ]

    branches = [
        sparse(lambda m2a, m2b, m3a, m3b: ([m2a], [])),
        sparse(lambda m2a, m2b, m3a, m3b: ([m2a, m2b], [])),
        sparse(lambda m2a, m2b, m3a, m3b: ([m2a], [m3a[:FEWER]])),
        sparse(lambda m2a, m2b, m3a, m3b: ([m2a], [m3a[:FEW]])),
        sparse(lambda m2a, m2b, m3a, m3b: ([m2a[:FEW]], [m3a])),
        sparse(lambda m2a, m2b, m3a, m3b: ([m2a[:FEW]], [m3a, m3b])),
        dense,
    ]
    quarters = lax.switch(form[0], branches, narrow, m2a, m2b, m3a, m3b)
    mine = quarters[0]
    for t in (1, 2, 3):
        mine = mine + lax.ppermute(quarters[t], "col", [(q, q ^ t) for q in range(4)])
    places = [(r, q) for r in range(4) for q in range(4)]
    same = lax.ppermute(mine, ("row", "col"), [(r * 4 + q, q * 4 + r) for r, q in places])
    other = lax.ppermute(mine, ("row", "col"), [(r * 4 + q, (q ^ 2) * 4 + r) for r, q in places])
    upper = row // 2 == 1
    low = jnp.where(upper, other, same)
    high = jnp.where(upper, same, other)
    return jnp.concatenate([low, high], axis=0)


def on_any(amplitudes, integrals, occ_irrep, vir_irrep, screen):
    batch, occ_share, share, vir_total = amplitudes.shape
    row = lax.axis_index("row")
    col = lax.axis_index("col")
    occ_local = lax.dynamic_slice_in_dim(occ_irrep, col * occ_share, occ_share)
    vir_local = lax.dynamic_slice_in_dim(vir_irrep, row * share, share)
    screen_rows = lax.dynamic_slice_in_dim(screen, col * occ_share, occ_share, 0)
    fold = folded_integrals(
        integrals, occ_local, vir_local, vir_irrep, occ_irrep[batch], screen_rows
    )
    keep = (
        jnp.bitwise_xor(occ_irrep[:batch, None], occ_local[None, :])[:, :, None, None]
        == jnp.bitwise_xor(vir_local[:, None], vir_irrep[None, :])[None, None]
    )
    kept = jnp.where(keep, amplitudes, jnp.zeros_like(amplitudes))
    whole = lax.all_gather(fold, "row", axis=1, tiled=True)
    cycle = lax.dot_general(
        kept, whole, (((1, 3), (0, 1)), ((), ())), preferred_element_type=jnp.float32
    )
    cycle = lax.psum(cycle, "col")
    cycle = jnp.concatenate([cycle] * (vir_total // FOLD), axis=2)
    cycle = lax.all_to_all(cycle, "row", split_axis=2, concat_axis=1, tiled=True)
    a_size = vir_total // lax.axis_size("col")
    return lax.dynamic_slice_in_dim(cycle, col * a_size, a_size, 1)


def on_device(amplitudes, integrals, occ_irrep, vir_irrep, screen, occ_energy, vir_energy):
    batch, _, vir_share, vir_total = amplitudes.shape
    square = lax.axis_size("row") == 4 and lax.axis_size("col") == 4
    form = on_square if square else on_any
    cycle = form(amplitudes, integrals, occ_irrep, vir_irrep, screen)
    a_size = vir_total // lax.axis_size("col")
    return finish(
        cycle, occ_irrep, vir_irrep, occ_energy, vir_energy,
        lax.axis_index("col") * a_size, a_size, lax.axis_index("row") * vir_share, vir_share, batch,
    )


def solution(mesh):
    in_specs = (
        P("parts", "col", "row", None),
        P(("parts", "col"), "row", None),
        P("parts"),
        P("parts"),
        P("parts", None),
        P("parts"),
        P("parts"),
    )
    out_specs = P("row", "parts", "col")
    return jax.shard_map(
        on_device, mesh=mesh, in_specs=in_specs, out_specs=out_specs, check_vma=False
    )
```

```python
import jax
import jax.numpy as jnp
from jax import lax
from jax.experimental import pallas as pl
from jax.experimental.pallas import tpu as pltpu
from jax.sharding import PartitionSpec as P

FOLD = 256
K_STEP = 5


def folded_integrals(integrals, occ_local, vir_local, vir_irrep, pair_label, screen_rows):
    irrep_codes = jnp.arange(8, dtype=jnp.int32)
    screen_local = jnp.sum(
        screen_rows[:, None, :] * (vir_local[None, :, None] == irrep_codes).astype(jnp.int32),
        axis=2,
    )
    target = jnp.bitwise_xor(
        jnp.bitwise_xor(occ_local[:, None], vir_local[None, :]), pair_label
    )
    target = jnp.where(screen_local == 1, target, -1)
    keep = target[:, :, None] == vir_irrep[None, None, :]
    kept = jnp.where(keep, integrals, jnp.zeros_like(integrals))
    return kept[:, :, :FOLD] + kept[:, :, FOLD:]


NARROW = 64
WIDE_CAPS = (20, 5)
FEW_SHORT = 8
FEW_WIDE = 5


def largest_irrep(vir_ref):
    return jnp.where(vir_ref[0] == vir_ref[FOLD - 1], vir_ref[0], vir_ref[FOLD])


def label_columns(row_labels):
    return jnp.transpose(jnp.broadcast_to(row_labels, (8, row_labels.shape[1])))


def as_bf16(labels):
    return labels.astype(jnp.float32).astype(jnp.bfloat16)


def pack_kernel(
    occ_ref, vir_ref, screen_ref, place_ref, int_ref, row_ref,
    narrow_ref, few_ref, m2_ref, m3a_ref, m3b_ref, pos2_ref, pos3_ref, posx_ref, form_ref,
    mix_ref, spread_ref, big_mask_ref, column_ref, counts_ref, batch,
):
    step = pl.program_id(0)
    k_step, depth, total = int_ref.shape
    half = depth // 2
    row, col = place_ref[0], place_ref[1]
    pair_label = occ_ref[batch]
    big = largest_irrep(vir_ref)
    here = pl.ds(pl.multiple_of(row * depth, depth), depth)

    @pl.when(step == 0)
    def _():
        for n in range(3):
            counts_ref[n] = 0
        column_ref[...] = label_columns(row_ref[...])
        mix_ref[...] = as_bf16(jnp.bitwise_xor(column_ref[here, :1], row_ref[...]))
        b = lax.broadcasted_iota(jnp.int32, spread_ref.shape, 0)
        lane = lax.broadcasted_iota(jnp.int32, spread_ref.shape, 1)
        narrow = (b % NARROW == lane % NARROW) & (column_ref[:, :1] != big)
        spread_ref[...] = jnp.where(narrow, 1.0, 0.0).astype(jnp.bfloat16)
        is_big = jnp.where(row_ref[...] == big, 1.0, 0.0)
        big_mask_ref[...] = jnp.broadcast_to(is_big, big_mask_ref.shape).astype(jnp.bfloat16)

    lane = lax.broadcasted_iota(jnp.int32, (half, 2 * NARROW), 1)
    local = column_ref[here, :1]

    @pl.loop(0, k_step)
    def _(j):
        k = step * k_step + j
        k_whole = col * (k_step * pl.num_programs(0)) + k
        x = jnp.bitwise_xor(occ_ref[k_whole], pair_label)
        bits = screen_ref[k_whole, 0]
        for g in range(1, 8):
            bits = bits + screen_ref[k_whole, g] * (1 << g)
        wanted = as_bf16(jnp.full(mix_ref.shape, x))
        tile = int_ref[j]
        kept = jnp.where(mix_ref[...] == wanted, tile, jnp.zeros_like(tile))
        narrow = jnp.dot(kept, spread_ref[...], preferred_element_type=jnp.float32)
        on = jnp.bitwise_and(lax.shift_right_logical(jnp.full(local.shape, bits), local), 1) == 1
        narrow = jnp.where(on, narrow, 0.0)
        narrow = jnp.where(lane < NARROW, narrow[:half], narrow[half:]).astype(jnp.bfloat16)
        narrow_ref[j] = narrow
        wide = kept * big_mask_ref[...]
        wide = wide[:, :FOLD] + wide[:, FOLD:]
        on_big = screen_ref[k_whole, jnp.bitwise_xor(big, x)] == 1
        actives = (on_big & (x != 0), on_big & (x == 0), x != 0)
        pos2, pos3, posx = [jnp.where(active, counts_ref[n], -1) for n, active in enumerate(actives)]
        for n, active in enumerate(actives):
            counts_ref[n] = counts_ref[n] + active.astype(jnp.int32)
        pos2_ref[k], pos3_ref[k], posx_ref[k] = pos2, pos3, posx

        @pl.when(pos2 >= 0)
        def _():
            m2_ref[pos2] = wide[:half] + wide[half:]

        @pl.when((pos3 >= 0) & (pos3 < WIDE_CAPS[0]))
        def _():
            m3a_ref[pos3] = wide

        @pl.when(pos3 >= WIDE_CAPS[0])
        def _():
            m3b_ref[pos3 - WIDE_CAPS[0]] = wide

        @pl.when((posx >= 0) & (posx < FEW_SHORT))
        def _():
            few_ref[posx] = narrow

    @pl.when(step == pl.num_programs(0) - 1)
    def _():
        labels = row_ref[...]
        lanes = lax.broadcasted_iota(jnp.int32, labels.shape, 1)
        ahead = pltpu.roll(labels, total - NARROW, 1)
        long = (labels == ahead) & (lanes < total - NARROW) & (labels != big)
        too_long = jnp.max(long.astype(jnp.int32)) == 1
        n3, nx = counts_ref[1], counts_ref[2]
        one_label = occ_ref[0] == pair_label
        form = jnp.where(n3 <= WIDE_CAPS[0], 2, 3)
        form = jnp.where(nx <= FEW_SHORT, form, jnp.where(n3 <= FEW_WIDE, 1, 4))
        form = jnp.where(one_label, form, 5)
        form = jnp.where(n3 == 0, 0, form)
        form_ref[0] = jnp.where(too_long, 5, form)


def pack(integrals, occ_irrep, vir_irrep, screen, place, batch):
    occ_share, depth, total = integrals.shape
    shapes = [(occ_share, depth // 2, 2 * NARROW), (FEW_SHORT, depth // 2, 2 * NARROW)]
    shapes += [(occ_share, depth // 2, FOLD)] + [(n, depth, FOLD) for n in WIDE_CAPS]
    smem = pl.BlockSpec(memory_space=pltpu.SMEM)

    def kernel(*refs):
        pack_kernel(*refs, batch)

    return pl.pallas_call(
        kernel,
        grid_spec=pltpu.PrefetchScalarGridSpec(
            num_scalar_prefetch=4,
            grid=(occ_share // K_STEP,),
            in_specs=[
                pl.BlockSpec((K_STEP, depth, total), lambda k, *_: (k, 0, 0)),
                pl.BlockSpec((1, total), lambda k, *_: (0, 0)),
            ],
            out_specs=[pl.BlockSpec((K_STEP, depth // 2, 2 * NARROW), lambda k, *_: (k, 0, 0))]
            + [pl.BlockSpec(v, lambda k, *_: (0, 0, 0)) for v in shapes[1:]]
            + [smem] * 4,
            scratch_shapes=[
                pltpu.VMEM((depth, total), jnp.bfloat16),
                pltpu.VMEM((total, 2 * NARROW), jnp.bfloat16),
                pltpu.VMEM((depth, total), jnp.bfloat16),
                pltpu.VMEM((total, 8), jnp.int32),
                pltpu.SMEM((3,), jnp.int32),
            ],
        ),
        out_shape=[jax.ShapeDtypeStruct(v, jnp.bfloat16) for v in shapes]
        + [jax.ShapeDtypeStruct((n,), jnp.int32) for n in (occ_share, occ_share, occ_share, 1)],
        compiler_params=pltpu.CompilerParams(vmem_limit_bytes=32 * 1024 * 1024),
    )(occ_irrep, vir_irrep, screen, place, integrals, vir_irrep[None, :])


SLOTS = (0, 1, 3, 2)


def amplitude_rows(column_ref, row_ref, occ_ref, row, batch, share):
    column_ref[...] = label_columns(row_ref[...])
    column = column_ref[pl.ds(pl.multiple_of(row * share, share), share), :1]
    return jnp.concatenate([jnp.bitwise_xor(column, occ_ref[i]) for i in range(batch)], axis=0)


def write_quarters(total_ref, col, outs):
    rows, fold = total_ref.shape
    width, height = fold // 2, rows // 2
    for t, out_ref in enumerate(outs):
        goal = jnp.bitwise_xor(col, t)
        lanes = pl.ds(pl.multiple_of((goal % 2) * width, width), width)
        lines = pl.ds(pl.multiple_of((goal // 2) * height, height), height)
        out_ref[...] = total_ref[lines, lanes].reshape(out_ref.shape)


def chosen(refs, starts, pos, pick):
    block = None
    for n, group in enumerate(refs):
        inside = (pos >= starts[n]) & (pos < starts[n + 1])
        at = jnp.clip(pos - starts[n], 0, starts[n + 1] - starts[n] - 1)
        found = pick(group, at)
        found = jnp.where(inside, found, jnp.zeros_like(found))
        block = found if block is None else block + found
    return block


def make_sparse_kernel(few, n3, starts3):
    def kernel(occ_ref, vir_ref, pos2_ref, pos3_ref, posx_ref, place_ref, amp_ref, row_ref, *refs):
        narrow_refs, m2_ref = refs[:6], refs[6]
        m3_refs = [refs[7 + 3 * n:10 + 3 * n] for n in range(n3)]
        refs = refs[7 + 3 * n3:]
        outs, refs = (refs[:1], refs[1:]) if n3 else (refs[:4], refs[4:])
        (
            mix_ref, column_ref, narrow_sum, wide_sum, lhs_ref, fold_ref, narrow_rhs,
            short_rhs, wide_rhs, buffer, sems,
        ) = refs
        batch, k_all, share, total = amp_ref.shape
        rows = batch * share
        groups = k_all // K_STEP
        row, col = place_ref[0], place_ref[1]
        at_end = (row == 0) | (row == 3)
        big = largest_irrep(vir_ref)
        half = share // 2

        def fetch(group, slot):
            return pltpu.make_async_copy(
                amp_ref.at[:, pl.ds(group * K_STEP, K_STEP)], buffer.at[slot], sems.at[slot]
            )

        fetch(0, 0).start()
        column = amplitude_rows(column_ref, row_ref, occ_ref, row, batch, share)
        mix_ref[...] = as_bf16(jnp.bitwise_xor(column, row_ref[...]))
        narrow_sum[...] = jnp.zeros(narrow_sum.shape, jnp.float32)
        wide_sum[...] = jnp.zeros(wide_sum.shape, jnp.float32)
        lane = lax.broadcasted_iota(jnp.int32, (half, 2 * NARROW), 1)

        def spot(n, j):
            return pl.ds(pl.multiple_of((n * K_STEP + j) * share, share), share)

        @pl.loop(0, groups)
        def _(group):
            slot = group % 2

            @pl.when(group + 1 < groups)
            def _():
                fetch(group + 1, 1 - slot).start()

            fetch(group, slot).wait()

            @pl.loop(0, K_STEP)
            def _(j):
                k = group * K_STEP + j
                own, e1, o1 = [ref[k] for ref in narrow_refs[:3]]
                far = jnp.maximum(posx_ref[k], 0) if few else k
                e2, o2, e3 = [ref[far] for ref in narrow_refs[3:]]
                two = jnp.where(at_end, e2, o2)
                if few:
                    two, e3 = [jnp.where(posx_ref[k] >= 0, v, jnp.zeros_like(v)) for v in (two, e3)]
                for n, block in enumerate((own, e1, jnp.where(at_end, e3, o1), two)):
                    zero = jnp.zeros_like(block)
                    first = pl.multiple_of((n * K_STEP + j) * share, share)
                    narrow_rhs[pl.ds(first, half)] = jnp.where(lane < NARROW, block, zero)
                    narrow_rhs[pl.ds(first + half, half)] = jnp.where(lane < NARROW, zero, block)
                short = chosen([m2_ref], [0, m2_ref.shape[0]], pos2_ref[k], lambda ref, at: ref[at])
                short_rhs[spot(0, j)] = jnp.concatenate([short, short], axis=0)
                if n3:
                    for n in range(3):
                        block = chosen(m3_refs, starts3, pos3_ref[k], lambda group, at, n=n: group[n][at])
                        if n == 2:
                            block = jnp.where(at_end, jnp.zeros_like(block), block)
                        wide_rhs[spot(n, j)] = block
                wanted = as_bf16(jnp.full((rows, share), occ_ref[col * k_all + k]))
                folded = None
                for n, s in enumerate(SLOTS):
                    source = jnp.bitwise_xor(row, s)
                    place = pl.ds(pl.multiple_of(source * share, share), share)
                    tile = buffer[slot, :, j, :, place].reshape(rows, share)
                    piece = jnp.where(mix_ref[:, place] == wanted, tile, jnp.zeros_like(tile))
                    lhs_ref[:, spot(n, j)] = piece
                    folded = piece if folded is None else folded + piece
                fold_ref[:, spot(0, j)] = folded

            narrow_sum[...] += jnp.dot(lhs_ref[...], narrow_rhs[...], preferred_element_type=jnp.float32)
            wide = jnp.dot(fold_ref[...], short_rhs[...], preferred_element_type=jnp.float32)
            if n3:
                lhs = lhs_ref[:, :3 * K_STEP * share]
                wide += jnp.dot(lhs, wide_rhs[...], preferred_element_type=jnp.float32)
            wide_sum[...] += wide

        target = jnp.bitwise_xor(column, occ_ref[batch])
        both = narrow_sum[...]
        both = both + pltpu.roll(both, NARROW, 1)
        both = jnp.concatenate([both] * (FOLD // (2 * NARROW)), axis=1)
        combined = jnp.where(target == big, wide_sum[...], both)
        if n3:
            outs[0][...] = combined
        else:
            wide_sum[...] = combined
            write_quarters(wide_sum, col, outs)

    return kernel


def starts_of(arrays):
    starts = [0]
    for v in arrays:
        starts.append(starts[-1] + v.shape[0])
    return starts


def sparse_product(amplitudes, occ_irrep, vir_irrep, pos2, pos3, posx, place, narrow, few, m2, m3):
    batch, _, share, total = amplitudes.shape
    rows = batch * share
    vmem = pl.BlockSpec(memory_space=pltpu.VMEM)
    smem = pl.BlockSpec(memory_space=pltpu.SMEM)
    arrays = list(narrow) + [m2] + [v for group in m3 for v in group]
    depth = K_STEP * share
    if m3:
        out_shape = [jax.ShapeDtypeStruct((rows, FOLD), jnp.float32)]
    else:
        out_shape = [jax.ShapeDtypeStruct((batch // 2, share, FOLD // 2), jnp.float32)] * 4
    return pl.pallas_call(
        make_sparse_kernel(few, len(m3), starts_of([v[0] for v in m3])),
        in_specs=[smem] * 6 + [pl.BlockSpec(memory_space=pltpu.HBM)] + [vmem] * (1 + len(arrays)),
        out_specs=[vmem] * len(out_shape),
        out_shape=out_shape,
        scratch_shapes=[
            pltpu.VMEM((rows, total), jnp.bfloat16),
            pltpu.VMEM((total, 8), jnp.int32),
            pltpu.VMEM((rows, 2 * NARROW), jnp.float32),
            pltpu.VMEM((rows, FOLD), jnp.float32),
            pltpu.VMEM((rows, 4 * depth), jnp.bfloat16),
            pltpu.VMEM((rows, depth), jnp.bfloat16),
            pltpu.VMEM((4 * depth, 2 * NARROW), jnp.bfloat16),
            pltpu.VMEM((depth, FOLD), jnp.bfloat16),
            pltpu.VMEM((3 * depth if m3 else 16, FOLD), jnp.bfloat16),
            pltpu.VMEM((2, batch, K_STEP, share, total), jnp.bfloat16),
            pltpu.SemaphoreType.DMA((2,)),
        ],
        compiler_params=pltpu.CompilerParams(vmem_limit_bytes=48 * 1024 * 1024),
    )(occ_irrep, vir_irrep, pos2, pos3, posx, place, amplitudes, vir_irrep[None, :], *arrays)


def make_far_kernel(n3, starts3):
    def kernel(occ_ref, vir_ref, pos3_ref, place_ref, amp_ref, row_ref, total_in_ref, *refs):
        m3_refs = [refs[2 * n:2 * n + 2] for n in range(n3)]
        outs = refs[2 * n3:2 * n3 + 4]
        mix_ref, column_ref, total_ref, lhs_ref, rhs_ref, buffer, sems = refs[2 * n3 + 4:]
        batch, k_all, share, total = amp_ref.shape
        rows = batch * share
        groups = k_all // K_STEP
        row, col = place_ref[0], place_ref[1]
        at_end = (row == 0) | (row == 3)
        place = pl.ds(pl.multiple_of(jnp.bitwise_xor(row, 2) * share, share), share)

        def fetch(group):
            return pltpu.make_async_copy(
                amp_ref.at[:, pl.ds(group * K_STEP, K_STEP), :, place], buffer.at[group], sems.at[group]
            )

        for group in range(groups):
            fetch(group).start()
        column = amplitude_rows(column_ref, row_ref, occ_ref, row, batch, share)
        target = jnp.bitwise_xor(column, occ_ref[batch])
        mixed = jnp.bitwise_xor(column, row_ref[:, place])
        mix_ref[...] = as_bf16(jnp.where(target == largest_irrep(vir_ref), mixed, -1))
        total_ref[...] = total_in_ref[...]

        @pl.loop(0, groups)
        def _(group):
            fetch(group).wait()

            @pl.loop(0, K_STEP)
            def _(j):
                k = group * K_STEP + j
                wanted = as_bf16(jnp.full((rows, share), occ_ref[col * k_all + k]))
                tile = buffer[group, :, j].reshape(rows, share)
                here = pl.ds(pl.multiple_of(j * share, share), share)
                lhs_ref[:, here] = jnp.where(mix_ref[...] == wanted, tile, jnp.zeros_like(tile))
                rhs_ref[here] = chosen(
                    m3_refs, starts3, pos3_ref[k], lambda pair, at: jnp.where(at_end, pair[0][at], pair[1][at])
                )

            total_ref[...] += jnp.dot(lhs_ref[...], rhs_ref[...], preferred_element_type=jnp.float32)

        write_quarters(total_ref, col, outs)

    return kernel


def far_product(total, amplitudes, occ_irrep, vir_irrep, pos3, place, m3):
    batch, k_all, share, vir_total = amplitudes.shape
    rows = batch * share
    vmem = pl.BlockSpec(memory_space=pltpu.VMEM)
    smem = pl.BlockSpec(memory_space=pltpu.SMEM)
    groups = k_all // K_STEP
    return pl.pallas_call(
        make_far_kernel(len(m3), starts_of([v[0] for v in m3])),
        in_specs=[smem] * 4 + [pl.BlockSpec(memory_space=pltpu.HBM)] + [vmem] * (2 + 2 * len(m3)),
        out_specs=[vmem] * 4,
        out_shape=[jax.ShapeDtypeStruct((batch // 2, share, FOLD // 2), jnp.float32)] * 4,
        scratch_shapes=[
            pltpu.VMEM((rows, share), jnp.bfloat16),
            pltpu.VMEM((vir_total, 8), jnp.int32),
            pltpu.VMEM((rows, FOLD), jnp.float32),
            pltpu.VMEM((rows, K_STEP * share), jnp.bfloat16),
            pltpu.VMEM((K_STEP * share, FOLD), jnp.bfloat16),
            pltpu.VMEM((groups, batch, K_STEP, share, share), jnp.bfloat16),
            pltpu.SemaphoreType.DMA((groups,)),
        ],
        compiler_params=pltpu.CompilerParams(vmem_limit_bytes=48 * 1024 * 1024),
    )(occ_irrep, vir_irrep, pos3, place, amplitudes, vir_irrep[None, :], total, *[v for g in m3 for v in g])


def dense_product(amplitudes, whole, occ_irrep, occ_local, vir_local, vir_irrep):
    batch = amplitudes.shape[0]
    keep = (
        jnp.bitwise_xor(occ_irrep[:batch, None], occ_local[None, :])[:, :, None, None]
        == jnp.bitwise_xor(vir_local[:, None], vir_irrep[None, :])[None, None]
    )
    kept = jnp.where(keep, amplitudes, jnp.zeros_like(amplitudes))
    return lax.dot_general(
        kept, whole, (((1, 3), (0, 1)), ((), ())), preferred_element_type=jnp.float32
    )


def finish(cycle, occ_irrep, vir_irrep, occ_energy, vir_energy, a_start, a_size, b_start, b_size, batch):
    label_a = lax.dynamic_slice_in_dim(vir_irrep, a_start, a_size)
    label_b = lax.dynamic_slice_in_dim(vir_irrep, b_start, b_size)
    energy_a = lax.dynamic_slice_in_dim(vir_energy, a_start, a_size)
    energy_b = lax.dynamic_slice_in_dim(vir_energy, b_start, b_size)
    target = jnp.bitwise_xor(
        jnp.bitwise_xor(occ_irrep[:batch, None], occ_irrep[batch]), label_a[None, :]
    )
    keep = label_b[:, None, None] == target[None, :, :]
    denominator = (
        occ_energy[:batch][None, :, None]
        + occ_energy[batch]
        - energy_a[None, None, :]
        - energy_b[:, None, None]
    )
    swapped = jnp.transpose(cycle, (2, 0, 1))
    return jnp.where(keep, swapped, 0.0) / denominator


def on_square(amplitudes, integrals, occ_irrep, vir_irrep, screen):
    batch, occ_share, share, vir_total = amplitudes.shape
    row = lax.axis_index("row")
    col = lax.axis_index("col")
    place = jnp.stack([row, col]).astype(jnp.int32)
    narrow, few, m2, m3a, m3b, pos2, pos3, posx, form = pack(
        integrals, occ_irrep, vir_irrep, screen, place, batch
    )
    outer = [(0, 1), (1, 0), (2, 3), (3, 2)]
    inner = [(1, 2), (2, 1)]
    outward = [(1, 0), (2, 3)]
    ends = [(0, 3), (3, 0)]
    second = [(r, r ^ 2) for r in range(4)]

    def move(v, pairs):
        return lax.ppermute(v, "row", pairs)

    def summed(own):
        first = move(own, [(0, 1), (3, 2)])
        middle = move(own + first, inner)
        last = move(own + middle, outward)
        return own + first + middle + last

    def sparse(use_few, choose):
        def run(narrow, few, m2, m3a, m3b):
            short, wides = choose(m2, m3a, m3b)
            e1, o1 = move(narrow, outer), move(narrow, inner)
            if use_few:
                two = move(few, second)
                blocks = (narrow, e1, o1, two, two, move(few, ends))
            else:
                e2, o2 = move(o1, outward), move(e1, inner)
                blocks = (narrow, e1, o1, e2, o2, move(o2, outward))
            short = summed(short)
            near = [(own, move(own, outer), move(own, inner)) for own in wides]
            far = [(move(o, outward), move(e, inner)) for _, e, o in near]
            result = sparse_product(
                amplitudes, occ_irrep, vir_irrep, pos2, pos3, posx, place, blocks, use_few, short, near
            )
            if far:
                result = far_product(result[0], amplitudes, occ_irrep, vir_irrep, pos3, place, far)
            return list(result)

        return run

    def dense(*_):
        occ_local = lax.dynamic_slice_in_dim(occ_irrep, col * occ_share, occ_share)
        vir_local = lax.dynamic_slice_in_dim(vir_irrep, row * share, share)
        screen_rows = lax.dynamic_slice_in_dim(screen, col * occ_share, occ_share, 0)
        fold = folded_integrals(
            integrals, occ_local, vir_local, vir_irrep, occ_irrep[batch], screen_rows
        )
        whole = jnp.zeros((occ_share, vir_total, FOLD), fold.dtype)
        for s in range(4):
            block = move(fold, [(r, r ^ s) for r in range(4)]) if s else fold
            whole = lax.dynamic_update_slice_in_dim(whole, block, jnp.bitwise_xor(row, s) * share, 1)
        total = dense_product(amplitudes, whole, occ_irrep, occ_local, vir_local, vir_irrep)
        quarter = (batch // 2, share, FOLD // 2)
        goals = [jnp.bitwise_xor(col, t) for t in range(4)]
        return [
            lax.dynamic_slice(total, (g // 2 * quarter[0], 0, g % 2 * quarter[2]), quarter) for g in goals
        ]

    branches = [
        sparse(False, lambda m2, m3a, m3b: (m2, [])),
        sparse(False, lambda m2, m3a, m3b: (m2, [m3a[:FEW_WIDE]])),
        sparse(True, lambda m2, m3a, m3b: (m2[:FEW_SHORT], [m3a])),
        sparse(True, lambda m2, m3a, m3b: (m2[:FEW_SHORT], [m3a, m3b])),
        sparse(False, lambda m2, m3a, m3b: (m2, [m3a, m3b])),
        dense,
    ]
    quarters = lax.switch(form[0], branches, narrow, few, m2, m3a, m3b)
    mine = quarters[0]
    for t in (1, 2, 3):
        mine = mine + lax.ppermute(quarters[t], "col", [(q, q ^ t) for q in range(4)])
    places = [(r, q) for r in range(4) for q in range(4)]
    same = lax.ppermute(mine, ("row", "col"), [(r * 4 + q, q * 4 + r) for r, q in places])
    other = lax.ppermute(mine, ("row", "col"), [(r * 4 + q, (q ^ 2) * 4 + r) for r, q in places])
    upper = row // 2 == 1
    low = jnp.where(upper, other, same)
    high = jnp.where(upper, same, other)
    return jnp.concatenate([low, high], axis=0)


def on_any(amplitudes, integrals, occ_irrep, vir_irrep, screen):
    batch, occ_share, share, vir_total = amplitudes.shape
    row = lax.axis_index("row")
    col = lax.axis_index("col")
    occ_local = lax.dynamic_slice_in_dim(occ_irrep, col * occ_share, occ_share)
    vir_local = lax.dynamic_slice_in_dim(vir_irrep, row * share, share)
    screen_rows = lax.dynamic_slice_in_dim(screen, col * occ_share, occ_share, 0)
    fold = folded_integrals(
        integrals, occ_local, vir_local, vir_irrep, occ_irrep[batch], screen_rows
    )
    whole = lax.all_gather(fold, "row", axis=1, tiled=True)
    cycle = dense_product(amplitudes, whole, occ_irrep, occ_local, vir_local, vir_irrep)
    cycle = lax.psum(cycle, "col")
    cycle = jnp.concatenate([cycle] * (vir_total // FOLD), axis=2)
    cycle = lax.all_to_all(cycle, "row", split_axis=2, concat_axis=1, tiled=True)
    a_size = vir_total // lax.axis_size("col")
    return lax.dynamic_slice_in_dim(cycle, col * a_size, a_size, 1)


def on_device(amplitudes, integrals, occ_irrep, vir_irrep, screen, occ_energy, vir_energy):
    batch, _, vir_share, vir_total = amplitudes.shape
    square = lax.axis_size("row") == 4 and lax.axis_size("col") == 4
    form = on_square if square else on_any
    cycle = form(amplitudes, integrals, occ_irrep, vir_irrep, screen)
    a_size = vir_total // lax.axis_size("col")
    return finish(
        cycle, occ_irrep, vir_irrep, occ_energy, vir_energy,
        lax.axis_index("col") * a_size, a_size, lax.axis_index("row") * vir_share, vir_share, batch,
    )


def solution(mesh):
    in_specs = (
        P("parts", "col", "row", None),
        P(("parts", "col"), "row", None),
        P("parts"),
        P("parts"),
        P("parts", None),
        P("parts"),
        P("parts"),
    )
    out_specs = P("row", "parts", "col")
    return jax.shard_map(
        on_device, mesh=mesh, in_specs=in_specs, out_specs=out_specs, check_vma=False
    )
```

```python
import jax
import jax.numpy as jnp
from jax import lax
from jax.experimental import pallas as pl
from jax.experimental.pallas import tpu as pltpu
from jax.sharding import PartitionSpec as P

FOLD = 256
K_STEP = 5


def folded_integrals(integrals, occ_local, vir_local, vir_irrep, pair_label, screen_rows):
    irrep_codes = jnp.arange(8, dtype=jnp.int32)
    screen_local = jnp.sum(
        screen_rows[:, None, :] * (vir_local[None, :, None] == irrep_codes).astype(jnp.int32),
        axis=2,
    )
    target = jnp.bitwise_xor(
        jnp.bitwise_xor(occ_local[:, None], vir_local[None, :]), pair_label
    )
    target = jnp.where(screen_local == 1, target, -1)
    keep = target[:, :, None] == vir_irrep[None, None, :]
    kept = jnp.where(keep, integrals, jnp.zeros_like(integrals))
    return kept[:, :, :FOLD] + kept[:, :, FOLD:]


NARROW = 64
CAPS = (22, 3)
FEW_SHORT = 8
FEW_WIDE = 5


def largest_irrep(vir_ref):
    return jnp.where(vir_ref[0] == vir_ref[FOLD - 1], vir_ref[0], vir_ref[FOLD])


def label_columns(row_labels):
    return jnp.transpose(jnp.broadcast_to(row_labels, (8, row_labels.shape[1])))


def as_bf16(labels):
    return labels.astype(jnp.float32).astype(jnp.bfloat16)


def pack_kernel(
    occ_ref, vir_ref, screen_ref, place_ref, int_ref, row_ref,
    narrow_ref, few_ref, m2a_ref, m2b_ref, m3a_ref, m3b_ref, pos2_ref, pos3_ref, posx_ref, form_ref,
    mix_ref, big_mask_ref, column_ref, counts_ref, batch,
):
    step = pl.program_id(0)
    k_step, depth, total = int_ref.shape
    half = depth // 2
    row, col = place_ref[0], place_ref[1]
    pair_label = occ_ref[batch]
    big = largest_irrep(vir_ref)
    here = pl.ds(pl.multiple_of(row * depth, depth), depth)

    @pl.when(step == 0)
    def _():
        for n in range(3):
            counts_ref[n] = 0
        column_ref[...] = label_columns(row_ref[...])
        mix_ref[...] = as_bf16(jnp.bitwise_xor(column_ref[here, :1], row_ref[...]))
        is_big = jnp.where(row_ref[...] == big, 1.0, 0.0)
        big_mask_ref[...] = jnp.broadcast_to(is_big, big_mask_ref.shape).astype(jnp.bfloat16)

    lane = lax.broadcasted_iota(jnp.int32, (half, 2 * NARROW), 1)
    local = column_ref[here, :1]

    @pl.loop(0, k_step)
    def _(j):
        k = step * k_step + j
        k_whole = col * (k_step * pl.num_programs(0)) + k
        x = jnp.bitwise_xor(occ_ref[k_whole], pair_label)
        bits = screen_ref[k_whole, 0]
        for g in range(1, 8):
            bits = bits + screen_ref[k_whole, g] * (1 << g)
        wanted = as_bf16(jnp.full(mix_ref.shape, x))
        tile = int_ref[j]
        kept = jnp.where(mix_ref[...] == wanted, tile, jnp.zeros_like(tile))
        wide = kept * big_mask_ref[...]
        narrow = kept - wide
        wide = wide[:, :FOLD] + wide[:, FOLD:]
        narrow = narrow[:, :FOLD] + narrow[:, FOLD:]
        narrow = (narrow[:, : 2 * NARROW] + narrow[:, 2 * NARROW:]).astype(jnp.float32)
        narrow = narrow + pltpu.roll(narrow, NARROW, 1)
        on = jnp.bitwise_and(lax.shift_right_logical(jnp.full(local.shape, bits), local), 1) == 1
        narrow = jnp.where(on, narrow, 0.0)
        narrow = jnp.where(lane < NARROW, narrow[:half], narrow[half:]).astype(jnp.bfloat16)
        narrow_ref[j] = narrow
        on_big = screen_ref[k_whole, jnp.bitwise_xor(big, x)] == 1
        actives = (on_big & (x != 0), on_big & (x == 0), x != 0)
        pos2, pos3, posx = [jnp.where(active, counts_ref[n], -1) for n, active in enumerate(actives)]
        for n, active in enumerate(actives):
            counts_ref[n] = counts_ref[n] + active.astype(jnp.int32)
        pos2_ref[k], pos3_ref[k], posx_ref[k] = pos2, pos3, posx

        @pl.when((pos2 >= 0) & (pos2 < CAPS[0]))
        def _():
            m2a_ref[pos2] = wide[:half] + wide[half:]

        @pl.when(pos2 >= CAPS[0])
        def _():
            m2b_ref[pos2 - CAPS[0]] = wide[:half] + wide[half:]

        @pl.when((pos3 >= 0) & (pos3 < CAPS[0]))
        def _():
            m3a_ref[pos3] = wide

        @pl.when(pos3 >= CAPS[0])
        def _():
            m3b_ref[pos3 - CAPS[0]] = wide

        @pl.when((posx >= 0) & (posx < FEW_SHORT))
        def _():
            few_ref[posx] = narrow

    @pl.when(step == pl.num_programs(0) - 1)
    def _():
        labels = row_ref[...]
        lanes = lax.broadcasted_iota(jnp.int32, labels.shape, 1)
        ahead = pltpu.roll(labels, total - NARROW, 1)
        long = (labels == ahead) & (lanes < total - NARROW) & (labels != big)
        too_long = jnp.max(long.astype(jnp.int32)) == 1
        n2, n3, nx = counts_ref[0], counts_ref[1], counts_ref[2]
        one_label = occ_ref[0] == pair_label
        form = jnp.where((n3 <= CAPS[0]) & (nx <= FEW_SHORT), 2, 3)
        form = jnp.where((n3 <= FEW_WIDE) & (n2 <= CAPS[0]), 1, form)
        form = jnp.where(one_label, form, 4)
        form = jnp.where((n3 == 0) & (n2 <= CAPS[0]), 0, form)
        form_ref[0] = jnp.where(too_long, 4, form)


def pack(integrals, occ_irrep, vir_irrep, screen, place, batch):
    occ_share, depth, total = integrals.shape
    shapes = [(occ_share, depth // 2, 2 * NARROW), (FEW_SHORT, depth // 2, 2 * NARROW)]
    shapes += [(n, depth // 2, FOLD) for n in CAPS] + [(n, depth, FOLD) for n in CAPS]
    smem = pl.BlockSpec(memory_space=pltpu.SMEM)

    def kernel(*refs):
        pack_kernel(*refs, batch)

    return pl.pallas_call(
        kernel,
        grid_spec=pltpu.PrefetchScalarGridSpec(
            num_scalar_prefetch=4,
            grid=(occ_share // K_STEP,),
            in_specs=[
                pl.BlockSpec((K_STEP, depth, total), lambda k, *_: (k, 0, 0)),
                pl.BlockSpec((1, total), lambda k, *_: (0, 0)),
            ],
            out_specs=[pl.BlockSpec((K_STEP, depth // 2, 2 * NARROW), lambda k, *_: (k, 0, 0))]
            + [pl.BlockSpec(v, lambda k, *_: (0, 0, 0)) for v in shapes[1:]]
            + [smem] * 4,
            scratch_shapes=[
                pltpu.VMEM((depth, total), jnp.bfloat16),
                pltpu.VMEM((depth, total), jnp.bfloat16),
                pltpu.VMEM((total, 8), jnp.int32),
                pltpu.SMEM((3,), jnp.int32),
            ],
        ),
        out_shape=[jax.ShapeDtypeStruct(v, jnp.bfloat16) for v in shapes]
        + [jax.ShapeDtypeStruct((n,), jnp.int32) for n in (occ_share, occ_share, occ_share, 1)],
        compiler_params=pltpu.CompilerParams(vmem_limit_bytes=32 * 1024 * 1024),
    )(occ_irrep, vir_irrep, screen, place, integrals, vir_irrep[None, :])


SLOTS = (0, 1, 3, 2)


def amplitude_rows(column_ref, row_ref, occ_ref, row, batch, share):
    column_ref[...] = label_columns(row_ref[...])
    column = column_ref[pl.ds(pl.multiple_of(row * share, share), share), :1]
    return jnp.concatenate([jnp.bitwise_xor(column, occ_ref[i]) for i in range(batch)], axis=0)


def write_quarters(total_ref, col, outs):
    rows, fold = total_ref.shape
    width, height = fold // 2, rows // 2
    for t, out_ref in enumerate(outs):
        goal = jnp.bitwise_xor(col, t)
        lanes = pl.ds(pl.multiple_of((goal % 2) * width, width), width)
        lines = pl.ds(pl.multiple_of((goal // 2) * height, height), height)
        out_ref[...] = total_ref[lines, lanes].reshape(out_ref.shape)


def chosen(refs, starts, pos, pick):
    block = None
    for n, group in enumerate(refs):
        inside = (pos >= starts[n]) & (pos < starts[n + 1])
        at = jnp.clip(pos - starts[n], 0, starts[n + 1] - starts[n] - 1)
        found = pick(group, at)
        found = jnp.where(inside, found, jnp.zeros_like(found))
        block = found if block is None else block + found
    return block


def starts_of(arrays):
    starts = [0]
    for v in arrays:
        starts.append(starts[-1] + v.shape[0])
    return starts


def mask_kernel(occ_ref, place_ref, amp_ref, row_ref, lhs_ref, fold_ref, mix_ref, column_ref):
    group = pl.program_id(0)
    batch, k_step, share, total = amp_ref.shape
    rows = batch * share
    row, col = place_ref[0], place_ref[1]

    @pl.when(group == 0)
    def _():
        column = amplitude_rows(column_ref, row_ref, occ_ref, row, batch, share)
        mix_ref[...] = as_bf16(jnp.bitwise_xor(column, row_ref[...]))

    @pl.loop(0, k_step)
    def _(j):
        k_whole = (col * pl.num_programs(0) + group) * k_step + j
        wanted = as_bf16(jnp.full((rows, share), occ_ref[k_whole]))
        folded = None
        for n, s in enumerate(SLOTS):
            place = pl.ds(pl.multiple_of(jnp.bitwise_xor(row, s) * share, share), share)
            tile = amp_ref[:, j, :, place].reshape(rows, share)
            piece = jnp.where(mix_ref[:, place] == wanted, tile, jnp.zeros_like(tile))
            lhs_ref[0, :, pl.ds(pl.multiple_of((n * k_step + j) * share, share), share)] = piece
            folded = piece if folded is None else folded + piece
        fold_ref[0, :, pl.ds(pl.multiple_of(j * share, share), share)] = folded


def masked_amplitudes(amplitudes, occ_irrep, vir_irrep, place):
    batch, k_all, share, total = amplitudes.shape
    rows, groups = batch * share, k_all // K_STEP
    smem = pl.BlockSpec(memory_space=pltpu.SMEM)
    widths = (len(SLOTS) * K_STEP * share, K_STEP * share)
    return pl.pallas_call(
        mask_kernel,
        grid=(groups,),
        in_specs=[smem] * 2 + [
            pl.BlockSpec((batch, K_STEP, share, total), lambda g: (0, g, 0, 0)),
            pl.BlockSpec((1, total), lambda g: (0, 0)),
        ],
        out_specs=[pl.BlockSpec((1, rows, w), lambda g: (g, 0, 0)) for w in widths],
        out_shape=[jax.ShapeDtypeStruct((groups, rows, w), jnp.bfloat16) for w in widths],
        scratch_shapes=[pltpu.VMEM((rows, total), jnp.bfloat16), pltpu.VMEM((total, 8), jnp.int32)],
        compiler_params=pltpu.CompilerParams(vmem_limit_bytes=32 * 1024 * 1024),
    )(occ_irrep, place, amplitudes, vir_irrep[None, :])


def make_first_kernel(few, n3, starts3):
    def kernel(pos3_ref, posx_ref, place_ref, lhs_ref, *refs):
        narrow_refs = refs[:6]
        m3_refs = [refs[6 + 3 * n:9 + 3 * n] for n in range(n3)]
        narrow_sum, wide_sum, narrow_rhs, wide_rhs = refs[6 + 3 * n3:]
        group = pl.program_id(0)
        row = place_ref[0]
        at_end = (row == 0) | (row == 3)
        depth = lhs_ref.shape[2]
        share = depth // (len(SLOTS) * K_STEP)
        half = share // 2
        lane = lax.broadcasted_iota(jnp.int32, (half, 2 * NARROW), 1)

        @pl.when(group == 0)
        def _():
            narrow_sum[...] = jnp.zeros(narrow_sum.shape, jnp.float32)
            wide_sum[...] = jnp.zeros(wide_sum.shape, jnp.float32)

        @pl.loop(0, K_STEP)
        def _(j):
            k = group * K_STEP + j
            own, e1, o1 = [ref[k] for ref in narrow_refs[:3]]
            far = jnp.maximum(posx_ref[k], 0) if few else k
            e2, o2, e3 = [ref[far] for ref in narrow_refs[3:]]
            two = jnp.where(at_end, e2, o2)
            if few:
                two, e3 = [jnp.where(posx_ref[k] >= 0, v, jnp.zeros_like(v)) for v in (two, e3)]
            for n, block in enumerate((own, e1, jnp.where(at_end, e3, o1), two)):
                zero = jnp.zeros_like(block)
                first = pl.multiple_of((n * K_STEP + j) * share, share)
                narrow_rhs[pl.ds(first, half)] = jnp.where(lane < NARROW, block, zero)
                narrow_rhs[pl.ds(first + half, half)] = jnp.where(lane < NARROW, zero, block)
            for n in range(3 if n3 else 0):
                block = chosen(m3_refs, starts3, pos3_ref[k], lambda group, at, n=n: group[n][at])
                if n == 2:
                    block = jnp.where(at_end, jnp.zeros_like(block), block)
                wide_rhs[pl.ds(pl.multiple_of((n * K_STEP + j) * share, share), share)] = block

        narrow_sum[...] += jnp.dot(lhs_ref[0], narrow_rhs[...], preferred_element_type=jnp.float32)
        if n3:
            lhs = lhs_ref[0, :, :3 * K_STEP * share]
            wide_sum[...] += jnp.dot(lhs, wide_rhs[...], preferred_element_type=jnp.float32)

    return kernel


def first_product(lhs, pos3, posx, place, narrow, few, m3):
    groups, rows, depth = lhs.shape
    vmem = pl.BlockSpec(memory_space=pltpu.VMEM)
    smem = pl.BlockSpec(memory_space=pltpu.SMEM)
    arrays = list(narrow) + [v for group in m3 for v in group]
    wide = (rows, FOLD) if m3 else (16, FOLD)
    wide_depth = 3 * depth // len(SLOTS) if m3 else 16
    return pl.pallas_call(
        make_first_kernel(few, len(m3), starts_of([v[0] for v in m3])),
        grid=(groups,),
        in_specs=[smem] * 3 + [pl.BlockSpec((1, rows, depth), lambda g: (g, 0, 0))] + [vmem] * len(arrays),
        out_specs=[pl.BlockSpec(v, lambda g: (0, 0)) for v in ((rows, 2 * NARROW), wide)],
        out_shape=[jax.ShapeDtypeStruct(v, jnp.float32) for v in ((rows, 2 * NARROW), wide)],
        scratch_shapes=[
            pltpu.VMEM((depth, 2 * NARROW), jnp.bfloat16),
            pltpu.VMEM((wide_depth, FOLD), jnp.bfloat16),
        ],
        compiler_params=pltpu.CompilerParams(vmem_limit_bytes=48 * 1024 * 1024),
    )(pos3, posx, place, lhs, *arrays)


def make_last_kernel(n2, starts2, n3, starts3):
    def kernel(occ_ref, vir_ref, pos2_ref, pos3_ref, place_ref, fold_ref, far_ref, row_ref, narrow_ref, wide_ref, *refs):
        m2_refs = refs[:n2]
        m3_refs = [refs[n2 + 2 * n:n2 + 2 * n + 2] for n in range(n3)]
        refs = refs[n2 + 2 * n3:]
        outs, (column_ref, total_ref, short_rhs, far_rhs) = refs[:4], refs[4:]
        group = pl.program_id(0)
        row, col = place_ref[0], place_ref[1]
        at_end = (row == 0) | (row == 3)
        share = fold_ref.shape[2] // K_STEP
        batch = fold_ref.shape[1] // share

        @pl.when(group == 0)
        def _():
            total_ref[...] = wide_ref[...] if n3 else jnp.zeros(total_ref.shape, jnp.float32)

        @pl.loop(0, K_STEP)
        def _(j):
            k = group * K_STEP + j
            here = pl.ds(pl.multiple_of(j * share, share), share)
            short = chosen(m2_refs, starts2, pos2_ref[k], lambda ref, at: ref[at])
            short_rhs[here] = jnp.concatenate([short, short], axis=0)
            if n3:
                far_rhs[here] = chosen(
                    m3_refs, starts3, pos3_ref[k], lambda pair, at: jnp.where(at_end, pair[0][at], pair[1][at])
                )

        part = jnp.dot(fold_ref[0], short_rhs[...], preferred_element_type=jnp.float32)
        if n3:
            part += jnp.dot(far_ref[0], far_rhs[...], preferred_element_type=jnp.float32)
        total_ref[...] += part

        @pl.when(group == pl.num_programs(0) - 1)
        def _():
            column = amplitude_rows(column_ref, row_ref, occ_ref, row, batch, share)
            target = jnp.bitwise_xor(column, occ_ref[batch])
            both = narrow_ref[...]
            both = both + pltpu.roll(both, NARROW, 1)
            both = jnp.concatenate([both] * (FOLD // (2 * NARROW)), axis=1)
            total_ref[...] = jnp.where(target == largest_irrep(vir_ref), total_ref[...], both)
            write_quarters(total_ref, col, outs)

    return kernel


def last_product(lhs, fold, occ_irrep, vir_irrep, pos2, pos3, place, narrow_sum, wide_sum, m2, m3, batch):
    groups, rows, width = fold.shape
    share = rows // batch
    vmem = pl.BlockSpec(memory_space=pltpu.VMEM)
    smem = pl.BlockSpec(memory_space=pltpu.SMEM)
    arrays = [narrow_sum, wide_sum] + list(m2) + [v for group in m3 for v in group]
    last = len(SLOTS) - 1
    far_map = (lambda g: (g, 0, last)) if m3 else (lambda g: (0, 0, 0))
    quarter = (batch // 2, share, FOLD // 2)
    return pl.pallas_call(
        make_last_kernel(len(m2), starts_of(m2), len(m3), starts_of([v[0] for v in m3])),
        grid=(groups,),
        in_specs=[smem] * 5 + [
            pl.BlockSpec((1, rows, width), lambda g: (g, 0, 0)),
            pl.BlockSpec((1, rows, width), far_map) if m3 else pl.BlockSpec((1, 16, 128), far_map),
            pl.BlockSpec((1, vir_irrep.shape[0]), lambda g: (0, 0)),
        ] + [vmem] * len(arrays),
        out_specs=[pl.BlockSpec(quarter, lambda g: (0, 0, 0))] * 4,
        out_shape=[jax.ShapeDtypeStruct(quarter, jnp.float32)] * 4,
        scratch_shapes=[
            pltpu.VMEM((vir_irrep.shape[0], 8), jnp.int32),
            pltpu.VMEM((rows, FOLD), jnp.float32),
            pltpu.VMEM((width, FOLD), jnp.bfloat16),
            pltpu.VMEM((width if m3 else 16, FOLD), jnp.bfloat16),
        ],
        compiler_params=pltpu.CompilerParams(vmem_limit_bytes=48 * 1024 * 1024),
    )(occ_irrep, vir_irrep, pos2, pos3, place, fold, lhs, vir_irrep[None, :], *arrays)


def dense_product(amplitudes, whole, occ_irrep, occ_local, vir_local, vir_irrep):
    batch = amplitudes.shape[0]
    keep = (
        jnp.bitwise_xor(occ_irrep[:batch, None], occ_local[None, :])[:, :, None, None]
        == jnp.bitwise_xor(vir_local[:, None], vir_irrep[None, :])[None, None]
    )
    kept = jnp.where(keep, amplitudes, jnp.zeros_like(amplitudes))
    return lax.dot_general(
        kept, whole, (((1, 3), (0, 1)), ((), ())), preferred_element_type=jnp.float32
    )


def finish(cycle, occ_irrep, vir_irrep, occ_energy, vir_energy, a_start, a_size, b_start, b_size, batch):
    label_a = lax.dynamic_slice_in_dim(vir_irrep, a_start, a_size)
    label_b = lax.dynamic_slice_in_dim(vir_irrep, b_start, b_size)
    energy_a = lax.dynamic_slice_in_dim(vir_energy, a_start, a_size)
    energy_b = lax.dynamic_slice_in_dim(vir_energy, b_start, b_size)
    target = jnp.bitwise_xor(
        jnp.bitwise_xor(occ_irrep[:batch, None], occ_irrep[batch]), label_a[None, :]
    )
    keep = label_b[:, None, None] == target[None, :, :]
    denominator = (
        occ_energy[:batch][None, :, None]
        + occ_energy[batch]
        - energy_a[None, None, :]
        - energy_b[:, None, None]
    )
    swapped = jnp.transpose(cycle, (2, 0, 1))
    return jnp.where(keep, swapped, 0.0) / denominator


def on_square(amplitudes, integrals, occ_irrep, vir_irrep, screen):
    batch, occ_share, share, vir_total = amplitudes.shape
    row = lax.axis_index("row")
    col = lax.axis_index("col")
    place = jnp.stack([row, col]).astype(jnp.int32)
    narrow, few, m2a, m2b, m3a, m3b, pos2, pos3, posx, form = pack(
        integrals, occ_irrep, vir_irrep, screen, place, batch
    )
    outer = [(0, 1), (1, 0), (2, 3), (3, 2)]
    inner = [(1, 2), (2, 1)]
    inward = [(0, 1), (3, 2)]
    outward = [(1, 0), (2, 3)]
    ends = [(0, 3), (3, 0)]
    second = [(r, r ^ 2) for r in range(4)]

    def move(v, pairs):
        return lax.ppermute(v, "row", pairs)

    def sparse(use_few, choose):
        def run(narrow, few, m2a, m2b, m3a, m3b):
            shorts, wides = choose(m2a, m2b, m3a, m3b)
            h1 = [move(v, inward) for v in shorts]
            e1, o1 = move(narrow, outer), move(narrow, inner)
            near = [(own, move(own, outer), move(own, inner)) for own in wides]
            two, three = (move(few, second), move(few, ends)) if use_few else (None, None)
            lhs, fold = masked_amplitudes(amplitudes, occ_irrep, vir_irrep, place)
            h1, e1, o1, near, two, three, lhs, fold = lax.optimization_barrier(
                (h1, e1, o1, near, two, three, lhs, fold)
            )
            h2 = [move(own + v, inner) for own, v in zip(shorts, h1)]
            far = [(move(o, outward), move(e, inner)) for _, e, o in near]
            if use_few:
                blocks = (narrow, e1, o1, two, two, three)
            else:
                e2, o2 = move(o1, outward), move(e1, inner)
                h2, e2, o2 = lax.optimization_barrier((h2, e2, o2))
                blocks = (narrow, e1, o1, e2, o2, move(o2, outward))
            h3 = [move(own + v, outward) for own, v in zip(shorts, h2)]
            sums = [a + b + c + d for a, b, c, d in zip(shorts, h1, h2, h3)]
            narrow_sum, wide_sum = first_product(lhs, pos3, posx, place, blocks, use_few, near)
            return list(last_product(
                lhs, fold, occ_irrep, vir_irrep, pos2, pos3, place, narrow_sum, wide_sum, sums, far, batch
            ))

        return run

    def dense(*_):
        occ_local = lax.dynamic_slice_in_dim(occ_irrep, col * occ_share, occ_share)
        vir_local = lax.dynamic_slice_in_dim(vir_irrep, row * share, share)
        screen_rows = lax.dynamic_slice_in_dim(screen, col * occ_share, occ_share, 0)
        fold = folded_integrals(
            integrals, occ_local, vir_local, vir_irrep, occ_irrep[batch], screen_rows
        )
        whole = jnp.zeros((occ_share, vir_total, FOLD), fold.dtype)
        for s in range(4):
            block = move(fold, [(r, r ^ s) for r in range(4)]) if s else fold
            whole = lax.dynamic_update_slice_in_dim(whole, block, jnp.bitwise_xor(row, s) * share, 1)
        total = dense_product(amplitudes, whole, occ_irrep, occ_local, vir_local, vir_irrep)
        quarter = (batch // 2, share, FOLD // 2)
        goals = [jnp.bitwise_xor(col, t) for t in range(4)]
        return [
            lax.dynamic_slice(total, (g // 2 * quarter[0], 0, g % 2 * quarter[2]), quarter) for g in goals
        ]

    branches = [
        sparse(False, lambda m2a, m2b, m3a, m3b: ([m2a], [])),
        sparse(False, lambda m2a, m2b, m3a, m3b: ([m2a], [m3a[:FEW_WIDE]])),
        sparse(True, lambda m2a, m2b, m3a, m3b: ([m2a[:FEW_SHORT]], [m3a])),
        sparse(False, lambda m2a, m2b, m3a, m3b: ([m2a, m2b], [m3a, m3b])),
        dense,
    ]
    quarters = lax.switch(form[0], branches, narrow, few, m2a, m2b, m3a, m3b)
    mine = quarters[0]
    for t in (1, 2, 3):
        mine = mine + lax.ppermute(quarters[t], "col", [(q, q ^ t) for q in range(4)])
    places = [(r, q) for r in range(4) for q in range(4)]
    same = lax.ppermute(mine, ("row", "col"), [(r * 4 + q, q * 4 + r) for r, q in places])
    other = lax.ppermute(mine, ("row", "col"), [(r * 4 + q, (q ^ 2) * 4 + r) for r, q in places])
    upper = row // 2 == 1
    low = jnp.where(upper, other, same)
    high = jnp.where(upper, same, other)
    return jnp.concatenate([low, high], axis=0)


def on_any(amplitudes, integrals, occ_irrep, vir_irrep, screen):
    batch, occ_share, share, vir_total = amplitudes.shape
    row = lax.axis_index("row")
    col = lax.axis_index("col")
    occ_local = lax.dynamic_slice_in_dim(occ_irrep, col * occ_share, occ_share)
    vir_local = lax.dynamic_slice_in_dim(vir_irrep, row * share, share)
    screen_rows = lax.dynamic_slice_in_dim(screen, col * occ_share, occ_share, 0)
    fold = folded_integrals(
        integrals, occ_local, vir_local, vir_irrep, occ_irrep[batch], screen_rows
    )
    whole = lax.all_gather(fold, "row", axis=1, tiled=True)
    cycle = dense_product(amplitudes, whole, occ_irrep, occ_local, vir_local, vir_irrep)
    cycle = lax.psum(cycle, "col")
    cycle = jnp.concatenate([cycle] * (vir_total // FOLD), axis=2)
    cycle = lax.all_to_all(cycle, "row", split_axis=2, concat_axis=1, tiled=True)
    a_size = vir_total // lax.axis_size("col")
    return lax.dynamic_slice_in_dim(cycle, col * a_size, a_size, 1)


def on_device(amplitudes, integrals, occ_irrep, vir_irrep, screen, occ_energy, vir_energy):
    batch, _, vir_share, vir_total = amplitudes.shape
    square = lax.axis_size("row") == 4 and lax.axis_size("col") == 4
    form = on_square if square else on_any
    cycle = form(amplitudes, integrals, occ_irrep, vir_irrep, screen)
    a_size = vir_total // lax.axis_size("col")
    return finish(
        cycle, occ_irrep, vir_irrep, occ_energy, vir_energy,
        lax.axis_index("col") * a_size, a_size, lax.axis_index("row") * vir_share, vir_share, batch,
    )


def solution(mesh):
    in_specs = (
        P("parts", "col", "row", None),
        P(("parts", "col"), "row", None),
        P("parts"),
        P("parts"),
        P("parts", None),
        P("parts"),
        P("parts"),
    )
    out_specs = P("row", "parts", "col")
    return jax.shard_map(
        on_device, mesh=mesh, in_specs=in_specs, out_specs=out_specs, check_vma=False
    )
```

```python
import jax
import jax.numpy as jnp
from jax import lax
from jax.experimental import pallas as pl
from jax.experimental.pallas import tpu as pltpu
from jax.sharding import PartitionSpec as P

FOLD = 256
K_STEP = 5


def folded_integrals(integrals, occ_local, vir_local, vir_irrep, pair_label, screen_rows):
    irrep_codes = jnp.arange(8, dtype=jnp.int32)
    screen_local = jnp.sum(
        screen_rows[:, None, :] * (vir_local[None, :, None] == irrep_codes).astype(jnp.int32),
        axis=2,
    )
    target = jnp.bitwise_xor(
        jnp.bitwise_xor(occ_local[:, None], vir_local[None, :]), pair_label
    )
    target = jnp.where(screen_local == 1, target, -1)
    keep = target[:, :, None] == vir_irrep[None, None, :]
    kept = jnp.where(keep, integrals, jnp.zeros_like(integrals))
    return kept[:, :, :FOLD] + kept[:, :, FOLD:]


NARROW = 64
CAPS = (22, 3)
FEW_SHORT = 8
FEW_WIDE = 5


def largest_irrep(vir_ref):
    return jnp.where(vir_ref[0] == vir_ref[FOLD - 1], vir_ref[0], vir_ref[FOLD])


def label_columns(row_labels):
    return jnp.transpose(jnp.broadcast_to(row_labels, (8, row_labels.shape[1])))


def as_bf16(labels):
    return labels.astype(jnp.float32).astype(jnp.bfloat16)


def pack_kernel(
    occ_ref, vir_ref, screen_ref, place_ref, int_ref, row_ref,
    narrow_ref, few_ref, m2a_ref, m2b_ref, m3a_ref, m3b_ref, pos2_ref, pos3_ref, posx_ref, form_ref,
    mix_ref, big_mask_ref, column_ref, counts_ref, batch,
):
    step = pl.program_id(0)
    k_step, depth, total = int_ref.shape
    half = depth // 2
    row, col = place_ref[0], place_ref[1]
    pair_label = occ_ref[batch]
    big = largest_irrep(vir_ref)
    here = pl.ds(pl.multiple_of(row * depth, depth), depth)

    @pl.when(step == 0)
    def _():
        for n in range(3):
            counts_ref[n] = 0
        column_ref[...] = label_columns(row_ref[...])
        mix_ref[...] = as_bf16(jnp.bitwise_xor(column_ref[here, :1], row_ref[...]))
        is_big = jnp.where(row_ref[...] == big, 1.0, 0.0)
        big_mask_ref[...] = jnp.broadcast_to(is_big, big_mask_ref.shape).astype(jnp.bfloat16)

    lane = lax.broadcasted_iota(jnp.int32, (half, 2 * NARROW), 1)
    local = column_ref[here, :1]

    for j in range(k_step):
        k = step * k_step + j
        k_whole = col * (k_step * pl.num_programs(0)) + k
        x = jnp.bitwise_xor(occ_ref[k_whole], pair_label)
        bits = screen_ref[k_whole, 0]
        for g in range(1, 8):
            bits = bits + screen_ref[k_whole, g] * (1 << g)
        wanted = as_bf16(jnp.full(mix_ref.shape, x))
        tile = int_ref[j]
        kept = jnp.where(mix_ref[...] == wanted, tile, jnp.zeros_like(tile))
        wide = kept * big_mask_ref[...]
        narrow = kept - wide
        wide = wide[:, :FOLD] + wide[:, FOLD:]
        narrow = narrow[:, :FOLD] + narrow[:, FOLD:]
        narrow = (narrow[:, : 2 * NARROW] + narrow[:, 2 * NARROW:]).astype(jnp.float32)
        narrow = narrow + pltpu.roll(narrow, NARROW, 1)
        on = jnp.bitwise_and(lax.shift_right_logical(jnp.full(local.shape, bits), local), 1) == 1
        narrow = jnp.where(on, narrow, 0.0)
        narrow = jnp.where(lane < NARROW, narrow[:half], narrow[half:]).astype(jnp.bfloat16)
        narrow_ref[j] = narrow
        on_big = screen_ref[k_whole, jnp.bitwise_xor(big, x)] == 1
        actives = (on_big & (x != 0), on_big & (x == 0), x != 0)
        pos2, pos3, posx = [jnp.where(active, counts_ref[n], -1) for n, active in enumerate(actives)]
        for n, active in enumerate(actives):
            counts_ref[n] = counts_ref[n] + active.astype(jnp.int32)
        pos2_ref[k], pos3_ref[k], posx_ref[k] = pos2, pos3, posx

        @pl.when((pos2 >= 0) & (pos2 < CAPS[0]))
        def _():
            m2a_ref[pos2] = wide[:half] + wide[half:]

        @pl.when(pos2 >= CAPS[0])
        def _():
            m2b_ref[pos2 - CAPS[0]] = wide[:half] + wide[half:]

        @pl.when((pos3 >= 0) & (pos3 < CAPS[0]))
        def _():
            m3a_ref[pos3] = wide

        @pl.when(pos3 >= CAPS[0])
        def _():
            m3b_ref[pos3 - CAPS[0]] = wide

        @pl.when((posx >= 0) & (posx < FEW_SHORT))
        def _():
            few_ref[posx] = narrow

    @pl.when(step == pl.num_programs(0) - 1)
    def _():
        labels = row_ref[...]
        lanes = lax.broadcasted_iota(jnp.int32, labels.shape, 1)
        ahead = pltpu.roll(labels, total - NARROW, 1)
        long = (labels == ahead) & (lanes < total - NARROW) & (labels != big)
        too_long = jnp.max(long.astype(jnp.int32)) == 1
        n2, n3, nx = counts_ref[0], counts_ref[1], counts_ref[2]
        one_label = occ_ref[0] == pair_label
        form = jnp.where((n3 <= CAPS[0]) & (nx <= FEW_SHORT), 2, 3)
        form = jnp.where((n3 <= FEW_WIDE) & (n2 <= CAPS[0]), 1, form)
        form = jnp.where(one_label, form, 4)
        form = jnp.where((n3 == 0) & (n2 <= CAPS[0]), 0, form)
        form_ref[0] = jnp.where(too_long, 4, form)


def pack(integrals, occ_irrep, vir_irrep, screen, place, batch):
    occ_share, depth, total = integrals.shape
    shapes = [(occ_share, depth // 2, 2 * NARROW), (FEW_SHORT, depth // 2, 2 * NARROW)]
    shapes += [(n, depth // 2, FOLD) for n in CAPS] + [(n, depth, FOLD) for n in CAPS]
    smem = pl.BlockSpec(memory_space=pltpu.SMEM)

    def kernel(*refs):
        pack_kernel(*refs, batch)

    return pl.pallas_call(
        kernel,
        grid_spec=pltpu.PrefetchScalarGridSpec(
            num_scalar_prefetch=4,
            grid=(occ_share // K_STEP,),
            in_specs=[
                pl.BlockSpec((K_STEP, depth, total), lambda k, *_: (k, 0, 0)),
                pl.BlockSpec((1, total), lambda k, *_: (0, 0)),
            ],
            out_specs=[pl.BlockSpec((K_STEP, depth // 2, 2 * NARROW), lambda k, *_: (k, 0, 0))]
            + [pl.BlockSpec(v, lambda k, *_: (0, 0, 0)) for v in shapes[1:]]
            + [smem] * 4,
            scratch_shapes=[
                pltpu.VMEM((depth, total), jnp.bfloat16),
                pltpu.VMEM((depth, total), jnp.bfloat16),
                pltpu.VMEM((total, 8), jnp.int32),
                pltpu.SMEM((3,), jnp.int32),
            ],
        ),
        out_shape=[jax.ShapeDtypeStruct(v, jnp.bfloat16) for v in shapes]
        + [jax.ShapeDtypeStruct((n,), jnp.int32) for n in (occ_share, occ_share, occ_share, 1)],
        compiler_params=pltpu.CompilerParams(vmem_limit_bytes=32 * 1024 * 1024),
    )(occ_irrep, vir_irrep, screen, place, integrals, vir_irrep[None, :])


SLOTS = (0, 1, 3, 2)


def amplitude_rows(column_ref, row_ref, occ_ref, row, batch, share):
    column_ref[...] = label_columns(row_ref[...])
    column = column_ref[pl.ds(pl.multiple_of(row * share, share), share), :1]
    return jnp.concatenate([jnp.bitwise_xor(column, occ_ref[i]) for i in range(batch)], axis=0)


def write_quarters(total_ref, col, outs):
    rows, fold = total_ref.shape
    width, height = fold // 2, rows // 2
    for t, out_ref in enumerate(outs):
        goal = jnp.bitwise_xor(col, t)
        lanes = pl.ds(pl.multiple_of((goal % 2) * width, width), width)
        lines = pl.ds(pl.multiple_of((goal // 2) * height, height), height)
        out_ref[...] = total_ref[lines, lanes].reshape(out_ref.shape)


def chosen(refs, starts, pos, pick):
    block = None
    for n, group in enumerate(refs):
        inside = (pos >= starts[n]) & (pos < starts[n + 1])
        at = jnp.clip(pos - starts[n], 0, starts[n + 1] - starts[n] - 1)
        found = pick(group, at)
        found = jnp.where(inside, found, jnp.zeros_like(found))
        block = found if block is None else block + found
    return block


def starts_of(arrays):
    starts = [0]
    for v in arrays:
        starts.append(starts[-1] + v.shape[0])
    return starts


def cost(micros):
    return pl.CostEstimate(flops=int(micros * 1e9), bytes_accessed=int(micros * 3e6), transcendentals=0)


def mask_kernel(occ_ref, place_ref, amp_ref, row_ref, lhs_ref, fold_ref, mix_ref, column_ref, amp_buffer, sems):
    batch, k_all, share, total = amp_ref.shape
    rows, groups = batch * share, k_all // K_STEP
    row, col = place_ref[0], place_ref[1]

    def fetch(group):
        slot = group % 2
        source = amp_ref.at[:, pl.ds(group * K_STEP, K_STEP)]
        return pltpu.make_async_copy(source, amp_buffer.at[slot], sems.at[slot])

    fetch(0).start()
    column = amplitude_rows(column_ref, row_ref, occ_ref, row, batch, share)
    mix_ref[...] = as_bf16(jnp.bitwise_xor(column, row_ref[...]))

    @pl.loop(0, groups)
    def _(group):
        slot = group % 2

        @pl.when(group + 1 < groups)
        def _():
            fetch(group + 1).start()

        fetch(group).wait()

        @pl.loop(0, K_STEP)
        def _(j):
            wanted = as_bf16(jnp.full((rows, share), occ_ref[col * k_all + group * K_STEP + j]))
            folded = None
            for n, s in enumerate(SLOTS):
                place = pl.ds(pl.multiple_of(jnp.bitwise_xor(row, s) * share, share), share)
                tile = amp_buffer[slot, :, j, :, place].reshape(rows, share)
                piece = jnp.where(mix_ref[:, place] == wanted, tile, jnp.zeros_like(tile))
                lhs_ref[group, :, pl.ds(pl.multiple_of((n * K_STEP + j) * share, share), share)] = piece
                folded = piece if folded is None else folded + piece
            fold_ref[group, :, pl.ds(pl.multiple_of(j * share, share), share)] = folded


def masked_amplitudes(amplitudes, occ_irrep, vir_irrep, place):
    batch, k_all, share, total = amplitudes.shape
    rows, groups = batch * share, k_all // K_STEP
    smem = pl.BlockSpec(memory_space=pltpu.SMEM)
    vmem = pl.BlockSpec(memory_space=pltpu.VMEM)
    hbm = pl.BlockSpec(memory_space=pltpu.HBM)
    widths = (len(SLOTS) * K_STEP * share, K_STEP * share)
    return pl.pallas_call(
        mask_kernel,
        in_specs=[smem, smem, hbm, vmem],
        out_specs=[vmem, vmem],
        out_shape=[jax.ShapeDtypeStruct((groups, rows, w), jnp.bfloat16) for w in widths],
        scratch_shapes=[
            pltpu.VMEM((rows, total), jnp.bfloat16),
            pltpu.VMEM((total, 8), jnp.int32),
            pltpu.VMEM((2, batch, K_STEP, share, total), jnp.bfloat16),
            pltpu.SemaphoreType.DMA((2,)),
        ],
        cost_estimate=cost(7),
        compiler_params=pltpu.CompilerParams(vmem_limit_bytes=28 * 1024 * 1024),
    )(occ_irrep, place, amplitudes, vir_irrep[None, :])


def make_first_kernel(few, n3, starts3):
    def kernel(pos3_ref, posx_ref, place_ref, lhs_ref, *refs):
        narrow_refs = refs[:6]
        m3_refs = [refs[6 + 3 * n:9 + 3 * n] for n in range(n3)]
        narrow_sum, wide_sum, narrow_rhs, wide_rhs = refs[6 + 3 * n3:]
        row = place_ref[0]
        at_end = (row == 0) | (row == 3)
        groups, _, depth = lhs_ref.shape
        share = depth // (len(SLOTS) * K_STEP)
        half = share // 2
        lane = lax.broadcasted_iota(jnp.int32, (half, 2 * NARROW), 1)

        narrow_sum[...] = jnp.zeros(narrow_sum.shape, jnp.float32)
        wide_sum[...] = jnp.zeros(wide_sum.shape, jnp.float32)

        @pl.loop(0, groups)
        def _(group):
            @pl.loop(0, K_STEP)
            def _(j):
                k = group * K_STEP + j
                own, e1, o1 = [ref[k] for ref in narrow_refs[:3]]
                far = jnp.maximum(posx_ref[k], 0) if few else k
                e2, o2, e3 = [ref[far] for ref in narrow_refs[3:]]
                two = jnp.where(at_end, e2, o2)
                if few:
                    two, e3 = [jnp.where(posx_ref[k] >= 0, v, jnp.zeros_like(v)) for v in (two, e3)]
                for n, block in enumerate((own, e1, jnp.where(at_end, e3, o1), two)):
                    zero = jnp.zeros_like(block)
                    first = pl.multiple_of((n * K_STEP + j) * share, share)
                    narrow_rhs[pl.ds(first, half)] = jnp.where(lane < NARROW, block, zero)
                    narrow_rhs[pl.ds(first + half, half)] = jnp.where(lane < NARROW, zero, block)
                for n in range(3 if n3 else 0):
                    block = chosen(m3_refs, starts3, pos3_ref[k], lambda group, at, n=n: group[n][at])
                    if n == 2:
                        block = jnp.where(at_end, jnp.zeros_like(block), block)
                    wide_rhs[pl.ds(pl.multiple_of((n * K_STEP + j) * share, share), share)] = block

            narrow_sum[...] += jnp.dot(lhs_ref[group], narrow_rhs[...], preferred_element_type=jnp.float32)
            if n3:
                lhs = lhs_ref[group, :, :3 * K_STEP * share]
                wide_sum[...] += jnp.dot(lhs, wide_rhs[...], preferred_element_type=jnp.float32)

    return kernel


def first_product(lhs, pos3, posx, place, narrow, few, m3):
    groups, rows, depth = lhs.shape
    vmem = pl.BlockSpec(memory_space=pltpu.VMEM)
    smem = pl.BlockSpec(memory_space=pltpu.SMEM)
    arrays = list(narrow) + [v for group in m3 for v in group]
    wide = (rows, FOLD) if m3 else (16, FOLD)
    wide_depth = 3 * depth // len(SLOTS) if m3 else 16
    return pl.pallas_call(
        make_first_kernel(few, len(m3), starts_of([v[0] for v in m3])),
        in_specs=[smem] * 3 + [vmem] * (1 + len(arrays)),
        out_specs=[vmem] * 2,
        out_shape=[jax.ShapeDtypeStruct(v, jnp.float32) for v in ((rows, 2 * NARROW), wide)],
        scratch_shapes=[
            pltpu.VMEM((depth, 2 * NARROW), jnp.bfloat16),
            pltpu.VMEM((wide_depth, FOLD), jnp.bfloat16),
        ],
        cost_estimate=cost(9 if m3 else 6),
        compiler_params=pltpu.CompilerParams(vmem_limit_bytes=32 * 1024 * 1024),
    )(pos3, posx, place, lhs, *arrays)


def make_last_kernel(n2, starts2, n3, starts3):
    def kernel(occ_ref, vir_ref, pos2_ref, pos3_ref, place_ref, fold_ref, lhs_ref, row_ref, narrow_ref, wide_ref, *refs):
        m2_refs = refs[:n2]
        m3_refs = [refs[n2 + 2 * n:n2 + 2 * n + 2] for n in range(n3)]
        refs = refs[n2 + 2 * n3:]
        outs = refs[:4]
        column_ref, total_ref, short_rhs, far_rhs = refs[4:]
        row, col = place_ref[0], place_ref[1]
        at_end = (row == 0) | (row == 3)
        groups, rows, width = fold_ref.shape
        share = width // K_STEP
        batch = rows // share
        last = len(SLOTS) - 1

        @pl.loop(0, groups * K_STEP)
        def _(k):
            here = pl.ds(pl.multiple_of(k * share, share), share)
            short = chosen(m2_refs, starts2, pos2_ref[k], lambda ref, at: ref[at])
            short_rhs[here] = jnp.concatenate([short, short], axis=0)
            if n3:
                far_rhs[here] = chosen(
                    m3_refs, starts3, pos3_ref[k], lambda pair, at: jnp.where(at_end, pair[0][at], pair[1][at])
                )

        column = amplitude_rows(column_ref, row_ref, occ_ref, row, batch, share)
        target = jnp.bitwise_xor(column, occ_ref[batch])
        both = narrow_ref[...]
        both = both + pltpu.roll(both, NARROW, 1)
        both = jnp.concatenate([both] * (FOLD // (2 * NARROW)), axis=1)
        part = wide_ref[...] if n3 else 0.0
        for group in range(groups):
            here = pl.ds(group * width, width)
            part += jnp.dot(fold_ref[group], short_rhs[here], preferred_element_type=jnp.float32)
            if n3:
                far = lhs_ref[group, :, last * width:]
                part += jnp.dot(far, far_rhs[here], preferred_element_type=jnp.float32)
        total_ref[...] = jnp.where(target == largest_irrep(vir_ref), part, both)
        write_quarters(total_ref, col, outs)

    return kernel


def last_product(lhs, fold, occ_irrep, vir_irrep, pos2, pos3, place, narrow_sum, wide_sum, m2, m3, batch):
    groups, rows, width = fold.shape
    share = rows // batch
    vmem = pl.BlockSpec(memory_space=pltpu.VMEM)
    smem = pl.BlockSpec(memory_space=pltpu.SMEM)
    arrays = [narrow_sum, wide_sum] + list(m2) + [v for group in m3 for v in group]
    quarter = (batch // 2, share, FOLD // 2)
    whole = groups * width
    lhs = [lhs] if m3 else [jnp.zeros((8, 128), jnp.bfloat16)]
    return pl.pallas_call(
        make_last_kernel(len(m2), starts_of(m2), len(m3), starts_of([v[0] for v in m3])),
        in_specs=[smem] * 5 + [vmem] * (3 + len(arrays)),
        out_specs=[vmem] * 4,
        out_shape=[jax.ShapeDtypeStruct(quarter, jnp.float32)] * 4,
        scratch_shapes=[
            pltpu.VMEM((vir_irrep.shape[0], 8), jnp.int32),
            pltpu.VMEM((rows, FOLD), jnp.float32),
            pltpu.VMEM((whole, FOLD), jnp.bfloat16),
            pltpu.VMEM((whole if m3 else 16, FOLD), jnp.bfloat16),
        ],
        cost_estimate=cost(4 if m3 else 2),
        compiler_params=pltpu.CompilerParams(vmem_limit_bytes=32 * 1024 * 1024),
    )(occ_irrep, vir_irrep, pos2, pos3, place, fold, *lhs, vir_irrep[None, :], *arrays)


def dense_product(amplitudes, whole, occ_irrep, occ_local, vir_local, vir_irrep):
    batch = amplitudes.shape[0]
    keep = (
        jnp.bitwise_xor(occ_irrep[:batch, None], occ_local[None, :])[:, :, None, None]
        == jnp.bitwise_xor(vir_local[:, None], vir_irrep[None, :])[None, None]
    )
    kept = jnp.where(keep, amplitudes, jnp.zeros_like(amplitudes))
    return lax.dot_general(
        kept, whole, (((1, 3), (0, 1)), ((), ())), preferred_element_type=jnp.float32
    )


def finish(cycle, occ_irrep, vir_irrep, occ_energy, vir_energy, a_start, a_size, b_start, b_size, batch):
    label_a = lax.dynamic_slice_in_dim(vir_irrep, a_start, a_size)
    label_b = lax.dynamic_slice_in_dim(vir_irrep, b_start, b_size)
    energy_a = lax.dynamic_slice_in_dim(vir_energy, a_start, a_size)
    energy_b = lax.dynamic_slice_in_dim(vir_energy, b_start, b_size)
    target = jnp.bitwise_xor(
        jnp.bitwise_xor(occ_irrep[:batch, None], occ_irrep[batch]), label_a[None, :]
    )
    keep = label_b[:, None, None] == target[None, :, :]
    denominator = (
        occ_energy[:batch][None, :, None]
        + occ_energy[batch]
        - energy_a[None, None, :]
        - energy_b[:, None, None]
    )
    swapped = jnp.transpose(cycle, (2, 0, 1))
    return jnp.where(keep, swapped, 0.0) / denominator


def on_square(amplitudes, integrals, occ_irrep, vir_irrep, screen):
    batch, occ_share, share, vir_total = amplitudes.shape
    row = lax.axis_index("row")
    col = lax.axis_index("col")
    place = jnp.stack([row, col]).astype(jnp.int32)
    narrow, few, m2a, m2b, m3a, m3b, pos2, pos3, posx, form = pack(
        integrals, occ_irrep, vir_irrep, screen, place, batch
    )
    outer = [(0, 1), (1, 0), (2, 3), (3, 2)]
    inner = [(1, 2), (2, 1)]
    inward = [(0, 1), (3, 2)]
    outward = [(1, 0), (2, 3)]
    ends = [(0, 3), (3, 0)]
    second = [(r, r ^ 2) for r in range(4)]

    def move(v, pairs):
        return lax.ppermute(v, "row", pairs)

    def sparse(use_few, choose):
        def run(narrow, few, m2a, m2b, m3a, m3b):
            shorts, wides = choose(m2a, m2b, m3a, m3b)
            h1 = [move(v, inward) for v in shorts]
            e1, o1 = move(narrow, outer), move(narrow, inner)
            near = [(own, move(own, outer), move(own, inner)) for own in wides]
            two, three = (move(few, second), move(few, ends)) if use_few else (None, None)
            lhs, fold = masked_amplitudes(amplitudes, occ_irrep, vir_irrep, place)
            near, e1, o1, two, three = lax.optimization_barrier((near, e1, o1, two, three))
            h1, e1, o1, _ = lax.optimization_barrier((h1, e1, o1, fold))
            h2 = [move(own + v, inner) for own, v in zip(shorts, h1)]
            far = [(move(o, outward), move(e, inner)) for _, e, o in near]
            if use_few:
                blocks = (narrow, e1, o1, two, two, three)
            else:
                e2, o2 = move(o1, outward), move(e1, inner)
                h2, e2, o2 = lax.optimization_barrier((h2, e2, o2))
                blocks = (narrow, e1, o1, e2, o2, move(o2, outward))
            h3 = [move(own + v, outward) for own, v in zip(shorts, h2)]
            sums = [a + b + c + d for a, b, c, d in zip(shorts, h1, h2, h3)]
            narrow_sum, wide_sum = first_product(lhs, pos3, posx, place, blocks, use_few, near)
            return list(last_product(
                lhs, fold, occ_irrep, vir_irrep, pos2, pos3, place, narrow_sum, wide_sum, sums, far, batch
            ))

        return run

    def dense(*_):
        occ_local = lax.dynamic_slice_in_dim(occ_irrep, col * occ_share, occ_share)
        vir_local = lax.dynamic_slice_in_dim(vir_irrep, row * share, share)
        screen_rows = lax.dynamic_slice_in_dim(screen, col * occ_share, occ_share, 0)
        fold = folded_integrals(
            integrals, occ_local, vir_local, vir_irrep, occ_irrep[batch], screen_rows
        )
        whole = jnp.zeros((occ_share, vir_total, FOLD), fold.dtype)
        for s in range(4):
            block = move(fold, [(r, r ^ s) for r in range(4)]) if s else fold
            whole = lax.dynamic_update_slice_in_dim(whole, block, jnp.bitwise_xor(row, s) * share, 1)
        total = dense_product(amplitudes, whole, occ_irrep, occ_local, vir_local, vir_irrep)
        quarter = (batch // 2, share, FOLD // 2)
        goals = [jnp.bitwise_xor(col, t) for t in range(4)]
        return [
            lax.dynamic_slice(total, (g // 2 * quarter[0], 0, g % 2 * quarter[2]), quarter) for g in goals
        ]

    branches = [
        sparse(False, lambda m2a, m2b, m3a, m3b: ([m2a], [])),
        sparse(False, lambda m2a, m2b, m3a, m3b: ([m2a], [m3a[:FEW_WIDE]])),
        sparse(True, lambda m2a, m2b, m3a, m3b: ([m2a[:FEW_SHORT]], [m3a])),
        sparse(False, lambda m2a, m2b, m3a, m3b: ([m2a, m2b], [m3a, m3b])),
        dense,
    ]
    quarters = lax.switch(form[0], branches, narrow, few, m2a, m2b, m3a, m3b)
    mine = quarters[0]
    for t in (1, 2, 3):
        mine = mine + lax.ppermute(quarters[t], "col", [(q, q ^ t) for q in range(4)])
    places = [(r, q) for r in range(4) for q in range(4)]
    same = lax.ppermute(mine, ("row", "col"), [(r * 4 + q, q * 4 + r) for r, q in places])
    other = lax.ppermute(mine, ("row", "col"), [(r * 4 + q, (q ^ 2) * 4 + r) for r, q in places])
    upper = row // 2 == 1
    low = jnp.where(upper, other, same)
    high = jnp.where(upper, same, other)
    return jnp.concatenate([low, high], axis=0)


def on_any(amplitudes, integrals, occ_irrep, vir_irrep, screen):
    batch, occ_share, share, vir_total = amplitudes.shape
    row = lax.axis_index("row")
    col = lax.axis_index("col")
    occ_local = lax.dynamic_slice_in_dim(occ_irrep, col * occ_share, occ_share)
    vir_local = lax.dynamic_slice_in_dim(vir_irrep, row * share, share)
    screen_rows = lax.dynamic_slice_in_dim(screen, col * occ_share, occ_share, 0)
    fold = folded_integrals(
        integrals, occ_local, vir_local, vir_irrep, occ_irrep[batch], screen_rows
    )
    whole = lax.all_gather(fold, "row", axis=1, tiled=True)
    cycle = dense_product(amplitudes, whole, occ_irrep, occ_local, vir_local, vir_irrep)
    cycle = lax.psum(cycle, "col")
    cycle = jnp.concatenate([cycle] * (vir_total // FOLD), axis=2)
    cycle = lax.all_to_all(cycle, "row", split_axis=2, concat_axis=1, tiled=True)
    a_size = vir_total // lax.axis_size("col")
    return lax.dynamic_slice_in_dim(cycle, col * a_size, a_size, 1)


def on_device(amplitudes, integrals, occ_irrep, vir_irrep, screen, occ_energy, vir_energy):
    batch, _, vir_share, vir_total = amplitudes.shape
    square = lax.axis_size("row") == 4 and lax.axis_size("col") == 4
    form = on_square if square else on_any
    cycle = form(amplitudes, integrals, occ_irrep, vir_irrep, screen)
    a_size = vir_total // lax.axis_size("col")
    return finish(
        cycle, occ_irrep, vir_irrep, occ_energy, vir_energy,
        lax.axis_index("col") * a_size, a_size, lax.axis_index("row") * vir_share, vir_share, batch,
    )


def solution(mesh):
    in_specs = (
        P("parts", "col", "row", None),
        P(("parts", "col"), "row", None),
        P("parts"),
        P("parts"),
        P("parts", None),
        P("parts"),
        P("parts"),
    )
    out_specs = P("row", "parts", "col")
    return jax.shard_map(
        on_device, mesh=mesh, in_specs=in_specs, out_specs=out_specs, check_vma=False
    )
```

```python
import jax
import jax.numpy as jnp
from jax import lax
from jax.experimental import pallas as pl
from jax.experimental.pallas import tpu as pltpu
from jax.sharding import PartitionSpec as P

FOLD = 256
K_STEP = 5


def folded_integrals(integrals, occ_local, vir_local, vir_irrep, pair_label, screen_rows):
    irrep_codes = jnp.arange(8, dtype=jnp.int32)
    screen_local = jnp.sum(
        screen_rows[:, None, :] * (vir_local[None, :, None] == irrep_codes).astype(jnp.int32),
        axis=2,
    )
    target = jnp.bitwise_xor(
        jnp.bitwise_xor(occ_local[:, None], vir_local[None, :]), pair_label
    )
    target = jnp.where(screen_local == 1, target, -1)
    keep = target[:, :, None] == vir_irrep[None, None, :]
    kept = jnp.where(keep, integrals, jnp.zeros_like(integrals))
    return kept[:, :, :FOLD] + kept[:, :, FOLD:]


NARROW = 64
CAPS = (22, 3)
FEW_SHORT = 8
FEW_WIDE = 5


def largest_irrep(vir_ref):
    return jnp.where(vir_ref[0] == vir_ref[FOLD - 1], vir_ref[0], vir_ref[FOLD])


def label_columns(row_labels):
    return jnp.transpose(jnp.broadcast_to(row_labels, (8, row_labels.shape[1])))


def as_bf16(labels):
    return labels.astype(jnp.float32).astype(jnp.bfloat16)


def pack_kernel(
    occ_ref, vir_ref, screen_ref, place_ref, int_ref, row_ref,
    narrow_ref, few_ref, m2a_ref, m2b_ref, m3a_ref, m3b_ref, pos2_ref, pos3_ref, posx_ref, form_ref,
    mix_ref, big_mask_ref, column_ref, counts_ref, batch,
):
    step = pl.program_id(0)
    k_step, depth, total = int_ref.shape
    half = depth // 2
    row, col = place_ref[0], place_ref[1]
    pair_label = occ_ref[batch]
    big = largest_irrep(vir_ref)
    here = pl.ds(pl.multiple_of(row * depth, depth), depth)

    @pl.when(step == 0)
    def _():
        for n in range(3):
            counts_ref[n] = 0
        column_ref[...] = label_columns(row_ref[...])
        mix_ref[...] = as_bf16(jnp.bitwise_xor(column_ref[here, :1], row_ref[...]))
        is_big = jnp.where(row_ref[...] == big, 1.0, 0.0)
        big_mask_ref[...] = jnp.broadcast_to(is_big, big_mask_ref.shape).astype(jnp.bfloat16)

    lane = lax.broadcasted_iota(jnp.int32, (half, 2 * NARROW), 1)
    local = column_ref[here, :1]

    for j in range(k_step):
        k = step * k_step + j
        k_whole = col * (k_step * pl.num_programs(0)) + k
        x = jnp.bitwise_xor(occ_ref[k_whole], pair_label)
        bits = screen_ref[k_whole, 0]
        for g in range(1, 8):
            bits = bits + screen_ref[k_whole, g] * (1 << g)
        wanted = as_bf16(jnp.full(mix_ref.shape, x))
        tile = int_ref[j]
        kept = jnp.where(mix_ref[...] == wanted, tile, jnp.zeros_like(tile))
        wide = kept * big_mask_ref[...]
        narrow = kept - wide
        wide = wide[:, :FOLD] + wide[:, FOLD:]
        narrow = narrow[:, :FOLD] + narrow[:, FOLD:]
        narrow = (narrow[:, : 2 * NARROW] + narrow[:, 2 * NARROW:]).astype(jnp.float32)
        narrow = narrow + pltpu.roll(narrow, NARROW, 1)
        on = jnp.bitwise_and(lax.shift_right_logical(jnp.full(local.shape, bits), local), 1) == 1
        narrow = jnp.where(on, narrow, 0.0)
        narrow = jnp.where(lane < NARROW, narrow[:half], narrow[half:]).astype(jnp.bfloat16)
        narrow_ref[j] = narrow
        on_big = screen_ref[k_whole, jnp.bitwise_xor(big, x)] == 1
        actives = (on_big & (x != 0), on_big & (x == 0), x != 0)
        pos2, pos3, posx = [jnp.where(active, counts_ref[n], -1) for n, active in enumerate(actives)]
        for n, active in enumerate(actives):
            counts_ref[n] = counts_ref[n] + active.astype(jnp.int32)
        pos2_ref[k], pos3_ref[k], posx_ref[k] = pos2, pos3, posx

        @pl.when((pos2 >= 0) & (pos2 < CAPS[0]))
        def _():
            m2a_ref[pos2] = wide[:half] + wide[half:]

        @pl.when(pos2 >= CAPS[0])
        def _():
            m2b_ref[pos2 - CAPS[0]] = wide[:half] + wide[half:]

        @pl.when((pos3 >= 0) & (pos3 < CAPS[0]))
        def _():
            m3a_ref[pos3] = wide

        @pl.when(pos3 >= CAPS[0])
        def _():
            m3b_ref[pos3 - CAPS[0]] = wide

        @pl.when((posx >= 0) & (posx < FEW_SHORT))
        def _():
            few_ref[posx] = narrow

    @pl.when(step == pl.num_programs(0) - 1)
    def _():
        labels = row_ref[...]
        lanes = lax.broadcasted_iota(jnp.int32, labels.shape, 1)
        ahead = pltpu.roll(labels, total - NARROW, 1)
        long = (labels == ahead) & (lanes < total - NARROW) & (labels != big)
        too_long = jnp.max(long.astype(jnp.int32)) == 1
        n2, n3, nx = counts_ref[0], counts_ref[1], counts_ref[2]
        one_label = occ_ref[0] == pair_label
        form = jnp.where((n3 <= CAPS[0]) & (nx <= FEW_SHORT), 2, 3)
        form = jnp.where((n3 <= FEW_WIDE) & (n2 <= CAPS[0]), 1, form)
        form = jnp.where(one_label, form, 4)
        form = jnp.where((n3 == 0) & (n2 <= CAPS[0]), 0, form)
        form_ref[0] = jnp.where(too_long, 4, form)


def pack(integrals, occ_irrep, vir_irrep, screen, place, batch):
    occ_share, depth, total = integrals.shape
    shapes = [(occ_share, depth // 2, 2 * NARROW), (FEW_SHORT, depth // 2, 2 * NARROW)]
    shapes += [(n, depth // 2, FOLD) for n in CAPS] + [(n, depth, FOLD) for n in CAPS]
    smem = pl.BlockSpec(memory_space=pltpu.SMEM)

    def kernel(*refs):
        pack_kernel(*refs, batch)

    return pl.pallas_call(
        kernel,
        grid_spec=pltpu.PrefetchScalarGridSpec(
            num_scalar_prefetch=4,
            grid=(occ_share // K_STEP,),
            in_specs=[
                pl.BlockSpec((K_STEP, depth, total), lambda k, *_: (k, 0, 0)),
                pl.BlockSpec((1, total), lambda k, *_: (0, 0)),
            ],
            out_specs=[pl.BlockSpec((K_STEP, depth // 2, 2 * NARROW), lambda k, *_: (k, 0, 0))]
            + [pl.BlockSpec(v, lambda k, *_: (0, 0, 0)) for v in shapes[1:]]
            + [smem] * 4,
            scratch_shapes=[
                pltpu.VMEM((depth, total), jnp.bfloat16),
                pltpu.VMEM((depth, total), jnp.bfloat16),
                pltpu.VMEM((total, 8), jnp.int32),
                pltpu.SMEM((3,), jnp.int32),
            ],
        ),
        out_shape=[jax.ShapeDtypeStruct(v, jnp.bfloat16) for v in shapes]
        + [jax.ShapeDtypeStruct((n,), jnp.int32) for n in (occ_share, occ_share, occ_share, 1)],
        compiler_params=pltpu.CompilerParams(vmem_limit_bytes=32 * 1024 * 1024),
    )(occ_irrep, vir_irrep, screen, place, integrals, vir_irrep[None, :])


SLOTS = (0, 1, 3, 2)
NEAR = 3


def amplitude_rows(column_ref, row_ref, occ_ref, row, batch, share):
    column_ref[...] = label_columns(row_ref[...])
    column = column_ref[pl.ds(pl.multiple_of(row * share, share), share), :1]
    return jnp.concatenate([jnp.bitwise_xor(column, occ_ref[i]) for i in range(batch)], axis=0)


def write_quarters(total_ref, col, outs):
    rows, fold = total_ref.shape
    width, height = fold // 2, rows // 2
    for t, out_ref in enumerate(outs):
        goal = jnp.bitwise_xor(col, t)
        lanes = pl.ds(pl.multiple_of((goal % 2) * width, width), width)
        lines = pl.ds(pl.multiple_of((goal // 2) * height, height), height)
        out_ref[...] = total_ref[lines, lanes].reshape(out_ref.shape)


def chosen(refs, starts, pos, pick):
    block = None
    for n, group in enumerate(refs):
        inside = (pos >= starts[n]) & (pos < starts[n + 1])
        at = jnp.clip(pos - starts[n], 0, starts[n + 1] - starts[n] - 1)
        found = pick(group, at)
        found = jnp.where(inside, found, jnp.zeros_like(found))
        block = found if block is None else block + found
    return block


def starts_of(arrays):
    starts = [0]
    for v in arrays:
        starts.append(starts[-1] + v.shape[0])
    return starts


def cost(micros):
    return pl.CostEstimate(flops=int(micros * 1e9), bytes_accessed=int(micros * 3e6), transcendentals=0)


def mask_kernel(occ_ref, place_ref, amp_ref, row_ref, lhs_ref, far_ref, fold_ref, mix_ref, column_ref, amp_buffer, sems):
    batch, k_all, share, total = amp_ref.shape
    rows, groups = batch * share, k_all // K_STEP
    row, col = place_ref[0], place_ref[1]

    def fetch(group):
        slot = group % 2
        source = amp_ref.at[:, pl.ds(group * K_STEP, K_STEP)]
        return pltpu.make_async_copy(source, amp_buffer.at[slot], sems.at[slot])

    fetch(0).start()
    column = amplitude_rows(column_ref, row_ref, occ_ref, row, batch, share)
    mix_ref[...] = as_bf16(jnp.bitwise_xor(column, row_ref[...]))

    @pl.loop(0, groups)
    def _(group):
        slot = group % 2

        @pl.when(group + 1 < groups)
        def _():
            fetch(group + 1).start()

        fetch(group).wait()

        @pl.loop(0, K_STEP)
        def _(j):
            wanted = as_bf16(jnp.full((rows, share), occ_ref[col * k_all + group * K_STEP + j]))
            folded = None
            for n, s in enumerate(SLOTS):
                place = pl.ds(pl.multiple_of(jnp.bitwise_xor(row, s) * share, share), share)
                tile = amp_buffer[slot, :, j, :, place].reshape(rows, share)
                piece = jnp.where(mix_ref[:, place] == wanted, tile, jnp.zeros_like(tile))
                if n < NEAR:
                    lhs_ref[group, :, pl.ds(pl.multiple_of((n * K_STEP + j) * share, share), share)] = piece
                else:
                    far_ref[group, :, pl.ds(pl.multiple_of(j * share, share), share)] = piece
                folded = piece if folded is None else folded + piece
            fold_ref[group, :, pl.ds(pl.multiple_of(j * share, share), share)] = folded


def masked_amplitudes(amplitudes, occ_irrep, vir_irrep, place):
    batch, k_all, share, total = amplitudes.shape
    rows, groups = batch * share, k_all // K_STEP
    smem = pl.BlockSpec(memory_space=pltpu.SMEM)
    vmem = pl.BlockSpec(memory_space=pltpu.VMEM)
    hbm = pl.BlockSpec(memory_space=pltpu.HBM)
    widths = (NEAR * K_STEP * share, K_STEP * share, K_STEP * share)
    return pl.pallas_call(
        mask_kernel,
        in_specs=[smem, smem, hbm, vmem],
        out_specs=[vmem] * 3,
        out_shape=[jax.ShapeDtypeStruct((groups, rows, w), jnp.bfloat16) for w in widths],
        scratch_shapes=[
            pltpu.VMEM((rows, total), jnp.bfloat16),
            pltpu.VMEM((total, 8), jnp.int32),
            pltpu.VMEM((2, batch, K_STEP, share, total), jnp.bfloat16),
            pltpu.SemaphoreType.DMA((2,)),
        ],
        cost_estimate=cost(7),
        compiler_params=pltpu.CompilerParams(vmem_limit_bytes=28 * 1024 * 1024),
    )(occ_irrep, place, amplitudes, vir_irrep[None, :])


def make_first_kernel(few, n3, starts3):
    def kernel(pos3_ref, posx_ref, place_ref, lhs_ref, far_ref, *refs):
        narrow_refs = refs[:6]
        m3_refs = [refs[6 + 3 * n:9 + 3 * n] for n in range(n3)]
        narrow_sum, wide_sum, narrow_rhs, wide_rhs = refs[6 + 3 * n3:]
        row = place_ref[0]
        at_end = (row == 0) | (row == 3)
        groups, _, depth = lhs_ref.shape
        share = depth // (NEAR * K_STEP)
        half = share // 2
        lane = lax.broadcasted_iota(jnp.int32, (half, 2 * NARROW), 1)

        narrow_sum[...] = jnp.zeros(narrow_sum.shape, jnp.float32)
        wide_sum[...] = jnp.zeros(wide_sum.shape, jnp.float32)

        @pl.loop(0, groups)
        def _(group):
            @pl.loop(0, K_STEP)
            def _(j):
                k = group * K_STEP + j
                own, e1, o1 = [ref[k] for ref in narrow_refs[:3]]
                far = jnp.maximum(posx_ref[k], 0) if few else k
                e2, o2, e3 = [ref[far] for ref in narrow_refs[3:]]
                two = jnp.where(at_end, e2, o2)
                if few:
                    two, e3 = [jnp.where(posx_ref[k] >= 0, v, jnp.zeros_like(v)) for v in (two, e3)]
                for n, block in enumerate((own, e1, jnp.where(at_end, e3, o1), two)):
                    zero = jnp.zeros_like(block)
                    first = pl.multiple_of((n * K_STEP + j) * share, share)
                    narrow_rhs[pl.ds(first, half)] = jnp.where(lane < NARROW, block, zero)
                    narrow_rhs[pl.ds(first + half, half)] = jnp.where(lane < NARROW, zero, block)
                for n in range(3 if n3 else 0):
                    block = chosen(m3_refs, starts3, pos3_ref[k], lambda group, at, n=n: group[n][at])
                    if n == 2:
                        block = jnp.where(at_end, jnp.zeros_like(block), block)
                    wide_rhs[pl.ds(pl.multiple_of((n * K_STEP + j) * share, share), share)] = block

            narrow = jnp.dot(lhs_ref[group], narrow_rhs[:depth], preferred_element_type=jnp.float32)
            narrow += jnp.dot(far_ref[group], narrow_rhs[depth:], preferred_element_type=jnp.float32)
            narrow_sum[...] += narrow
            if n3:
                wide_sum[...] += jnp.dot(lhs_ref[group], wide_rhs[...], preferred_element_type=jnp.float32)

    return kernel


def first_product(lhs, far_lhs, pos3, posx, place, narrow, few, m3):
    groups, rows, depth = lhs.shape
    vmem = pl.BlockSpec(memory_space=pltpu.VMEM)
    smem = pl.BlockSpec(memory_space=pltpu.SMEM)
    arrays = list(narrow) + [v for group in m3 for v in group]
    wide = (rows, FOLD) if m3 else (16, FOLD)
    wide_depth = depth if m3 else 16
    return pl.pallas_call(
        make_first_kernel(few, len(m3), starts_of([v[0] for v in m3])),
        in_specs=[smem] * 3 + [vmem] * (2 + len(arrays)),
        out_specs=[vmem] * 2,
        out_shape=[jax.ShapeDtypeStruct(v, jnp.float32) for v in ((rows, 2 * NARROW), wide)],
        scratch_shapes=[
            pltpu.VMEM((depth // NEAR * len(SLOTS), 2 * NARROW), jnp.bfloat16),
            pltpu.VMEM((wide_depth, FOLD), jnp.bfloat16),
        ],
        cost_estimate=cost(9 if m3 else 6),
        compiler_params=pltpu.CompilerParams(vmem_limit_bytes=32 * 1024 * 1024),
    )(pos3, posx, place, lhs, far_lhs, *arrays)


def make_last_kernel(n2, starts2, n3, starts3):
    def kernel(occ_ref, vir_ref, pos2_ref, pos3_ref, place_ref, fold_ref, far_ref, row_ref, narrow_ref, wide_ref, *refs):
        m2_refs = refs[:n2]
        m3_refs = [refs[n2 + 2 * n:n2 + 2 * n + 2] for n in range(n3)]
        refs = refs[n2 + 2 * n3:]
        outs = refs[:4]
        column_ref, total_ref, short_rhs, far_rhs = refs[4:]
        row, col = place_ref[0], place_ref[1]
        at_end = (row == 0) | (row == 3)
        groups, rows, width = fold_ref.shape
        share = width // K_STEP
        batch = rows // share
        @pl.loop(0, groups * K_STEP)
        def _(k):
            here = pl.ds(pl.multiple_of(k * share, share), share)
            short = chosen(m2_refs, starts2, pos2_ref[k], lambda ref, at: ref[at])
            short_rhs[here] = jnp.concatenate([short, short], axis=0)
            if n3:
                far_rhs[here] = chosen(
                    m3_refs, starts3, pos3_ref[k], lambda pair, at: jnp.where(at_end, pair[0][at], pair[1][at])
                )

        column = amplitude_rows(column_ref, row_ref, occ_ref, row, batch, share)
        target = jnp.bitwise_xor(column, occ_ref[batch])
        both = narrow_ref[...]
        both = both + pltpu.roll(both, NARROW, 1)
        both = jnp.concatenate([both] * (FOLD // (2 * NARROW)), axis=1)
        part = wide_ref[...] if n3 else 0.0
        for group in range(groups):
            here = pl.ds(group * width, width)
            part += jnp.dot(fold_ref[group], short_rhs[here], preferred_element_type=jnp.float32)
            if n3:
                part += jnp.dot(far_ref[group], far_rhs[here], preferred_element_type=jnp.float32)
        total_ref[...] = jnp.where(target == largest_irrep(vir_ref), part, both)
        write_quarters(total_ref, col, outs)

    return kernel


def last_product(far_lhs, fold, occ_irrep, vir_irrep, pos2, pos3, place, narrow_sum, wide_sum, m2, m3, batch):
    groups, rows, width = fold.shape
    share = rows // batch
    vmem = pl.BlockSpec(memory_space=pltpu.VMEM)
    smem = pl.BlockSpec(memory_space=pltpu.SMEM)
    arrays = [narrow_sum, wide_sum] + list(m2) + [v for group in m3 for v in group]
    quarter = (batch // 2, share, FOLD // 2)
    whole = groups * width
    far_lhs = far_lhs if m3 else jnp.zeros((8, 128), jnp.bfloat16)
    return pl.pallas_call(
        make_last_kernel(len(m2), starts_of(m2), len(m3), starts_of([v[0] for v in m3])),
        in_specs=[smem] * 5 + [vmem] * (3 + len(arrays)),
        out_specs=[vmem] * 4,
        out_shape=[jax.ShapeDtypeStruct(quarter, jnp.float32)] * 4,
        scratch_shapes=[
            pltpu.VMEM((vir_irrep.shape[0], 8), jnp.int32),
            pltpu.VMEM((rows, FOLD), jnp.float32),
            pltpu.VMEM((whole, FOLD), jnp.bfloat16),
            pltpu.VMEM((whole if m3 else 16, FOLD), jnp.bfloat16),
        ],
        cost_estimate=cost(4 if m3 else 2),
        compiler_params=pltpu.CompilerParams(vmem_limit_bytes=32 * 1024 * 1024),
    )(occ_irrep, vir_irrep, pos2, pos3, place, fold, far_lhs, vir_irrep[None, :], *arrays)


def dense_product(amplitudes, whole, occ_irrep, occ_local, vir_local, vir_irrep):
    batch = amplitudes.shape[0]
    keep = (
        jnp.bitwise_xor(occ_irrep[:batch, None], occ_local[None, :])[:, :, None, None]
        == jnp.bitwise_xor(vir_local[:, None], vir_irrep[None, :])[None, None]
    )
    kept = jnp.where(keep, amplitudes, jnp.zeros_like(amplitudes))
    return lax.dot_general(
        kept, whole, (((1, 3), (0, 1)), ((), ())), preferred_element_type=jnp.float32
    )


def finish(cycle, occ_irrep, vir_irrep, occ_energy, vir_energy, a_start, a_size, b_start, b_size, batch):
    label_a = lax.dynamic_slice_in_dim(vir_irrep, a_start, a_size)
    label_b = lax.dynamic_slice_in_dim(vir_irrep, b_start, b_size)
    energy_a = lax.dynamic_slice_in_dim(vir_energy, a_start, a_size)
    energy_b = lax.dynamic_slice_in_dim(vir_energy, b_start, b_size)
    target = jnp.bitwise_xor(
        jnp.bitwise_xor(occ_irrep[:batch, None], occ_irrep[batch]), label_a[None, :]
    )
    keep = label_b[:, None, None] == target[None, :, :]
    denominator = (
        occ_energy[:batch][None, :, None]
        + occ_energy[batch]
        - energy_a[None, None, :]
        - energy_b[:, None, None]
    )
    swapped = jnp.transpose(cycle, (2, 0, 1))
    return jnp.where(keep, swapped, 0.0) / denominator


def on_square(amplitudes, integrals, occ_irrep, vir_irrep, screen):
    batch, occ_share, share, vir_total = amplitudes.shape
    row = lax.axis_index("row")
    col = lax.axis_index("col")
    place = jnp.stack([row, col]).astype(jnp.int32)
    narrow, few, m2a, m2b, m3a, m3b, pos2, pos3, posx, form = pack(
        integrals, occ_irrep, vir_irrep, screen, place, batch
    )
    outer = [(0, 1), (1, 0), (2, 3), (3, 2)]
    inner = [(1, 2), (2, 1)]
    inward = [(0, 1), (3, 2)]
    outward = [(1, 0), (2, 3)]
    ends = [(0, 3), (3, 0)]
    second = [(r, r ^ 2) for r in range(4)]

    def move(v, pairs):
        return lax.ppermute(v, "row", pairs)

    def sparse(use_few, choose):
        def run(narrow, few, m2a, m2b, m3a, m3b):
            shorts, wides = choose(m2a, m2b, m3a, m3b)
            h1 = [move(v, inward) for v in shorts]
            e1, o1 = move(narrow, outer), move(narrow, inner)
            near = [(own, move(own, outer), move(own, inner)) for own in wides]
            two, three = (move(few, second), move(few, ends)) if use_few else (None, None)
            near, e1, o1, two, three = lax.optimization_barrier((near, e1, o1, two, three))
            amps = amplitudes
            if use_few:
                amps, near = lax.optimization_barrier((amps, near))
            lhs, far_lhs, fold = masked_amplitudes(amps, occ_irrep, vir_irrep, place)
            if not use_few:
                h1, e1, o1, _ = lax.optimization_barrier((h1, e1, o1, fold))
            h2 = [move(own + v, inner) for own, v in zip(shorts, h1)]
            far = [(move(o, outward), move(e, inner)) for _, e, o in near]
            if use_few:
                blocks = (narrow, e1, o1, two, two, three)
            else:
                e2, o2 = move(o1, outward), move(e1, inner)
                h2, e2, o2 = lax.optimization_barrier((h2, e2, o2))
                blocks = (narrow, e1, o1, e2, o2, move(o2, outward))
            h3 = [move(own + v, outward) for own, v in zip(shorts, h2)]
            sums = [a + b + c + d for a, b, c, d in zip(shorts, h1, h2, h3)]
            narrow_sum, wide_sum = first_product(
                lhs, far_lhs, pos3, posx, place, blocks, use_few, near
            )
            return list(last_product(
                far_lhs, fold, occ_irrep, vir_irrep, pos2, pos3, place, narrow_sum, wide_sum, sums, far, batch
            ))

        return run

    def dense(*_):
        occ_local = lax.dynamic_slice_in_dim(occ_irrep, col * occ_share, occ_share)
        vir_local = lax.dynamic_slice_in_dim(vir_irrep, row * share, share)
        screen_rows = lax.dynamic_slice_in_dim(screen, col * occ_share, occ_share, 0)
        fold = folded_integrals(
            integrals, occ_local, vir_local, vir_irrep, occ_irrep[batch], screen_rows
        )
        whole = jnp.zeros((occ_share, vir_total, FOLD), fold.dtype)
        for s in range(4):
            block = move(fold, [(r, r ^ s) for r in range(4)]) if s else fold
            whole = lax.dynamic_update_slice_in_dim(whole, block, jnp.bitwise_xor(row, s) * share, 1)
        total = dense_product(amplitudes, whole, occ_irrep, occ_local, vir_local, vir_irrep)
        quarter = (batch // 2, share, FOLD // 2)
        goals = [jnp.bitwise_xor(col, t) for t in range(4)]
        return [
            lax.dynamic_slice(total, (g // 2 * quarter[0], 0, g % 2 * quarter[2]), quarter) for g in goals
        ]

    branches = [
        sparse(False, lambda m2a, m2b, m3a, m3b: ([m2a], [])),
        sparse(False, lambda m2a, m2b, m3a, m3b: ([m2a], [m3a[:FEW_WIDE]])),
        sparse(True, lambda m2a, m2b, m3a, m3b: ([m2a[:FEW_SHORT]], [m3a])),
        sparse(False, lambda m2a, m2b, m3a, m3b: ([m2a, m2b], [m3a, m3b])),
        dense,
    ]
    quarters = lax.switch(form[0], branches, narrow, few, m2a, m2b, m3a, m3b)
    mine = quarters[0]
    for t in (1, 2, 3):
        mine = mine + lax.ppermute(quarters[t], "col", [(q, q ^ t) for q in range(4)])
    places = [(r, q) for r in range(4) for q in range(4)]
    same = lax.ppermute(mine, ("row", "col"), [(r * 4 + q, q * 4 + r) for r, q in places])
    other = lax.ppermute(mine, ("row", "col"), [(r * 4 + q, (q ^ 2) * 4 + r) for r, q in places])
    upper = row // 2 == 1
    low = jnp.where(upper, other, same)
    high = jnp.where(upper, same, other)
    return jnp.concatenate([low, high], axis=0)


def on_any(amplitudes, integrals, occ_irrep, vir_irrep, screen):
    batch, occ_share, share, vir_total = amplitudes.shape
    row = lax.axis_index("row")
    col = lax.axis_index("col")
    occ_local = lax.dynamic_slice_in_dim(occ_irrep, col * occ_share, occ_share)
    vir_local = lax.dynamic_slice_in_dim(vir_irrep, row * share, share)
    screen_rows = lax.dynamic_slice_in_dim(screen, col * occ_share, occ_share, 0)
    fold = folded_integrals(
        integrals, occ_local, vir_local, vir_irrep, occ_irrep[batch], screen_rows
    )
    whole = lax.all_gather(fold, "row", axis=1, tiled=True)
    cycle = dense_product(amplitudes, whole, occ_irrep, occ_local, vir_local, vir_irrep)
    cycle = lax.psum(cycle, "col")
    cycle = jnp.concatenate([cycle] * (vir_total // FOLD), axis=2)
    cycle = lax.all_to_all(cycle, "row", split_axis=2, concat_axis=1, tiled=True)
    a_size = vir_total // lax.axis_size("col")
    return lax.dynamic_slice_in_dim(cycle, col * a_size, a_size, 1)


def on_device(amplitudes, integrals, occ_irrep, vir_irrep, screen, occ_energy, vir_energy):
    batch, _, vir_share, vir_total = amplitudes.shape
    square = lax.axis_size("row") == 4 and lax.axis_size("col") == 4
    form = on_square if square else on_any
    cycle = form(amplitudes, integrals, occ_irrep, vir_irrep, screen)
    a_size = vir_total // lax.axis_size("col")
    return finish(
        cycle, occ_irrep, vir_irrep, occ_energy, vir_energy,
        lax.axis_index("col") * a_size, a_size, lax.axis_index("row") * vir_share, vir_share, batch,
    )


def solution(mesh):
    in_specs = (
        P("parts", "col", "row", None),
        P(("parts", "col"), "row", None),
        P("parts"),
        P("parts"),
        P("parts", None),
        P("parts"),
        P("parts"),
    )
    out_specs = P("row", "parts", "col")
    return jax.shard_map(
        on_device, mesh=mesh, in_specs=in_specs, out_specs=out_specs, check_vma=False
    )
```

```python
import jax
import jax.numpy as jnp
from jax import lax
from jax.experimental import pallas as pl
from jax.experimental.pallas import tpu as pltpu
from jax.sharding import PartitionSpec as P

FOLD = 256
K_STEP = 5


def folded_integrals(integrals, occ_local, vir_local, vir_irrep, pair_label, screen_rows):
    irrep_codes = jnp.arange(8, dtype=jnp.int32)
    screen_local = jnp.sum(
        screen_rows[:, None, :] * (vir_local[None, :, None] == irrep_codes).astype(jnp.int32),
        axis=2,
    )
    target = jnp.bitwise_xor(
        jnp.bitwise_xor(occ_local[:, None], vir_local[None, :]), pair_label
    )
    target = jnp.where(screen_local == 1, target, -1)
    keep = target[:, :, None] == vir_irrep[None, None, :]
    kept = jnp.where(keep, integrals, jnp.zeros_like(integrals))
    return kept[:, :, :FOLD] + kept[:, :, FOLD:]


NARROW = 64
CAPS = (22, 3)
FEW_SHORT = 8
FEW_WIDE = 5


def largest_irrep(vir_ref):
    return jnp.where(vir_ref[0] == vir_ref[FOLD - 1], vir_ref[0], vir_ref[FOLD])


def label_columns(row_labels):
    return jnp.transpose(jnp.broadcast_to(row_labels, (8, row_labels.shape[1])))


def as_bf16(labels):
    return labels.astype(jnp.float32).astype(jnp.bfloat16)


def pack_kernel(
    occ_ref, vir_ref, screen_ref, place_ref, int_ref, row_ref,
    narrow_ref, few_ref, m2a_ref, m2b_ref, m3a_ref, m3b_ref, pos2_ref, pos3_ref, posx_ref, form_ref,
    mix_ref, big_mask_ref, column_ref, counts_ref, batch,
):
    step = pl.program_id(0)
    k_step, depth, total = int_ref.shape
    half = depth // 2
    row, col = place_ref[0], place_ref[1]
    pair_label = occ_ref[batch]
    big = largest_irrep(vir_ref)
    here = pl.ds(pl.multiple_of(row * depth, depth), depth)

    @pl.when(step == 0)
    def _():
        for n in range(3):
            counts_ref[n] = 0
        column_ref[...] = label_columns(row_ref[...])
        mix_ref[...] = as_bf16(jnp.bitwise_xor(column_ref[here, :1], row_ref[...]))
        is_big = jnp.where(row_ref[...] == big, 1.0, 0.0)
        big_mask_ref[...] = jnp.broadcast_to(is_big, big_mask_ref.shape).astype(jnp.bfloat16)

    lane = lax.broadcasted_iota(jnp.int32, (half, 2 * NARROW), 1)
    local = column_ref[here, :1]

    for j in range(k_step):
        k = step * k_step + j
        k_whole = col * (k_step * pl.num_programs(0)) + k
        x = jnp.bitwise_xor(occ_ref[k_whole], pair_label)
        bits = screen_ref[k_whole, 0]
        for g in range(1, 8):
            bits = bits + screen_ref[k_whole, g] * (1 << g)
        wanted = as_bf16(jnp.full(mix_ref.shape, x))
        tile = int_ref[j]
        kept = jnp.where(mix_ref[...] == wanted, tile, jnp.zeros_like(tile))
        wide = kept * big_mask_ref[...]
        narrow = kept - wide
        wide = wide[:, :FOLD] + wide[:, FOLD:]
        narrow = narrow[:, :FOLD] + narrow[:, FOLD:]
        narrow = (narrow[:, : 2 * NARROW] + narrow[:, 2 * NARROW:]).astype(jnp.float32)
        narrow = narrow + pltpu.roll(narrow, NARROW, 1)
        on = jnp.bitwise_and(lax.shift_right_logical(jnp.full(local.shape, bits), local), 1) == 1
        narrow = jnp.where(on, narrow, 0.0)
        narrow = jnp.where(lane < NARROW, narrow[:half], narrow[half:]).astype(jnp.bfloat16)
        narrow_ref[j] = narrow
        on_big = screen_ref[k_whole, jnp.bitwise_xor(big, x)] == 1
        actives = (on_big & (x != 0), on_big & (x == 0), x != 0)
        pos2, pos3, posx = [jnp.where(active, counts_ref[n], -1) for n, active in enumerate(actives)]
        for n, active in enumerate(actives):
            counts_ref[n] = counts_ref[n] + active.astype(jnp.int32)
        pos2_ref[k], pos3_ref[k], posx_ref[k] = pos2, pos3, posx

        @pl.when((pos2 >= 0) & (pos2 < CAPS[0]))
        def _():
            m2a_ref[pos2] = wide[:half] + wide[half:]

        @pl.when(pos2 >= CAPS[0])
        def _():
            m2b_ref[pos2 - CAPS[0]] = wide[:half] + wide[half:]

        @pl.when((pos3 >= 0) & (pos3 < CAPS[0]))
        def _():
            m3a_ref[pos3] = wide

        @pl.when(pos3 >= CAPS[0])
        def _():
            m3b_ref[pos3 - CAPS[0]] = wide

        @pl.when((posx >= 0) & (posx < FEW_SHORT))
        def _():
            few_ref[posx] = narrow

    @pl.when(step == pl.num_programs(0) - 1)
    def _():
        labels = row_ref[...]
        lanes = lax.broadcasted_iota(jnp.int32, labels.shape, 1)
        ahead = pltpu.roll(labels, total - NARROW, 1)
        long = (labels == ahead) & (lanes < total - NARROW) & (labels != big)
        too_long = jnp.max(long.astype(jnp.int32)) == 1
        n2, n3, nx = counts_ref[0], counts_ref[1], counts_ref[2]
        one_label = occ_ref[0] == pair_label
        form = jnp.where((n3 <= CAPS[0]) & (nx <= FEW_SHORT), 2, 3)
        form = jnp.where((n3 <= FEW_WIDE) & (n2 <= CAPS[0]), 1, form)
        form = jnp.where(one_label, form, 4)
        form = jnp.where((n3 == 0) & (n2 <= CAPS[0]), 0, form)
        form_ref[0] = jnp.where(too_long, 4, form)


def pack(integrals, occ_irrep, vir_irrep, screen, place, batch):
    occ_share, depth, total = integrals.shape
    shapes = [(occ_share, depth // 2, 2 * NARROW), (FEW_SHORT, depth // 2, 2 * NARROW)]
    shapes += [(n, depth // 2, FOLD) for n in CAPS] + [(n, depth, FOLD) for n in CAPS]
    smem = pl.BlockSpec(memory_space=pltpu.SMEM)

    def kernel(*refs):
        pack_kernel(*refs, batch)

    return pl.pallas_call(
        kernel,
        grid_spec=pltpu.PrefetchScalarGridSpec(
            num_scalar_prefetch=4,
            grid=(occ_share // K_STEP,),
            in_specs=[
                pl.BlockSpec((K_STEP, depth, total), lambda k, *_: (k, 0, 0)),
                pl.BlockSpec((1, total), lambda k, *_: (0, 0)),
            ],
            out_specs=[pl.BlockSpec((K_STEP, depth // 2, 2 * NARROW), lambda k, *_: (k, 0, 0))]
            + [pl.BlockSpec(v, lambda k, *_: (0, 0, 0)) for v in shapes[1:]]
            + [smem] * 4,
            scratch_shapes=[
                pltpu.VMEM((depth, total), jnp.bfloat16),
                pltpu.VMEM((depth, total), jnp.bfloat16),
                pltpu.VMEM((total, 8), jnp.int32),
                pltpu.SMEM((3,), jnp.int32),
            ],
        ),
        out_shape=[jax.ShapeDtypeStruct(v, jnp.bfloat16) for v in shapes]
        + [jax.ShapeDtypeStruct((n,), jnp.int32) for n in (occ_share, occ_share, occ_share, 1)],
        compiler_params=pltpu.CompilerParams(vmem_limit_bytes=32 * 1024 * 1024),
    )(occ_irrep, vir_irrep, screen, place, integrals, vir_irrep[None, :])


SLOTS = (0, 1, 3, 2)
NEAR = 3


def amplitude_rows(column_ref, row_ref, occ_ref, row, batch, share):
    column_ref[...] = label_columns(row_ref[...])
    column = column_ref[pl.ds(pl.multiple_of(row * share, share), share), :1]
    return jnp.concatenate([jnp.bitwise_xor(column, occ_ref[i]) for i in range(batch)], axis=0)


def write_quarters(total_ref, col, outs):
    rows, fold = total_ref.shape
    width, height = fold // 2, rows // 2
    for t, out_ref in enumerate(outs):
        goal = jnp.bitwise_xor(col, t)
        lanes = pl.ds(pl.multiple_of((goal % 2) * width, width), width)
        lines = pl.ds(pl.multiple_of((goal // 2) * height, height), height)
        out_ref[...] = total_ref[lines, lanes].reshape(out_ref.shape)


def chosen(refs, starts, pos, pick):
    block = None
    for n, group in enumerate(refs):
        inside = (pos >= starts[n]) & (pos < starts[n + 1])
        at = jnp.clip(pos - starts[n], 0, starts[n + 1] - starts[n] - 1)
        found = pick(group, at)
        found = jnp.where(inside, found, jnp.zeros_like(found))
        block = found if block is None else block + found
    return block


def starts_of(arrays):
    starts = [0]
    for v in arrays:
        starts.append(starts[-1] + v.shape[0])
    return starts


def cost(micros):
    return pl.CostEstimate(flops=int(micros * 1e9), bytes_accessed=int(micros * 3e6), transcendentals=0)


def mask_kernel(occ_ref, place_ref, amp_ref, row_ref, lhs_ref, far_ref, fold_ref, mix_ref, column_ref, amp_buffer, sems):
    batch, k_all, share, total = amp_ref.shape
    rows, groups = batch * share, k_all // K_STEP
    row, col = place_ref[0], place_ref[1]

    def fetch(group):
        slot = group % 2
        source = amp_ref.at[:, pl.ds(group * K_STEP, K_STEP)]
        return pltpu.make_async_copy(source, amp_buffer.at[slot], sems.at[slot])

    fetch(0).start()
    column = amplitude_rows(column_ref, row_ref, occ_ref, row, batch, share)
    mix_ref[...] = as_bf16(jnp.bitwise_xor(column, row_ref[...]))

    @pl.loop(0, groups)
    def _(group):
        slot = group % 2

        @pl.when(group + 1 < groups)
        def _():
            fetch(group + 1).start()

        fetch(group).wait()

        @pl.loop(0, K_STEP)
        def _(j):
            wanted = as_bf16(jnp.full((rows, share), occ_ref[col * k_all + group * K_STEP + j]))
            folded = None
            for n, s in enumerate(SLOTS):
                place = pl.ds(pl.multiple_of(jnp.bitwise_xor(row, s) * share, share), share)
                tile = amp_buffer[slot, :, j, :, place].reshape(rows, share)
                piece = jnp.where(mix_ref[:, place] == wanted, tile, jnp.zeros_like(tile))
                if n < NEAR:
                    lhs_ref[group, :, pl.ds(pl.multiple_of((n * K_STEP + j) * share, share), share)] = piece
                else:
                    far_ref[group, :, pl.ds(pl.multiple_of(j * share, share), share)] = piece
                folded = piece if folded is None else folded + piece
            fold_ref[group, :, pl.ds(pl.multiple_of(j * share, share), share)] = folded


def masked_amplitudes(amplitudes, occ_irrep, vir_irrep, place):
    batch, k_all, share, total = amplitudes.shape
    rows, groups = batch * share, k_all // K_STEP
    smem = pl.BlockSpec(memory_space=pltpu.SMEM)
    vmem = pl.BlockSpec(memory_space=pltpu.VMEM)
    hbm = pl.BlockSpec(memory_space=pltpu.HBM)
    widths = (NEAR * K_STEP * share, K_STEP * share, K_STEP * share)
    return pl.pallas_call(
        mask_kernel,
        in_specs=[smem, smem, hbm, vmem],
        out_specs=[vmem] * 3,
        out_shape=[jax.ShapeDtypeStruct((groups, rows, w), jnp.bfloat16) for w in widths],
        scratch_shapes=[
            pltpu.VMEM((rows, total), jnp.bfloat16),
            pltpu.VMEM((total, 8), jnp.int32),
            pltpu.VMEM((2, batch, K_STEP, share, total), jnp.bfloat16),
            pltpu.SemaphoreType.DMA((2,)),
        ],
        cost_estimate=cost(7),
        compiler_params=pltpu.CompilerParams(vmem_limit_bytes=28 * 1024 * 1024),
    )(occ_irrep, place, amplitudes, vir_irrep[None, :])


def make_first_kernel(few, n3, starts3):
    def kernel(pos3_ref, posx_ref, place_ref, lhs_ref, far_ref, *refs):
        narrow_refs = refs[:6]
        m3_refs = [refs[6 + 3 * n:9 + 3 * n] for n in range(n3)]
        narrow_sum, wide_sum, narrow_rhs, wide_rhs = refs[6 + 3 * n3:]
        row = place_ref[0]
        at_end = (row == 0) | (row == 3)
        groups, _, depth = lhs_ref.shape
        share = depth // (NEAR * K_STEP)
        half = share // 2
        lane = lax.broadcasted_iota(jnp.int32, (half, 2 * NARROW), 1)

        narrow_sum[...] = jnp.zeros(narrow_sum.shape, jnp.float32)
        wide_sum[...] = jnp.zeros(wide_sum.shape, jnp.float32)

        @pl.loop(0, groups)
        def _(group):
            @pl.loop(0, K_STEP)
            def _(j):
                k = group * K_STEP + j
                own, e1, o1 = [ref[k] for ref in narrow_refs[:3]]
                far = jnp.maximum(posx_ref[k], 0) if few else k
                e2, o2, e3 = [ref[far] for ref in narrow_refs[3:]]
                two = jnp.where(at_end, e2, o2)
                if few:
                    two, e3 = [jnp.where(posx_ref[k] >= 0, v, jnp.zeros_like(v)) for v in (two, e3)]
                for n, block in enumerate((own, e1, jnp.where(at_end, e3, o1), two)):
                    zero = jnp.zeros_like(block)
                    first = pl.multiple_of((n * K_STEP + j) * share, share)
                    narrow_rhs[pl.ds(first, half)] = jnp.where(lane < NARROW, block, zero)
                    narrow_rhs[pl.ds(first + half, half)] = jnp.where(lane < NARROW, zero, block)
                for n in range(3 if n3 else 0):
                    block = chosen(m3_refs, starts3, pos3_ref[k], lambda group, at, n=n: group[n][at])
                    if n == 2:
                        block = jnp.where(at_end, jnp.zeros_like(block), block)
                    wide_rhs[pl.ds(pl.multiple_of((n * K_STEP + j) * share, share), share)] = block

            narrow = jnp.dot(lhs_ref[group], narrow_rhs[:depth], preferred_element_type=jnp.float32)
            narrow += jnp.dot(far_ref[group], narrow_rhs[depth:], preferred_element_type=jnp.float32)
            narrow_sum[...] += narrow
            if n3:
                wide_sum[...] += jnp.dot(lhs_ref[group], wide_rhs[...], preferred_element_type=jnp.float32)

    return kernel


def first_product(lhs, far_lhs, pos3, posx, place, narrow, few, m3):
    groups, rows, depth = lhs.shape
    vmem = pl.BlockSpec(memory_space=pltpu.VMEM)
    smem = pl.BlockSpec(memory_space=pltpu.SMEM)
    arrays = list(narrow) + [v for group in m3 for v in group]
    wide = (rows, FOLD) if m3 else (16, FOLD)
    wide_depth = depth if m3 else 16
    return pl.pallas_call(
        make_first_kernel(few, len(m3), starts_of([v[0] for v in m3])),
        in_specs=[smem] * 3 + [vmem] * (2 + len(arrays)),
        out_specs=[vmem] * 2,
        out_shape=[jax.ShapeDtypeStruct(v, jnp.float32) for v in ((rows, 2 * NARROW), wide)],
        scratch_shapes=[
            pltpu.VMEM((depth // NEAR * len(SLOTS), 2 * NARROW), jnp.bfloat16),
            pltpu.VMEM((wide_depth, FOLD), jnp.bfloat16),
        ],
        cost_estimate=cost(9 if m3 else 6),
        compiler_params=pltpu.CompilerParams(vmem_limit_bytes=32 * 1024 * 1024),
    )(pos3, posx, place, lhs, far_lhs, *arrays)


def make_last_kernel(n2, starts2, n3, starts3):
    def kernel(occ_ref, vir_ref, pos2_ref, pos3_ref, place_ref, fold_ref, far_ref, row_ref, narrow_ref, wide_ref, *refs):
        m2_refs = refs[:n2]
        m3_refs = [refs[n2 + 2 * n:n2 + 2 * n + 2] for n in range(n3)]
        refs = refs[n2 + 2 * n3:]
        outs = refs[:4]
        column_ref, total_ref, short_rhs, far_rhs = refs[4:]
        row, col = place_ref[0], place_ref[1]
        at_end = (row == 0) | (row == 3)
        groups, rows, width = fold_ref.shape
        share = width // K_STEP
        batch = rows // share
        @pl.loop(0, groups * K_STEP)
        def _(k):
            here = pl.ds(pl.multiple_of(k * share, share), share)
            short = chosen(m2_refs, starts2, pos2_ref[k], lambda ref, at: ref[at])
            short_rhs[here] = jnp.concatenate([short, short], axis=0)
            if n3:
                far_rhs[here] = chosen(
                    m3_refs, starts3, pos3_ref[k], lambda pair, at: jnp.where(at_end, pair[0][at], pair[1][at])
                )

        column = amplitude_rows(column_ref, row_ref, occ_ref, row, batch, share)
        target = jnp.bitwise_xor(column, occ_ref[batch])
        both = narrow_ref[...]
        both = both + pltpu.roll(both, NARROW, 1)
        both = jnp.concatenate([both] * (FOLD // (2 * NARROW)), axis=1)
        part = wide_ref[...] if n3 else 0.0
        for group in range(groups):
            here = pl.ds(group * width, width)
            part += jnp.dot(fold_ref[group], short_rhs[here], preferred_element_type=jnp.float32)
            if n3:
                part += jnp.dot(far_ref[group], far_rhs[here], preferred_element_type=jnp.float32)
        total_ref[...] = jnp.where(target == largest_irrep(vir_ref), part, both)
        write_quarters(total_ref, col, outs)

    return kernel


def last_product(far_lhs, fold, occ_irrep, vir_irrep, pos2, pos3, place, narrow_sum, wide_sum, m2, m3, batch):
    groups, rows, width = fold.shape
    share = rows // batch
    vmem = pl.BlockSpec(memory_space=pltpu.VMEM)
    smem = pl.BlockSpec(memory_space=pltpu.SMEM)
    arrays = [narrow_sum, wide_sum] + list(m2) + [v for group in m3 for v in group]
    quarter = (batch // 2, share, FOLD // 2)
    whole = groups * width
    far_lhs = far_lhs if m3 else jnp.zeros((8, 128), jnp.bfloat16)
    return pl.pallas_call(
        make_last_kernel(len(m2), starts_of(m2), len(m3), starts_of([v[0] for v in m3])),
        in_specs=[smem] * 5 + [vmem] * (3 + len(arrays)),
        out_specs=[vmem] * 4,
        out_shape=[jax.ShapeDtypeStruct(quarter, jnp.float32)] * 4,
        scratch_shapes=[
            pltpu.VMEM((vir_irrep.shape[0], 8), jnp.int32),
            pltpu.VMEM((rows, FOLD), jnp.float32),
            pltpu.VMEM((whole, FOLD), jnp.bfloat16),
            pltpu.VMEM((whole if m3 else 16, FOLD), jnp.bfloat16),
        ],
        cost_estimate=cost(4 if m3 else 2),
        compiler_params=pltpu.CompilerParams(vmem_limit_bytes=32 * 1024 * 1024),
    )(occ_irrep, vir_irrep, pos2, pos3, place, fold, far_lhs, vir_irrep[None, :], *arrays)


def dense_product(amplitudes, whole, occ_irrep, occ_local, vir_local, vir_irrep):
    batch = amplitudes.shape[0]
    keep = (
        jnp.bitwise_xor(occ_irrep[:batch, None], occ_local[None, :])[:, :, None, None]
        == jnp.bitwise_xor(vir_local[:, None], vir_irrep[None, :])[None, None]
    )
    kept = jnp.where(keep, amplitudes, jnp.zeros_like(amplitudes))
    return lax.dot_general(
        kept, whole, (((1, 3), (0, 1)), ((), ())), preferred_element_type=jnp.float32
    )


def finish(cycle, occ_irrep, vir_irrep, occ_energy, vir_energy, a_start, a_size, b_start, b_size, batch):
    label_a = lax.dynamic_slice_in_dim(vir_irrep, a_start, a_size)
    label_b = lax.dynamic_slice_in_dim(vir_irrep, b_start, b_size)
    energy_a = lax.dynamic_slice_in_dim(vir_energy, a_start, a_size)
    energy_b = lax.dynamic_slice_in_dim(vir_energy, b_start, b_size)
    target = jnp.bitwise_xor(
        jnp.bitwise_xor(occ_irrep[:batch, None], occ_irrep[batch]), label_a[None, :]
    )
    keep = label_b[:, None, None] == target[None, :, :]
    denominator = (
        occ_energy[:batch][None, :, None]
        + occ_energy[batch]
        - energy_a[None, None, :]
        - energy_b[:, None, None]
    )
    swapped = jnp.transpose(cycle, (2, 0, 1))
    return jnp.where(keep, swapped, 0.0) / denominator


def on_square(amplitudes, integrals, occ_irrep, vir_irrep, screen):
    batch, occ_share, share, vir_total = amplitudes.shape
    row = lax.axis_index("row")
    col = lax.axis_index("col")
    place = jnp.stack([row, col]).astype(jnp.int32)
    narrow, few, m2a, m2b, m3a, m3b, pos2, pos3, posx, form = pack(
        integrals, occ_irrep, vir_irrep, screen, place, batch
    )
    outer = [(0, 1), (1, 0), (2, 3), (3, 2)]
    inner = [(1, 2), (2, 1)]
    inward = [(0, 1), (3, 2)]
    outward = [(1, 0), (2, 3)]
    ends = [(0, 3), (3, 0)]
    second = [(r, r ^ 2) for r in range(4)]

    def move(v, pairs):
        return lax.ppermute(v, "row", pairs)

    def sparse(use_few, choose):
        def run(narrow, few, m2a, m2b, m3a, m3b):
            shorts, wides = choose(m2a, m2b, m3a, m3b)
            h1 = [move(v, inward) for v in shorts]
            e1, o1 = move(narrow, outer), move(narrow, inner)
            near = [(own, move(own, outer), move(own, inner)) for own in wides]
            two, three = (move(few, second), move(few, ends)) if use_few else (None, None)
            amps = amplitudes
            if use_few:
                amps, near = lax.optimization_barrier((amps, near))
            else:
                near, e1, o1 = lax.optimization_barrier((near, e1, o1))
            lhs, far_lhs, fold = masked_amplitudes(amps, occ_irrep, vir_irrep, place)
            if not use_few:
                h1, e1, o1, _ = lax.optimization_barrier((h1, e1, o1, fold))
            h2 = [move(own + v, inner) for own, v in zip(shorts, h1)]
            far = [(move(o, outward), move(e, inner)) for _, e, o in near]
            if use_few:
                blocks = (narrow, e1, o1, two, two, three)
            else:
                e2, o2 = move(o1, outward), move(e1, inner)
                h2, e2, o2 = lax.optimization_barrier((h2, e2, o2))
                blocks = (narrow, e1, o1, e2, o2, move(o2, outward))
            h3 = [move(own + v, outward) for own, v in zip(shorts, h2)]
            sums = [a + b + c + d for a, b, c, d in zip(shorts, h1, h2, h3)]
            narrow_sum, wide_sum = first_product(
                lhs, far_lhs, pos3, posx, place, blocks, use_few, near
            )
            return list(last_product(
                far_lhs, fold, occ_irrep, vir_irrep, pos2, pos3, place, narrow_sum, wide_sum, sums, far, batch
            ))

        return run

    def dense(*_):
        occ_local = lax.dynamic_slice_in_dim(occ_irrep, col * occ_share, occ_share)
        vir_local = lax.dynamic_slice_in_dim(vir_irrep, row * share, share)
        screen_rows = lax.dynamic_slice_in_dim(screen, col * occ_share, occ_share, 0)
        fold = folded_integrals(
            integrals, occ_local, vir_local, vir_irrep, occ_irrep[batch], screen_rows
        )
        whole = jnp.zeros((occ_share, vir_total, FOLD), fold.dtype)
        for s in range(4):
            block = move(fold, [(r, r ^ s) for r in range(4)]) if s else fold
            whole = lax.dynamic_update_slice_in_dim(whole, block, jnp.bitwise_xor(row, s) * share, 1)
        total = dense_product(amplitudes, whole, occ_irrep, occ_local, vir_local, vir_irrep)
        quarter = (batch // 2, share, FOLD // 2)
        goals = [jnp.bitwise_xor(col, t) for t in range(4)]
        return [
            lax.dynamic_slice(total, (g // 2 * quarter[0], 0, g % 2 * quarter[2]), quarter) for g in goals
        ]

    branches = [
        sparse(False, lambda m2a, m2b, m3a, m3b: ([m2a], [])),
        sparse(False, lambda m2a, m2b, m3a, m3b: ([m2a], [m3a[:FEW_WIDE]])),
        sparse(True, lambda m2a, m2b, m3a, m3b: ([m2a[:FEW_SHORT]], [m3a])),
        sparse(False, lambda m2a, m2b, m3a, m3b: ([m2a, m2b], [m3a, m3b])),
        dense,
    ]
    quarters = lax.switch(form[0], branches, narrow, few, m2a, m2b, m3a, m3b)
    mine = quarters[0]
    for t in (1, 2, 3):
        mine = mine + lax.ppermute(quarters[t], "col", [(q, q ^ t) for q in range(4)])
    places = [(r, q) for r in range(4) for q in range(4)]
    same = lax.ppermute(mine, ("row", "col"), [(r * 4 + q, q * 4 + r) for r, q in places])
    other = lax.ppermute(mine, ("row", "col"), [(r * 4 + q, (q ^ 2) * 4 + r) for r, q in places])
    upper = row // 2 == 1
    low = jnp.where(upper, other, same)
    high = jnp.where(upper, same, other)
    return jnp.concatenate([low, high], axis=0)


def on_any(amplitudes, integrals, occ_irrep, vir_irrep, screen):
    batch, occ_share, share, vir_total = amplitudes.shape
    row = lax.axis_index("row")
    col = lax.axis_index("col")
    occ_local = lax.dynamic_slice_in_dim(occ_irrep, col * occ_share, occ_share)
    vir_local = lax.dynamic_slice_in_dim(vir_irrep, row * share, share)
    screen_rows = lax.dynamic_slice_in_dim(screen, col * occ_share, occ_share, 0)
    fold = folded_integrals(
        integrals, occ_local, vir_local, vir_irrep, occ_irrep[batch], screen_rows
    )
    whole = lax.all_gather(fold, "row", axis=1, tiled=True)
    cycle = dense_product(amplitudes, whole, occ_irrep, occ_local, vir_local, vir_irrep)
    cycle = lax.psum(cycle, "col")
    cycle = jnp.concatenate([cycle] * (vir_total // FOLD), axis=2)
    cycle = lax.all_to_all(cycle, "row", split_axis=2, concat_axis=1, tiled=True)
    a_size = vir_total // lax.axis_size("col")
    return lax.dynamic_slice_in_dim(cycle, col * a_size, a_size, 1)


def on_device(amplitudes, integrals, occ_irrep, vir_irrep, screen, occ_energy, vir_energy):
    batch, _, vir_share, vir_total = amplitudes.shape
    square = lax.axis_size("row") == 4 and lax.axis_size("col") == 4
    form = on_square if square else on_any
    cycle = form(amplitudes, integrals, occ_irrep, vir_irrep, screen)
    a_size = vir_total // lax.axis_size("col")
    return finish(
        cycle, occ_irrep, vir_irrep, occ_energy, vir_energy,
        lax.axis_index("col") * a_size, a_size, lax.axis_index("row") * vir_share, vir_share, batch,
    )


def solution(mesh):
    in_specs = (
        P("parts", "col", "row", None),
        P(("parts", "col"), "row", None),
        P("parts"),
        P("parts"),
        P("parts", None),
        P("parts"),
        P("parts"),
    )
    out_specs = P("row", "parts", "col")
    return jax.shard_map(
        on_device, mesh=mesh, in_specs=in_specs, out_specs=out_specs, check_vma=False
    )
```

```python
import jax
import jax.numpy as jnp
from jax import lax
from jax.experimental import pallas as pl
from jax.experimental.pallas import tpu as pltpu
from jax.sharding import PartitionSpec as P

FOLD = 256
K_STEP = 5


def folded_integrals(integrals, occ_local, vir_local, vir_irrep, pair_label, screen_rows):
    irrep_codes = jnp.arange(8, dtype=jnp.int32)
    screen_local = jnp.sum(
        screen_rows[:, None, :] * (vir_local[None, :, None] == irrep_codes).astype(jnp.int32),
        axis=2,
    )
    target = jnp.bitwise_xor(
        jnp.bitwise_xor(occ_local[:, None], vir_local[None, :]), pair_label
    )
    target = jnp.where(screen_local == 1, target, -1)
    keep = target[:, :, None] == vir_irrep[None, None, :]
    kept = jnp.where(keep, integrals, jnp.zeros_like(integrals))
    return kept[:, :, :FOLD] + kept[:, :, FOLD:]


NARROW = 64
CAPS = (22, 3)
FEW_SHORT = 8
FEW_WIDE = 5


def largest_irrep(vir_ref):
    return jnp.where(vir_ref[0] == vir_ref[FOLD - 1], vir_ref[0], vir_ref[FOLD])


def label_columns(row_labels):
    return jnp.transpose(jnp.broadcast_to(row_labels, (8, row_labels.shape[1])))


def as_bf16(labels):
    return labels.astype(jnp.float32).astype(jnp.bfloat16)


def label_mix(mix_ref, column_ref, row_ref, row, big, keep_big):
    depth = mix_ref.shape[0]
    column_ref[...] = label_columns(row_ref[...])
    column = column_ref[pl.ds(pl.multiple_of(row * depth, depth), depth), :1]
    is_big = row_ref[...] == big
    wanted = is_big if keep_big else jnp.logical_not(is_big)
    mix_ref[...] = as_bf16(jnp.where(wanted, jnp.bitwise_xor(column, row_ref[...]), 8))


def kept_folded(int_ref, mix_ref, j, x):
    tile = int_ref[j]
    wanted = as_bf16(jnp.full(mix_ref.shape, x))
    kept = jnp.where(mix_ref[...] == wanted, tile, jnp.zeros_like(tile))
    return kept[:, :FOLD] + kept[:, FOLD:]


def wide_kernel(
    occ_ref, vir_ref, screen_ref, place_ref, int_ref, row_ref,
    m2a_ref, m2b_ref, m3a_ref, m3b_ref, pos2_ref, pos3_ref, posx_ref, form_ref,
    mix_ref, column_ref, counts_ref, batch,
):
    step = pl.program_id(0)
    k_step, depth, total = int_ref.shape
    half = depth // 2
    row, col = place_ref[0], place_ref[1]
    pair_label = occ_ref[batch]
    big = largest_irrep(vir_ref)

    @pl.when(step == 0)
    def _():
        for n in range(3):
            counts_ref[n] = 0
        label_mix(mix_ref, column_ref, row_ref, row, big, True)

    @pl.loop(0, k_step)
    def _(j):
        k = step * k_step + j
        k_whole = col * (k_step * pl.num_programs(0)) + k
        x = jnp.bitwise_xor(occ_ref[k_whole], pair_label)
        on_big = screen_ref[jnp.bitwise_xor(big, x), k_whole] == 1
        actives = (on_big & (x != 0), on_big & (x == 0), x != 0)
        pos2, pos3, posx = [jnp.where(active, counts_ref[n], -1) for n, active in enumerate(actives)]
        for n, active in enumerate(actives):
            counts_ref[n] = counts_ref[n] + active.astype(jnp.int32)
        pos2_ref[k], pos3_ref[k], posx_ref[k] = pos2, pos3, posx

        @pl.when(pos2 >= 0)
        def _():
            wide = kept_folded(int_ref, mix_ref, j, x)
            short = wide[:half] + wide[half:]

            @pl.when(pos2 < CAPS[0])
            def _():
                m2a_ref[pos2] = short

            @pl.when(pos2 >= CAPS[0])
            def _():
                m2b_ref[pos2 - CAPS[0]] = short

        @pl.when(pos3 >= 0)
        def _():
            wide = kept_folded(int_ref, mix_ref, j, x)

            @pl.when(pos3 < CAPS[0])
            def _():
                m3a_ref[pos3] = wide

            @pl.when(pos3 >= CAPS[0])
            def _():
                m3b_ref[pos3 - CAPS[0]] = wide

    @pl.when(step == pl.num_programs(0) - 1)
    def _():
        labels = row_ref[...]
        lanes = lax.broadcasted_iota(jnp.int32, labels.shape, 1)
        ahead = pltpu.roll(labels, total - NARROW, 1)
        long = (labels == ahead) & (lanes < total - NARROW) & (labels != big)
        too_long = jnp.max(long.astype(jnp.int32)) == 1
        n2, n3, nx = counts_ref[0], counts_ref[1], counts_ref[2]
        one_label = occ_ref[0] == pair_label
        form = jnp.where((n3 <= CAPS[0]) & (nx <= FEW_SHORT), 2, 3)
        form = jnp.where((n3 <= FEW_WIDE) & (n2 <= CAPS[0]), 1, form)
        form = jnp.where(one_label, form, 4)
        form = jnp.where((n3 == 0) & (n2 <= CAPS[0]), 0, form)
        form_ref[0] = jnp.where(too_long, 4, form)


def wide_blocks(integrals, occ_irrep, vir_irrep, screen, place, batch):
    occ_share, depth, total = integrals.shape
    shapes = [(n, depth // 2, FOLD) for n in CAPS] + [(n, depth, FOLD) for n in CAPS]
    smem = pl.BlockSpec(memory_space=pltpu.SMEM)

    def kernel(*refs):
        wide_kernel(*refs, batch)

    return pl.pallas_call(
        kernel,
        grid_spec=pltpu.PrefetchScalarGridSpec(
            num_scalar_prefetch=4,
            grid=(occ_share // K_STEP,),
            in_specs=[
                pl.BlockSpec((K_STEP, depth, total), lambda k, *_: (k, 0, 0)),
                pl.BlockSpec((1, total), lambda k, *_: (0, 0)),
            ],
            out_specs=[pl.BlockSpec(v, lambda k, *_: (0, 0, 0)) for v in shapes] + [smem] * 4,
            scratch_shapes=[
                pltpu.VMEM((depth, total), jnp.bfloat16),
                pltpu.VMEM((total, 8), jnp.int32),
                pltpu.SMEM((3,), jnp.int32),
            ],
        ),
        out_shape=[jax.ShapeDtypeStruct(v, jnp.bfloat16) for v in shapes]
        + [jax.ShapeDtypeStruct((n,), jnp.int32) for n in (occ_share, occ_share, occ_share, 1)],
        cost_estimate=cost(5),
        compiler_params=pltpu.CompilerParams(vmem_limit_bytes=24 * 1024 * 1024),
    )(occ_irrep, vir_irrep, screen.T, place, integrals, vir_irrep[None, :])


def narrow_kernel(
    occ_ref, vir_ref, screen_ref, place_ref, posx_ref, int_ref, row_ref, narrow_ref, few_ref,
    mix_ref, column_ref, batch,
):
    step = pl.program_id(0)
    k_step, depth, total = int_ref.shape
    half = depth // 2
    row, col = place_ref[0], place_ref[1]

    @pl.when(step == 0)
    def _():
        label_mix(mix_ref, column_ref, row_ref, row, largest_irrep(vir_ref), False)

    lane = lax.broadcasted_iota(jnp.int32, (half, 2 * NARROW), 1)
    local = column_ref[pl.ds(pl.multiple_of(row * depth, depth), depth), :1]
    for j in range(k_step):
        k = step * k_step + j
        k_whole = col * (k_step * pl.num_programs(0)) + k
        x = jnp.bitwise_xor(occ_ref[k_whole], occ_ref[batch])
        bits = screen_ref[0, k_whole]
        for g in range(1, 8):
            bits = bits + screen_ref[g, k_whole] * (1 << g)
        narrow = kept_folded(int_ref, mix_ref, j, x)
        narrow = (narrow[:, : 2 * NARROW] + narrow[:, 2 * NARROW:]).astype(jnp.float32)
        narrow = narrow + pltpu.roll(narrow, NARROW, 1)
        on = jnp.bitwise_and(lax.shift_right_logical(jnp.full(local.shape, bits), local), 1) == 1
        narrow = jnp.where(on, narrow, 0.0)
        narrow = jnp.where(lane < NARROW, narrow[:half], narrow[half:]).astype(jnp.bfloat16)
        narrow_ref[j] = narrow
        posx = posx_ref[k]

        @pl.when((posx >= 0) & (posx < FEW_SHORT))
        def _(narrow=narrow, posx=posx):
            few_ref[posx] = narrow


def narrow_blocks(integrals, occ_irrep, vir_irrep, screen, place, posx, batch):
    occ_share, depth, total = integrals.shape
    shapes = [(n, depth // 2, 2 * NARROW) for n in (occ_share, FEW_SHORT)]

    def kernel(*refs):
        narrow_kernel(*refs, batch)

    return pl.pallas_call(
        kernel,
        grid_spec=pltpu.PrefetchScalarGridSpec(
            num_scalar_prefetch=5,
            grid=(occ_share // K_STEP,),
            in_specs=[
                pl.BlockSpec((K_STEP, depth, total), lambda k, *_: (k, 0, 0)),
                pl.BlockSpec((1, total), lambda k, *_: (0, 0)),
            ],
            out_specs=[
                pl.BlockSpec((K_STEP, depth // 2, 2 * NARROW), lambda k, *_: (k, 0, 0)),
                pl.BlockSpec(shapes[1], lambda k, *_: (0, 0, 0)),
            ],
            scratch_shapes=[pltpu.VMEM((depth, total), jnp.bfloat16), pltpu.VMEM((total, 8), jnp.int32)],
        ),
        out_shape=[jax.ShapeDtypeStruct(v, jnp.bfloat16) for v in shapes],
        cost_estimate=cost(6),
        compiler_params=pltpu.CompilerParams(vmem_limit_bytes=16 * 1024 * 1024),
    )(occ_irrep, vir_irrep, screen.T, place, posx, integrals, vir_irrep[None, :])


def cost(micros):
    return pl.CostEstimate(flops=int(micros * 1e9), bytes_accessed=int(micros * 3e6), transcendentals=0)


SLOTS = (0, 1, 3, 2)
NEAR = 3


def amplitude_rows(column_ref, row_ref, occ_ref, row, batch, share):
    column_ref[...] = label_columns(row_ref[...])
    column = column_ref[pl.ds(pl.multiple_of(row * share, share), share), :1]
    return jnp.concatenate([jnp.bitwise_xor(column, occ_ref[i]) for i in range(batch)], axis=0)


def write_quarters(total_ref, col, outs):
    rows, fold = total_ref.shape
    width, height = fold // 2, rows // 2
    for t, out_ref in enumerate(outs):
        goal = jnp.bitwise_xor(col, t)
        lanes = pl.ds(pl.multiple_of((goal % 2) * width, width), width)
        lines = pl.ds(pl.multiple_of((goal // 2) * height, height), height)
        out_ref[...] = total_ref[lines, lanes].reshape(out_ref.shape)


def chosen(refs, starts, pos, pick):
    block = None
    for n, group in enumerate(refs):
        inside = (pos >= starts[n]) & (pos < starts[n + 1])
        at = jnp.clip(pos - starts[n], 0, starts[n + 1] - starts[n] - 1)
        found = pick(group, at)
        found = jnp.where(inside, found, jnp.zeros_like(found))
        block = found if block is None else block + found
    return block


def starts_of(arrays):
    starts = [0]
    for v in arrays:
        starts.append(starts[-1] + v.shape[0])
    return starts


def mask_kernel(occ_ref, place_ref, amp_ref, row_ref, lhs_ref, far_ref, fold_ref, mix_ref, column_ref, amp_buffer, sems):
    batch, k_all, share, total = amp_ref.shape
    rows, groups = batch * share, k_all // K_STEP
    row, col = place_ref[0], place_ref[1]

    def fetch(group):
        slot = group % 2
        source = amp_ref.at[:, pl.ds(group * K_STEP, K_STEP)]
        return pltpu.make_async_copy(source, amp_buffer.at[slot], sems.at[slot])

    fetch(0).start()
    column = amplitude_rows(column_ref, row_ref, occ_ref, row, batch, share)
    mix_ref[...] = as_bf16(jnp.bitwise_xor(column, row_ref[...]))

    @pl.loop(0, groups)
    def _(group):
        slot = group % 2

        @pl.when(group + 1 < groups)
        def _():
            fetch(group + 1).start()

        fetch(group).wait()

        @pl.loop(0, K_STEP)
        def _(j):
            wanted = as_bf16(jnp.full((rows, share), occ_ref[col * k_all + group * K_STEP + j]))
            folded = None
            for n, s in enumerate(SLOTS):
                place = pl.ds(pl.multiple_of(jnp.bitwise_xor(row, s) * share, share), share)
                tile = amp_buffer[slot, :, j, :, place].reshape(rows, share)
                piece = jnp.where(mix_ref[:, place] == wanted, tile, jnp.zeros_like(tile))
                if n < NEAR:
                    lhs_ref[group, :, pl.ds(pl.multiple_of((n * K_STEP + j) * share, share), share)] = piece
                else:
                    far_ref[group, :, pl.ds(pl.multiple_of(j * share, share), share)] = piece
                folded = piece if folded is None else folded + piece
            fold_ref[group, :, pl.ds(pl.multiple_of(j * share, share), share)] = folded


def masked_amplitudes(amplitudes, occ_irrep, vir_irrep, place):
    batch, k_all, share, total = amplitudes.shape
    rows, groups = batch * share, k_all // K_STEP
    smem = pl.BlockSpec(memory_space=pltpu.SMEM)
    vmem = pl.BlockSpec(memory_space=pltpu.VMEM)
    hbm = pl.BlockSpec(memory_space=pltpu.HBM)
    widths = (NEAR * K_STEP * share, K_STEP * share, K_STEP * share)
    return pl.pallas_call(
        mask_kernel,
        in_specs=[smem, smem, hbm, vmem],
        out_specs=[vmem] * 3,
        out_shape=[jax.ShapeDtypeStruct((groups, rows, w), jnp.bfloat16) for w in widths],
        scratch_shapes=[
            pltpu.VMEM((rows, total), jnp.bfloat16),
            pltpu.VMEM((total, 8), jnp.int32),
            pltpu.VMEM((2, batch, K_STEP, share, total), jnp.bfloat16),
            pltpu.SemaphoreType.DMA((2,)),
        ],
        cost_estimate=cost(7),
        compiler_params=pltpu.CompilerParams(vmem_limit_bytes=28 * 1024 * 1024),
    )(occ_irrep, place, amplitudes, vir_irrep[None, :])


def make_first_kernel(few, n3, starts3):
    def kernel(pos3_ref, posx_ref, place_ref, lhs_ref, far_ref, *refs):
        narrow_refs = refs[:6]
        m3_refs = [refs[6 + 3 * n:9 + 3 * n] for n in range(n3)]
        narrow_sum, wide_sum, narrow_rhs, wide_rhs = refs[6 + 3 * n3:]
        row = place_ref[0]
        at_end = (row == 0) | (row == 3)
        groups, _, depth = lhs_ref.shape
        share = depth // (NEAR * K_STEP)
        half = share // 2
        lane = lax.broadcasted_iota(jnp.int32, (half, 2 * NARROW), 1)

        narrow_sum[...] = jnp.zeros(narrow_sum.shape, jnp.float32)
        wide_sum[...] = jnp.zeros(wide_sum.shape, jnp.float32)

        @pl.loop(0, groups)
        def _(group):
            @pl.loop(0, K_STEP)
            def _(j):
                k = group * K_STEP + j
                own, e1, o1 = [ref[k] for ref in narrow_refs[:3]]
                far = jnp.maximum(posx_ref[k], 0) if few else k
                e2, o2, e3 = [ref[far] for ref in narrow_refs[3:]]
                two = jnp.where(at_end, e2, o2)
                if few:
                    two, e3 = [jnp.where(posx_ref[k] >= 0, v, jnp.zeros_like(v)) for v in (two, e3)]
                for n, block in enumerate((own, e1, jnp.where(at_end, e3, o1), two)):
                    zero = jnp.zeros_like(block)
                    first = pl.multiple_of((n * K_STEP + j) * share, share)
                    narrow_rhs[pl.ds(first, half)] = jnp.where(lane < NARROW, block, zero)
                    narrow_rhs[pl.ds(first + half, half)] = jnp.where(lane < NARROW, zero, block)
                for n in range(3 if n3 else 0):
                    block = chosen(m3_refs, starts3, pos3_ref[k], lambda group, at, n=n: group[n][at])
                    if n == 2:
                        block = jnp.where(at_end, jnp.zeros_like(block), block)
                    wide_rhs[pl.ds(pl.multiple_of((n * K_STEP + j) * share, share), share)] = block

            narrow = jnp.dot(lhs_ref[group], narrow_rhs[:depth], preferred_element_type=jnp.float32)
            narrow += jnp.dot(far_ref[group], narrow_rhs[depth:], preferred_element_type=jnp.float32)
            narrow_sum[...] += narrow
            if n3:
                wide_sum[...] += jnp.dot(lhs_ref[group], wide_rhs[...], preferred_element_type=jnp.float32)

    return kernel


def first_product(lhs, far_lhs, pos3, posx, place, narrow, few, m3):
    groups, rows, depth = lhs.shape
    vmem = pl.BlockSpec(memory_space=pltpu.VMEM)
    smem = pl.BlockSpec(memory_space=pltpu.SMEM)
    arrays = list(narrow) + [v for group in m3 for v in group]
    wide = (rows, FOLD) if m3 else (16, FOLD)
    wide_depth = depth if m3 else 16
    return pl.pallas_call(
        make_first_kernel(few, len(m3), starts_of([v[0] for v in m3])),
        in_specs=[smem] * 3 + [vmem] * (2 + len(arrays)),
        out_specs=[vmem] * 2,
        out_shape=[jax.ShapeDtypeStruct(v, jnp.float32) for v in ((rows, 2 * NARROW), wide)],
        scratch_shapes=[
            pltpu.VMEM((depth // NEAR * len(SLOTS), 2 * NARROW), jnp.bfloat16),
            pltpu.VMEM((wide_depth, FOLD), jnp.bfloat16),
        ],
        cost_estimate=cost(9 if m3 else 6),
        compiler_params=pltpu.CompilerParams(vmem_limit_bytes=32 * 1024 * 1024),
    )(pos3, posx, place, lhs, far_lhs, *arrays)


def make_last_kernel(n2, starts2, n3, starts3):
    def kernel(occ_ref, vir_ref, pos2_ref, pos3_ref, place_ref, fold_ref, far_ref, row_ref, narrow_ref, wide_ref, *refs):
        m2_refs = refs[:n2]
        m3_refs = [refs[n2 + 2 * n:n2 + 2 * n + 2] for n in range(n3)]
        refs = refs[n2 + 2 * n3:]
        outs = refs[:4]
        column_ref, total_ref, short_rhs, far_rhs = refs[4:]
        row, col = place_ref[0], place_ref[1]
        at_end = (row == 0) | (row == 3)
        groups, rows, width = fold_ref.shape
        share = width // K_STEP
        batch = rows // share
        @pl.loop(0, groups * K_STEP)
        def _(k):
            here = pl.ds(pl.multiple_of(k * share, share), share)
            short = chosen(m2_refs, starts2, pos2_ref[k], lambda ref, at: ref[at])
            short_rhs[here] = jnp.concatenate([short, short], axis=0)
            if n3:
                far_rhs[here] = chosen(
                    m3_refs, starts3, pos3_ref[k], lambda pair, at: jnp.where(at_end, pair[0][at], pair[1][at])
                )

        column = amplitude_rows(column_ref, row_ref, occ_ref, row, batch, share)
        target = jnp.bitwise_xor(column, occ_ref[batch])
        both = narrow_ref[...]
        both = both + pltpu.roll(both, NARROW, 1)
        both = jnp.concatenate([both] * (FOLD // (2 * NARROW)), axis=1)
        part = wide_ref[...] if n3 else 0.0
        for group in range(groups):
            here = pl.ds(group * width, width)
            part += jnp.dot(fold_ref[group], short_rhs[here], preferred_element_type=jnp.float32)
            if n3:
                part += jnp.dot(far_ref[group], far_rhs[here], preferred_element_type=jnp.float32)
        total_ref[...] = jnp.where(target == largest_irrep(vir_ref), part, both)
        write_quarters(total_ref, col, outs)

    return kernel


def last_product(far_lhs, fold, occ_irrep, vir_irrep, pos2, pos3, place, narrow_sum, wide_sum, m2, m3, batch):
    groups, rows, width = fold.shape
    share = rows // batch
    vmem = pl.BlockSpec(memory_space=pltpu.VMEM)
    smem = pl.BlockSpec(memory_space=pltpu.SMEM)
    arrays = [narrow_sum, wide_sum] + list(m2) + [v for group in m3 for v in group]
    quarter = (batch // 2, share, FOLD // 2)
    whole = groups * width
    far_lhs = far_lhs if m3 else jnp.zeros((8, 128), jnp.bfloat16)
    return pl.pallas_call(
        make_last_kernel(len(m2), starts_of(m2), len(m3), starts_of([v[0] for v in m3])),
        in_specs=[smem] * 5 + [vmem] * (3 + len(arrays)),
        out_specs=[vmem] * 4,
        out_shape=[jax.ShapeDtypeStruct(quarter, jnp.float32)] * 4,
        scratch_shapes=[
            pltpu.VMEM((vir_irrep.shape[0], 8), jnp.int32),
            pltpu.VMEM((rows, FOLD), jnp.float32),
            pltpu.VMEM((whole, FOLD), jnp.bfloat16),
            pltpu.VMEM((whole if m3 else 16, FOLD), jnp.bfloat16),
        ],
        cost_estimate=cost(4 if m3 else 2),
        compiler_params=pltpu.CompilerParams(vmem_limit_bytes=32 * 1024 * 1024),
    )(occ_irrep, vir_irrep, pos2, pos3, place, fold, far_lhs, vir_irrep[None, :], *arrays)


def dense_product(amplitudes, whole, occ_irrep, occ_local, vir_local, vir_irrep):
    batch = amplitudes.shape[0]
    keep = (
        jnp.bitwise_xor(occ_irrep[:batch, None], occ_local[None, :])[:, :, None, None]
        == jnp.bitwise_xor(vir_local[:, None], vir_irrep[None, :])[None, None]
    )
    kept = jnp.where(keep, amplitudes, jnp.zeros_like(amplitudes))
    return lax.dot_general(
        kept, whole, (((1, 3), (0, 1)), ((), ())), preferred_element_type=jnp.float32
    )


def finish(cycle, occ_irrep, vir_irrep, occ_energy, vir_energy, a_start, a_size, b_start, b_size, batch):
    label_a = lax.dynamic_slice_in_dim(vir_irrep, a_start, a_size)
    label_b = lax.dynamic_slice_in_dim(vir_irrep, b_start, b_size)
    energy_a = lax.dynamic_slice_in_dim(vir_energy, a_start, a_size)
    energy_b = lax.dynamic_slice_in_dim(vir_energy, b_start, b_size)
    target = jnp.bitwise_xor(
        jnp.bitwise_xor(occ_irrep[:batch, None], occ_irrep[batch]), label_a[None, :]
    )
    keep = label_b[:, None, None] == target[None, :, :]
    denominator = (
        occ_energy[:batch][None, :, None]
        + occ_energy[batch]
        - energy_a[None, None, :]
        - energy_b[:, None, None]
    )
    swapped = jnp.transpose(cycle, (2, 0, 1))
    return jnp.where(keep, swapped, 0.0) / denominator


def on_square(amplitudes, integrals, occ_irrep, vir_irrep, screen):
    batch, occ_share, share, vir_total = amplitudes.shape
    row = lax.axis_index("row")
    col = lax.axis_index("col")
    place = jnp.stack([row, col]).astype(jnp.int32)
    m2a, m2b, m3a, m3b, pos2, pos3, posx, form = wide_blocks(
        integrals, occ_irrep, vir_irrep, screen, place, batch
    )
    outer = [(0, 1), (1, 0), (2, 3), (3, 2)]
    inner = [(1, 2), (2, 1)]
    inward = [(0, 1), (3, 2)]
    outward = [(1, 0), (2, 3)]
    ends = [(0, 3), (3, 0)]
    second = [(r, r ^ 2) for r in range(4)]

    def move(v, pairs):
        return lax.ppermute(v, "row", pairs)

    def sparse(use_few, choose):
        def run(m2a, m2b, m3a, m3b):
            shorts, wides = choose(m2a, m2b, m3a, m3b)
            near = [(own, move(own, outer), move(own, inner)) for own in wides]
            narrow, few = narrow_blocks(integrals, occ_irrep, vir_irrep, screen, place, posx, batch)
            amps = amplitudes
            if use_few:
                amps, shorts, near = lax.optimization_barrier((amps, shorts, near))
            h1 = [move(v, inward) for v in shorts]
            e1, o1 = move(narrow, outer), move(narrow, inner)
            two, three = (move(few, second), move(few, ends)) if use_few else (None, None)
            lhs, far_lhs, fold = masked_amplitudes(amps, occ_irrep, vir_irrep, place)
            if not use_few:
                near, h1, e1, o1, _ = lax.optimization_barrier((near, h1, e1, o1, fold))
            h2 = [move(own + v, inner) for own, v in zip(shorts, h1)]
            far = [(move(o, outward), move(e, inner)) for _, e, o in near]
            if use_few:
                blocks = (narrow, e1, o1, two, two, three)
            else:
                e2, o2 = move(o1, outward), move(e1, inner)
                h2, e2, o2 = lax.optimization_barrier((h2, e2, o2))
                blocks = (narrow, e1, o1, e2, o2, move(o2, outward))
            h3 = [move(own + v, outward) for own, v in zip(shorts, h2)]
            sums = [a + b + c + d for a, b, c, d in zip(shorts, h1, h2, h3)]
            narrow_sum, wide_sum = first_product(
                lhs, far_lhs, pos3, posx, place, blocks, use_few, near
            )
            return list(last_product(
                far_lhs, fold, occ_irrep, vir_irrep, pos2, pos3, place, narrow_sum, wide_sum, sums, far, batch
            ))

        return run

    def dense(*_):
        occ_local = lax.dynamic_slice_in_dim(occ_irrep, col * occ_share, occ_share)
        vir_local = lax.dynamic_slice_in_dim(vir_irrep, row * share, share)
        screen_rows = lax.dynamic_slice_in_dim(screen, col * occ_share, occ_share, 0)
        fold = folded_integrals(
            integrals, occ_local, vir_local, vir_irrep, occ_irrep[batch], screen_rows
        )
        whole = jnp.zeros((occ_share, vir_total, FOLD), fold.dtype)
        for s in range(4):
            block = move(fold, [(r, r ^ s) for r in range(4)]) if s else fold
            whole = lax.dynamic_update_slice_in_dim(whole, block, jnp.bitwise_xor(row, s) * share, 1)
        total = dense_product(amplitudes, whole, occ_irrep, occ_local, vir_local, vir_irrep)
        quarter = (batch // 2, share, FOLD // 2)
        goals = [jnp.bitwise_xor(col, t) for t in range(4)]
        return [
            lax.dynamic_slice(total, (g // 2 * quarter[0], 0, g % 2 * quarter[2]), quarter) for g in goals
        ]

    branches = [
        sparse(False, lambda m2a, m2b, m3a, m3b: ([m2a], [])),
        sparse(False, lambda m2a, m2b, m3a, m3b: ([m2a], [m3a[:FEW_WIDE]])),
        sparse(True, lambda m2a, m2b, m3a, m3b: ([m2a[:FEW_SHORT]], [m3a])),
        sparse(False, lambda m2a, m2b, m3a, m3b: ([m2a, m2b], [m3a, m3b])),
        dense,
    ]
    quarters = lax.switch(form[0], branches, m2a, m2b, m3a, m3b)
    mine = quarters[0]
    for t in (1, 2, 3):
        mine = mine + lax.ppermute(quarters[t], "col", [(q, q ^ t) for q in range(4)])
    places = [(r, q) for r in range(4) for q in range(4)]
    same = lax.ppermute(mine, ("row", "col"), [(r * 4 + q, q * 4 + r) for r, q in places])
    other = lax.ppermute(mine, ("row", "col"), [(r * 4 + q, (q ^ 2) * 4 + r) for r, q in places])
    upper = row // 2 == 1
    low = jnp.where(upper, other, same)
    high = jnp.where(upper, same, other)
    return jnp.concatenate([low, high], axis=0)


def on_any(amplitudes, integrals, occ_irrep, vir_irrep, screen):
    batch, occ_share, share, vir_total = amplitudes.shape
    row = lax.axis_index("row")
    col = lax.axis_index("col")
    occ_local = lax.dynamic_slice_in_dim(occ_irrep, col * occ_share, occ_share)
    vir_local = lax.dynamic_slice_in_dim(vir_irrep, row * share, share)
    screen_rows = lax.dynamic_slice_in_dim(screen, col * occ_share, occ_share, 0)
    fold = folded_integrals(
        integrals, occ_local, vir_local, vir_irrep, occ_irrep[batch], screen_rows
    )
    whole = lax.all_gather(fold, "row", axis=1, tiled=True)
    cycle = dense_product(amplitudes, whole, occ_irrep, occ_local, vir_local, vir_irrep)
    cycle = lax.psum(cycle, "col")
    cycle = jnp.concatenate([cycle] * (vir_total // FOLD), axis=2)
    cycle = lax.all_to_all(cycle, "row", split_axis=2, concat_axis=1, tiled=True)
    a_size = vir_total // lax.axis_size("col")
    return lax.dynamic_slice_in_dim(cycle, col * a_size, a_size, 1)


def on_device(amplitudes, integrals, occ_irrep, vir_irrep, screen, occ_energy, vir_energy):
    batch, _, vir_share, vir_total = amplitudes.shape
    square = lax.axis_size("row") == 4 and lax.axis_size("col") == 4
    form = on_square if square else on_any
    cycle = form(amplitudes, integrals, occ_irrep, vir_irrep, screen)
    a_size = vir_total // lax.axis_size("col")
    return finish(
        cycle, occ_irrep, vir_irrep, occ_energy, vir_energy,
        lax.axis_index("col") * a_size, a_size, lax.axis_index("row") * vir_share, vir_share, batch,
    )


def solution(mesh):
    in_specs = (
        P("parts", "col", "row", None),
        P(("parts", "col"), "row", None),
        P("parts"),
        P("parts"),
        P("parts", None),
        P("parts"),
        P("parts"),
    )
    out_specs = P("row", "parts", "col")
    return jax.shard_map(
        on_device, mesh=mesh, in_specs=in_specs, out_specs=out_specs, check_vma=False
    )
```

```python
import jax
import jax.numpy as jnp
from jax import lax
from jax.experimental import pallas as pl
from jax.experimental.pallas import tpu as pltpu
from jax.sharding import PartitionSpec as P

FOLD = 256
K_STEP = 5


def folded_integrals(integrals, occ_local, vir_local, vir_irrep, pair_label, screen_rows):
    irrep_codes = jnp.arange(8, dtype=jnp.int32)
    screen_local = jnp.sum(
        screen_rows[:, None, :] * (vir_local[None, :, None] == irrep_codes).astype(jnp.int32),
        axis=2,
    )
    target = jnp.bitwise_xor(
        jnp.bitwise_xor(occ_local[:, None], vir_local[None, :]), pair_label
    )
    target = jnp.where(screen_local == 1, target, -1)
    keep = target[:, :, None] == vir_irrep[None, None, :]
    kept = jnp.where(keep, integrals, jnp.zeros_like(integrals))
    return kept[:, :, :FOLD] + kept[:, :, FOLD:]


NARROW = 64
CAPS = (22, 3)
FEW_SHORT = 8
FEW_WIDE = 5


def largest_irrep(vir_ref):
    return jnp.where(vir_ref[0] == vir_ref[FOLD - 1], vir_ref[0], vir_ref[FOLD])


def label_columns(row_labels):
    return jnp.transpose(jnp.broadcast_to(row_labels, (8, row_labels.shape[1])))


def as_bf16(labels):
    return labels.astype(jnp.float32).astype(jnp.bfloat16)


def label_mix(mix_ref, column_ref, row_ref, row, big, keep_big):
    depth = mix_ref.shape[0]
    column_ref[...] = label_columns(row_ref[...])
    column = column_ref[pl.ds(pl.multiple_of(row * depth, depth), depth), :1]
    is_big = row_ref[...] == big
    wanted = is_big if keep_big else jnp.logical_not(is_big)
    mix_ref[...] = as_bf16(jnp.where(wanted, jnp.bitwise_xor(column, row_ref[...]), 8))


def kept_folded(int_ref, mix_ref, j, x):
    tile = int_ref[j]
    wanted = as_bf16(jnp.full(mix_ref.shape, x))
    kept = jnp.where(mix_ref[...] == wanted, tile, jnp.zeros_like(tile))
    return kept[:, :FOLD] + kept[:, FOLD:]


def wide_kernel(
    occ_ref, vir_ref, screen_ref, place_ref, int_ref, row_ref,
    m2a_ref, m2b_ref, m3a_ref, m3b_ref, pos2_ref, pos3_ref, posx_ref, form_ref,
    mix_ref, column_ref, counts_ref, batch,
):
    step = pl.program_id(0)
    k_step, depth, total = int_ref.shape
    half = depth // 2
    row, col = place_ref[0], place_ref[1]
    pair_label = occ_ref[batch]
    big = largest_irrep(vir_ref)

    @pl.when(step == 0)
    def _():
        for n in range(3):
            counts_ref[n] = 0
        label_mix(mix_ref, column_ref, row_ref, row, big, True)

    @pl.loop(0, k_step)
    def _(j):
        k = step * k_step + j
        k_whole = col * (k_step * pl.num_programs(0)) + k
        x = jnp.bitwise_xor(occ_ref[k_whole], pair_label)
        on_big = screen_ref[jnp.bitwise_xor(big, x), k_whole] == 1
        actives = (on_big & (x != 0), on_big & (x == 0), x != 0)
        pos2, pos3, posx = [jnp.where(active, counts_ref[n], -1) for n, active in enumerate(actives)]
        for n, active in enumerate(actives):
            counts_ref[n] = counts_ref[n] + active.astype(jnp.int32)
        pos2_ref[k], pos3_ref[k], posx_ref[k] = pos2, pos3, posx

        @pl.when(pos2 >= 0)
        def _():
            wide = kept_folded(int_ref, mix_ref, j, x)
            short = wide[:half] + wide[half:]

            @pl.when(pos2 < CAPS[0])
            def _():
                m2a_ref[pos2] = short

            @pl.when(pos2 >= CAPS[0])
            def _():
                m2b_ref[pos2 - CAPS[0]] = short

        @pl.when(pos3 >= 0)
        def _():
            wide = kept_folded(int_ref, mix_ref, j, x)

            @pl.when(pos3 < CAPS[0])
            def _():
                m3a_ref[pos3] = wide

            @pl.when(pos3 >= CAPS[0])
            def _():
                m3b_ref[pos3 - CAPS[0]] = wide

    @pl.when(step == pl.num_programs(0) - 1)
    def _():
        labels = row_ref[...]
        lanes = lax.broadcasted_iota(jnp.int32, labels.shape, 1)
        ahead = pltpu.roll(labels, total - NARROW, 1)
        long = (labels == ahead) & (lanes < total - NARROW) & (labels != big)
        too_long = jnp.max(long.astype(jnp.int32)) == 1
        n2, n3, nx = counts_ref[0], counts_ref[1], counts_ref[2]
        one_label = occ_ref[0] == pair_label
        form = jnp.where((n3 <= CAPS[0]) & (nx <= FEW_SHORT), 2, 3)
        form = jnp.where((n3 <= FEW_WIDE) & (n2 <= CAPS[0]), 1, form)
        form = jnp.where(one_label, form, 4)
        form = jnp.where((n3 == 0) & (n2 <= CAPS[0]), 0, form)
        form_ref[0] = jnp.where(too_long, 4, form)


def wide_blocks(integrals, occ_irrep, vir_irrep, screen, place, batch):
    occ_share, depth, total = integrals.shape
    shapes = [(n, depth // 2, FOLD) for n in CAPS] + [(n, depth, FOLD) for n in CAPS]
    smem = pl.BlockSpec(memory_space=pltpu.SMEM)

    def kernel(*refs):
        wide_kernel(*refs, batch)

    return pl.pallas_call(
        kernel,
        grid_spec=pltpu.PrefetchScalarGridSpec(
            num_scalar_prefetch=4,
            grid=(occ_share // K_STEP,),
            in_specs=[
                pl.BlockSpec((K_STEP, depth, total), lambda k, *_: (k, 0, 0)),
                pl.BlockSpec((1, total), lambda k, *_: (0, 0)),
            ],
            out_specs=[pl.BlockSpec(v, lambda k, *_: (0, 0, 0)) for v in shapes] + [smem] * 4,
            scratch_shapes=[
                pltpu.VMEM((depth, total), jnp.bfloat16),
                pltpu.VMEM((total, 8), jnp.int32),
                pltpu.SMEM((3,), jnp.int32),
            ],
        ),
        out_shape=[jax.ShapeDtypeStruct(v, jnp.bfloat16) for v in shapes]
        + [jax.ShapeDtypeStruct((n,), jnp.int32) for n in (occ_share, occ_share, occ_share, 1)],
        cost_estimate=cost(5),
        compiler_params=pltpu.CompilerParams(vmem_limit_bytes=24 * 1024 * 1024),
    )(occ_irrep, vir_irrep, screen.T, place, integrals, vir_irrep[None, :])


def narrow_kernel(
    occ_ref, vir_ref, screen_ref, place_ref, posx_ref, int_ref, row_ref, narrow_ref, few_ref,
    mix_ref, column_ref, batch,
):
    step = pl.program_id(0)
    k_step, depth, total = int_ref.shape
    half = depth // 2
    row, col = place_ref[0], place_ref[1]

    @pl.when(step == 0)
    def _():
        label_mix(mix_ref, column_ref, row_ref, row, largest_irrep(vir_ref), False)

    lane = lax.broadcasted_iota(jnp.int32, (half, 2 * NARROW), 1)
    local = column_ref[pl.ds(pl.multiple_of(row * depth, depth), depth), :1]
    for j in range(k_step):
        k = step * k_step + j
        k_whole = col * (k_step * pl.num_programs(0)) + k
        x = jnp.bitwise_xor(occ_ref[k_whole], occ_ref[batch])
        bits = screen_ref[0, k_whole]
        for g in range(1, 8):
            bits = bits + screen_ref[g, k_whole] * (1 << g)
        narrow = kept_folded(int_ref, mix_ref, j, x)
        narrow = (narrow[:, : 2 * NARROW] + narrow[:, 2 * NARROW:]).astype(jnp.float32)
        narrow = narrow + pltpu.roll(narrow, NARROW, 1)
        on = jnp.bitwise_and(lax.shift_right_logical(jnp.full(local.shape, bits), local), 1) == 1
        narrow = jnp.where(on, narrow, 0.0)
        narrow = jnp.where(lane < NARROW, narrow[:half], narrow[half:]).astype(jnp.bfloat16)
        narrow_ref[j] = narrow
        posx = posx_ref[k]

        @pl.when((posx >= 0) & (posx < FEW_SHORT))
        def _(narrow=narrow, posx=posx):
            few_ref[posx] = narrow


def narrow_blocks(integrals, occ_irrep, vir_irrep, screen, place, posx, batch):
    occ_share, depth, total = integrals.shape
    shapes = [(n, depth // 2, 2 * NARROW) for n in (occ_share, FEW_SHORT)]

    def kernel(*refs):
        narrow_kernel(*refs, batch)

    return pl.pallas_call(
        kernel,
        grid_spec=pltpu.PrefetchScalarGridSpec(
            num_scalar_prefetch=5,
            grid=(occ_share // K_STEP,),
            in_specs=[
                pl.BlockSpec((K_STEP, depth, total), lambda k, *_: (k, 0, 0)),
                pl.BlockSpec((1, total), lambda k, *_: (0, 0)),
            ],
            out_specs=[
                pl.BlockSpec((K_STEP, depth // 2, 2 * NARROW), lambda k, *_: (k, 0, 0)),
                pl.BlockSpec(shapes[1], lambda k, *_: (0, 0, 0)),
            ],
            scratch_shapes=[pltpu.VMEM((depth, total), jnp.bfloat16), pltpu.VMEM((total, 8), jnp.int32)],
        ),
        out_shape=[jax.ShapeDtypeStruct(v, jnp.bfloat16) for v in shapes],
        cost_estimate=cost(6),
        compiler_params=pltpu.CompilerParams(vmem_limit_bytes=16 * 1024 * 1024),
    )(occ_irrep, vir_irrep, screen.T, place, posx, integrals, vir_irrep[None, :])


def cost(micros):
    return pl.CostEstimate(flops=int(micros * 1e9), bytes_accessed=int(micros * 3e6), transcendentals=0)


SLOTS = (0, 1, 3, 2)
NEAR = 3


def amplitude_rows(column_ref, row_ref, occ_ref, row, batch, share):
    column_ref[...] = label_columns(row_ref[...])
    column = column_ref[pl.ds(pl.multiple_of(row * share, share), share), :1]
    return jnp.concatenate([jnp.bitwise_xor(column, occ_ref[i]) for i in range(batch)], axis=0)


def write_quarters(total_ref, col, outs):
    rows, fold = total_ref.shape
    width, height = fold // 2, rows // 2
    for t, out_ref in enumerate(outs):
        goal = jnp.bitwise_xor(col, t)
        lanes = pl.ds(pl.multiple_of((goal % 2) * width, width), width)
        lines = pl.ds(pl.multiple_of((goal // 2) * height, height), height)
        out_ref[...] = total_ref[lines, lanes].reshape(out_ref.shape)


def chosen(refs, starts, pos, pick):
    block = None
    for n, group in enumerate(refs):
        inside = (pos >= starts[n]) & (pos < starts[n + 1])
        at = jnp.clip(pos - starts[n], 0, starts[n + 1] - starts[n] - 1)
        found = pick(group, at)
        found = jnp.where(inside, found, jnp.zeros_like(found))
        block = found if block is None else block + found
    return block


def starts_of(arrays):
    starts = [0]
    for v in arrays:
        starts.append(starts[-1] + v.shape[0])
    return starts


def mask_kernel(occ_ref, place_ref, amp_ref, row_ref, lhs_ref, far_ref, fold_ref, mix_ref, column_ref, amp_buffer, sems):
    batch, k_all, share, total = amp_ref.shape
    rows, groups = batch * share, k_all // K_STEP
    row, col = place_ref[0], place_ref[1]

    def fetch(group):
        slot = group % 2
        source = amp_ref.at[:, pl.ds(group * K_STEP, K_STEP)]
        return pltpu.make_async_copy(source, amp_buffer.at[slot], sems.at[slot])

    fetch(0).start()
    column = amplitude_rows(column_ref, row_ref, occ_ref, row, batch, share)
    mix_ref[...] = as_bf16(jnp.bitwise_xor(column, row_ref[...]))

    @pl.loop(0, groups)
    def _(group):
        slot = group % 2

        @pl.when(group + 1 < groups)
        def _():
            fetch(group + 1).start()

        fetch(group).wait()

        @pl.loop(0, K_STEP)
        def _(j):
            wanted = as_bf16(jnp.full((rows, share), occ_ref[col * k_all + group * K_STEP + j]))
            folded = None
            for n, s in enumerate(SLOTS):
                place = pl.ds(pl.multiple_of(jnp.bitwise_xor(row, s) * share, share), share)
                tile = amp_buffer[slot, :, j, :, place].reshape(rows, share)
                piece = jnp.where(mix_ref[:, place] == wanted, tile, jnp.zeros_like(tile))
                if n < NEAR:
                    lhs_ref[group, :, pl.ds(pl.multiple_of((n * K_STEP + j) * share, share), share)] = piece
                else:
                    far_ref[group, :, pl.ds(pl.multiple_of(j * share, share), share)] = piece
                folded = piece if folded is None else folded + piece
            fold_ref[group, :, pl.ds(pl.multiple_of(j * share, share), share)] = folded


def masked_amplitudes(amplitudes, occ_irrep, vir_irrep, place):
    batch, k_all, share, total = amplitudes.shape
    rows, groups = batch * share, k_all // K_STEP
    smem = pl.BlockSpec(memory_space=pltpu.SMEM)
    vmem = pl.BlockSpec(memory_space=pltpu.VMEM)
    hbm = pl.BlockSpec(memory_space=pltpu.HBM)
    widths = (NEAR * K_STEP * share, K_STEP * share, K_STEP * share)
    return pl.pallas_call(
        mask_kernel,
        in_specs=[smem, smem, hbm, vmem],
        out_specs=[vmem] * 3,
        out_shape=[jax.ShapeDtypeStruct((groups, rows, w), jnp.bfloat16) for w in widths],
        scratch_shapes=[
            pltpu.VMEM((rows, total), jnp.bfloat16),
            pltpu.VMEM((total, 8), jnp.int32),
            pltpu.VMEM((2, batch, K_STEP, share, total), jnp.bfloat16),
            pltpu.SemaphoreType.DMA((2,)),
        ],
        cost_estimate=cost(7),
        compiler_params=pltpu.CompilerParams(vmem_limit_bytes=28 * 1024 * 1024),
    )(occ_irrep, place, amplitudes, vir_irrep[None, :])


def make_first_kernel(few, n3, starts3):
    def kernel(pos3_ref, posx_ref, place_ref, lhs_ref, far_ref, *refs):
        narrow_refs = refs[:6]
        m3_refs = [refs[6 + 3 * n:9 + 3 * n] for n in range(n3)]
        narrow_sum, wide_sum, narrow_rhs, wide_rhs = refs[6 + 3 * n3:]
        row = place_ref[0]
        at_end = (row == 0) | (row == 3)
        groups, _, depth = lhs_ref.shape
        share = depth // (NEAR * K_STEP)
        half = share // 2
        lane = lax.broadcasted_iota(jnp.int32, (half, 2 * NARROW), 1)

        narrow_sum[...] = jnp.zeros(narrow_sum.shape, jnp.float32)
        wide_sum[...] = jnp.zeros(wide_sum.shape, jnp.float32)

        @pl.loop(0, groups)
        def _(group):
            @pl.loop(0, K_STEP)
            def _(j):
                k = group * K_STEP + j
                own, e1, o1 = [ref[k] for ref in narrow_refs[:3]]
                far = jnp.maximum(posx_ref[k], 0) if few else k
                e2, o2, e3 = [ref[far] for ref in narrow_refs[3:]]
                two = jnp.where(at_end, e2, o2)
                if few:
                    two, e3 = [jnp.where(posx_ref[k] >= 0, v, jnp.zeros_like(v)) for v in (two, e3)]
                for n, block in enumerate((own, e1, jnp.where(at_end, e3, o1), two)):
                    zero = jnp.zeros_like(block)
                    first = pl.multiple_of((n * K_STEP + j) * share, share)
                    narrow_rhs[pl.ds(first, half)] = jnp.where(lane < NARROW, block, zero)
                    narrow_rhs[pl.ds(first + half, half)] = jnp.where(lane < NARROW, zero, block)
                for n in range(3 if n3 else 0):
                    block = chosen(m3_refs, starts3, pos3_ref[k], lambda group, at, n=n: group[n][at])
                    if n == 2:
                        block = jnp.where(at_end, jnp.zeros_like(block), block)
                    wide_rhs[pl.ds(pl.multiple_of((n * K_STEP + j) * share, share), share)] = block

            narrow = jnp.dot(lhs_ref[group], narrow_rhs[:depth], preferred_element_type=jnp.float32)
            narrow += jnp.dot(far_ref[group], narrow_rhs[depth:], preferred_element_type=jnp.float32)
            narrow_sum[...] += narrow
            if n3:
                wide_sum[...] += jnp.dot(lhs_ref[group], wide_rhs[...], preferred_element_type=jnp.float32)

    return kernel


def first_product(lhs, far_lhs, pos3, posx, place, narrow, few, m3):
    groups, rows, depth = lhs.shape
    vmem = pl.BlockSpec(memory_space=pltpu.VMEM)
    smem = pl.BlockSpec(memory_space=pltpu.SMEM)
    arrays = list(narrow) + [v for group in m3 for v in group]
    wide = (rows, FOLD) if m3 else (16, FOLD)
    wide_depth = depth if m3 else 16
    return pl.pallas_call(
        make_first_kernel(few, len(m3), starts_of([v[0] for v in m3])),
        in_specs=[smem] * 3 + [vmem] * (2 + len(arrays)),
        out_specs=[vmem] * 2,
        out_shape=[jax.ShapeDtypeStruct(v, jnp.float32) for v in ((rows, 2 * NARROW), wide)],
        scratch_shapes=[
            pltpu.VMEM((depth // NEAR * len(SLOTS), 2 * NARROW), jnp.bfloat16),
            pltpu.VMEM((wide_depth, FOLD), jnp.bfloat16),
        ],
        cost_estimate=cost(9 if m3 else 6),
        compiler_params=pltpu.CompilerParams(vmem_limit_bytes=32 * 1024 * 1024),
    )(pos3, posx, place, lhs, far_lhs, *arrays)


def make_last_kernel(n2, starts2, n3, starts3):
    def kernel(occ_ref, vir_ref, pos2_ref, pos3_ref, place_ref, fold_ref, far_ref, row_ref, narrow_ref, wide_ref, *refs):
        m2_refs = refs[:n2]
        m3_refs = [refs[n2 + 2 * n:n2 + 2 * n + 2] for n in range(n3)]
        refs = refs[n2 + 2 * n3:]
        outs = refs[:4]
        column_ref, total_ref, short_rhs, far_rhs = refs[4:]
        row, col = place_ref[0], place_ref[1]
        at_end = (row == 0) | (row == 3)
        groups, rows, width = fold_ref.shape
        share = width // K_STEP
        batch = rows // share
        @pl.loop(0, groups * K_STEP)
        def _(k):
            here = pl.ds(pl.multiple_of(k * share, share), share)
            short = chosen(m2_refs, starts2, pos2_ref[k], lambda ref, at: ref[at])
            short_rhs[here] = jnp.concatenate([short, short], axis=0)
            if n3:
                far_rhs[here] = chosen(
                    m3_refs, starts3, pos3_ref[k], lambda pair, at: jnp.where(at_end, pair[0][at], pair[1][at])
                )

        column = amplitude_rows(column_ref, row_ref, occ_ref, row, batch, share)
        target = jnp.bitwise_xor(column, occ_ref[batch])
        both = narrow_ref[...]
        both = both + pltpu.roll(both, NARROW, 1)
        both = jnp.concatenate([both] * (FOLD // (2 * NARROW)), axis=1)
        part = wide_ref[...] if n3 else 0.0
        for group in range(groups):
            here = pl.ds(group * width, width)
            part += jnp.dot(fold_ref[group], short_rhs[here], preferred_element_type=jnp.float32)
            if n3:
                part += jnp.dot(far_ref[group], far_rhs[here], preferred_element_type=jnp.float32)
        total_ref[...] = jnp.where(target == largest_irrep(vir_ref), part, both)
        write_quarters(total_ref, col, outs)

    return kernel


def last_product(far_lhs, fold, occ_irrep, vir_irrep, pos2, pos3, place, narrow_sum, wide_sum, m2, m3, batch):
    groups, rows, width = fold.shape
    share = rows // batch
    vmem = pl.BlockSpec(memory_space=pltpu.VMEM)
    smem = pl.BlockSpec(memory_space=pltpu.SMEM)
    arrays = [narrow_sum, wide_sum] + list(m2) + [v for group in m3 for v in group]
    quarter = (batch // 2, share, FOLD // 2)
    whole = groups * width
    far_lhs = far_lhs if m3 else jnp.zeros((8, 128), jnp.bfloat16)
    return pl.pallas_call(
        make_last_kernel(len(m2), starts_of(m2), len(m3), starts_of([v[0] for v in m3])),
        in_specs=[smem] * 5 + [vmem] * (3 + len(arrays)),
        out_specs=[vmem] * 4,
        out_shape=[jax.ShapeDtypeStruct(quarter, jnp.float32)] * 4,
        scratch_shapes=[
            pltpu.VMEM((vir_irrep.shape[0], 8), jnp.int32),
            pltpu.VMEM((rows, FOLD), jnp.float32),
            pltpu.VMEM((whole, FOLD), jnp.bfloat16),
            pltpu.VMEM((whole if m3 else 16, FOLD), jnp.bfloat16),
        ],
        cost_estimate=cost(4 if m3 else 2),
        compiler_params=pltpu.CompilerParams(vmem_limit_bytes=32 * 1024 * 1024),
    )(occ_irrep, vir_irrep, pos2, pos3, place, fold, far_lhs, vir_irrep[None, :], *arrays)


def dense_product(amplitudes, whole, occ_irrep, occ_local, vir_local, vir_irrep):
    batch = amplitudes.shape[0]
    keep = (
        jnp.bitwise_xor(occ_irrep[:batch, None], occ_local[None, :])[:, :, None, None]
        == jnp.bitwise_xor(vir_local[:, None], vir_irrep[None, :])[None, None]
    )
    kept = jnp.where(keep, amplitudes, jnp.zeros_like(amplitudes))
    return lax.dot_general(
        kept, whole, (((1, 3), (0, 1)), ((), ())), preferred_element_type=jnp.float32
    )


def finish(cycle, occ_irrep, vir_irrep, occ_energy, vir_energy, a_start, a_size, b_start, b_size, batch):
    label_a = lax.dynamic_slice_in_dim(vir_irrep, a_start, a_size)
    label_b = lax.dynamic_slice_in_dim(vir_irrep, b_start, b_size)
    energy_a = lax.dynamic_slice_in_dim(vir_energy, a_start, a_size)
    energy_b = lax.dynamic_slice_in_dim(vir_energy, b_start, b_size)
    target = jnp.bitwise_xor(
        jnp.bitwise_xor(occ_irrep[:batch, None], occ_irrep[batch]), label_a[None, :]
    )
    keep = label_b[:, None, None] == target[None, :, :]
    denominator = (
        occ_energy[:batch][None, :, None]
        + occ_energy[batch]
        - energy_a[None, None, :]
        - energy_b[:, None, None]
    )
    swapped = jnp.transpose(cycle, (2, 0, 1))
    return jnp.where(keep, swapped, 0.0) / denominator


def on_square(amplitudes, integrals, occ_irrep, vir_irrep, screen):
    batch, occ_share, share, vir_total = amplitudes.shape
    row = lax.axis_index("row")
    col = lax.axis_index("col")
    place = jnp.stack([row, col]).astype(jnp.int32)
    m2a, m2b, m3a, m3b, pos2, pos3, posx, form = wide_blocks(
        integrals, occ_irrep, vir_irrep, screen, place, batch
    )
    outer = [(0, 1), (1, 0), (2, 3), (3, 2)]
    inner = [(1, 2), (2, 1)]
    inward = [(0, 1), (3, 2)]
    outward = [(1, 0), (2, 3)]
    ends = [(0, 3), (3, 0)]
    second = [(r, r ^ 2) for r in range(4)]

    def move(v, pairs):
        return lax.ppermute(v, "row", pairs)

    def sparse(use_few, choose):
        def run(m2a, m2b, m3a, m3b):
            shorts, wides = choose(m2a, m2b, m3a, m3b)
            near = [(own, move(own, outer), move(own, inner)) for own in wides]
            narrow, few = narrow_blocks(integrals, occ_irrep, vir_irrep, screen, place, posx, batch)
            h1 = [move(v, inward) for v in shorts]
            e1, o1 = move(narrow, outer), move(narrow, inner)
            two, three = (move(few, second), move(few, ends)) if use_few else (None, None)
            lhs, far_lhs, fold = masked_amplitudes(amplitudes, occ_irrep, vir_irrep, place)
            near, h1, e1, o1, two, three, _ = lax.optimization_barrier((near, h1, e1, o1, two, three, fold))
            h2 = [move(own + v, inner) for own, v in zip(shorts, h1)]
            far = [(move(o, outward), move(e, inner)) for _, e, o in near]
            if use_few:
                blocks = (narrow, e1, o1, two, two, three)
            else:
                e2, o2 = move(o1, outward), move(e1, inner)
                h2, e2, o2 = lax.optimization_barrier((h2, e2, o2))
                blocks = (narrow, e1, o1, e2, o2, move(o2, outward))
            h3 = [move(own + v, outward) for own, v in zip(shorts, h2)]
            sums = [a + b + c + d for a, b, c, d in zip(shorts, h1, h2, h3)]
            narrow_sum, wide_sum = first_product(
                lhs, far_lhs, pos3, posx, place, blocks, use_few, near
            )
            return list(last_product(
                far_lhs, fold, occ_irrep, vir_irrep, pos2, pos3, place, narrow_sum, wide_sum, sums, far, batch
            ))

        return run

    def dense(*_):
        occ_local = lax.dynamic_slice_in_dim(occ_irrep, col * occ_share, occ_share)
        vir_local = lax.dynamic_slice_in_dim(vir_irrep, row * share, share)
        screen_rows = lax.dynamic_slice_in_dim(screen, col * occ_share, occ_share, 0)
        fold = folded_integrals(
            integrals, occ_local, vir_local, vir_irrep, occ_irrep[batch], screen_rows
        )
        whole = jnp.zeros((occ_share, vir_total, FOLD), fold.dtype)
        for s in range(4):
            block = move(fold, [(r, r ^ s) for r in range(4)]) if s else fold
            whole = lax.dynamic_update_slice_in_dim(whole, block, jnp.bitwise_xor(row, s) * share, 1)
        total = dense_product(amplitudes, whole, occ_irrep, occ_local, vir_local, vir_irrep)
        quarter = (batch // 2, share, FOLD // 2)
        goals = [jnp.bitwise_xor(col, t) for t in range(4)]
        return [
            lax.dynamic_slice(total, (g // 2 * quarter[0], 0, g % 2 * quarter[2]), quarter) for g in goals
        ]

    branches = [
        sparse(False, lambda m2a, m2b, m3a, m3b: ([m2a], [])),
        sparse(False, lambda m2a, m2b, m3a, m3b: ([m2a], [m3a[:FEW_WIDE]])),
        sparse(True, lambda m2a, m2b, m3a, m3b: ([m2a[:FEW_SHORT]], [m3a])),
        sparse(False, lambda m2a, m2b, m3a, m3b: ([m2a, m2b], [m3a, m3b])),
        dense,
    ]
    quarters = lax.switch(form[0], branches, m2a, m2b, m3a, m3b)
    mine = quarters[0]
    for t in (1, 2, 3):
        mine = mine + lax.ppermute(quarters[t], "col", [(q, q ^ t) for q in range(4)])
    places = [(r, q) for r in range(4) for q in range(4)]
    same = lax.ppermute(mine, ("row", "col"), [(r * 4 + q, q * 4 + r) for r, q in places])
    other = lax.ppermute(mine, ("row", "col"), [(r * 4 + q, (q ^ 2) * 4 + r) for r, q in places])
    upper = row // 2 == 1
    low = jnp.where(upper, other, same)
    high = jnp.where(upper, same, other)
    return jnp.concatenate([low, high], axis=0)


def on_any(amplitudes, integrals, occ_irrep, vir_irrep, screen):
    batch, occ_share, share, vir_total = amplitudes.shape
    row = lax.axis_index("row")
    col = lax.axis_index("col")
    occ_local = lax.dynamic_slice_in_dim(occ_irrep, col * occ_share, occ_share)
    vir_local = lax.dynamic_slice_in_dim(vir_irrep, row * share, share)
    screen_rows = lax.dynamic_slice_in_dim(screen, col * occ_share, occ_share, 0)
    fold = folded_integrals(
        integrals, occ_local, vir_local, vir_irrep, occ_irrep[batch], screen_rows
    )
    whole = lax.all_gather(fold, "row", axis=1, tiled=True)
    cycle = dense_product(amplitudes, whole, occ_irrep, occ_local, vir_local, vir_irrep)
    cycle = lax.psum(cycle, "col")
    cycle = jnp.concatenate([cycle] * (vir_total // FOLD), axis=2)
    cycle = lax.all_to_all(cycle, "row", split_axis=2, concat_axis=1, tiled=True)
    a_size = vir_total // lax.axis_size("col")
    return lax.dynamic_slice_in_dim(cycle, col * a_size, a_size, 1)


def on_device(amplitudes, integrals, occ_irrep, vir_irrep, screen, occ_energy, vir_energy):
    batch, _, vir_share, vir_total = amplitudes.shape
    square = lax.axis_size("row") == 4 and lax.axis_size("col") == 4
    form = on_square if square else on_any
    cycle = form(amplitudes, integrals, occ_irrep, vir_irrep, screen)
    a_size = vir_total // lax.axis_size("col")
    return finish(
        cycle, occ_irrep, vir_irrep, occ_energy, vir_energy,
        lax.axis_index("col") * a_size, a_size, lax.axis_index("row") * vir_share, vir_share, batch,
    )


def solution(mesh):
    in_specs = (
        P("parts", "col", "row", None),
        P(("parts", "col"), "row", None),
        P("parts"),
        P("parts"),
        P("parts", None),
        P("parts"),
        P("parts"),
    )
    out_specs = P("row", "parts", "col")
    return jax.shard_map(
        on_device, mesh=mesh, in_specs=in_specs, out_specs=out_specs, check_vma=False
    )
```

```python
import jax
import jax.numpy as jnp
from jax import lax
from jax.experimental import pallas as pl
from jax.experimental.pallas import tpu as pltpu
from jax.sharding import PartitionSpec as P

FOLD = 256
K_STEP = 5


def folded_integrals(integrals, occ_local, vir_local, vir_irrep, pair_label, screen_rows):
    irrep_codes = jnp.arange(8, dtype=jnp.int32)
    screen_local = jnp.sum(
        screen_rows[:, None, :] * (vir_local[None, :, None] == irrep_codes).astype(jnp.int32),
        axis=2,
    )
    target = jnp.bitwise_xor(
        jnp.bitwise_xor(occ_local[:, None], vir_local[None, :]), pair_label
    )
    target = jnp.where(screen_local == 1, target, -1)
    keep = target[:, :, None] == vir_irrep[None, None, :]
    kept = jnp.where(keep, integrals, jnp.zeros_like(integrals))
    return kept[:, :, :FOLD] + kept[:, :, FOLD:]


NARROW = 64
CAPS = (22, 3)
FEW_SHORT = 8
FEW_WIDE = 5


def largest_irrep(vir_ref):
    return jnp.where(vir_ref[0] == vir_ref[FOLD - 1], vir_ref[0], vir_ref[FOLD])


def label_columns(row_labels):
    return jnp.transpose(jnp.broadcast_to(row_labels, (8, row_labels.shape[1])))


def as_bf16(labels):
    return labels.astype(jnp.float32).astype(jnp.bfloat16)


def label_mix(mix_ref, column_ref, row_ref, row, big, keep_big):
    depth = mix_ref.shape[0]
    column_ref[...] = label_columns(row_ref[...])
    column = column_ref[pl.ds(pl.multiple_of(row * depth, depth), depth), :1]
    is_big = row_ref[...] == big
    wanted = is_big if keep_big else jnp.logical_not(is_big)
    mix_ref[...] = as_bf16(jnp.where(wanted, jnp.bitwise_xor(column, row_ref[...]), 8))


def kept_folded(int_ref, mix_ref, j, x):
    tile = int_ref[j]
    wanted = as_bf16(jnp.full(mix_ref.shape, x))
    kept = jnp.where(mix_ref[...] == wanted, tile, jnp.zeros_like(tile))
    return kept[:, :FOLD] + kept[:, FOLD:]


def wide_kernel(
    occ_ref, vir_ref, screen_ref, place_ref, int_ref, row_ref,
    m2a_ref, m2b_ref, m3a_ref, m3b_ref, pos2_ref, pos3_ref, posx_ref, form_ref,
    mix_ref, column_ref, counts_ref, batch,
):
    step = pl.program_id(0)
    k_step, depth, total = int_ref.shape
    half = depth // 2
    row, col = place_ref[0], place_ref[1]
    pair_label = occ_ref[batch]
    big = largest_irrep(vir_ref)

    @pl.when(step == 0)
    def _():
        for n in range(3):
            counts_ref[n] = 0
        label_mix(mix_ref, column_ref, row_ref, row, big, True)

    @pl.loop(0, k_step)
    def _(j):
        k = step * k_step + j
        k_whole = col * (k_step * pl.num_programs(0)) + k
        x = jnp.bitwise_xor(occ_ref[k_whole], pair_label)
        on_big = screen_ref[jnp.bitwise_xor(big, x), k_whole] == 1
        actives = (on_big & (x != 0), on_big & (x == 0), x != 0)
        pos2, pos3, posx = [jnp.where(active, counts_ref[n], -1) for n, active in enumerate(actives)]
        for n, active in enumerate(actives):
            counts_ref[n] = counts_ref[n] + active.astype(jnp.int32)
        pos2_ref[k], pos3_ref[k], posx_ref[k] = pos2, pos3, posx

        @pl.when(pos2 >= 0)
        def _():
            wide = kept_folded(int_ref, mix_ref, j, x)
            short = wide[:half] + wide[half:]

            @pl.when(pos2 < CAPS[0])
            def _():
                m2a_ref[pos2] = short

            @pl.when(pos2 >= CAPS[0])
            def _():
                m2b_ref[pos2 - CAPS[0]] = short

        @pl.when(pos3 >= 0)
        def _():
            wide = kept_folded(int_ref, mix_ref, j, x)

            @pl.when(pos3 < CAPS[0])
            def _():
                m3a_ref[pos3] = wide

            @pl.when(pos3 >= CAPS[0])
            def _():
                m3b_ref[pos3 - CAPS[0]] = wide

    @pl.when(step == pl.num_programs(0) - 1)
    def _():
        labels = row_ref[...]
        lanes = lax.broadcasted_iota(jnp.int32, labels.shape, 1)
        ahead = pltpu.roll(labels, total - NARROW, 1)
        long = (labels == ahead) & (lanes < total - NARROW) & (labels != big)
        too_long = jnp.max(long.astype(jnp.int32)) == 1
        n2, n3, nx = counts_ref[0], counts_ref[1], counts_ref[2]
        one_label = occ_ref[0] == pair_label
        form = jnp.where((n3 <= CAPS[0]) & (nx <= FEW_SHORT), 2, 3)
        form = jnp.where((n3 <= FEW_WIDE) & (n2 <= CAPS[0]), 1, form)
        form = jnp.where(one_label, form, 4)
        form = jnp.where((n3 == 0) & (n2 <= CAPS[0]), 0, form)
        form_ref[0] = jnp.where(too_long, 4, form)


def wide_blocks(integrals, occ_irrep, vir_irrep, screen, place, batch):
    occ_share, depth, total = integrals.shape
    shapes = [(n, depth // 2, FOLD) for n in CAPS] + [(n, depth, FOLD) for n in CAPS]
    smem = pl.BlockSpec(memory_space=pltpu.SMEM)

    def kernel(*refs):
        wide_kernel(*refs, batch)

    return pl.pallas_call(
        kernel,
        grid_spec=pltpu.PrefetchScalarGridSpec(
            num_scalar_prefetch=4,
            grid=(occ_share // K_STEP,),
            in_specs=[
                pl.BlockSpec((K_STEP, depth, total), lambda k, *_: (k, 0, 0)),
                pl.BlockSpec((1, total), lambda k, *_: (0, 0)),
            ],
            out_specs=[pl.BlockSpec(v, lambda k, *_: (0, 0, 0)) for v in shapes] + [smem] * 4,
            scratch_shapes=[
                pltpu.VMEM((depth, total), jnp.bfloat16),
                pltpu.VMEM((total, 8), jnp.int32),
                pltpu.SMEM((3,), jnp.int32),
            ],
        ),
        out_shape=[jax.ShapeDtypeStruct(v, jnp.bfloat16) for v in shapes]
        + [jax.ShapeDtypeStruct((n,), jnp.int32) for n in (occ_share, occ_share, occ_share, 1)],
        cost_estimate=cost(5),
        compiler_params=pltpu.CompilerParams(vmem_limit_bytes=24 * 1024 * 1024),
    )(occ_irrep, vir_irrep, screen.T, place, integrals, vir_irrep[None, :])


def narrow_kernel(
    occ_ref, vir_ref, screen_ref, place_ref, posx_ref, int_ref, row_ref, short_ref, narrow_ref, few_ref,
    mix_ref, column_ref, batch,
):
    step = pl.program_id(0)
    k_step, depth, total = int_ref.shape
    half = depth // 2
    row, col = place_ref[0], place_ref[1]

    @pl.when(step == 0)
    def _():
        label_mix(mix_ref, column_ref, row_ref, row, largest_irrep(vir_ref), False)
        if few_ref is not None:
            for n in range(FEW_SHORT):
                for piece in range(2):
                    block = short_ref[n, :, piece * 2 * NARROW:(piece + 1) * 2 * NARROW]
                    narrow_ref[k_step * pl.num_programs(0) + 2 * n + piece] = block
                    few_ref[FEW_SHORT + 2 * n + piece] = block

    lane = lax.broadcasted_iota(jnp.int32, (half, 2 * NARROW), 1)
    local = column_ref[pl.ds(pl.multiple_of(row * depth, depth), depth), :1]
    for j in range(k_step):
        k = step * k_step + j
        k_whole = col * (k_step * pl.num_programs(0)) + k
        x = jnp.bitwise_xor(occ_ref[k_whole], occ_ref[batch])
        bits = screen_ref[0, k_whole]
        for g in range(1, 8):
            bits = bits + screen_ref[g, k_whole] * (1 << g)
        narrow = kept_folded(int_ref, mix_ref, j, x)
        narrow = (narrow[:, : 2 * NARROW] + narrow[:, 2 * NARROW:]).astype(jnp.float32)
        narrow = narrow + pltpu.roll(narrow, NARROW, 1)
        on = jnp.bitwise_and(lax.shift_right_logical(jnp.full(local.shape, bits), local), 1) == 1
        narrow = jnp.where(on, narrow, 0.0)
        narrow = jnp.where(lane < NARROW, narrow[:half], narrow[half:]).astype(jnp.bfloat16)
        narrow_ref[k] = narrow
        if few_ref is not None:
            posx = posx_ref[k]

            @pl.when((posx >= 0) & (posx < FEW_SHORT))
            def _(narrow=narrow, posx=posx):
                few_ref[posx] = narrow


def narrow_blocks(integrals, occ_irrep, vir_irrep, screen, place, posx, short, batch):
    occ_share, depth, total = integrals.shape
    few = short is not None
    counts = (occ_share + 2 * FEW_SHORT, 3 * FEW_SHORT) if few else (occ_share,)
    shapes = [(n, depth // 2, 2 * NARROW) for n in counts]
    fixed = lambda k, *_: (0, 0, 0)

    def kernel(*refs):
        if few:
            narrow_kernel(*refs, batch)
        else:
            narrow_kernel(*refs[:7], None, refs[7], None, *refs[8:], batch)

    return pl.pallas_call(
        kernel,
        grid_spec=pltpu.PrefetchScalarGridSpec(
            num_scalar_prefetch=5,
            grid=(occ_share // K_STEP,),
            in_specs=[
                pl.BlockSpec((K_STEP, depth, total), lambda k, *_: (k, 0, 0)),
                pl.BlockSpec((1, total), lambda k, *_: (0, 0)),
            ] + ([pl.BlockSpec((FEW_SHORT, depth // 2, FOLD), fixed)] if few else []),
            out_specs=[pl.BlockSpec(v, fixed) for v in shapes],
            scratch_shapes=[pltpu.VMEM((depth, total), jnp.bfloat16), pltpu.VMEM((total, 8), jnp.int32)],
        ),
        out_shape=[jax.ShapeDtypeStruct(v, jnp.bfloat16) for v in shapes],
        cost_estimate=cost(5),
        compiler_params=pltpu.CompilerParams(vmem_limit_bytes=16 * 1024 * 1024),
    )(occ_irrep, vir_irrep, screen.T, place, posx, integrals, vir_irrep[None, :], *([short] if few else []))


def cost(micros):
    return pl.CostEstimate(flops=int(micros * 1e9), bytes_accessed=int(micros * 3e6), transcendentals=0)


SLOTS = (0, 1, 3, 2)
NEAR = 3


def amplitude_rows(column_ref, row_ref, occ_ref, row, batch, share):
    column_ref[...] = label_columns(row_ref[...])
    column = column_ref[pl.ds(pl.multiple_of(row * share, share), share), :1]
    return jnp.concatenate([jnp.bitwise_xor(column, occ_ref[i]) for i in range(batch)], axis=0)


def write_quarters(total_ref, col, outs):
    rows, fold = total_ref.shape
    width, height = fold // 2, rows // 2
    for t, out_ref in enumerate(outs):
        goal = jnp.bitwise_xor(col, t)
        lanes = pl.ds(pl.multiple_of((goal % 2) * width, width), width)
        lines = pl.ds(pl.multiple_of((goal // 2) * height, height), height)
        out_ref[...] = total_ref[lines, lanes].reshape(out_ref.shape)


def chosen(refs, starts, pos, pick):
    block = None
    for n, group in enumerate(refs):
        inside = (pos >= starts[n]) & (pos < starts[n + 1])
        at = jnp.clip(pos - starts[n], 0, starts[n + 1] - starts[n] - 1)
        found = pick(group, at)
        found = jnp.where(inside, found, jnp.zeros_like(found))
        block = found if block is None else block + found
    return block


def starts_of(arrays):
    starts = [0]
    for v in arrays:
        starts.append(starts[-1] + v.shape[0])
    return starts


def mask_kernel(occ_ref, place_ref, amp_ref, row_ref, lhs_ref, far_ref, fold_ref, mix_ref, column_ref, amp_buffer, sems):
    batch, k_all, share, total = amp_ref.shape
    rows, groups = batch * share, k_all // K_STEP
    row, col = place_ref[0], place_ref[1]

    def fetch(group):
        slot = group % 2
        source = amp_ref.at[:, pl.ds(group * K_STEP, K_STEP)]
        return pltpu.make_async_copy(source, amp_buffer.at[slot], sems.at[slot])

    fetch(0).start()
    column = amplitude_rows(column_ref, row_ref, occ_ref, row, batch, share)
    mix_ref[...] = as_bf16(jnp.bitwise_xor(column, row_ref[...]))

    @pl.loop(0, groups)
    def _(group):
        slot = group % 2

        @pl.when(group + 1 < groups)
        def _():
            fetch(group + 1).start()

        fetch(group).wait()

        @pl.loop(0, K_STEP)
        def _(j):
            wanted = as_bf16(jnp.full((rows, share), occ_ref[col * k_all + group * K_STEP + j]))
            folded = None
            for n, s in enumerate(SLOTS):
                place = pl.ds(pl.multiple_of(jnp.bitwise_xor(row, s) * share, share), share)
                tile = amp_buffer[slot, :, j, :, place].reshape(rows, share)
                piece = jnp.where(mix_ref[:, place] == wanted, tile, jnp.zeros_like(tile))
                if n < NEAR:
                    lhs_ref[group, :, pl.ds(pl.multiple_of((n * K_STEP + j) * share, share), share)] = piece
                else:
                    far_ref[group, :, pl.ds(pl.multiple_of(j * share, share), share)] = piece
                folded = piece if folded is None else folded + piece
            fold_ref[group, :, pl.ds(pl.multiple_of(j * share, share), share)] = folded


def masked_amplitudes(amplitudes, occ_irrep, vir_irrep, place):
    batch, k_all, share, total = amplitudes.shape
    rows, groups = batch * share, k_all // K_STEP
    smem = pl.BlockSpec(memory_space=pltpu.SMEM)
    vmem = pl.BlockSpec(memory_space=pltpu.VMEM)
    hbm = pl.BlockSpec(memory_space=pltpu.HBM)
    widths = (NEAR * K_STEP * share, K_STEP * share, K_STEP * share)
    return pl.pallas_call(
        mask_kernel,
        in_specs=[smem, smem, hbm, vmem],
        out_specs=[vmem] * 3,
        out_shape=[jax.ShapeDtypeStruct((groups, rows, w), jnp.bfloat16) for w in widths],
        scratch_shapes=[
            pltpu.VMEM((rows, total), jnp.bfloat16),
            pltpu.VMEM((total, 8), jnp.int32),
            pltpu.VMEM((2, batch, K_STEP, share, total), jnp.bfloat16),
            pltpu.SemaphoreType.DMA((2,)),
        ],
        cost_estimate=cost(7),
        compiler_params=pltpu.CompilerParams(vmem_limit_bytes=28 * 1024 * 1024),
    )(occ_irrep, place, amplitudes, vir_irrep[None, :])


def make_first_kernel(few, n3, starts3):
    def kernel(pos3_ref, posx_ref, place_ref, lhs_ref, far_ref, *refs):
        narrow_refs = refs[:6]
        m3_refs = [refs[6 + 3 * n:9 + 3 * n] for n in range(n3)]
        narrow_sum, wide_sum, narrow_rhs, wide_rhs = refs[6 + 3 * n3:]
        row = place_ref[0]
        at_end = (row == 0) | (row == 3)
        groups, _, depth = lhs_ref.shape
        share = depth // (NEAR * K_STEP)
        half = share // 2
        lane = lax.broadcasted_iota(jnp.int32, (half, 2 * NARROW), 1)

        narrow_sum[...] = jnp.zeros(narrow_sum.shape, jnp.float32)
        wide_sum[...] = jnp.zeros(wide_sum.shape, jnp.float32)

        @pl.loop(0, groups)
        def _(group):
            @pl.loop(0, K_STEP)
            def _(j):
                k = group * K_STEP + j
                own, e1, o1 = [ref[k] for ref in narrow_refs[:3]]
                far = jnp.maximum(posx_ref[k], 0) if few else k
                e2, o2, e3 = [ref[far] for ref in narrow_refs[3:]]
                two = jnp.where(at_end, e2, o2)
                if few:
                    two, e3 = [jnp.where(posx_ref[k] >= 0, v, jnp.zeros_like(v)) for v in (two, e3)]
                for n, block in enumerate((own, e1, jnp.where(at_end, e3, o1), two)):
                    zero = jnp.zeros_like(block)
                    first = pl.multiple_of((n * K_STEP + j) * share, share)
                    narrow_rhs[pl.ds(first, half)] = jnp.where(lane < NARROW, block, zero)
                    narrow_rhs[pl.ds(first + half, half)] = jnp.where(lane < NARROW, zero, block)
                for n in range(3 if n3 else 0):
                    block = chosen(m3_refs, starts3, pos3_ref[k], lambda group, at, n=n: group[n][at])
                    if n == 2:
                        block = jnp.where(at_end, jnp.zeros_like(block), block)
                    wide_rhs[pl.ds(pl.multiple_of((n * K_STEP + j) * share, share), share)] = block

            narrow = jnp.dot(lhs_ref[group], narrow_rhs[:depth], preferred_element_type=jnp.float32)
            narrow += jnp.dot(far_ref[group], narrow_rhs[depth:], preferred_element_type=jnp.float32)
            narrow_sum[...] += narrow
            if n3:
                wide_sum[...] += jnp.dot(lhs_ref[group], wide_rhs[...], preferred_element_type=jnp.float32)

    return kernel


def first_product(lhs, far_lhs, pos3, posx, place, narrow, few, m3):
    groups, rows, depth = lhs.shape
    vmem = pl.BlockSpec(memory_space=pltpu.VMEM)
    smem = pl.BlockSpec(memory_space=pltpu.SMEM)
    arrays = list(narrow) + [v for group in m3 for v in group]
    wide = (rows, FOLD) if m3 else (16, FOLD)
    wide_depth = depth if m3 else 16
    return pl.pallas_call(
        make_first_kernel(few, len(m3), starts_of([v[0] for v in m3])),
        in_specs=[smem] * 3 + [vmem] * (2 + len(arrays)),
        out_specs=[vmem] * 2,
        out_shape=[jax.ShapeDtypeStruct(v, jnp.float32) for v in ((rows, 2 * NARROW), wide)],
        scratch_shapes=[
            pltpu.VMEM((depth // NEAR * len(SLOTS), 2 * NARROW), jnp.bfloat16),
            pltpu.VMEM((wide_depth, FOLD), jnp.bfloat16),
        ],
        cost_estimate=cost(9 if m3 else 6),
        compiler_params=pltpu.CompilerParams(vmem_limit_bytes=32 * 1024 * 1024),
    )(pos3, posx, place, lhs, far_lhs, *arrays)


def make_last_kernel(few, n2, starts2, n3, starts3):
    def kernel(occ_ref, vir_ref, pos2_ref, pos3_ref, place_ref, fold_ref, far_ref, row_ref, narrow_ref, wide_ref, *refs):
        m2_refs = refs[:n2]
        m3_refs = [refs[n2 + 2 * n:n2 + 2 * n + 2] for n in range(n3)]
        refs = refs[n2 + 2 * n3:]
        outs = refs[:4]
        column_ref, total_ref, short_rhs, far_rhs = refs[4:]
        row, col = place_ref[0], place_ref[1]
        at_end = (row == 0) | (row == 3)
        groups, rows, width = fold_ref.shape
        share = width // K_STEP
        batch = rows // share
        @pl.loop(0, groups * K_STEP)
        def _(k):
            here = pl.ds(pl.multiple_of(k * share, share), share)
            if few:
                pos2 = pos2_ref[k]
                at = 2 * jnp.maximum(pos2, 0)
                pieces = []
                for piece in range(2):
                    close = groups * K_STEP + at + piece
                    own, e1, o1 = [ref[close] for ref in m2_refs[:3]]
                    two, three = [ref[FEW_SHORT + at + piece] for ref in m2_refs[3:]]
                    block = own + e1 + two + jnp.where(at_end, three, o1)
                    pieces.append(jnp.where(pos2 >= 0, block, jnp.zeros_like(block)))
                short = jnp.concatenate(pieces, axis=1)
            else:
                short = chosen(m2_refs, starts2, pos2_ref[k], lambda ref, at: ref[at])
            short_rhs[here] = jnp.concatenate([short, short], axis=0)
            if n3:
                far_rhs[here] = chosen(
                    m3_refs, starts3, pos3_ref[k], lambda pair, at: jnp.where(at_end, pair[0][at], pair[1][at])
                )

        column = amplitude_rows(column_ref, row_ref, occ_ref, row, batch, share)
        target = jnp.bitwise_xor(column, occ_ref[batch])
        both = narrow_ref[...]
        both = both + pltpu.roll(both, NARROW, 1)
        both = jnp.concatenate([both] * (FOLD // (2 * NARROW)), axis=1)
        part = wide_ref[...] if n3 else 0.0
        for group in range(groups):
            here = pl.ds(group * width, width)
            part += jnp.dot(fold_ref[group], short_rhs[here], preferred_element_type=jnp.float32)
            if n3:
                part += jnp.dot(far_ref[group], far_rhs[here], preferred_element_type=jnp.float32)
        total_ref[...] = jnp.where(target == largest_irrep(vir_ref), part, both)
        write_quarters(total_ref, col, outs)

    return kernel


def last_product(far_lhs, fold, occ_irrep, vir_irrep, pos2, pos3, place, narrow_sum, wide_sum, few, m2, m3, batch):
    groups, rows, width = fold.shape
    share = rows // batch
    vmem = pl.BlockSpec(memory_space=pltpu.VMEM)
    smem = pl.BlockSpec(memory_space=pltpu.SMEM)
    arrays = [narrow_sum, wide_sum] + list(m2) + [v for group in m3 for v in group]
    quarter = (batch // 2, share, FOLD // 2)
    whole = groups * width
    far_lhs = far_lhs if m3 else jnp.zeros((8, 128), jnp.bfloat16)
    return pl.pallas_call(
        make_last_kernel(few, len(m2), starts_of(m2), len(m3), starts_of([v[0] for v in m3])),
        in_specs=[smem] * 5 + [vmem] * (3 + len(arrays)),
        out_specs=[vmem] * 4,
        out_shape=[jax.ShapeDtypeStruct(quarter, jnp.float32)] * 4,
        scratch_shapes=[
            pltpu.VMEM((vir_irrep.shape[0], 8), jnp.int32),
            pltpu.VMEM((rows, FOLD), jnp.float32),
            pltpu.VMEM((whole, FOLD), jnp.bfloat16),
            pltpu.VMEM((whole if m3 else 16, FOLD), jnp.bfloat16),
        ],
        cost_estimate=cost(4 if m3 else 2),
        compiler_params=pltpu.CompilerParams(vmem_limit_bytes=32 * 1024 * 1024),
    )(occ_irrep, vir_irrep, pos2, pos3, place, fold, far_lhs, vir_irrep[None, :], *arrays)


def dense_product(amplitudes, whole, occ_irrep, occ_local, vir_local, vir_irrep):
    batch = amplitudes.shape[0]
    keep = (
        jnp.bitwise_xor(occ_irrep[:batch, None], occ_local[None, :])[:, :, None, None]
        == jnp.bitwise_xor(vir_local[:, None], vir_irrep[None, :])[None, None]
    )
    kept = jnp.where(keep, amplitudes, jnp.zeros_like(amplitudes))
    return lax.dot_general(
        kept, whole, (((1, 3), (0, 1)), ((), ())), preferred_element_type=jnp.float32
    )


def finish(cycle, occ_irrep, vir_irrep, occ_energy, vir_energy, a_start, a_size, b_start, b_size, batch):
    label_a = lax.dynamic_slice_in_dim(vir_irrep, a_start, a_size)
    label_b = lax.dynamic_slice_in_dim(vir_irrep, b_start, b_size)
    energy_a = lax.dynamic_slice_in_dim(vir_energy, a_start, a_size)
    energy_b = lax.dynamic_slice_in_dim(vir_energy, b_start, b_size)
    target = jnp.bitwise_xor(
        jnp.bitwise_xor(occ_irrep[:batch, None], occ_irrep[batch]), label_a[None, :]
    )
    keep = label_b[:, None, None] == target[None, :, :]
    denominator = (
        occ_energy[:batch][None, :, None]
        + occ_energy[batch]
        - energy_a[None, None, :]
        - energy_b[:, None, None]
    )
    swapped = jnp.transpose(cycle, (2, 0, 1))
    return jnp.where(keep, swapped, 0.0) / denominator


def on_square(amplitudes, integrals, occ_irrep, vir_irrep, screen):
    batch, occ_share, share, vir_total = amplitudes.shape
    row = lax.axis_index("row")
    col = lax.axis_index("col")
    place = jnp.stack([row, col]).astype(jnp.int32)
    m2a, m2b, m3a, m3b, pos2, pos3, posx, form = wide_blocks(
        integrals, occ_irrep, vir_irrep, screen, place, batch
    )
    outer = [(0, 1), (1, 0), (2, 3), (3, 2)]
    inner = [(1, 2), (2, 1)]
    inward = [(0, 1), (3, 2)]
    outward = [(1, 0), (2, 3)]
    ends = [(0, 3), (3, 0)]
    second = [(r, r ^ 2) for r in range(4)]

    def move(v, pairs):
        return lax.ppermute(v, "row", pairs)

    def sparse(use_few, choose):
        def run(m2a, m2b, m3a, m3b):
            shorts, wides = choose(m2a, m2b, m3a, m3b)
            near = [(own, move(own, outer), move(own, inner)) for own in wides]
            if use_few:
                narrow, few = narrow_blocks(integrals, occ_irrep, vir_irrep, screen, place, posx, m2a, batch)
                e1, o1 = move(narrow, outer), move(narrow, inner)
                lhs, far_lhs, fold = masked_amplitudes(amplitudes, occ_irrep, vir_irrep, place)
                near, e1, o1, _ = lax.optimization_barrier((near, e1, o1, fold))
                two, three = move(few, second), move(few, ends)
                blocks = (narrow, e1, o1, two, two, three)
                sums = (narrow, e1, o1, two, three)
            else:
                h1 = [move(v, inward) for v in shorts]
                (narrow,) = narrow_blocks(integrals, occ_irrep, vir_irrep, screen, place, posx, None, batch)
                o1, e1 = move(narrow, inner), move(narrow, outward)
                lhs, far_lhs, fold = masked_amplitudes(amplitudes, occ_irrep, vir_irrep, place)
                near, h1, o1, e1, _ = lax.optimization_barrier((near, h1, o1, e1, fold))
                h2 = [move(own + v, inner) for own, v in zip(shorts, h1)]
                e1 = e1 + move(narrow, inward)
                e2 = move(o1, outward)
                h2, e1, e2 = lax.optimization_barrier((h2, e1, e2))
                h3 = [move(own + v, outward) for own, v in zip(shorts, h2)]
                o2 = move(e1, inner)
                blocks = (narrow, e1, o1, e2, o2, move(o2, outward))
                sums = [a + b + c + d for a, b, c, d in zip(shorts, h1, h2, h3)]
            far = [(move(o, outward), move(e, inner)) for _, e, o in near]
            narrow_sum, wide_sum = first_product(
                lhs, far_lhs, pos3, posx, place, blocks, use_few, near
            )
            return list(last_product(
                far_lhs, fold, occ_irrep, vir_irrep, pos2, pos3, place, narrow_sum, wide_sum, use_few, sums, far,
                batch
            ))

        return run

    def dense(*_):
        occ_local = lax.dynamic_slice_in_dim(occ_irrep, col * occ_share, occ_share)
        vir_local = lax.dynamic_slice_in_dim(vir_irrep, row * share, share)
        screen_rows = lax.dynamic_slice_in_dim(screen, col * occ_share, occ_share, 0)
        fold = folded_integrals(
            integrals, occ_local, vir_local, vir_irrep, occ_irrep[batch], screen_rows
        )
        whole = jnp.zeros((occ_share, vir_total, FOLD), fold.dtype)
        for s in range(4):
            block = move(fold, [(r, r ^ s) for r in range(4)]) if s else fold
            whole = lax.dynamic_update_slice_in_dim(whole, block, jnp.bitwise_xor(row, s) * share, 1)
        total = dense_product(amplitudes, whole, occ_irrep, occ_local, vir_local, vir_irrep)
        quarter = (batch // 2, share, FOLD // 2)
        goals = [jnp.bitwise_xor(col, t) for t in range(4)]
        return [
            lax.dynamic_slice(total, (g // 2 * quarter[0], 0, g % 2 * quarter[2]), quarter) for g in goals
        ]

    branches = [
        sparse(False, lambda m2a, m2b, m3a, m3b: ([m2a], [])),
        sparse(False, lambda m2a, m2b, m3a, m3b: ([m2a], [m3a[:FEW_WIDE]])),
        sparse(True, lambda m2a, m2b, m3a, m3b: ([], [m3a])),
        sparse(False, lambda m2a, m2b, m3a, m3b: ([m2a, m2b], [m3a, m3b])),
        dense,
    ]
    quarters = lax.switch(form[0], branches, m2a, m2b, m3a, m3b)
    mine = quarters[0]
    for t in (1, 2, 3):
        mine = mine + lax.ppermute(quarters[t], "col", [(q, q ^ t) for q in range(4)])
    places = [(r, q) for r in range(4) for q in range(4)]
    same = lax.ppermute(mine, ("row", "col"), [(r * 4 + q, q * 4 + r) for r, q in places])
    other = lax.ppermute(mine, ("row", "col"), [(r * 4 + q, (q ^ 2) * 4 + r) for r, q in places])
    upper = row // 2 == 1
    low = jnp.where(upper, other, same)
    high = jnp.where(upper, same, other)
    return jnp.concatenate([low, high], axis=0)


def on_any(amplitudes, integrals, occ_irrep, vir_irrep, screen):
    batch, occ_share, share, vir_total = amplitudes.shape
    row = lax.axis_index("row")
    col = lax.axis_index("col")
    occ_local = lax.dynamic_slice_in_dim(occ_irrep, col * occ_share, occ_share)
    vir_local = lax.dynamic_slice_in_dim(vir_irrep, row * share, share)
    screen_rows = lax.dynamic_slice_in_dim(screen, col * occ_share, occ_share, 0)
    fold = folded_integrals(
        integrals, occ_local, vir_local, vir_irrep, occ_irrep[batch], screen_rows
    )
    whole = lax.all_gather(fold, "row", axis=1, tiled=True)
    cycle = dense_product(amplitudes, whole, occ_irrep, occ_local, vir_local, vir_irrep)
    cycle = lax.psum(cycle, "col")
    cycle = jnp.concatenate([cycle] * (vir_total // FOLD), axis=2)
    cycle = lax.all_to_all(cycle, "row", split_axis=2, concat_axis=1, tiled=True)
    a_size = vir_total // lax.axis_size("col")
    return lax.dynamic_slice_in_dim(cycle, col * a_size, a_size, 1)


def on_device(amplitudes, integrals, occ_irrep, vir_irrep, screen, occ_energy, vir_energy):
    batch, _, vir_share, vir_total = amplitudes.shape
    square = lax.axis_size("row") == 4 and lax.axis_size("col") == 4
    form = on_square if square else on_any
    cycle = form(amplitudes, integrals, occ_irrep, vir_irrep, screen)
    a_size = vir_total // lax.axis_size("col")
    return finish(
        cycle, occ_irrep, vir_irrep, occ_energy, vir_energy,
        lax.axis_index("col") * a_size, a_size, lax.axis_index("row") * vir_share, vir_share, batch,
    )


def solution(mesh):
    in_specs = (
        P("parts", "col", "row", None),
        P(("parts", "col"), "row", None),
        P("parts"),
        P("parts"),
        P("parts", None),
        P("parts"),
        P("parts"),
    )
    out_specs = P("row", "parts", "col")
    return jax.shard_map(
        on_device, mesh=mesh, in_specs=in_specs, out_specs=out_specs, check_vma=False
    )
```

```python
import jax
import jax.numpy as jnp
from jax import lax
from jax.experimental import pallas as pl
from jax.experimental.pallas import tpu as pltpu
from jax.sharding import PartitionSpec as P

FOLD = 256
K_STEP = 5


def folded_integrals(integrals, occ_local, vir_local, vir_irrep, pair_label, screen_rows):
    irrep_codes = jnp.arange(8, dtype=jnp.int32)
    screen_local = jnp.sum(
        screen_rows[:, None, :] * (vir_local[None, :, None] == irrep_codes).astype(jnp.int32),
        axis=2,
    )
    target = jnp.bitwise_xor(
        jnp.bitwise_xor(occ_local[:, None], vir_local[None, :]), pair_label
    )
    target = jnp.where(screen_local == 1, target, -1)
    keep = target[:, :, None] == vir_irrep[None, None, :]
    kept = jnp.where(keep, integrals, jnp.zeros_like(integrals))
    return kept[:, :, :FOLD] + kept[:, :, FOLD:]


NARROW = 64
CAPS = (22, 3)
FEW_SHORT = 8
FEW_WIDE = 5


def largest_irrep(vir_ref):
    return jnp.where(vir_ref[0] == vir_ref[FOLD - 1], vir_ref[0], vir_ref[FOLD])


def label_columns(row_labels):
    return jnp.transpose(jnp.broadcast_to(row_labels, (8, row_labels.shape[1])))


def as_bf16(labels):
    return labels.astype(jnp.float32).astype(jnp.bfloat16)


def label_mix(mix_ref, column_ref, row_ref, row, big, keep_big):
    depth = mix_ref.shape[0]
    column_ref[...] = label_columns(row_ref[...])
    column = column_ref[pl.ds(pl.multiple_of(row * depth, depth), depth), :1]
    is_big = row_ref[...] == big
    wanted = is_big if keep_big else jnp.logical_not(is_big)
    mix_ref[...] = as_bf16(jnp.where(wanted, jnp.bitwise_xor(column, row_ref[...]), 8))


def kept_folded(int_ref, mix_ref, j, x):
    tile = int_ref[j]
    wanted = as_bf16(jnp.full(mix_ref.shape, x))
    kept = jnp.where(mix_ref[...] == wanted, tile, jnp.zeros_like(tile))
    return kept[:, :FOLD] + kept[:, FOLD:]


def wide_kernel(
    occ_ref, vir_ref, screen_ref, place_ref, int_ref, row_ref,
    m2a_ref, m2b_ref, m3a_ref, m3b_ref, pos2_ref, pos3_ref, posx_ref, form_ref,
    mix_ref, column_ref, counts_ref, batch,
):
    step = pl.program_id(0)
    k_step, depth, total = int_ref.shape
    half = depth // 2
    row, col = place_ref[0], place_ref[1]
    pair_label = occ_ref[batch]
    big = largest_irrep(vir_ref)

    @pl.when(step == 0)
    def _():
        for n in range(3):
            counts_ref[n] = 0
        label_mix(mix_ref, column_ref, row_ref, row, big, True)

    @pl.loop(0, k_step)
    def _(j):
        k = step * k_step + j
        k_whole = col * (k_step * pl.num_programs(0)) + k
        x = jnp.bitwise_xor(occ_ref[k_whole], pair_label)
        on_big = screen_ref[jnp.bitwise_xor(big, x), k_whole] == 1
        actives = (on_big & (x != 0), on_big & (x == 0), x != 0)
        pos2, pos3, posx = [jnp.where(active, counts_ref[n], -1) for n, active in enumerate(actives)]
        for n, active in enumerate(actives):
            counts_ref[n] = counts_ref[n] + active.astype(jnp.int32)
        pos2_ref[k], pos3_ref[k], posx_ref[k] = pos2, pos3, posx

        @pl.when(pos2 >= 0)
        def _():
            wide = kept_folded(int_ref, mix_ref, j, x)
            short = wide[:half] + wide[half:]

            @pl.when(pos2 < CAPS[0])
            def _():
                m2a_ref[pos2] = short

            @pl.when(pos2 >= CAPS[0])
            def _():
                m2b_ref[pos2 - CAPS[0]] = short

        @pl.when(pos3 >= 0)
        def _():
            wide = kept_folded(int_ref, mix_ref, j, x)

            @pl.when(pos3 < CAPS[0])
            def _():
                m3a_ref[pos3] = wide

            @pl.when(pos3 >= CAPS[0])
            def _():
                m3b_ref[pos3 - CAPS[0]] = wide

    @pl.when(step == pl.num_programs(0) - 1)
    def _():
        labels = row_ref[...]
        lanes = lax.broadcasted_iota(jnp.int32, labels.shape, 1)
        ahead = pltpu.roll(labels, total - NARROW, 1)
        long = (labels == ahead) & (lanes < total - NARROW) & (labels != big)
        too_long = jnp.max(long.astype(jnp.int32)) == 1
        n2, n3, nx = counts_ref[0], counts_ref[1], counts_ref[2]
        one_label = occ_ref[0] == pair_label
        form = jnp.where(nx <= FEW_SHORT, jnp.where(n3 <= CAPS[0], 3, 4), 5)
        form = jnp.where((n3 <= FEW_WIDE) & (n2 <= CAPS[0]), 2, form)
        form = jnp.where(one_label, form, 6)
        form = jnp.where(n3 == 0, jnp.where(n2 <= CAPS[0], 0, 1), form)
        form_ref[0] = jnp.where(too_long, 6, form)


def wide_blocks(integrals, occ_irrep, vir_irrep, screen, place, batch):
    occ_share, depth, total = integrals.shape
    shapes = [(n, depth // 2, FOLD) for n in CAPS] + [(n, depth, FOLD) for n in CAPS]
    smem = pl.BlockSpec(memory_space=pltpu.SMEM)

    def kernel(*refs):
        wide_kernel(*refs, batch)

    return pl.pallas_call(
        kernel,
        grid_spec=pltpu.PrefetchScalarGridSpec(
            num_scalar_prefetch=4,
            grid=(occ_share // K_STEP,),
            in_specs=[
                pl.BlockSpec((K_STEP, depth, total), lambda k, *_: (k, 0, 0)),
                pl.BlockSpec((1, total), lambda k, *_: (0, 0)),
            ],
            out_specs=[pl.BlockSpec(v, lambda k, *_: (0, 0, 0)) for v in shapes] + [smem] * 4,
            scratch_shapes=[
                pltpu.VMEM((depth, total), jnp.bfloat16),
                pltpu.VMEM((total, 8), jnp.int32),
                pltpu.SMEM((3,), jnp.int32),
            ],
        ),
        out_shape=[jax.ShapeDtypeStruct(v, jnp.bfloat16) for v in shapes]
        + [jax.ShapeDtypeStruct((n,), jnp.int32) for n in (occ_share, occ_share, occ_share, 1)],
        cost_estimate=cost(5),
        compiler_params=pltpu.CompilerParams(vmem_limit_bytes=24 * 1024 * 1024),
    )(occ_irrep, vir_irrep, screen.T, place, integrals, vir_irrep[None, :])


def narrow_kernel(
    occ_ref, vir_ref, screen_ref, place_ref, posx_ref, int_ref, row_ref, short_ref, narrow_ref, few_ref,
    mix_ref, column_ref, batch,
):
    step = pl.program_id(0)
    k_step, depth, total = int_ref.shape
    half = depth // 2
    row, col = place_ref[0], place_ref[1]

    @pl.when(step == 0)
    def _():
        label_mix(mix_ref, column_ref, row_ref, row, largest_irrep(vir_ref), False)
        if few_ref is not None:
            for n in range(FEW_SHORT):
                for piece in range(2):
                    block = short_ref[n, :, piece * 2 * NARROW:(piece + 1) * 2 * NARROW]
                    narrow_ref[k_step * pl.num_programs(0) + 2 * n + piece] = block
                    few_ref[FEW_SHORT + 2 * n + piece] = block

    lane = lax.broadcasted_iota(jnp.int32, (half, 2 * NARROW), 1)
    local = column_ref[pl.ds(pl.multiple_of(row * depth, depth), depth), :1]
    for j in range(k_step):
        k = step * k_step + j
        k_whole = col * (k_step * pl.num_programs(0)) + k
        x = jnp.bitwise_xor(occ_ref[k_whole], occ_ref[batch])
        bits = screen_ref[0, k_whole]
        for g in range(1, 8):
            bits = bits + screen_ref[g, k_whole] * (1 << g)
        narrow = kept_folded(int_ref, mix_ref, j, x)
        narrow = (narrow[:, : 2 * NARROW] + narrow[:, 2 * NARROW:]).astype(jnp.float32)
        narrow = narrow + pltpu.roll(narrow, NARROW, 1)
        on = jnp.bitwise_and(lax.shift_right_logical(jnp.full(local.shape, bits), local), 1) == 1
        narrow = jnp.where(on, narrow, 0.0)
        narrow = jnp.where(lane < NARROW, narrow[:half], narrow[half:]).astype(jnp.bfloat16)
        narrow_ref[k] = narrow
        if few_ref is not None:
            posx = posx_ref[k]

            @pl.when((posx >= 0) & (posx < FEW_SHORT))
            def _(narrow=narrow, posx=posx):
                few_ref[posx] = narrow


def narrow_blocks(integrals, occ_irrep, vir_irrep, screen, place, posx, short, batch):
    occ_share, depth, total = integrals.shape
    few = short is not None
    counts = (occ_share + 2 * FEW_SHORT, 3 * FEW_SHORT) if few else (occ_share,)
    shapes = [(n, depth // 2, 2 * NARROW) for n in counts]
    fixed = lambda k, *_: (0, 0, 0)

    def kernel(*refs):
        if few:
            narrow_kernel(*refs, batch)
        else:
            narrow_kernel(*refs[:7], None, refs[7], None, *refs[8:], batch)

    return pl.pallas_call(
        kernel,
        grid_spec=pltpu.PrefetchScalarGridSpec(
            num_scalar_prefetch=5,
            grid=(occ_share // K_STEP,),
            in_specs=[
                pl.BlockSpec((K_STEP, depth, total), lambda k, *_: (k, 0, 0)),
                pl.BlockSpec((1, total), lambda k, *_: (0, 0)),
            ] + ([pl.BlockSpec((FEW_SHORT, depth // 2, FOLD), fixed)] if few else []),
            out_specs=[pl.BlockSpec(v, fixed) for v in shapes],
            scratch_shapes=[pltpu.VMEM((depth, total), jnp.bfloat16), pltpu.VMEM((total, 8), jnp.int32)],
        ),
        out_shape=[jax.ShapeDtypeStruct(v, jnp.bfloat16) for v in shapes],
        cost_estimate=cost(5),
        compiler_params=pltpu.CompilerParams(vmem_limit_bytes=16 * 1024 * 1024),
    )(occ_irrep, vir_irrep, screen.T, place, posx, integrals, vir_irrep[None, :], *([short] if few else []))


def cost(micros):
    return pl.CostEstimate(flops=int(micros * 1e9), bytes_accessed=int(micros * 3e6), transcendentals=0)


SLOTS = (0, 1, 3, 2)
NEAR = 3


def amplitude_rows(column_ref, row_ref, occ_ref, row, batch, share):
    column_ref[...] = label_columns(row_ref[...])
    column = column_ref[pl.ds(pl.multiple_of(row * share, share), share), :1]
    return jnp.concatenate([jnp.bitwise_xor(column, occ_ref[i]) for i in range(batch)], axis=0)


def write_quarters(total_ref, col, outs):
    rows, fold = total_ref.shape
    width, height = fold // 2, rows // 2
    for t, out_ref in enumerate(outs):
        goal = jnp.bitwise_xor(col, t)
        lanes = pl.ds(pl.multiple_of((goal % 2) * width, width), width)
        lines = pl.ds(pl.multiple_of((goal // 2) * height, height), height)
        out_ref[...] = total_ref[lines, lanes].reshape(out_ref.shape)


def chosen(refs, starts, pos, pick):
    block = None
    for n, group in enumerate(refs):
        inside = (pos >= starts[n]) & (pos < starts[n + 1])
        at = jnp.clip(pos - starts[n], 0, starts[n + 1] - starts[n] - 1)
        found = pick(group, at)
        found = jnp.where(inside, found, jnp.zeros_like(found))
        block = found if block is None else block + found
    return block


def starts_of(arrays):
    starts = [0]
    for v in arrays:
        starts.append(starts[-1] + v.shape[0])
    return starts


def mask_kernel(occ_ref, place_ref, amp_ref, row_ref, lhs_ref, far_ref, fold_ref, mix_ref, column_ref, amp_buffer, sems):
    batch, k_all, share, total = amp_ref.shape
    rows, groups = batch * share, k_all // K_STEP
    row, col = place_ref[0], place_ref[1]

    def fetch(group):
        slot = group % 2
        source = amp_ref.at[:, pl.ds(group * K_STEP, K_STEP)]
        return pltpu.make_async_copy(source, amp_buffer.at[slot], sems.at[slot])

    fetch(0).start()
    column = amplitude_rows(column_ref, row_ref, occ_ref, row, batch, share)
    mix_ref[...] = as_bf16(jnp.bitwise_xor(column, row_ref[...]))

    @pl.loop(0, groups)
    def _(group):
        slot = group % 2

        @pl.when(group + 1 < groups)
        def _():
            fetch(group + 1).start()

        fetch(group).wait()

        @pl.loop(0, K_STEP)
        def _(j):
            wanted = as_bf16(jnp.full((rows, share), occ_ref[col * k_all + group * K_STEP + j]))
            folded = None
            for n, s in enumerate(SLOTS):
                place = pl.ds(pl.multiple_of(jnp.bitwise_xor(row, s) * share, share), share)
                tile = amp_buffer[slot, :, j, :, place].reshape(rows, share)
                piece = jnp.where(mix_ref[:, place] == wanted, tile, jnp.zeros_like(tile))
                if n < NEAR:
                    lhs_ref[group, :, pl.ds(pl.multiple_of((n * K_STEP + j) * share, share), share)] = piece
                else:
                    far_ref[group, :, pl.ds(pl.multiple_of(j * share, share), share)] = piece
                folded = piece if folded is None else folded + piece
            fold_ref[group, :, pl.ds(pl.multiple_of(j * share, share), share)] = folded


def masked_amplitudes(amplitudes, occ_irrep, vir_irrep, place):
    batch, k_all, share, total = amplitudes.shape
    rows, groups = batch * share, k_all // K_STEP
    smem = pl.BlockSpec(memory_space=pltpu.SMEM)
    vmem = pl.BlockSpec(memory_space=pltpu.VMEM)
    hbm = pl.BlockSpec(memory_space=pltpu.HBM)
    widths = (NEAR * K_STEP * share, K_STEP * share, K_STEP * share)
    return pl.pallas_call(
        mask_kernel,
        in_specs=[smem, smem, hbm, vmem],
        out_specs=[vmem] * 3,
        out_shape=[jax.ShapeDtypeStruct((groups, rows, w), jnp.bfloat16) for w in widths],
        scratch_shapes=[
            pltpu.VMEM((rows, total), jnp.bfloat16),
            pltpu.VMEM((total, 8), jnp.int32),
            pltpu.VMEM((2, batch, K_STEP, share, total), jnp.bfloat16),
            pltpu.SemaphoreType.DMA((2,)),
        ],
        cost_estimate=cost(7),
        compiler_params=pltpu.CompilerParams(vmem_limit_bytes=28 * 1024 * 1024),
    )(occ_irrep, place, amplitudes, vir_irrep[None, :])


def make_first_kernel(few, n3, starts3):
    def kernel(pos3_ref, posx_ref, place_ref, lhs_ref, far_ref, *refs):
        narrow_refs = refs[:6]
        m3_refs = [refs[6 + 3 * n:9 + 3 * n] for n in range(n3)]
        narrow_sum, wide_sum, narrow_rhs, wide_rhs = refs[6 + 3 * n3:]
        row = place_ref[0]
        at_end = (row == 0) | (row == 3)
        groups, _, depth = lhs_ref.shape
        share = depth // (NEAR * K_STEP)
        half = share // 2
        lane = lax.broadcasted_iota(jnp.int32, (half, 2 * NARROW), 1)

        narrow_sum[...] = jnp.zeros(narrow_sum.shape, jnp.float32)
        wide_sum[...] = jnp.zeros(wide_sum.shape, jnp.float32)

        @pl.loop(0, groups)
        def _(group):
            @pl.loop(0, K_STEP)
            def _(j):
                k = group * K_STEP + j
                own, e1, o1 = [ref[k] for ref in narrow_refs[:3]]
                far = jnp.maximum(posx_ref[k], 0) if few else k
                e2, o2, e3 = [ref[far] for ref in narrow_refs[3:]]
                two = jnp.where(at_end, e2, o2)
                if few:
                    two, e3 = [jnp.where(posx_ref[k] >= 0, v, jnp.zeros_like(v)) for v in (two, e3)]
                for n, block in enumerate((own, e1, jnp.where(at_end, e3, o1), two)):
                    zero = jnp.zeros_like(block)
                    first = pl.multiple_of((n * K_STEP + j) * share, share)
                    narrow_rhs[pl.ds(first, half)] = jnp.where(lane < NARROW, block, zero)
                    narrow_rhs[pl.ds(first + half, half)] = jnp.where(lane < NARROW, zero, block)
                for n in range(3 if n3 else 0):
                    block = chosen(m3_refs, starts3, pos3_ref[k], lambda group, at, n=n: group[n][at])
                    if n == 2:
                        block = jnp.where(at_end, jnp.zeros_like(block), block)
                    wide_rhs[pl.ds(pl.multiple_of((n * K_STEP + j) * share, share), share)] = block

            narrow = jnp.dot(lhs_ref[group], narrow_rhs[:depth], preferred_element_type=jnp.float32)
            narrow += jnp.dot(far_ref[group], narrow_rhs[depth:], preferred_element_type=jnp.float32)
            narrow_sum[...] += narrow
            if n3:
                wide_sum[...] += jnp.dot(lhs_ref[group], wide_rhs[...], preferred_element_type=jnp.float32)

    return kernel


def first_product(lhs, far_lhs, pos3, posx, place, narrow, few, m3):
    groups, rows, depth = lhs.shape
    vmem = pl.BlockSpec(memory_space=pltpu.VMEM)
    smem = pl.BlockSpec(memory_space=pltpu.SMEM)
    arrays = list(narrow) + [v for group in m3 for v in group]
    wide = (rows, FOLD) if m3 else (16, FOLD)
    wide_depth = depth if m3 else 16
    return pl.pallas_call(
        make_first_kernel(few, len(m3), starts_of([v[0] for v in m3])),
        in_specs=[smem] * 3 + [vmem] * (2 + len(arrays)),
        out_specs=[vmem] * 2,
        out_shape=[jax.ShapeDtypeStruct(v, jnp.float32) for v in ((rows, 2 * NARROW), wide)],
        scratch_shapes=[
            pltpu.VMEM((depth // NEAR * len(SLOTS), 2 * NARROW), jnp.bfloat16),
            pltpu.VMEM((wide_depth, FOLD), jnp.bfloat16),
        ],
        cost_estimate=cost(9 if m3 else 6),
        compiler_params=pltpu.CompilerParams(vmem_limit_bytes=32 * 1024 * 1024),
    )(pos3, posx, place, lhs, far_lhs, *arrays)


def make_last_kernel(few, n2, starts2, n3, starts3):
    def kernel(occ_ref, vir_ref, pos2_ref, pos3_ref, place_ref, fold_ref, far_ref, row_ref, narrow_ref, wide_ref, *refs):
        m2_refs = refs[:n2]
        m3_refs = [refs[n2 + 2 * n:n2 + 2 * n + 2] for n in range(n3)]
        refs = refs[n2 + 2 * n3:]
        outs = refs[:4]
        column_ref, total_ref, short_rhs, far_rhs = refs[4:]
        row, col = place_ref[0], place_ref[1]
        at_end = (row == 0) | (row == 3)
        groups, rows, width = fold_ref.shape
        share = width // K_STEP
        batch = rows // share
        @pl.loop(0, groups * K_STEP)
        def _(k):
            here = pl.ds(pl.multiple_of(k * share, share), share)
            if few:
                pos2 = pos2_ref[k]
                at = 2 * jnp.maximum(pos2, 0)
                pieces = []
                for piece in range(2):
                    close = groups * K_STEP + at + piece
                    own, e1, o1 = [ref[close] for ref in m2_refs[:3]]
                    two, three = [ref[FEW_SHORT + at + piece] for ref in m2_refs[3:]]
                    block = own + e1 + two + jnp.where(at_end, three, o1)
                    pieces.append(jnp.where(pos2 >= 0, block, jnp.zeros_like(block)))
                short = jnp.concatenate(pieces, axis=1)
            else:
                short = chosen(m2_refs, starts2, pos2_ref[k], lambda ref, at: ref[at])
            short_rhs[here] = jnp.concatenate([short, short], axis=0)
            if n3:
                far_rhs[here] = chosen(
                    m3_refs, starts3, pos3_ref[k], lambda pair, at: jnp.where(at_end, pair[0][at], pair[1][at])
                )

        column = amplitude_rows(column_ref, row_ref, occ_ref, row, batch, share)
        target = jnp.bitwise_xor(column, occ_ref[batch])
        both = narrow_ref[...]
        both = both + pltpu.roll(both, NARROW, 1)
        both = jnp.concatenate([both] * (FOLD // (2 * NARROW)), axis=1)
        part = wide_ref[...] if n3 else 0.0
        for group in range(groups):
            here = pl.ds(group * width, width)
            part += jnp.dot(fold_ref[group], short_rhs[here], preferred_element_type=jnp.float32)
            if n3:
                part += jnp.dot(far_ref[group], far_rhs[here], preferred_element_type=jnp.float32)
        total_ref[...] = jnp.where(target == largest_irrep(vir_ref), part, both)
        write_quarters(total_ref, col, outs)

    return kernel


def last_product(far_lhs, fold, occ_irrep, vir_irrep, pos2, pos3, place, narrow_sum, wide_sum, few, m2, m3, batch):
    groups, rows, width = fold.shape
    share = rows // batch
    vmem = pl.BlockSpec(memory_space=pltpu.VMEM)
    smem = pl.BlockSpec(memory_space=pltpu.SMEM)
    arrays = [narrow_sum, wide_sum] + list(m2) + [v for group in m3 for v in group]
    quarter = (batch // 2, share, FOLD // 2)
    whole = groups * width
    far_lhs = far_lhs if m3 else jnp.zeros((8, 128), jnp.bfloat16)
    return pl.pallas_call(
        make_last_kernel(few, len(m2), starts_of(m2), len(m3), starts_of([v[0] for v in m3])),
        in_specs=[smem] * 5 + [vmem] * (3 + len(arrays)),
        out_specs=[vmem] * 4,
        out_shape=[jax.ShapeDtypeStruct(quarter, jnp.float32)] * 4,
        scratch_shapes=[
            pltpu.VMEM((vir_irrep.shape[0], 8), jnp.int32),
            pltpu.VMEM((rows, FOLD), jnp.float32),
            pltpu.VMEM((whole, FOLD), jnp.bfloat16),
            pltpu.VMEM((whole if m3 else 16, FOLD), jnp.bfloat16),
        ],
        cost_estimate=cost(4 if m3 else 2),
        compiler_params=pltpu.CompilerParams(vmem_limit_bytes=32 * 1024 * 1024),
    )(occ_irrep, vir_irrep, pos2, pos3, place, fold, far_lhs, vir_irrep[None, :], *arrays)


def dense_product(amplitudes, whole, occ_irrep, occ_local, vir_local, vir_irrep):
    batch = amplitudes.shape[0]
    keep = (
        jnp.bitwise_xor(occ_irrep[:batch, None], occ_local[None, :])[:, :, None, None]
        == jnp.bitwise_xor(vir_local[:, None], vir_irrep[None, :])[None, None]
    )
    kept = jnp.where(keep, amplitudes, jnp.zeros_like(amplitudes))
    return lax.dot_general(
        kept, whole, (((1, 3), (0, 1)), ((), ())), preferred_element_type=jnp.float32
    )


def finish(cycle, occ_irrep, vir_irrep, occ_energy, vir_energy, a_start, a_size, b_start, b_size, batch):
    label_a = lax.dynamic_slice_in_dim(vir_irrep, a_start, a_size)
    label_b = lax.dynamic_slice_in_dim(vir_irrep, b_start, b_size)
    energy_a = lax.dynamic_slice_in_dim(vir_energy, a_start, a_size)
    energy_b = lax.dynamic_slice_in_dim(vir_energy, b_start, b_size)
    target = jnp.bitwise_xor(
        jnp.bitwise_xor(occ_irrep[:batch, None], occ_irrep[batch]), label_a[None, :]
    )
    keep = label_b[:, None, None] == target[None, :, :]
    denominator = (
        occ_energy[:batch][None, :, None]
        + occ_energy[batch]
        - energy_a[None, None, :]
        - energy_b[:, None, None]
    )
    swapped = jnp.transpose(cycle, (2, 0, 1))
    return jnp.where(keep, swapped, 0.0) / denominator


def on_square(amplitudes, integrals, occ_irrep, vir_irrep, screen):
    batch, occ_share, share, vir_total = amplitudes.shape
    row = lax.axis_index("row")
    col = lax.axis_index("col")
    place = jnp.stack([row, col]).astype(jnp.int32)
    m2a, m2b, m3a, m3b, pos2, pos3, posx, form = wide_blocks(
        integrals, occ_irrep, vir_irrep, screen, place, batch
    )
    outer = [(0, 1), (1, 0), (2, 3), (3, 2)]
    inner = [(1, 2), (2, 1)]
    inward = [(0, 1), (3, 2)]
    outward = [(1, 0), (2, 3)]
    ends = [(0, 3), (3, 0)]
    second = [(r, r ^ 2) for r in range(4)]

    def move(v, pairs):
        return lax.ppermute(v, "row", pairs)

    def sparse(use_few, choose):
        def run(m2a, m2b, m3a, m3b):
            shorts, wides = choose(m2a, m2b, m3a, m3b)
            near = [(own, move(own, outer), move(own, inner)) for own in wides]
            if use_few:
                narrow, few = narrow_blocks(integrals, occ_irrep, vir_irrep, screen, place, posx, m2a, batch)
                e1, o1 = move(narrow, outer), move(narrow, inner)
                two, three = move(few, second), move(few, ends)
                lhs, far_lhs, fold = masked_amplitudes(amplitudes, occ_irrep, vir_irrep, place)
                near, e1, o1, two, three, _ = lax.optimization_barrier((near, e1, o1, two, three, fold))
                blocks = (narrow, e1, o1, two, two, three)
                sums = (narrow, e1, o1, two, three)
            else:
                h1 = [move(v, inward) for v in shorts]
                (narrow,) = narrow_blocks(integrals, occ_irrep, vir_irrep, screen, place, posx, None, batch)
                o1, e1 = move(narrow, inner), move(narrow, outward)
                lhs, far_lhs, fold = masked_amplitudes(amplitudes, occ_irrep, vir_irrep, place)
                near, h1, o1, e1, _ = lax.optimization_barrier((near, h1, o1, e1, fold))
                h2 = [move(own + v, inner) for own, v in zip(shorts, h1)]
                e1 = e1 + move(narrow, inward)
                e2 = move(o1, outward)
                h2, e1, e2 = lax.optimization_barrier((h2, e1, e2))
                h3 = [move(own + v, outward) for own, v in zip(shorts, h2)]
                o2 = move(e1, inner)
                blocks = (narrow, e1, o1, e2, o2, move(o2, outward))
                sums = [a + b + c + d for a, b, c, d in zip(shorts, h1, h2, h3)]
            far = [(move(o, outward), move(e, inner)) for _, e, o in near]
            narrow_sum, wide_sum = first_product(
                lhs, far_lhs, pos3, posx, place, blocks, use_few, near
            )
            return list(last_product(
                far_lhs, fold, occ_irrep, vir_irrep, pos2, pos3, place, narrow_sum, wide_sum, use_few, sums, far,
                batch
            ))

        return run

    def dense(*_):
        occ_local = lax.dynamic_slice_in_dim(occ_irrep, col * occ_share, occ_share)
        vir_local = lax.dynamic_slice_in_dim(vir_irrep, row * share, share)
        screen_rows = lax.dynamic_slice_in_dim(screen, col * occ_share, occ_share, 0)
        fold = folded_integrals(
            integrals, occ_local, vir_local, vir_irrep, occ_irrep[batch], screen_rows
        )
        whole = jnp.zeros((occ_share, vir_total, FOLD), fold.dtype)
        for s in range(4):
            block = move(fold, [(r, r ^ s) for r in range(4)]) if s else fold
            whole = lax.dynamic_update_slice_in_dim(whole, block, jnp.bitwise_xor(row, s) * share, 1)
        total = dense_product(amplitudes, whole, occ_irrep, occ_local, vir_local, vir_irrep)
        quarter = (batch // 2, share, FOLD // 2)
        goals = [jnp.bitwise_xor(col, t) for t in range(4)]
        return [
            lax.dynamic_slice(total, (g // 2 * quarter[0], 0, g % 2 * quarter[2]), quarter) for g in goals
        ]

    branches = [
        sparse(False, lambda m2a, m2b, m3a, m3b: ([m2a], [])),
        sparse(False, lambda m2a, m2b, m3a, m3b: ([m2a, m2b], [])),
        sparse(False, lambda m2a, m2b, m3a, m3b: ([m2a], [m3a[:FEW_WIDE]])),
        sparse(True, lambda m2a, m2b, m3a, m3b: ([], [m3a])),
        sparse(True, lambda m2a, m2b, m3a, m3b: ([], [m3a, m3b])),
        sparse(False, lambda m2a, m2b, m3a, m3b: ([m2a, m2b], [m3a, m3b])),
        dense,
    ]
    quarters = lax.switch(form[0], branches, m2a, m2b, m3a, m3b)
    mine = quarters[0]
    for t in (1, 2, 3):
        mine = mine + lax.ppermute(quarters[t], "col", [(q, q ^ t) for q in range(4)])
    places = [(r, q) for r in range(4) for q in range(4)]
    same = lax.ppermute(mine, ("row", "col"), [(r * 4 + q, q * 4 + r) for r, q in places])
    other = lax.ppermute(mine, ("row", "col"), [(r * 4 + q, (q ^ 2) * 4 + r) for r, q in places])
    upper = row // 2 == 1
    low = jnp.where(upper, other, same)
    high = jnp.where(upper, same, other)
    return jnp.concatenate([low, high], axis=0)


def on_any(amplitudes, integrals, occ_irrep, vir_irrep, screen):
    batch, occ_share, share, vir_total = amplitudes.shape
    row = lax.axis_index("row")
    col = lax.axis_index("col")
    occ_local = lax.dynamic_slice_in_dim(occ_irrep, col * occ_share, occ_share)
    vir_local = lax.dynamic_slice_in_dim(vir_irrep, row * share, share)
    screen_rows = lax.dynamic_slice_in_dim(screen, col * occ_share, occ_share, 0)
    fold = folded_integrals(
        integrals, occ_local, vir_local, vir_irrep, occ_irrep[batch], screen_rows
    )
    whole = lax.all_gather(fold, "row", axis=1, tiled=True)
    cycle = dense_product(amplitudes, whole, occ_irrep, occ_local, vir_local, vir_irrep)
    cycle = lax.psum(cycle, "col")
    cycle = jnp.concatenate([cycle] * (vir_total // FOLD), axis=2)
    cycle = lax.all_to_all(cycle, "row", split_axis=2, concat_axis=1, tiled=True)
    a_size = vir_total // lax.axis_size("col")
    return lax.dynamic_slice_in_dim(cycle, col * a_size, a_size, 1)


def on_device(amplitudes, integrals, occ_irrep, vir_irrep, screen, occ_energy, vir_energy):
    batch, _, vir_share, vir_total = amplitudes.shape
    square = lax.axis_size("row") == 4 and lax.axis_size("col") == 4
    form = on_square if square else on_any
    cycle = form(amplitudes, integrals, occ_irrep, vir_irrep, screen)
    a_size = vir_total // lax.axis_size("col")
    return finish(
        cycle, occ_irrep, vir_irrep, occ_energy, vir_energy,
        lax.axis_index("col") * a_size, a_size, lax.axis_index("row") * vir_share, vir_share, batch,
    )


def solution(mesh):
    in_specs = (
        P("parts", "col", "row", None),
        P(("parts", "col"), "row", None),
        P("parts"),
        P("parts"),
        P("parts", None),
        P("parts"),
        P("parts"),
    )
    out_specs = P("row", "parts", "col")
    return jax.shard_map(
        on_device, mesh=mesh, in_specs=in_specs, out_specs=out_specs, check_vma=False
    )
```

```python
import jax
import jax.numpy as jnp
from jax import lax
from jax.experimental import pallas as pl
from jax.experimental.pallas import tpu as pltpu
from jax.sharding import PartitionSpec as P

FOLD = 256
K_STEP = 5


def folded_integrals(integrals, occ_local, vir_local, vir_irrep, pair_label, screen_rows):
    irrep_codes = jnp.arange(8, dtype=jnp.int32)
    screen_local = jnp.sum(
        screen_rows[:, None, :] * (vir_local[None, :, None] == irrep_codes).astype(jnp.int32),
        axis=2,
    )
    target = jnp.bitwise_xor(
        jnp.bitwise_xor(occ_local[:, None], vir_local[None, :]), pair_label
    )
    target = jnp.where(screen_local == 1, target, -1)
    keep = target[:, :, None] == vir_irrep[None, None, :]
    kept = jnp.where(keep, integrals, jnp.zeros_like(integrals))
    return kept[:, :, :FOLD] + kept[:, :, FOLD:]


NARROW = 64
CAPS = (22, 3)
FEW_SHORT = 8
FEW_WIDE = 5


def largest_irrep(vir_ref):
    return jnp.where(vir_ref[0] == vir_ref[FOLD - 1], vir_ref[0], vir_ref[FOLD])


def label_columns(row_labels):
    return jnp.transpose(jnp.broadcast_to(row_labels, (8, row_labels.shape[1])))


def as_bf16(labels):
    return labels.astype(jnp.float32).astype(jnp.bfloat16)


def label_mix(mix_ref, column_ref, row_ref, row, big, keep_big):
    depth = mix_ref.shape[0]
    column_ref[...] = label_columns(row_ref[...])
    column = column_ref[pl.ds(pl.multiple_of(row * depth, depth), depth), :1]
    is_big = row_ref[...] == big
    wanted = is_big if keep_big else jnp.logical_not(is_big)
    mix_ref[...] = as_bf16(jnp.where(wanted, jnp.bitwise_xor(column, row_ref[...]), 8))


def kept_folded(int_ref, mix_ref, j, x):
    tile = int_ref[j]
    wanted = as_bf16(jnp.full(mix_ref.shape, x))
    kept = jnp.where(mix_ref[...] == wanted, tile, jnp.zeros_like(tile))
    return kept[:, :FOLD] + kept[:, FOLD:]


def wide_kernel(
    occ_ref, vir_ref, screen_ref, place_ref, int_ref, row_ref,
    m2a_ref, m2b_ref, m3a_ref, m3b_ref, pos2_ref, pos3_ref, posx_ref, form_ref,
    mix_ref, column_ref, counts_ref, batch,
):
    step = pl.program_id(0)
    k_step, depth, total = int_ref.shape
    half = depth // 2
    row, col = place_ref[0], place_ref[1]
    pair_label = occ_ref[batch]
    big = largest_irrep(vir_ref)

    @pl.when(step == 0)
    def _():
        for n in range(3):
            counts_ref[n] = 0
        label_mix(mix_ref, column_ref, row_ref, row, big, True)

    @pl.loop(0, k_step)
    def _(j):
        k = step * k_step + j
        k_whole = col * (k_step * pl.num_programs(0)) + k
        x = jnp.bitwise_xor(occ_ref[k_whole], pair_label)
        on_big = screen_ref[jnp.bitwise_xor(big, x), k_whole] == 1
        actives = (on_big & (x != 0), on_big & (x == 0), x != 0)
        pos2, pos3, posx = [jnp.where(active, counts_ref[n], -1) for n, active in enumerate(actives)]
        for n, active in enumerate(actives):
            counts_ref[n] = counts_ref[n] + active.astype(jnp.int32)
        pos2_ref[k], pos3_ref[k], posx_ref[k] = pos2, pos3, posx

        @pl.when(pos2 >= 0)
        def _():
            wide = kept_folded(int_ref, mix_ref, j, x)
            short = wide[:half] + wide[half:]

            @pl.when(pos2 < CAPS[0])
            def _():
                m2a_ref[pos2] = short

            @pl.when(pos2 >= CAPS[0])
            def _():
                m2b_ref[pos2 - CAPS[0]] = short

        @pl.when(pos3 >= 0)
        def _():
            wide = kept_folded(int_ref, mix_ref, j, x)

            @pl.when(pos3 < CAPS[0])
            def _():
                m3a_ref[pos3] = wide

            @pl.when(pos3 >= CAPS[0])
            def _():
                m3b_ref[pos3 - CAPS[0]] = wide

    @pl.when(step == pl.num_programs(0) - 1)
    def _():
        labels = row_ref[...]
        lanes = lax.broadcasted_iota(jnp.int32, labels.shape, 1)
        ahead = pltpu.roll(labels, total - NARROW, 1)
        long = (labels == ahead) & (lanes < total - NARROW) & (labels != big)
        too_long = jnp.max(long.astype(jnp.int32)) == 1
        n2, n3, nx = counts_ref[0], counts_ref[1], counts_ref[2]
        one_label = occ_ref[0] == pair_label
        form = jnp.where(nx <= FEW_SHORT, jnp.where(n3 <= CAPS[0], 3, 4), 5)
        form = jnp.where((n3 <= FEW_WIDE) & (n2 <= CAPS[0]), 2, form)
        form = jnp.where(one_label, form, 6)
        form = jnp.where(n3 == 0, jnp.where(n2 <= CAPS[0], 0, 1), form)
        form_ref[0] = jnp.where(too_long, 6, form)


def wide_blocks(integrals, occ_irrep, vir_irrep, screen, place, batch):
    occ_share, depth, total = integrals.shape
    shapes = [(n, depth // 2, FOLD) for n in CAPS] + [(n, depth, FOLD) for n in CAPS]
    smem = pl.BlockSpec(memory_space=pltpu.SMEM)

    def kernel(*refs):
        wide_kernel(*refs, batch)

    return pl.pallas_call(
        kernel,
        grid_spec=pltpu.PrefetchScalarGridSpec(
            num_scalar_prefetch=4,
            grid=(occ_share // K_STEP,),
            in_specs=[
                pl.BlockSpec((K_STEP, depth, total), lambda k, *_: (k, 0, 0)),
                pl.BlockSpec((1, total), lambda k, *_: (0, 0)),
            ],
            out_specs=[pl.BlockSpec(v, lambda k, *_: (0, 0, 0)) for v in shapes] + [smem] * 4,
            scratch_shapes=[
                pltpu.VMEM((depth, total), jnp.bfloat16),
                pltpu.VMEM((total, 8), jnp.int32),
                pltpu.SMEM((3,), jnp.int32),
            ],
        ),
        out_shape=[jax.ShapeDtypeStruct(v, jnp.bfloat16) for v in shapes]
        + [jax.ShapeDtypeStruct((n,), jnp.int32) for n in (occ_share, occ_share, occ_share, 1)],
        cost_estimate=cost(5),
        compiler_params=pltpu.CompilerParams(vmem_limit_bytes=24 * 1024 * 1024),
    )(occ_irrep, vir_irrep, screen.T, place, integrals, vir_irrep[None, :])


def narrow_kernel(
    occ_ref, vir_ref, screen_ref, place_ref, posx_ref, int_ref, row_ref, short_ref, narrow_ref, few_ref,
    mix_ref, column_ref, batch,
):
    step = pl.program_id(0)
    k_step, depth, total = int_ref.shape
    half = depth // 2
    row, col = place_ref[0], place_ref[1]

    @pl.when(step == 0)
    def _():
        label_mix(mix_ref, column_ref, row_ref, row, largest_irrep(vir_ref), False)
        if few_ref is not None:
            for n in range(FEW_SHORT):
                for piece in range(2):
                    block = short_ref[n, :, piece * 2 * NARROW:(piece + 1) * 2 * NARROW]
                    narrow_ref[k_step * pl.num_programs(0) + 2 * n + piece] = block
                    few_ref[FEW_SHORT + 2 * n + piece] = block

    lane = lax.broadcasted_iota(jnp.int32, (half, 2 * NARROW), 1)
    local = column_ref[pl.ds(pl.multiple_of(row * depth, depth), depth), :1]
    for j in range(k_step):
        k = step * k_step + j
        k_whole = col * (k_step * pl.num_programs(0)) + k
        x = jnp.bitwise_xor(occ_ref[k_whole], occ_ref[batch])
        bits = screen_ref[0, k_whole]
        for g in range(1, 8):
            bits = bits + screen_ref[g, k_whole] * (1 << g)
        narrow = kept_folded(int_ref, mix_ref, j, x)
        narrow = (narrow[:, : 2 * NARROW] + narrow[:, 2 * NARROW:]).astype(jnp.float32)
        narrow = narrow + pltpu.roll(narrow, NARROW, 1)
        on = jnp.bitwise_and(lax.shift_right_logical(jnp.full(local.shape, bits), local), 1) == 1
        narrow = jnp.where(on, narrow, 0.0)
        narrow = jnp.where(lane < NARROW, narrow[:half], narrow[half:]).astype(jnp.bfloat16)
        narrow_ref[k] = narrow
        if few_ref is not None:
            posx = posx_ref[k]

            @pl.when((posx >= 0) & (posx < FEW_SHORT))
            def _(narrow=narrow, posx=posx):
                few_ref[posx] = narrow


def narrow_blocks(integrals, occ_irrep, vir_irrep, screen, place, posx, short, batch):
    occ_share, depth, total = integrals.shape
    few = short is not None
    counts = (occ_share + 2 * FEW_SHORT, 3 * FEW_SHORT) if few else (occ_share,)
    shapes = [(n, depth // 2, 2 * NARROW) for n in counts]
    fixed = lambda k, *_: (0, 0, 0)

    def kernel(*refs):
        if few:
            narrow_kernel(*refs, batch)
        else:
            narrow_kernel(*refs[:7], None, refs[7], None, *refs[8:], batch)

    return pl.pallas_call(
        kernel,
        grid_spec=pltpu.PrefetchScalarGridSpec(
            num_scalar_prefetch=5,
            grid=(occ_share // K_STEP,),
            in_specs=[
                pl.BlockSpec((K_STEP, depth, total), lambda k, *_: (k, 0, 0)),
                pl.BlockSpec((1, total), lambda k, *_: (0, 0)),
            ] + ([pl.BlockSpec((FEW_SHORT, depth // 2, FOLD), fixed)] if few else []),
            out_specs=[pl.BlockSpec(v, fixed) for v in shapes],
            scratch_shapes=[pltpu.VMEM((depth, total), jnp.bfloat16), pltpu.VMEM((total, 8), jnp.int32)],
        ),
        out_shape=[jax.ShapeDtypeStruct(v, jnp.bfloat16) for v in shapes],
        cost_estimate=cost(5),
        compiler_params=pltpu.CompilerParams(vmem_limit_bytes=16 * 1024 * 1024),
    )(occ_irrep, vir_irrep, screen.T, place, posx, integrals, vir_irrep[None, :], *([short] if few else []))


def cost(micros):
    return pl.CostEstimate(flops=int(micros * 1e9), bytes_accessed=int(micros * 3e6), transcendentals=0)


SLOTS = (0, 1, 3, 2)
NEAR = 3


def amplitude_rows(column_ref, row_ref, occ_ref, row, batch, share):
    column_ref[...] = label_columns(row_ref[...])
    column = column_ref[pl.ds(pl.multiple_of(row * share, share), share), :1]
    return jnp.concatenate([jnp.bitwise_xor(column, occ_ref[i]) for i in range(batch)], axis=0)


def write_quarters(total_ref, col, outs):
    rows, fold = total_ref.shape
    width, height = fold // 2, rows // 2
    for t, out_ref in enumerate(outs):
        goal = jnp.bitwise_xor(col, t)
        lanes = pl.ds(pl.multiple_of((goal % 2) * width, width), width)
        lines = pl.ds(pl.multiple_of((goal // 2) * height, height), height)
        out_ref[...] = total_ref[lines, lanes].reshape(out_ref.shape)


def chosen(refs, starts, pos, pick):
    block = None
    for n, group in enumerate(refs):
        inside = (pos >= starts[n]) & (pos < starts[n + 1])
        at = jnp.clip(pos - starts[n], 0, starts[n + 1] - starts[n] - 1)
        found = pick(group, at)
        found = jnp.where(inside, found, jnp.zeros_like(found))
        block = found if block is None else block + found
    return block


def starts_of(arrays):
    starts = [0]
    for v in arrays:
        starts.append(starts[-1] + v.shape[0])
    return starts


def mask_kernel(occ_ref, place_ref, amp_ref, row_ref, lhs_ref, far_ref, fold_ref, mix_ref, column_ref, amp_buffer, sems):
    batch, k_all, share, total = amp_ref.shape
    rows, groups = batch * share, k_all // K_STEP
    row, col = place_ref[0], place_ref[1]

    def fetch(group):
        slot = group % 2
        source = amp_ref.at[:, pl.ds(group * K_STEP, K_STEP)]
        return pltpu.make_async_copy(source, amp_buffer.at[slot], sems.at[slot])

    fetch(0).start()
    column = amplitude_rows(column_ref, row_ref, occ_ref, row, batch, share)
    mix_ref[...] = as_bf16(jnp.bitwise_xor(column, row_ref[...]))

    @pl.loop(0, groups)
    def _(group):
        slot = group % 2

        @pl.when(group + 1 < groups)
        def _():
            fetch(group + 1).start()

        fetch(group).wait()

        @pl.loop(0, K_STEP)
        def _(j):
            wanted = as_bf16(jnp.full((rows, share), occ_ref[col * k_all + group * K_STEP + j]))
            folded = None
            for n, s in enumerate(SLOTS):
                place = pl.ds(pl.multiple_of(jnp.bitwise_xor(row, s) * share, share), share)
                tile = amp_buffer[slot, :, j, :, place].reshape(rows, share)
                piece = jnp.where(mix_ref[:, place] == wanted, tile, jnp.zeros_like(tile))
                if n < NEAR:
                    lhs_ref[group, :, pl.ds(pl.multiple_of((n * K_STEP + j) * share, share), share)] = piece
                else:
                    far_ref[group, :, pl.ds(pl.multiple_of(j * share, share), share)] = piece
                folded = piece if folded is None else folded + piece
            fold_ref[group, :, pl.ds(pl.multiple_of(j * share, share), share)] = folded


def masked_amplitudes(amplitudes, occ_irrep, vir_irrep, place):
    batch, k_all, share, total = amplitudes.shape
    rows, groups = batch * share, k_all // K_STEP
    smem = pl.BlockSpec(memory_space=pltpu.SMEM)
    vmem = pl.BlockSpec(memory_space=pltpu.VMEM)
    hbm = pl.BlockSpec(memory_space=pltpu.HBM)
    widths = (NEAR * K_STEP * share, K_STEP * share, K_STEP * share)
    return pl.pallas_call(
        mask_kernel,
        in_specs=[smem, smem, hbm, vmem],
        out_specs=[vmem] * 3,
        out_shape=[jax.ShapeDtypeStruct((groups, rows, w), jnp.bfloat16) for w in widths],
        scratch_shapes=[
            pltpu.VMEM((rows, total), jnp.bfloat16),
            pltpu.VMEM((total, 8), jnp.int32),
            pltpu.VMEM((2, batch, K_STEP, share, total), jnp.bfloat16),
            pltpu.SemaphoreType.DMA((2,)),
        ],
        cost_estimate=cost(7),
        compiler_params=pltpu.CompilerParams(vmem_limit_bytes=28 * 1024 * 1024),
    )(occ_irrep, place, amplitudes, vir_irrep[None, :])


def make_first_kernel(few, n3, starts3):
    def kernel(pos3_ref, posx_ref, place_ref, lhs_ref, far_ref, *refs):
        sources = 4 if few else 6
        narrow_refs, refs = refs[:sources], refs[sources:]
        m3_refs = [refs[3 * n:3 * n + 3] for n in range(n3)]
        narrow_sum, wide_sum, narrow_rhs, wide_rhs = refs[3 * n3:]
        row = place_ref[0]
        at_end = (row == 0) | (row == 3)
        groups, _, depth = lhs_ref.shape
        share = depth // (NEAR * K_STEP)
        half = share // 2
        lane = lax.broadcasted_iota(jnp.int32, (half, 2 * NARROW), 1)

        narrow_sum[...] = jnp.zeros(narrow_sum.shape, jnp.float32)
        wide_sum[...] = jnp.zeros(wide_sum.shape, jnp.float32)

        @pl.loop(0, groups)
        def _(group):
            @pl.loop(0, K_STEP)
            def _(j):
                k = group * K_STEP + j
                if few:
                    two = narrow_refs[3][jnp.maximum(posx_ref[k], 0)]
                    two = jnp.where(posx_ref[k] >= 0, two, jnp.zeros_like(two))
                    blocks = [ref[k] for ref in narrow_refs[:3]] + [two]
                else:
                    own, e1, o1, e2, o2, e3 = [ref[k] for ref in narrow_refs]
                    blocks = (own, e1, jnp.where(at_end, e3, o1), jnp.where(at_end, e2, o2))
                for n, block in enumerate(blocks):
                    zero = jnp.zeros_like(block)
                    first = pl.multiple_of((n * K_STEP + j) * share, share)
                    narrow_rhs[pl.ds(first, half)] = jnp.where(lane < NARROW, block, zero)
                    narrow_rhs[pl.ds(first + half, half)] = jnp.where(lane < NARROW, zero, block)
                for n in range(3 if n3 else 0):
                    block = chosen(m3_refs, starts3, pos3_ref[k], lambda group, at, n=n: group[n][at])
                    if n == 2:
                        block = jnp.where(at_end, jnp.zeros_like(block), block)
                    wide_rhs[pl.ds(pl.multiple_of((n * K_STEP + j) * share, share), share)] = block

            narrow = jnp.dot(lhs_ref[group], narrow_rhs[:depth], preferred_element_type=jnp.float32)
            narrow += jnp.dot(far_ref[group], narrow_rhs[depth:], preferred_element_type=jnp.float32)
            narrow_sum[...] += narrow
            if n3:
                wide_sum[...] += jnp.dot(lhs_ref[group], wide_rhs[...], preferred_element_type=jnp.float32)

    return kernel


def first_product(lhs, far_lhs, pos3, posx, place, narrow, few, m3):
    groups, rows, depth = lhs.shape
    vmem = pl.BlockSpec(memory_space=pltpu.VMEM)
    smem = pl.BlockSpec(memory_space=pltpu.SMEM)
    arrays = list(narrow) + [v for group in m3 for v in group]
    wide = (rows, FOLD) if m3 else (16, FOLD)
    wide_depth = depth if m3 else 16
    return pl.pallas_call(
        make_first_kernel(few, len(m3), starts_of([v[0] for v in m3])),
        in_specs=[smem] * 3 + [vmem] * (2 + len(arrays)),
        out_specs=[vmem] * 2,
        out_shape=[jax.ShapeDtypeStruct(v, jnp.float32) for v in ((rows, 2 * NARROW), wide)],
        scratch_shapes=[
            pltpu.VMEM((depth // NEAR * len(SLOTS), 2 * NARROW), jnp.bfloat16),
            pltpu.VMEM((wide_depth, FOLD), jnp.bfloat16),
        ],
        cost_estimate=cost(9 if m3 else 6),
        compiler_params=pltpu.CompilerParams(vmem_limit_bytes=32 * 1024 * 1024),
    )(pos3, posx, place, lhs, far_lhs, *arrays)


def make_last_kernel(few, n2, starts2, n3, starts3):
    def kernel(occ_ref, vir_ref, pos2_ref, pos3_ref, place_ref, fold_ref, far_ref, row_ref, narrow_ref, wide_ref, *refs):
        m2_refs = refs[:n2]
        m3_refs = [refs[n2 + 2 * n:n2 + 2 * n + 2] for n in range(n3)]
        refs = refs[n2 + 2 * n3:]
        outs = refs[:4]
        column_ref, total_ref, short_rhs, far_rhs = refs[4:]
        row, col = place_ref[0], place_ref[1]
        at_end = (row == 0) | (row == 3)
        groups, rows, width = fold_ref.shape
        share = width // K_STEP
        batch = rows // share
        @pl.loop(0, groups * K_STEP)
        def _(k):
            here = pl.ds(pl.multiple_of(k * share, share), share)
            if few:
                pos2 = pos2_ref[k]
                at = 2 * jnp.maximum(pos2, 0)
                pieces = []
                for piece in range(2):
                    close = groups * K_STEP + at + piece
                    own, one, three = [ref[close] for ref in m2_refs[:3]]
                    block = own + one + three + m2_refs[3][FEW_SHORT + at + piece]
                    pieces.append(jnp.where(pos2 >= 0, block, jnp.zeros_like(block)))
                short = jnp.concatenate(pieces, axis=1)
            else:
                short = chosen(m2_refs, starts2, pos2_ref[k], lambda ref, at: ref[at])
            short_rhs[here] = jnp.concatenate([short, short], axis=0)
            if n3:
                far_rhs[here] = chosen(
                    m3_refs, starts3, pos3_ref[k], lambda pair, at: jnp.where(at_end, pair[0][at], pair[1][at])
                )

        column = amplitude_rows(column_ref, row_ref, occ_ref, row, batch, share)
        target = jnp.bitwise_xor(column, occ_ref[batch])
        both = narrow_ref[...]
        both = both + pltpu.roll(both, NARROW, 1)
        both = jnp.concatenate([both] * (FOLD // (2 * NARROW)), axis=1)
        part = wide_ref[...] if n3 else 0.0
        for group in range(groups):
            here = pl.ds(group * width, width)
            part += jnp.dot(fold_ref[group], short_rhs[here], preferred_element_type=jnp.float32)
            if n3:
                part += jnp.dot(far_ref[group], far_rhs[here], preferred_element_type=jnp.float32)
        total_ref[...] = jnp.where(target == largest_irrep(vir_ref), part, both)
        write_quarters(total_ref, col, outs)

    return kernel


def last_product(far_lhs, fold, occ_irrep, vir_irrep, pos2, pos3, place, narrow_sum, wide_sum, few, m2, m3, batch):
    groups, rows, width = fold.shape
    share = rows // batch
    vmem = pl.BlockSpec(memory_space=pltpu.VMEM)
    smem = pl.BlockSpec(memory_space=pltpu.SMEM)
    arrays = [narrow_sum, wide_sum] + list(m2) + [v for group in m3 for v in group]
    quarter = (batch // 2, share, FOLD // 2)
    whole = groups * width
    far_lhs = far_lhs if m3 else jnp.zeros((8, 128), jnp.bfloat16)
    return pl.pallas_call(
        make_last_kernel(few, len(m2), starts_of(m2), len(m3), starts_of([v[0] for v in m3])),
        in_specs=[smem] * 5 + [vmem] * (3 + len(arrays)),
        out_specs=[vmem] * 4,
        out_shape=[jax.ShapeDtypeStruct(quarter, jnp.float32)] * 4,
        scratch_shapes=[
            pltpu.VMEM((vir_irrep.shape[0], 8), jnp.int32),
            pltpu.VMEM((rows, FOLD), jnp.float32),
            pltpu.VMEM((whole, FOLD), jnp.bfloat16),
            pltpu.VMEM((whole if m3 else 16, FOLD), jnp.bfloat16),
        ],
        cost_estimate=cost(4 if m3 else 2),
        compiler_params=pltpu.CompilerParams(vmem_limit_bytes=32 * 1024 * 1024),
    )(occ_irrep, vir_irrep, pos2, pos3, place, fold, far_lhs, vir_irrep[None, :], *arrays)


def dense_product(amplitudes, whole, occ_irrep, occ_local, vir_local, vir_irrep):
    batch = amplitudes.shape[0]
    keep = (
        jnp.bitwise_xor(occ_irrep[:batch, None], occ_local[None, :])[:, :, None, None]
        == jnp.bitwise_xor(vir_local[:, None], vir_irrep[None, :])[None, None]
    )
    kept = jnp.where(keep, amplitudes, jnp.zeros_like(amplitudes))
    return lax.dot_general(
        kept, whole, (((1, 3), (0, 1)), ((), ())), preferred_element_type=jnp.float32
    )


def finish(cycle, occ_irrep, vir_irrep, occ_energy, vir_energy, a_start, a_size, b_start, b_size, batch):
    label_a = lax.dynamic_slice_in_dim(vir_irrep, a_start, a_size)
    label_b = lax.dynamic_slice_in_dim(vir_irrep, b_start, b_size)
    energy_a = lax.dynamic_slice_in_dim(vir_energy, a_start, a_size)
    energy_b = lax.dynamic_slice_in_dim(vir_energy, b_start, b_size)
    target = jnp.bitwise_xor(
        jnp.bitwise_xor(occ_irrep[:batch, None], occ_irrep[batch]), label_a[None, :]
    )
    keep = label_b[:, None, None] == target[None, :, :]
    denominator = (
        occ_energy[:batch][None, :, None]
        + occ_energy[batch]
        - energy_a[None, None, :]
        - energy_b[:, None, None]
    )
    swapped = jnp.transpose(cycle, (2, 0, 1))
    return jnp.where(keep, swapped, 0.0) / denominator


def on_square(amplitudes, integrals, occ_irrep, vir_irrep, screen):
    batch, occ_share, share, vir_total = amplitudes.shape
    row = lax.axis_index("row")
    col = lax.axis_index("col")
    place = jnp.stack([row, col]).astype(jnp.int32)
    m2a, m2b, m3a, m3b, pos2, pos3, posx, form = wide_blocks(
        integrals, occ_irrep, vir_irrep, screen, place, batch
    )
    outer = [(0, 1), (1, 0), (2, 3), (3, 2)]
    inner = [(1, 2), (2, 1)]
    inward = [(0, 1), (3, 2)]
    outward = [(1, 0), (2, 3)]
    second = [(r, r ^ 2) for r in range(4)]
    third = [(r, r ^ 3) for r in range(4)]

    def move(v, pairs):
        return lax.ppermute(v, "row", pairs)

    def sparse(use_few, choose):
        def run(m2a, m2b, m3a, m3b):
            shorts, wides = choose(m2a, m2b, m3a, m3b)
            near = [(own, move(own, outer), move(own, inner)) for own in wides]
            if use_few:
                narrow, few = narrow_blocks(integrals, occ_irrep, vir_irrep, screen, place, posx, m2a, batch)
                one, two, three = move(narrow, outer), move(few, second), move(narrow, third)
                lhs, far_lhs, fold = masked_amplitudes(amplitudes, occ_irrep, vir_irrep, place)
                near, one, two, three, _ = lax.optimization_barrier((near, one, two, three, fold))
                blocks = (narrow, one, three, two)
                sums = (narrow, one, three, two)
            else:
                h1 = [move(v, inward) for v in shorts]
                (narrow,) = narrow_blocks(integrals, occ_irrep, vir_irrep, screen, place, posx, None, batch)
                o1, e1 = move(narrow, inner), move(narrow, outward)
                lhs, far_lhs, fold = masked_amplitudes(amplitudes, occ_irrep, vir_irrep, place)
                near, h1, o1, e1, _ = lax.optimization_barrier((near, h1, o1, e1, fold))
                h2 = [move(own + v, inner) for own, v in zip(shorts, h1)]
                e1 = e1 + move(narrow, inward)
                e2 = move(o1, outward)
                h2, e1, e2 = lax.optimization_barrier((h2, e1, e2))
                h3 = [move(own + v, outward) for own, v in zip(shorts, h2)]
                o2 = move(e1, inner)
                blocks = (narrow, e1, o1, e2, o2, move(o2, outward))
                sums = [a + b + c + d for a, b, c, d in zip(shorts, h1, h2, h3)]
            far = [(move(o, outward), move(e, inner)) for _, e, o in near]
            narrow_sum, wide_sum = first_product(
                lhs, far_lhs, pos3, posx, place, blocks, use_few, near
            )
            return list(last_product(
                far_lhs, fold, occ_irrep, vir_irrep, pos2, pos3, place, narrow_sum, wide_sum, use_few, sums, far,
                batch
            ))

        return run

    def dense(*_):
        occ_local = lax.dynamic_slice_in_dim(occ_irrep, col * occ_share, occ_share)
        vir_local = lax.dynamic_slice_in_dim(vir_irrep, row * share, share)
        screen_rows = lax.dynamic_slice_in_dim(screen, col * occ_share, occ_share, 0)
        fold = folded_integrals(
            integrals, occ_local, vir_local, vir_irrep, occ_irrep[batch], screen_rows
        )
        whole = jnp.zeros((occ_share, vir_total, FOLD), fold.dtype)
        for s in range(4):
            block = move(fold, [(r, r ^ s) for r in range(4)]) if s else fold
            whole = lax.dynamic_update_slice_in_dim(whole, block, jnp.bitwise_xor(row, s) * share, 1)
        total = dense_product(amplitudes, whole, occ_irrep, occ_local, vir_local, vir_irrep)
        quarter = (batch // 2, share, FOLD // 2)
        goals = [jnp.bitwise_xor(col, t) for t in range(4)]
        return [
            lax.dynamic_slice(total, (g // 2 * quarter[0], 0, g % 2 * quarter[2]), quarter) for g in goals
        ]

    branches = [
        sparse(False, lambda m2a, m2b, m3a, m3b: ([m2a], [])),
        sparse(False, lambda m2a, m2b, m3a, m3b: ([m2a, m2b], [])),
        sparse(False, lambda m2a, m2b, m3a, m3b: ([m2a], [m3a[:FEW_WIDE]])),
        sparse(True, lambda m2a, m2b, m3a, m3b: ([], [m3a])),
        sparse(True, lambda m2a, m2b, m3a, m3b: ([], [m3a, m3b])),
        sparse(False, lambda m2a, m2b, m3a, m3b: ([m2a, m2b], [m3a, m3b])),
        dense,
    ]
    quarters = lax.switch(form[0], branches, m2a, m2b, m3a, m3b)
    mine = quarters[0]
    for t in (1, 2, 3):
        mine = mine + lax.ppermute(quarters[t], "col", [(q, q ^ t) for q in range(4)])
    places = [(r, q) for r in range(4) for q in range(4)]
    same = lax.ppermute(mine, ("row", "col"), [(r * 4 + q, q * 4 + r) for r, q in places])
    other = lax.ppermute(mine, ("row", "col"), [(r * 4 + q, (q ^ 2) * 4 + r) for r, q in places])
    upper = row // 2 == 1
    low = jnp.where(upper, other, same)
    high = jnp.where(upper, same, other)
    return jnp.concatenate([low, high], axis=0)


def on_any(amplitudes, integrals, occ_irrep, vir_irrep, screen):
    batch, occ_share, share, vir_total = amplitudes.shape
    row = lax.axis_index("row")
    col = lax.axis_index("col")
    occ_local = lax.dynamic_slice_in_dim(occ_irrep, col * occ_share, occ_share)
    vir_local = lax.dynamic_slice_in_dim(vir_irrep, row * share, share)
    screen_rows = lax.dynamic_slice_in_dim(screen, col * occ_share, occ_share, 0)
    fold = folded_integrals(
        integrals, occ_local, vir_local, vir_irrep, occ_irrep[batch], screen_rows
    )
    whole = lax.all_gather(fold, "row", axis=1, tiled=True)
    cycle = dense_product(amplitudes, whole, occ_irrep, occ_local, vir_local, vir_irrep)
    cycle = lax.psum(cycle, "col")
    cycle = jnp.concatenate([cycle] * (vir_total // FOLD), axis=2)
    cycle = lax.all_to_all(cycle, "row", split_axis=2, concat_axis=1, tiled=True)
    a_size = vir_total // lax.axis_size("col")
    return lax.dynamic_slice_in_dim(cycle, col * a_size, a_size, 1)


def on_device(amplitudes, integrals, occ_irrep, vir_irrep, screen, occ_energy, vir_energy):
    batch, _, vir_share, vir_total = amplitudes.shape
    square = lax.axis_size("row") == 4 and lax.axis_size("col") == 4
    form = on_square if square else on_any
    cycle = form(amplitudes, integrals, occ_irrep, vir_irrep, screen)
    a_size = vir_total // lax.axis_size("col")
    return finish(
        cycle, occ_irrep, vir_irrep, occ_energy, vir_energy,
        lax.axis_index("col") * a_size, a_size, lax.axis_index("row") * vir_share, vir_share, batch,
    )


def solution(mesh):
    in_specs = (
        P("parts", "col", "row", None),
        P(("parts", "col"), "row", None),
        P("parts"),
        P("parts"),
        P("parts", None),
        P("parts"),
        P("parts"),
    )
    out_specs = P("row", "parts", "col")
    return jax.shard_map(
        on_device, mesh=mesh, in_specs=in_specs, out_specs=out_specs, check_vma=False
    )
```

```python
import jax
import jax.numpy as jnp
from jax import lax
from jax.experimental import pallas as pl
from jax.experimental.pallas import tpu as pltpu
from jax.sharding import PartitionSpec as P

FOLD = 256
K_STEP = 5


def folded_integrals(integrals, occ_local, vir_local, vir_irrep, pair_label, screen_rows):
    irrep_codes = jnp.arange(8, dtype=jnp.int32)
    screen_local = jnp.sum(
        screen_rows[:, None, :] * (vir_local[None, :, None] == irrep_codes).astype(jnp.int32),
        axis=2,
    )
    target = jnp.bitwise_xor(
        jnp.bitwise_xor(occ_local[:, None], vir_local[None, :]), pair_label
    )
    target = jnp.where(screen_local == 1, target, -1)
    keep = target[:, :, None] == vir_irrep[None, None, :]
    kept = jnp.where(keep, integrals, jnp.zeros_like(integrals))
    return kept[:, :, :FOLD] + kept[:, :, FOLD:]


NARROW = 64
CAPS = (22, 3)
FEW_CAPS = (4, 10)
FEW_WIDE = 5


def largest_irrep(vir_ref):
    return jnp.where(vir_ref[0] == vir_ref[FOLD - 1], vir_ref[0], vir_ref[FOLD])


def label_columns(row_labels):
    return jnp.transpose(jnp.broadcast_to(row_labels, (8, row_labels.shape[1])))


def as_bf16(labels):
    return labels.astype(jnp.float32).astype(jnp.bfloat16)


def label_mix(mix_ref, column_ref, row_ref, row, big, keep_big):
    depth = mix_ref.shape[0]
    column_ref[...] = label_columns(row_ref[...])
    column = column_ref[pl.ds(pl.multiple_of(row * depth, depth), depth), :1]
    is_big = row_ref[...] == big
    wanted = is_big if keep_big else jnp.logical_not(is_big)
    mix_ref[...] = as_bf16(jnp.where(wanted, jnp.bitwise_xor(column, row_ref[...]), 8))


def kept_folded(int_ref, mix_ref, j, x):
    tile = int_ref[j]
    wanted = as_bf16(jnp.full(mix_ref.shape, x))
    kept = jnp.where(mix_ref[...] == wanted, tile, jnp.zeros_like(tile))
    return kept[:, :FOLD] + kept[:, FOLD:]


def narrow_fold(kept, bits, local):
    half = kept.shape[0] // 2
    lane = lax.broadcasted_iota(jnp.int32, (half, 2 * NARROW), 1)
    narrow = (kept[:, : 2 * NARROW] + kept[:, 2 * NARROW:]).astype(jnp.float32)
    narrow = narrow + pltpu.roll(narrow, NARROW, 1)
    on = jnp.bitwise_and(lax.shift_right_logical(jnp.full(local.shape, bits), local), 1) == 1
    narrow = jnp.where(on, narrow, 0.0)
    return jnp.where(lane < NARROW, narrow[:half], narrow[half:]).astype(jnp.bfloat16)


def screen_bits(screen_ref, k):
    bits = screen_ref[0, k]
    for g in range(1, 8):
        bits = bits + screen_ref[g, k] * (1 << g)
    return bits


def wide_kernel(
    occ_ref, vir_ref, screen_ref, place_ref, int_ref, row_ref,
    few_ref, m2a_ref, m2b_ref, m3a_ref, m3b_ref, pos2_ref, pos3_ref, posx_ref, form_ref,
    mix_ref, small_mix_ref, column_ref, counts_ref, batch,
):
    step = pl.program_id(0)
    k_step, depth, total = int_ref.shape
    half = depth // 2
    row, col = place_ref[0], place_ref[1]
    pair_label = occ_ref[batch]
    big = largest_irrep(vir_ref)
    k_all = k_step * pl.num_programs(0)
    mostly_zero = (occ_ref[col * k_all] == pair_label) | (occ_ref[(col + 1) * k_all - 1] == pair_label)
    most = FEW_CAPS[-1]

    @pl.when(step == 0)
    def _():
        for n in range(3):
            counts_ref[n] = 0
        label_mix(mix_ref, column_ref, row_ref, row, big, True)

        @pl.when(mostly_zero)
        def _():
            label_mix(small_mix_ref, column_ref, row_ref, row, big, False)

    local = column_ref[pl.ds(pl.multiple_of(row * depth, depth), depth), :1]

    @pl.loop(0, k_step)
    def _(j):
        k = step * k_step + j
        k_whole = col * k_all + k
        x = jnp.bitwise_xor(occ_ref[k_whole], pair_label)
        on_big = screen_ref[jnp.bitwise_xor(big, x), k_whole] == 1
        actives = (on_big & (x != 0), on_big & (x == 0), x != 0)
        pos2, pos3, posx = [jnp.where(active, counts_ref[n], -1) for n, active in enumerate(actives)]
        for n, active in enumerate(actives):
            counts_ref[n] = counts_ref[n] + active.astype(jnp.int32)
        pos2_ref[k], pos3_ref[k], posx_ref[k] = pos2, pos3, posx

        @pl.when(pos2 >= 0)
        def _():
            wide = kept_folded(int_ref, mix_ref, j, x)
            short = wide[:half] + wide[half:]

            @pl.when(mostly_zero & (pos2 < most))
            def _():
                for piece in range(2):
                    few_ref[pos2, 1 + piece] = short[:, piece * 2 * NARROW:(piece + 1) * 2 * NARROW]

            @pl.when(pos2 < CAPS[0])
            def _():
                m2a_ref[pos2] = short

            @pl.when(pos2 >= CAPS[0])
            def _():
                m2b_ref[pos2 - CAPS[0]] = short

        @pl.when(mostly_zero & (posx >= 0) & (posx < most))
        def _():
            kept = kept_folded(int_ref, small_mix_ref, j, x)
            few_ref[posx, 0] = narrow_fold(kept, screen_bits(screen_ref, k_whole), local)

        @pl.when(pos3 >= 0)
        def _():
            wide = kept_folded(int_ref, mix_ref, j, x)

            @pl.when(pos3 < CAPS[0])
            def _():
                m3a_ref[pos3] = wide

            @pl.when(pos3 >= CAPS[0])
            def _():
                m3b_ref[pos3 - CAPS[0]] = wide

    @pl.when(step == pl.num_programs(0) - 1)
    def _():
        labels = row_ref[...]
        lanes = lax.broadcasted_iota(jnp.int32, labels.shape, 1)
        ahead = pltpu.roll(labels, total - NARROW, 1)
        long = (labels == ahead) & (lanes < total - NARROW) & (labels != big)
        too_long = jnp.max(long.astype(jnp.int32)) == 1
        n2, n3, nx = counts_ref[0], counts_ref[1], counts_ref[2]
        one_label = occ_ref[0] == pair_label
        form = jnp.where((nx <= FEW_CAPS[0]) & (n3 <= CAPS[0]), 3, jnp.where(nx <= FEW_CAPS[1], 4, 5))
        form = jnp.where(mostly_zero, form, 5)
        form = jnp.where((n3 <= FEW_WIDE) & (n2 <= CAPS[0]), 2, form)
        form = jnp.where(one_label, form, 6)
        form = jnp.where(n3 == 0, jnp.where(n2 <= CAPS[0], 0, 1), form)
        form_ref[0] = jnp.where(too_long, 6, form)


def wide_blocks(integrals, occ_irrep, vir_irrep, screen, place, batch):
    occ_share, depth, total = integrals.shape
    shapes = [(n, depth // 2, FOLD) for n in CAPS] + [(n, depth, FOLD) for n in CAPS]
    few = (FEW_CAPS[-1], 3, depth // 2, 2 * NARROW)
    smem = pl.BlockSpec(memory_space=pltpu.SMEM)

    def kernel(*refs):
        wide_kernel(*refs, batch)

    return pl.pallas_call(
        kernel,
        grid_spec=pltpu.PrefetchScalarGridSpec(
            num_scalar_prefetch=4,
            grid=(occ_share // K_STEP,),
            in_specs=[
                pl.BlockSpec((K_STEP, depth, total), lambda k, *_: (k, 0, 0)),
                pl.BlockSpec((1, total), lambda k, *_: (0, 0)),
            ],
            out_specs=[pl.BlockSpec(few, lambda k, *_: (0, 0, 0, 0))]
            + [pl.BlockSpec(v, lambda k, *_: (0, 0, 0)) for v in shapes]
            + [smem] * 4,
            scratch_shapes=[
                pltpu.VMEM((depth, total), jnp.bfloat16),
                pltpu.VMEM((depth, total), jnp.bfloat16),
                pltpu.VMEM((total, 8), jnp.int32),
                pltpu.SMEM((3,), jnp.int32),
            ],
        ),
        out_shape=[jax.ShapeDtypeStruct(v, jnp.bfloat16) for v in [few] + shapes]
        + [jax.ShapeDtypeStruct((n,), jnp.int32) for n in (occ_share, occ_share, occ_share, 1)],
        cost_estimate=cost(5),
        compiler_params=pltpu.CompilerParams(vmem_limit_bytes=24 * 1024 * 1024),
    )(occ_irrep, vir_irrep, screen.T, place, integrals, vir_irrep[None, :])


def narrow_kernel(
    occ_ref, vir_ref, screen_ref, place_ref, int_ref, row_ref, narrow_ref, mix_ref, column_ref, batch,
):
    step = pl.program_id(0)
    k_step, depth, total = int_ref.shape
    row, col = place_ref[0], place_ref[1]

    @pl.when(step == 0)
    def _():
        label_mix(mix_ref, column_ref, row_ref, row, largest_irrep(vir_ref), False)

    local = column_ref[pl.ds(pl.multiple_of(row * depth, depth), depth), :1]
    for j in range(k_step):
        k_whole = (col * pl.num_programs(0) + step) * k_step + j
        x = jnp.bitwise_xor(occ_ref[k_whole], occ_ref[batch])
        kept = kept_folded(int_ref, mix_ref, j, x)
        narrow_ref[j] = narrow_fold(kept, screen_bits(screen_ref, k_whole), local)


def narrow_blocks(integrals, occ_irrep, vir_irrep, screen, place, batch):
    occ_share, depth, total = integrals.shape
    shape = (depth // 2, 2 * NARROW)

    def kernel(*refs):
        narrow_kernel(*refs, batch)

    return pl.pallas_call(
        kernel,
        grid_spec=pltpu.PrefetchScalarGridSpec(
            num_scalar_prefetch=4,
            grid=(occ_share // K_STEP,),
            in_specs=[
                pl.BlockSpec((K_STEP, depth, total), lambda k, *_: (k, 0, 0)),
                pl.BlockSpec((1, total), lambda k, *_: (0, 0)),
            ],
            out_specs=pl.BlockSpec((K_STEP,) + shape, lambda k, *_: (k, 0, 0)),
            scratch_shapes=[pltpu.VMEM((depth, total), jnp.bfloat16), pltpu.VMEM((total, 8), jnp.int32)],
        ),
        out_shape=jax.ShapeDtypeStruct((occ_share,) + shape, jnp.bfloat16),
        cost_estimate=cost(5),
        compiler_params=pltpu.CompilerParams(vmem_limit_bytes=16 * 1024 * 1024),
    )(occ_irrep, vir_irrep, screen.T, place, integrals, vir_irrep[None, :])


def cost(micros):
    return pl.CostEstimate(flops=int(micros * 1e9), bytes_accessed=int(micros * 3e6), transcendentals=0)


SLOTS = (0, 1, 3, 2)
NEAR = 3


def amplitude_rows(column_ref, row_ref, occ_ref, row, batch, share):
    column_ref[...] = label_columns(row_ref[...])
    column = column_ref[pl.ds(pl.multiple_of(row * share, share), share), :1]
    return jnp.concatenate([jnp.bitwise_xor(column, occ_ref[i]) for i in range(batch)], axis=0)


def write_quarters(total_ref, col, outs):
    rows, fold = total_ref.shape
    width, height = fold // 2, rows // 2
    for t, out_ref in enumerate(outs):
        goal = jnp.bitwise_xor(col, t)
        lanes = pl.ds(pl.multiple_of((goal % 2) * width, width), width)
        lines = pl.ds(pl.multiple_of((goal // 2) * height, height), height)
        out_ref[...] = total_ref[lines, lanes].reshape(out_ref.shape)


def chosen(refs, starts, pos, pick):
    block = None
    for n, group in enumerate(refs):
        inside = (pos >= starts[n]) & (pos < starts[n + 1])
        at = jnp.clip(pos - starts[n], 0, starts[n + 1] - starts[n] - 1)
        found = pick(group, at)
        found = jnp.where(inside, found, jnp.zeros_like(found))
        block = found if block is None else block + found
    return block


def starts_of(arrays):
    starts = [0]
    for v in arrays:
        starts.append(starts[-1] + v.shape[0])
    return starts


def mask_kernel(occ_ref, place_ref, amp_ref, row_ref, lhs_ref, far_ref, fold_ref, mix_ref, column_ref, amp_buffer, sems):
    batch, k_all, share, total = amp_ref.shape
    rows, groups = batch * share, k_all // K_STEP
    row, col = place_ref[0], place_ref[1]

    def fetch(group):
        slot = group % 2
        source = amp_ref.at[:, pl.ds(group * K_STEP, K_STEP)]
        return pltpu.make_async_copy(source, amp_buffer.at[slot], sems.at[slot])

    fetch(0).start()
    column = amplitude_rows(column_ref, row_ref, occ_ref, row, batch, share)
    mix_ref[...] = as_bf16(jnp.bitwise_xor(column, row_ref[...]))

    @pl.loop(0, groups)
    def _(group):
        slot = group % 2

        @pl.when(group + 1 < groups)
        def _():
            fetch(group + 1).start()

        fetch(group).wait()

        @pl.loop(0, K_STEP)
        def _(j):
            wanted = as_bf16(jnp.full((rows, share), occ_ref[col * k_all + group * K_STEP + j]))
            folded = None
            for n, s in enumerate(SLOTS):
                place = pl.ds(pl.multiple_of(jnp.bitwise_xor(row, s) * share, share), share)
                tile = amp_buffer[slot, :, j, :, place].reshape(rows, share)
                piece = jnp.where(mix_ref[:, place] == wanted, tile, jnp.zeros_like(tile))
                if n < NEAR:
                    lhs_ref[group, :, pl.ds(pl.multiple_of((n * K_STEP + j) * share, share), share)] = piece
                else:
                    far_ref[group, :, pl.ds(pl.multiple_of(j * share, share), share)] = piece
                folded = piece if folded is None else folded + piece
            fold_ref[group, :, pl.ds(pl.multiple_of(j * share, share), share)] = folded


def masked_amplitudes(amplitudes, occ_irrep, vir_irrep, place):
    batch, k_all, share, total = amplitudes.shape
    rows, groups = batch * share, k_all // K_STEP
    smem = pl.BlockSpec(memory_space=pltpu.SMEM)
    vmem = pl.BlockSpec(memory_space=pltpu.VMEM)
    hbm = pl.BlockSpec(memory_space=pltpu.HBM)
    widths = (NEAR * K_STEP * share, K_STEP * share, K_STEP * share)
    return pl.pallas_call(
        mask_kernel,
        in_specs=[smem, smem, hbm, vmem],
        out_specs=[vmem] * 3,
        out_shape=[jax.ShapeDtypeStruct((groups, rows, w), jnp.bfloat16) for w in widths],
        scratch_shapes=[
            pltpu.VMEM((rows, total), jnp.bfloat16),
            pltpu.VMEM((total, 8), jnp.int32),
            pltpu.VMEM((2, batch, K_STEP, share, total), jnp.bfloat16),
            pltpu.SemaphoreType.DMA((2,)),
        ],
        cost_estimate=cost(7),
        compiler_params=pltpu.CompilerParams(vmem_limit_bytes=28 * 1024 * 1024),
    )(occ_irrep, place, amplitudes, vir_irrep[None, :])


def make_first_kernel(few, n3, starts3):
    def kernel(pos3_ref, posx_ref, place_ref, lhs_ref, far_ref, *refs):
        sources = 5 if few else 6
        narrow_refs, refs = refs[:sources], refs[sources:]
        m3_refs = [refs[3 * n:3 * n + 3] for n in range(n3)]
        narrow_sum, wide_sum, narrow_rhs, wide_rhs = refs[3 * n3:]
        row = place_ref[0]
        at_end = (row == 0) | (row == 3)
        groups, _, depth = lhs_ref.shape
        share = depth // (NEAR * K_STEP)
        half = share // 2
        lane = lax.broadcasted_iota(jnp.int32, (half, 2 * NARROW), 1)

        narrow_sum[...] = jnp.zeros(narrow_sum.shape, jnp.float32)
        wide_sum[...] = jnp.zeros(wide_sum.shape, jnp.float32)

        @pl.loop(0, groups)
        def _(group):
            @pl.loop(0, K_STEP)
            def _(j):
                k = group * K_STEP + j
                if few:
                    own, e1, o1 = [ref[k] for ref in narrow_refs[:3]]
                    posx = posx_ref[k]
                    two, three = [ref[jnp.maximum(posx, 0), 0] for ref in narrow_refs[3:]]
                    two, three = [jnp.where(posx >= 0, v, jnp.zeros_like(v)) for v in (two, three)]
                    blocks = (own, e1, jnp.where(at_end, three, o1), two)
                else:
                    own, e1, o1, e2, o2, e3 = [ref[k] for ref in narrow_refs]
                    blocks = (own, e1, jnp.where(at_end, e3, o1), jnp.where(at_end, e2, o2))
                for n, block in enumerate(blocks):
                    zero = jnp.zeros_like(block)
                    first = pl.multiple_of((n * K_STEP + j) * share, share)
                    narrow_rhs[pl.ds(first, half)] = jnp.where(lane < NARROW, block, zero)
                    narrow_rhs[pl.ds(first + half, half)] = jnp.where(lane < NARROW, zero, block)
                for n in range(3 if n3 else 0):
                    block = chosen(m3_refs, starts3, pos3_ref[k], lambda group, at, n=n: group[n][at])
                    if n == 2:
                        block = jnp.where(at_end, jnp.zeros_like(block), block)
                    wide_rhs[pl.ds(pl.multiple_of((n * K_STEP + j) * share, share), share)] = block

            narrow = jnp.dot(lhs_ref[group], narrow_rhs[:depth], preferred_element_type=jnp.float32)
            narrow += jnp.dot(far_ref[group], narrow_rhs[depth:], preferred_element_type=jnp.float32)
            narrow_sum[...] += narrow
            if n3:
                wide_sum[...] += jnp.dot(lhs_ref[group], wide_rhs[...], preferred_element_type=jnp.float32)

    return kernel


def first_product(lhs, far_lhs, pos3, posx, place, narrow, few, m3):
    groups, rows, depth = lhs.shape
    vmem = pl.BlockSpec(memory_space=pltpu.VMEM)
    smem = pl.BlockSpec(memory_space=pltpu.SMEM)
    arrays = list(narrow) + [v for group in m3 for v in group]
    wide = (rows, FOLD) if m3 else (16, FOLD)
    wide_depth = depth if m3 else 16
    return pl.pallas_call(
        make_first_kernel(few, len(m3), starts_of([v[0] for v in m3])),
        in_specs=[smem] * 3 + [vmem] * (2 + len(arrays)),
        out_specs=[vmem] * 2,
        out_shape=[jax.ShapeDtypeStruct(v, jnp.float32) for v in ((rows, 2 * NARROW), wide)],
        scratch_shapes=[
            pltpu.VMEM((depth // NEAR * len(SLOTS), 2 * NARROW), jnp.bfloat16),
            pltpu.VMEM((wide_depth, FOLD), jnp.bfloat16),
        ],
        cost_estimate=cost(9 if m3 else 6),
        compiler_params=pltpu.CompilerParams(vmem_limit_bytes=32 * 1024 * 1024),
    )(pos3, posx, place, lhs, far_lhs, *arrays)


def make_last_kernel(few, n2, starts2, n3, starts3):
    def kernel(occ_ref, vir_ref, pos2_ref, pos3_ref, place_ref, fold_ref, far_ref, row_ref, narrow_ref, wide_ref, *refs):
        m2_refs = refs[:n2]
        m3_refs = [refs[n2 + 2 * n:n2 + 2 * n + 2] for n in range(n3)]
        refs = refs[n2 + 2 * n3:]
        outs = refs[:4]
        column_ref, total_ref, short_rhs, far_rhs = refs[4:]
        row, col = place_ref[0], place_ref[1]
        at_end = (row == 0) | (row == 3)
        groups, rows, width = fold_ref.shape
        share = width // K_STEP
        batch = rows // share
        @pl.loop(0, groups * K_STEP)
        def _(k):
            here = pl.ds(pl.multiple_of(k * share, share), share)
            if few:
                pos2 = pos2_ref[k]
                pieces = []
                for piece in (1, 2):
                    own, one, two, three = [ref[jnp.maximum(pos2, 0), piece] for ref in m2_refs]
                    block = own + one + two + three
                    pieces.append(jnp.where(pos2 >= 0, block, jnp.zeros_like(block)))
                short = jnp.concatenate(pieces, axis=1)
            else:
                short = chosen(m2_refs, starts2, pos2_ref[k], lambda ref, at: ref[at])
            short_rhs[here] = jnp.concatenate([short, short], axis=0)
            if n3:
                far_rhs[here] = chosen(
                    m3_refs, starts3, pos3_ref[k], lambda pair, at: jnp.where(at_end, pair[0][at], pair[1][at])
                )

        column = amplitude_rows(column_ref, row_ref, occ_ref, row, batch, share)
        target = jnp.bitwise_xor(column, occ_ref[batch])
        both = narrow_ref[...]
        both = both + pltpu.roll(both, NARROW, 1)
        both = jnp.concatenate([both] * (FOLD // (2 * NARROW)), axis=1)
        part = wide_ref[...] if n3 else 0.0
        for group in range(groups):
            here = pl.ds(group * width, width)
            part += jnp.dot(fold_ref[group], short_rhs[here], preferred_element_type=jnp.float32)
            if n3:
                part += jnp.dot(far_ref[group], far_rhs[here], preferred_element_type=jnp.float32)
        total_ref[...] = jnp.where(target == largest_irrep(vir_ref), part, both)
        write_quarters(total_ref, col, outs)

    return kernel


def last_product(far_lhs, fold, occ_irrep, vir_irrep, pos2, pos3, place, narrow_sum, wide_sum, few, m2, m3, batch):
    groups, rows, width = fold.shape
    share = rows // batch
    vmem = pl.BlockSpec(memory_space=pltpu.VMEM)
    smem = pl.BlockSpec(memory_space=pltpu.SMEM)
    arrays = [narrow_sum, wide_sum] + list(m2) + [v for group in m3 for v in group]
    quarter = (batch // 2, share, FOLD // 2)
    whole = groups * width
    far_lhs = far_lhs if m3 else jnp.zeros((8, 128), jnp.bfloat16)
    return pl.pallas_call(
        make_last_kernel(few, len(m2), starts_of(m2), len(m3), starts_of([v[0] for v in m3])),
        in_specs=[smem] * 5 + [vmem] * (3 + len(arrays)),
        out_specs=[vmem] * 4,
        out_shape=[jax.ShapeDtypeStruct(quarter, jnp.float32)] * 4,
        scratch_shapes=[
            pltpu.VMEM((vir_irrep.shape[0], 8), jnp.int32),
            pltpu.VMEM((rows, FOLD), jnp.float32),
            pltpu.VMEM((whole, FOLD), jnp.bfloat16),
            pltpu.VMEM((whole if m3 else 16, FOLD), jnp.bfloat16),
        ],
        cost_estimate=cost(4 if m3 else 2),
        compiler_params=pltpu.CompilerParams(vmem_limit_bytes=32 * 1024 * 1024),
    )(occ_irrep, vir_irrep, pos2, pos3, place, fold, far_lhs, vir_irrep[None, :], *arrays)


def dense_product(amplitudes, whole, occ_irrep, occ_local, vir_local, vir_irrep):
    batch = amplitudes.shape[0]
    keep = (
        jnp.bitwise_xor(occ_irrep[:batch, None], occ_local[None, :])[:, :, None, None]
        == jnp.bitwise_xor(vir_local[:, None], vir_irrep[None, :])[None, None]
    )
    kept = jnp.where(keep, amplitudes, jnp.zeros_like(amplitudes))
    return lax.dot_general(
        kept, whole, (((1, 3), (0, 1)), ((), ())), preferred_element_type=jnp.float32
    )


def finish(cycle, occ_irrep, vir_irrep, occ_energy, vir_energy, a_start, a_size, b_start, b_size, batch):
    label_a = lax.dynamic_slice_in_dim(vir_irrep, a_start, a_size)
    label_b = lax.dynamic_slice_in_dim(vir_irrep, b_start, b_size)
    energy_a = lax.dynamic_slice_in_dim(vir_energy, a_start, a_size)
    energy_b = lax.dynamic_slice_in_dim(vir_energy, b_start, b_size)
    target = jnp.bitwise_xor(
        jnp.bitwise_xor(occ_irrep[:batch, None], occ_irrep[batch]), label_a[None, :]
    )
    keep = label_b[:, None, None] == target[None, :, :]
    denominator = (
        occ_energy[:batch][None, :, None]
        + occ_energy[batch]
        - energy_a[None, None, :]
        - energy_b[:, None, None]
    )
    swapped = jnp.transpose(cycle, (2, 0, 1))
    return jnp.where(keep, swapped, 0.0) / denominator


def on_square(amplitudes, integrals, occ_irrep, vir_irrep, screen):
    batch, occ_share, share, vir_total = amplitudes.shape
    row = lax.axis_index("row")
    col = lax.axis_index("col")
    place = jnp.stack([row, col]).astype(jnp.int32)
    few, m2a, m2b, m3a, m3b, pos2, pos3, posx, form = wide_blocks(
        integrals, occ_irrep, vir_irrep, screen, place, batch
    )
    outer = [(0, 1), (1, 0), (2, 3), (3, 2)]
    inner = [(1, 2), (2, 1)]
    inward = [(0, 1), (3, 2)]
    outward = [(1, 0), (2, 3)]

    def move(v, pairs):
        return lax.ppermute(v, "row", pairs)

    def sparse(use_few, choose):
        def run(few, m2a, m2b, m3a, m3b):
            shorts, wides = choose(m2a, m2b, m3a, m3b)
            if use_few:
                few = few[:use_few]
                one, two, three = [move(few, [(r, r ^ t) for r in range(4)]) for t in (1, 2, 3)]
                wides, one, two, three = lax.optimization_barrier((wides, one, two, three))
            near = [(own, move(own, outer), move(own, inner)) for own in wides]
            narrow = narrow_blocks(integrals, occ_irrep, vir_irrep, screen, place, batch)
            if use_few:
                e1, o1 = move(narrow, outer), move(narrow, inner)
                lhs, far_lhs, fold = masked_amplitudes(amplitudes, occ_irrep, vir_irrep, place)
                near, e1, o1, _ = lax.optimization_barrier((near, e1, o1, fold))
                blocks = (narrow, e1, o1, two, three)
                sums = (few, one, two, three)
            else:
                h1 = [move(v, inward) for v in shorts]
                o1, e1 = move(narrow, inner), move(narrow, outward)
                lhs, far_lhs, fold = masked_amplitudes(amplitudes, occ_irrep, vir_irrep, place)
                near, h1, o1, e1, _ = lax.optimization_barrier((near, h1, o1, e1, fold))
                h2 = [move(own + v, inner) for own, v in zip(shorts, h1)]
                e1 = e1 + move(narrow, inward)
                e2 = move(o1, outward)
                h2, e1, e2 = lax.optimization_barrier((h2, e1, e2))
                h3 = [move(own + v, outward) for own, v in zip(shorts, h2)]
                o2 = move(e1, inner)
                blocks = (narrow, e1, o1, e2, o2, move(o2, outward))
                sums = [a + b + c + d for a, b, c, d in zip(shorts, h1, h2, h3)]
            far = [(move(o, outward), move(e, inner)) for _, e, o in near]
            narrow_sum, wide_sum = first_product(
                lhs, far_lhs, pos3, posx, place, blocks, bool(use_few), near
            )
            return list(last_product(
                far_lhs, fold, occ_irrep, vir_irrep, pos2, pos3, place, narrow_sum, wide_sum, bool(use_few), sums,
                far, batch
            ))

        return run

    def dense(*_):
        occ_local = lax.dynamic_slice_in_dim(occ_irrep, col * occ_share, occ_share)
        vir_local = lax.dynamic_slice_in_dim(vir_irrep, row * share, share)
        screen_rows = lax.dynamic_slice_in_dim(screen, col * occ_share, occ_share, 0)
        fold = folded_integrals(
            integrals, occ_local, vir_local, vir_irrep, occ_irrep[batch], screen_rows
        )
        whole = jnp.zeros((occ_share, vir_total, FOLD), fold.dtype)
        for s in range(4):
            block = move(fold, [(r, r ^ s) for r in range(4)]) if s else fold
            whole = lax.dynamic_update_slice_in_dim(whole, block, jnp.bitwise_xor(row, s) * share, 1)
        total = dense_product(amplitudes, whole, occ_irrep, occ_local, vir_local, vir_irrep)
        quarter = (batch // 2, share, FOLD // 2)
        goals = [jnp.bitwise_xor(col, t) for t in range(4)]
        return [
            lax.dynamic_slice(total, (g // 2 * quarter[0], 0, g % 2 * quarter[2]), quarter) for g in goals
        ]

    branches = [
        sparse(0, lambda m2a, m2b, m3a, m3b: ([m2a], [])),
        sparse(0, lambda m2a, m2b, m3a, m3b: ([m2a, m2b], [])),
        sparse(0, lambda m2a, m2b, m3a, m3b: ([m2a], [m3a[:FEW_WIDE]])),
        sparse(FEW_CAPS[0], lambda m2a, m2b, m3a, m3b: ([], [m3a])),
        sparse(FEW_CAPS[1], lambda m2a, m2b, m3a, m3b: ([], [m3a, m3b])),
        sparse(0, lambda m2a, m2b, m3a, m3b: ([m2a, m2b], [m3a, m3b])),
        dense,
    ]
    quarters = lax.switch(form[0], branches, few, m2a, m2b, m3a, m3b)
    mine = quarters[0]
    for t in (1, 2, 3):
        mine = mine + lax.ppermute(quarters[t], "col", [(q, q ^ t) for q in range(4)])
    places = [(r, q) for r in range(4) for q in range(4)]
    same = lax.ppermute(mine, ("row", "col"), [(r * 4 + q, q * 4 + r) for r, q in places])
    other = lax.ppermute(mine, ("row", "col"), [(r * 4 + q, (q ^ 2) * 4 + r) for r, q in places])
    upper = row // 2 == 1
    low = jnp.where(upper, other, same)
    high = jnp.where(upper, same, other)
    return jnp.concatenate([low, high], axis=0)


def on_any(amplitudes, integrals, occ_irrep, vir_irrep, screen):
    batch, occ_share, share, vir_total = amplitudes.shape
    row = lax.axis_index("row")
    col = lax.axis_index("col")
    occ_local = lax.dynamic_slice_in_dim(occ_irrep, col * occ_share, occ_share)
    vir_local = lax.dynamic_slice_in_dim(vir_irrep, row * share, share)
    screen_rows = lax.dynamic_slice_in_dim(screen, col * occ_share, occ_share, 0)
    fold = folded_integrals(
        integrals, occ_local, vir_local, vir_irrep, occ_irrep[batch], screen_rows
    )
    whole = lax.all_gather(fold, "row", axis=1, tiled=True)
    cycle = dense_product(amplitudes, whole, occ_irrep, occ_local, vir_local, vir_irrep)
    cycle = lax.psum(cycle, "col")
    cycle = jnp.concatenate([cycle] * (vir_total // FOLD), axis=2)
    cycle = lax.all_to_all(cycle, "row", split_axis=2, concat_axis=1, tiled=True)
    a_size = vir_total // lax.axis_size("col")
    return lax.dynamic_slice_in_dim(cycle, col * a_size, a_size, 1)


def on_device(amplitudes, integrals, occ_irrep, vir_irrep, screen, occ_energy, vir_energy):
    batch, _, vir_share, vir_total = amplitudes.shape
    square = lax.axis_size("row") == 4 and lax.axis_size("col") == 4
    form = on_square if square else on_any
    cycle = form(amplitudes, integrals, occ_irrep, vir_irrep, screen)
    a_size = vir_total // lax.axis_size("col")
    return finish(
        cycle, occ_irrep, vir_irrep, occ_energy, vir_energy,
        lax.axis_index("col") * a_size, a_size, lax.axis_index("row") * vir_share, vir_share, batch,
    )


def solution(mesh):
    in_specs = (
        P("parts", "col", "row", None),
        P(("parts", "col"), "row", None),
        P("parts"),
        P("parts"),
        P("parts", None),
        P("parts"),
        P("parts"),
    )
    out_specs = P("row", "parts", "col")
    return jax.shard_map(
        on_device, mesh=mesh, in_specs=in_specs, out_specs=out_specs, check_vma=False
    )
```

```python
import jax
import jax.numpy as jnp
from jax import lax
from jax.experimental import pallas as pl
from jax.experimental.pallas import tpu as pltpu
from jax.sharding import PartitionSpec as P

FOLD = 256
K_STEP = 5


def folded_integrals(integrals, occ_local, vir_local, vir_irrep, pair_label, screen_rows):
    irrep_codes = jnp.arange(8, dtype=jnp.int32)
    screen_local = jnp.sum(
        screen_rows[:, None, :] * (vir_local[None, :, None] == irrep_codes).astype(jnp.int32),
        axis=2,
    )
    target = jnp.bitwise_xor(
        jnp.bitwise_xor(occ_local[:, None], vir_local[None, :]), pair_label
    )
    target = jnp.where(screen_local == 1, target, -1)
    keep = target[:, :, None] == vir_irrep[None, None, :]
    kept = jnp.where(keep, integrals, jnp.zeros_like(integrals))
    return kept[:, :, :FOLD] + kept[:, :, FOLD:]


NARROW = 64
CAPS = (22, 3)
FEW_CAPS = (4, 10)
FEW_WIDE = 5


def largest_irrep(vir_ref):
    return jnp.where(vir_ref[0] == vir_ref[FOLD - 1], vir_ref[0], vir_ref[FOLD])


def label_columns(row_labels):
    return jnp.transpose(jnp.broadcast_to(row_labels, (8, row_labels.shape[1])))


def as_bf16(labels):
    return labels.astype(jnp.float32).astype(jnp.bfloat16)


def label_mix(mix_ref, column_ref, row_ref, row, big, keep_big):
    depth = mix_ref.shape[0]
    column_ref[...] = label_columns(row_ref[...])
    column = column_ref[pl.ds(pl.multiple_of(row * depth, depth), depth), :1]
    is_big = row_ref[...] == big
    wanted = is_big if keep_big else jnp.logical_not(is_big)
    mix_ref[...] = as_bf16(jnp.where(wanted, jnp.bitwise_xor(column, row_ref[...]), 8))


def kept_folded(int_ref, mix_ref, j, x):
    tile = int_ref[j]
    wanted = as_bf16(jnp.full(mix_ref.shape, x))
    kept = jnp.where(mix_ref[...] == wanted, tile, jnp.zeros_like(tile))
    return kept[:, :FOLD] + kept[:, FOLD:]


def narrow_fold(kept, bits, local):
    half = kept.shape[0] // 2
    lane = lax.broadcasted_iota(jnp.int32, (half, 2 * NARROW), 1)
    narrow = (kept[:, : 2 * NARROW] + kept[:, 2 * NARROW:]).astype(jnp.float32)
    narrow = narrow + pltpu.roll(narrow, NARROW, 1)
    on = jnp.bitwise_and(lax.shift_right_logical(jnp.full(local.shape, bits), local), 1) == 1
    narrow = jnp.where(on, narrow, 0.0)
    return jnp.where(lane < NARROW, narrow[:half], narrow[half:]).astype(jnp.bfloat16)


def screen_bits(screen_ref, k):
    bits = screen_ref[0, k]
    for g in range(1, 8):
        bits = bits + screen_ref[g, k] * (1 << g)
    return bits


def wide_kernel(
    occ_ref, vir_ref, screen_ref, place_ref, int_ref, row_ref,
    few_ref, m2a_ref, m2b_ref, m3a_ref, m3b_ref, pos2_ref, pos3_ref, posx_ref, form_ref, count_ref,
    mix_ref, small_mix_ref, column_ref, counts_ref, batch,
):
    step = pl.program_id(0)
    k_step, depth, total = int_ref.shape
    half = depth // 2
    row, col = place_ref[0], place_ref[1]
    pair_label = occ_ref[batch]
    big = largest_irrep(vir_ref)
    k_all = k_step * pl.num_programs(0)
    mostly_zero = (occ_ref[col * k_all] == pair_label) | (occ_ref[(col + 1) * k_all - 1] == pair_label)
    most = FEW_CAPS[-1]

    @pl.when(step == 0)
    def _():
        for n in range(3):
            counts_ref[n] = 0
        label_mix(mix_ref, column_ref, row_ref, row, big, True)

        @pl.when(mostly_zero)
        def _():
            label_mix(small_mix_ref, column_ref, row_ref, row, big, False)

    local = column_ref[pl.ds(pl.multiple_of(row * depth, depth), depth), :1]

    @pl.loop(0, k_step)
    def _(j):
        k = step * k_step + j
        k_whole = col * k_all + k
        x = jnp.bitwise_xor(occ_ref[k_whole], pair_label)
        on_big = screen_ref[jnp.bitwise_xor(big, x), k_whole] == 1
        actives = (on_big & (x != 0), on_big & (x == 0), x != 0)
        pos2, pos3, posx = [jnp.where(active, counts_ref[n], -1) for n, active in enumerate(actives)]
        for n, active in enumerate(actives):
            counts_ref[n] = counts_ref[n] + active.astype(jnp.int32)
        pos2_ref[k], pos3_ref[k], posx_ref[k] = pos2, pos3, posx

        @pl.when(pos2 >= 0)
        def _():
            wide = kept_folded(int_ref, mix_ref, j, x)
            short = wide[:half] + wide[half:]

            @pl.when(mostly_zero & (pos2 < most))
            def _():
                for piece in range(2):
                    few_ref[pos2, 1 + piece] = short[:, piece * 2 * NARROW:(piece + 1) * 2 * NARROW]

            @pl.when(pos2 < CAPS[0])
            def _():
                m2a_ref[pos2] = short

            @pl.when(pos2 >= CAPS[0])
            def _():
                m2b_ref[pos2 - CAPS[0]] = short

        @pl.when(mostly_zero & (posx >= 0) & (posx < most))
        def _():
            kept = kept_folded(int_ref, small_mix_ref, j, x)
            few_ref[posx, 0] = narrow_fold(kept, screen_bits(screen_ref, k_whole), local)

        @pl.when(pos3 >= 0)
        def _():
            wide = kept_folded(int_ref, mix_ref, j, x)

            @pl.when(pos3 < CAPS[0])
            def _():
                m3a_ref[pos3] = wide

            @pl.when(pos3 >= CAPS[0])
            def _():
                m3b_ref[pos3 - CAPS[0]] = wide

    @pl.when(step == pl.num_programs(0) - 1)
    def _():
        labels = row_ref[...]
        lanes = lax.broadcasted_iota(jnp.int32, labels.shape, 1)
        ahead = pltpu.roll(labels, total - NARROW, 1)
        long = (labels == ahead) & (lanes < total - NARROW) & (labels != big)
        too_long = jnp.max(long.astype(jnp.int32)) == 1
        n2, n3, nx = counts_ref[0], counts_ref[1], counts_ref[2]
        count_ref[0] = nx
        one_label = occ_ref[0] == pair_label
        form = jnp.where((nx <= FEW_CAPS[0]) & (n3 <= CAPS[0]), 3, jnp.where(nx <= FEW_CAPS[1], 4, 5))
        form = jnp.where(mostly_zero, form, 5)
        form = jnp.where((n3 <= FEW_WIDE) & (n2 <= CAPS[0]), 2, form)
        form = jnp.where(one_label, form, 6)
        form = jnp.where(n3 == 0, jnp.where(n2 <= CAPS[0], 0, 1), form)
        form_ref[0] = jnp.where(too_long, 6, form)


def wide_blocks(integrals, occ_irrep, vir_irrep, screen, place, batch):
    occ_share, depth, total = integrals.shape
    shapes = [(n, depth // 2, FOLD) for n in CAPS] + [(n, depth, FOLD) for n in CAPS]
    few = (FEW_CAPS[-1], 3, depth // 2, 2 * NARROW)
    smem = pl.BlockSpec(memory_space=pltpu.SMEM)

    def kernel(*refs):
        wide_kernel(*refs, batch)

    return pl.pallas_call(
        kernel,
        grid_spec=pltpu.PrefetchScalarGridSpec(
            num_scalar_prefetch=4,
            grid=(occ_share // K_STEP,),
            in_specs=[
                pl.BlockSpec((K_STEP, depth, total), lambda k, *_: (k, 0, 0)),
                pl.BlockSpec((1, total), lambda k, *_: (0, 0)),
            ],
            out_specs=[pl.BlockSpec(few, lambda k, *_: (0, 0, 0, 0))]
            + [pl.BlockSpec(v, lambda k, *_: (0, 0, 0)) for v in shapes]
            + [smem] * 5,
            scratch_shapes=[
                pltpu.VMEM((depth, total), jnp.bfloat16),
                pltpu.VMEM((depth, total), jnp.bfloat16),
                pltpu.VMEM((total, 8), jnp.int32),
                pltpu.SMEM((3,), jnp.int32),
            ],
        ),
        out_shape=[jax.ShapeDtypeStruct(v, jnp.bfloat16) for v in [few] + shapes]
        + [jax.ShapeDtypeStruct((n,), jnp.int32) for n in (occ_share, occ_share, occ_share, 1, 1)],
        cost_estimate=cost(5),
        compiler_params=pltpu.CompilerParams(vmem_limit_bytes=24 * 1024 * 1024),
    )(occ_irrep, vir_irrep, screen.T, place, integrals, vir_irrep[None, :])


def narrow_kernel(
    occ_ref, vir_ref, screen_ref, place_ref, int_ref, row_ref, few_ref, narrow_ref, mix_ref, column_ref, batch,
):
    step = pl.program_id(0)
    k_step, depth, total = int_ref.shape
    row, col = place_ref[0], place_ref[1]

    @pl.when(step == 0)
    def _():
        label_mix(mix_ref, column_ref, row_ref, row, largest_irrep(vir_ref), False)
        if few_ref is not None:
            for n in range(few_ref.shape[0]):
                for piece in range(2):
                    narrow_ref[k_step * pl.num_programs(0) + 2 * n + piece] = few_ref[n, 1 + piece]

    local = column_ref[pl.ds(pl.multiple_of(row * depth, depth), depth), :1]
    for j in range(k_step):
        k_whole = (col * pl.num_programs(0) + step) * k_step + j
        x = jnp.bitwise_xor(occ_ref[k_whole], occ_ref[batch])
        kept = kept_folded(int_ref, mix_ref, j, x)
        narrow_ref[step * k_step + j] = narrow_fold(kept, screen_bits(screen_ref, k_whole), local)


def narrow_blocks(integrals, occ_irrep, vir_irrep, screen, place, few, batch):
    occ_share, depth, total = integrals.shape
    extra = [] if few is None else [few]
    count = occ_share + sum(2 * v.shape[0] for v in extra)
    shape = (count, depth // 2, 2 * NARROW)

    def kernel(*refs):
        narrow_kernel(*(refs if extra else refs[:6] + (None,) + refs[6:]), batch)

    return pl.pallas_call(
        kernel,
        grid_spec=pltpu.PrefetchScalarGridSpec(
            num_scalar_prefetch=4,
            grid=(occ_share // K_STEP,),
            in_specs=[
                pl.BlockSpec((K_STEP, depth, total), lambda k, *_: (k, 0, 0)),
                pl.BlockSpec((1, total), lambda k, *_: (0, 0)),
            ] + [pl.BlockSpec(v.shape, lambda k, *_: (0, 0, 0, 0)) for v in extra],
            out_specs=pl.BlockSpec(shape, lambda k, *_: (0, 0, 0)),
            scratch_shapes=[pltpu.VMEM((depth, total), jnp.bfloat16), pltpu.VMEM((total, 8), jnp.int32)],
        ),
        out_shape=jax.ShapeDtypeStruct(shape, jnp.bfloat16),
        cost_estimate=cost(5),
        compiler_params=pltpu.CompilerParams(vmem_limit_bytes=16 * 1024 * 1024),
    )(occ_irrep, vir_irrep, screen.T, place, integrals, vir_irrep[None, :], *extra)


def cost(micros):
    return pl.CostEstimate(flops=int(micros * 1e9), bytes_accessed=int(micros * 3e6), transcendentals=0)


SLOTS = (0, 1, 3, 2)
NEAR = 3


def amplitude_rows(column_ref, row_ref, occ_ref, row, batch, share):
    column_ref[...] = label_columns(row_ref[...])
    column = column_ref[pl.ds(pl.multiple_of(row * share, share), share), :1]
    return jnp.concatenate([jnp.bitwise_xor(column, occ_ref[i]) for i in range(batch)], axis=0)


def write_quarters(total_ref, col, outs):
    rows, fold = total_ref.shape
    width, height = fold // 2, rows // 2
    for t, out_ref in enumerate(outs):
        goal = jnp.bitwise_xor(col, t)
        lanes = pl.ds(pl.multiple_of((goal % 2) * width, width), width)
        lines = pl.ds(pl.multiple_of((goal // 2) * height, height), height)
        out_ref[...] = total_ref[lines, lanes].reshape(out_ref.shape)


def chosen(refs, starts, pos, pick):
    block = None
    for n, group in enumerate(refs):
        inside = (pos >= starts[n]) & (pos < starts[n + 1])
        at = jnp.clip(pos - starts[n], 0, starts[n + 1] - starts[n] - 1)
        found = pick(group, at)
        found = jnp.where(inside, found, jnp.zeros_like(found))
        block = found if block is None else block + found
    return block


def starts_of(arrays):
    starts = [0]
    for v in arrays:
        starts.append(starts[-1] + v.shape[0])
    return starts


def mask_kernel(
    occ_ref, place_ref, posx_ref, amp_ref, row_ref, lhs_ref, far_ref, fold_ref, few_lhs_ref,
    mix_ref, column_ref, amp_buffer, sems,
):
    batch, k_all, share, total = amp_ref.shape
    rows, groups = batch * share, k_all // K_STEP
    row, col = place_ref[0], place_ref[1]

    def fetch(group):
        slot = group % 2
        source = amp_ref.at[:, pl.ds(group * K_STEP, K_STEP)]
        return pltpu.make_async_copy(source, amp_buffer.at[slot], sems.at[slot])

    fetch(0).start()
    column = amplitude_rows(column_ref, row_ref, occ_ref, row, batch, share)
    mix_ref[...] = as_bf16(jnp.bitwise_xor(column, row_ref[...]))
    if few_lhs_ref is not None:
        few_lhs_ref[...] = jnp.zeros(few_lhs_ref.shape, jnp.bfloat16)

    @pl.loop(0, groups)
    def _(group):
        slot = group % 2

        @pl.when(group + 1 < groups)
        def _():
            fetch(group + 1).start()

        fetch(group).wait()

        @pl.loop(0, K_STEP)
        def _(j):
            wanted = as_bf16(jnp.full((rows, share), occ_ref[col * k_all + group * K_STEP + j]))
            folded = None
            for n, s in enumerate(SLOTS):
                place = pl.ds(pl.multiple_of(jnp.bitwise_xor(row, s) * share, share), share)
                tile = amp_buffer[slot, :, j, :, place].reshape(rows, share)
                piece = jnp.where(mix_ref[:, place] == wanted, tile, jnp.zeros_like(tile))
                if n < NEAR:
                    lhs_ref[group, :, pl.ds(pl.multiple_of((n * K_STEP + j) * share, share), share)] = piece
                else:
                    far_ref[group, :, pl.ds(pl.multiple_of(j * share, share), share)] = piece
                folded = piece if folded is None else folded + piece
            fold_ref[group, :, pl.ds(pl.multiple_of(j * share, share), share)] = folded
            if few_lhs_ref is not None:
                posx = posx_ref[group * K_STEP + j]

                @pl.when((posx >= 0) & (posx < few_lhs_ref.shape[0]))
                def _():
                    third = lhs_ref[group, :, pl.ds(pl.multiple_of((2 * K_STEP + j) * share, share), share)]
                    few_lhs_ref[posx, 0] = third
                    few_lhs_ref[posx, 1] = far_ref[group, :, pl.ds(pl.multiple_of(j * share, share), share)]


def masked_amplitudes(amplitudes, occ_irrep, vir_irrep, place, posx, few):
    batch, k_all, share, total = amplitudes.shape
    rows, groups = batch * share, k_all // K_STEP
    smem = pl.BlockSpec(memory_space=pltpu.SMEM)
    vmem = pl.BlockSpec(memory_space=pltpu.VMEM)
    hbm = pl.BlockSpec(memory_space=pltpu.HBM)
    shapes = [(groups, rows, w) for w in (NEAR * K_STEP * share, K_STEP * share, K_STEP * share)]
    shapes += [(few, 2, rows, share)] if few else []

    def kernel(*refs):
        mask_kernel(*(refs if few else refs[:8] + (None,) + refs[8:]))

    return pl.pallas_call(
        kernel,
        in_specs=[smem, smem, smem, hbm, vmem],
        out_specs=[vmem] * len(shapes),
        out_shape=[jax.ShapeDtypeStruct(v, jnp.bfloat16) for v in shapes],
        scratch_shapes=[
            pltpu.VMEM((rows, total), jnp.bfloat16),
            pltpu.VMEM((total, 8), jnp.int32),
            pltpu.VMEM((2, batch, K_STEP, share, total), jnp.bfloat16),
            pltpu.SemaphoreType.DMA((2,)),
        ],
        cost_estimate=cost(7),
        compiler_params=pltpu.CompilerParams(vmem_limit_bytes=28 * 1024 * 1024),
    )(occ_irrep, place, posx, amplitudes, vir_irrep[None, :])


def make_first_kernel(few, n3, starts3):
    def kernel(pos3_ref, posx_ref, place_ref, lhs_ref, far_ref, *refs):
        sources = 3 if few else 6
        narrow_refs, refs = refs[:sources], refs[sources:]
        m3_refs = [refs[3 * n:3 * n + 3] for n in range(n3)]
        narrow_sum, wide_sum, narrow_rhs, wide_rhs = refs[3 * n3:]
        row = place_ref[0]
        at_end = (row == 0) | (row == 3)
        groups, _, depth = lhs_ref.shape
        share = depth // (NEAR * K_STEP)
        half = share // 2
        lane = lax.broadcasted_iota(jnp.int32, (half, 2 * NARROW), 1)

        narrow_sum[...] = jnp.zeros(narrow_sum.shape, jnp.float32)
        wide_sum[...] = jnp.zeros(wide_sum.shape, jnp.float32)

        @pl.loop(0, groups)
        def _(group):
            @pl.loop(0, K_STEP)
            def _(j):
                k = group * K_STEP + j
                if few:
                    blocks = [ref[k] for ref in narrow_refs]
                else:
                    own, e1, o1, e2, o2, e3 = [ref[k] for ref in narrow_refs]
                    blocks = (own, e1, jnp.where(at_end, e3, o1), jnp.where(at_end, e2, o2))
                for n, block in enumerate(blocks):
                    zero = jnp.zeros_like(block)
                    first = pl.multiple_of((n * K_STEP + j) * share, share)
                    narrow_rhs[pl.ds(first, half)] = jnp.where(lane < NARROW, block, zero)
                    narrow_rhs[pl.ds(first + half, half)] = jnp.where(lane < NARROW, zero, block)
                for n in range(3 if n3 else 0):
                    block = chosen(m3_refs, starts3, pos3_ref[k], lambda group, at, n=n: group[n][at])
                    if n == 2:
                        block = jnp.where(at_end, jnp.zeros_like(block), block)
                    wide_rhs[pl.ds(pl.multiple_of((n * K_STEP + j) * share, share), share)] = block

            narrow = jnp.dot(lhs_ref[group], narrow_rhs[:depth], preferred_element_type=jnp.float32)
            if not few:
                narrow += jnp.dot(far_ref[group], narrow_rhs[depth:], preferred_element_type=jnp.float32)
            narrow_sum[...] += narrow
            if n3:
                wide_sum[...] += jnp.dot(lhs_ref[group], wide_rhs[...], preferred_element_type=jnp.float32)

    return kernel


def first_product(lhs, far_lhs, pos3, posx, place, narrow, few, m3):
    groups, rows, depth = lhs.shape
    vmem = pl.BlockSpec(memory_space=pltpu.VMEM)
    smem = pl.BlockSpec(memory_space=pltpu.SMEM)
    arrays = list(narrow) + [v for group in m3 for v in group]
    wide = (rows, FOLD) if m3 else (16, FOLD)
    wide_depth = depth if m3 else 16
    return pl.pallas_call(
        make_first_kernel(few, len(m3), starts_of([v[0] for v in m3])),
        in_specs=[smem] * 3 + [vmem] * (2 + len(arrays)),
        out_specs=[vmem] * 2,
        out_shape=[jax.ShapeDtypeStruct(v, jnp.float32) for v in ((rows, 2 * NARROW), wide)],
        scratch_shapes=[
            pltpu.VMEM((depth // NEAR * len(SLOTS), 2 * NARROW), jnp.bfloat16),
            pltpu.VMEM((wide_depth, FOLD), jnp.bfloat16),
        ],
        cost_estimate=cost(9 if m3 else 6),
        compiler_params=pltpu.CompilerParams(vmem_limit_bytes=32 * 1024 * 1024),
    )(pos3, posx, place, lhs, far_lhs, *arrays)


def make_last_kernel(few, n2, starts2, n3, starts3):
    def kernel(
        occ_ref, vir_ref, pos2_ref, pos3_ref, count_ref, place_ref, fold_ref, far_ref, row_ref, narrow_ref, wide_ref,
        *refs
    ):
        m2_refs, refs = refs[:n2], refs[n2:]
        m3_refs = [refs[2 * n:2 * n + 2] for n in range(n3)]
        refs = refs[2 * n3:]
        outs = refs[:4]
        column_ref, total_ref, short_rhs, far_rhs = refs[4:]
        row, col = place_ref[0], place_ref[1]
        at_end = (row == 0) | (row == 3)
        groups, rows, width = fold_ref.shape
        share = width // K_STEP
        batch = rows // share
        @pl.loop(0, groups * K_STEP)
        def _(k):
            here = pl.ds(pl.multiple_of(k * share, share), share)
            if few:
                pos2 = pos2_ref[k]
                at = jnp.maximum(pos2, 0)
                own, e1, o1, two, three, _ = m2_refs
                pieces = []
                for piece in range(2):
                    close = groups * K_STEP + 2 * at + piece
                    block = own[at, 1 + piece] + e1[close] + two[at, 1 + piece]
                    block = block + jnp.where(at_end, three[at, 1 + piece], o1[close])
                    pieces.append(jnp.where(pos2 >= 0, block, jnp.zeros_like(block)))
                short = jnp.concatenate(pieces, axis=1)
            else:
                short = chosen(m2_refs, starts2, pos2_ref[k], lambda ref, at: ref[at])
            short_rhs[here] = jnp.concatenate([short, short], axis=0)
            if n3:
                far_rhs[here] = chosen(
                    m3_refs, starts3, pos3_ref[k], lambda pair, at: jnp.where(at_end, pair[0][at], pair[1][at])
                )

        column = amplitude_rows(column_ref, row_ref, occ_ref, row, batch, share)
        target = jnp.bitwise_xor(column, occ_ref[batch])
        both = narrow_ref[...]
        if few:
            two, three, few_lhs_ref = m2_refs[3:]
            half = share // 2
            lane = lax.broadcasted_iota(jnp.int32, (half, 2 * NARROW), 1)
            for n in range(few_lhs_ref.shape[0]):
                used = n < count_ref[0]
                for slot, wanted, ref in ((0, used & at_end, three), (1, used, two)):
                    block = ref[n, 0]
                    zero = jnp.zeros_like(block)
                    block = jnp.where(wanted, block, zero)
                    rhs = jnp.concatenate(
                        [jnp.where(lane < NARROW, block, zero), jnp.where(lane < NARROW, zero, block)], axis=0
                    )
                    both += jnp.dot(few_lhs_ref[n, slot], rhs, preferred_element_type=jnp.float32)
        both = both + pltpu.roll(both, NARROW, 1)
        both = jnp.concatenate([both] * (FOLD // (2 * NARROW)), axis=1)
        part = wide_ref[...] if n3 else 0.0
        for group in range(groups):
            here = pl.ds(group * width, width)
            part += jnp.dot(fold_ref[group], short_rhs[here], preferred_element_type=jnp.float32)
            if n3:
                part += jnp.dot(far_ref[group], far_rhs[here], preferred_element_type=jnp.float32)
        total_ref[...] = jnp.where(target == largest_irrep(vir_ref), part, both)
        write_quarters(total_ref, col, outs)

    return kernel


def last_product(far_lhs, fold, occ_irrep, vir_irrep, pos2, pos3, count, place, narrow_sum, wide_sum, few, m2, m3, batch):
    groups, rows, width = fold.shape
    share = rows // batch
    vmem = pl.BlockSpec(memory_space=pltpu.VMEM)
    smem = pl.BlockSpec(memory_space=pltpu.SMEM)
    arrays = [narrow_sum, wide_sum] + list(m2) + [v for group in m3 for v in group]
    quarter = (batch // 2, share, FOLD // 2)
    whole = groups * width
    far_lhs = far_lhs if m3 else jnp.zeros((8, 128), jnp.bfloat16)
    return pl.pallas_call(
        make_last_kernel(few, len(m2), starts_of(m2), len(m3), starts_of([v[0] for v in m3])),
        in_specs=[smem] * 6 + [vmem] * (3 + len(arrays)),
        out_specs=[vmem] * 4,
        out_shape=[jax.ShapeDtypeStruct(quarter, jnp.float32)] * 4,
        scratch_shapes=[
            pltpu.VMEM((vir_irrep.shape[0], 8), jnp.int32),
            pltpu.VMEM((rows, FOLD), jnp.float32),
            pltpu.VMEM((whole, FOLD), jnp.bfloat16),
            pltpu.VMEM((whole if m3 else 16, FOLD), jnp.bfloat16),
        ],
        cost_estimate=cost(4 if m3 else 2),
        compiler_params=pltpu.CompilerParams(vmem_limit_bytes=32 * 1024 * 1024),
    )(occ_irrep, vir_irrep, pos2, pos3, count, place, fold, far_lhs, vir_irrep[None, :], *arrays)


def dense_product(amplitudes, whole, occ_irrep, occ_local, vir_local, vir_irrep):
    batch = amplitudes.shape[0]
    keep = (
        jnp.bitwise_xor(occ_irrep[:batch, None], occ_local[None, :])[:, :, None, None]
        == jnp.bitwise_xor(vir_local[:, None], vir_irrep[None, :])[None, None]
    )
    kept = jnp.where(keep, amplitudes, jnp.zeros_like(amplitudes))
    return lax.dot_general(
        kept, whole, (((1, 3), (0, 1)), ((), ())), preferred_element_type=jnp.float32
    )


def finish(cycle, occ_irrep, vir_irrep, occ_energy, vir_energy, a_start, a_size, b_start, b_size, batch):
    label_a = lax.dynamic_slice_in_dim(vir_irrep, a_start, a_size)
    label_b = lax.dynamic_slice_in_dim(vir_irrep, b_start, b_size)
    energy_a = lax.dynamic_slice_in_dim(vir_energy, a_start, a_size)
    energy_b = lax.dynamic_slice_in_dim(vir_energy, b_start, b_size)
    target = jnp.bitwise_xor(
        jnp.bitwise_xor(occ_irrep[:batch, None], occ_irrep[batch]), label_a[None, :]
    )
    keep = label_b[:, None, None] == target[None, :, :]
    denominator = (
        occ_energy[:batch][None, :, None]
        + occ_energy[batch]
        - energy_a[None, None, :]
        - energy_b[:, None, None]
    )
    swapped = jnp.transpose(cycle, (2, 0, 1))
    return jnp.where(keep, swapped, 0.0) / denominator


def on_square(amplitudes, integrals, occ_irrep, vir_irrep, screen):
    batch, occ_share, share, vir_total = amplitudes.shape
    row = lax.axis_index("row")
    col = lax.axis_index("col")
    place = jnp.stack([row, col]).astype(jnp.int32)
    few, m2a, m2b, m3a, m3b, pos2, pos3, posx, form, count = wide_blocks(
        integrals, occ_irrep, vir_irrep, screen, place, batch
    )
    outer = [(0, 1), (1, 0), (2, 3), (3, 2)]
    inner = [(1, 2), (2, 1)]
    inward = [(0, 1), (3, 2)]
    outward = [(1, 0), (2, 3)]
    ends = [(0, 3), (3, 0)]
    second = [(r, r ^ 2) for r in range(4)]

    def move(v, pairs):
        return lax.ppermute(v, "row", pairs)

    def sparse(use_few, choose):
        def run(few, m2a, m2b, m3a, m3b):
            shorts, wides = choose(m2a, m2b, m3a, m3b)
            near = [(own, move(own, outer), move(own, inner)) for own in wides]
            few = few[:use_few] if use_few else None
            narrow = narrow_blocks(integrals, occ_irrep, vir_irrep, screen, place, few, batch)
            if use_few:
                e1, o1 = move(narrow, outer), move(narrow, inner)
                lhs, far_lhs, fold, few_lhs = masked_amplitudes(
                    amplitudes, occ_irrep, vir_irrep, place, posx, use_few
                )
                near, e1, o1, few, _ = lax.optimization_barrier((near, e1, o1, few, fold))
                two, three = move(few, second), move(few, ends)
                blocks = (narrow, e1, o1)
                sums = (few, e1, o1, two, three, few_lhs)
            else:
                h1 = [move(v, inward) for v in shorts]
                o1, e1 = move(narrow, inner), move(narrow, outward)
                lhs, far_lhs, fold = masked_amplitudes(amplitudes, occ_irrep, vir_irrep, place, posx, 0)
                near, h1, o1, e1, _ = lax.optimization_barrier((near, h1, o1, e1, fold))
                h2 = [move(own + v, inner) for own, v in zip(shorts, h1)]
                e1 = e1 + move(narrow, inward)
                e2 = move(o1, outward)
                h2, e1, e2 = lax.optimization_barrier((h2, e1, e2))
                h3 = [move(own + v, outward) for own, v in zip(shorts, h2)]
                o2 = move(e1, inner)
                blocks = (narrow, e1, o1, e2, o2, move(o2, outward))
                sums = [a + b + c + d for a, b, c, d in zip(shorts, h1, h2, h3)]
            far = [(move(o, outward), move(e, inner)) for _, e, o in near]
            narrow_sum, wide_sum = first_product(
                lhs, far_lhs, pos3, posx, place, blocks, bool(use_few), near
            )
            return list(last_product(
                far_lhs, fold, occ_irrep, vir_irrep, pos2, pos3, count, place, narrow_sum, wide_sum, bool(use_few), sums,
                far, batch
            ))

        return run

    def dense(*_):
        occ_local = lax.dynamic_slice_in_dim(occ_irrep, col * occ_share, occ_share)
        vir_local = lax.dynamic_slice_in_dim(vir_irrep, row * share, share)
        screen_rows = lax.dynamic_slice_in_dim(screen, col * occ_share, occ_share, 0)
        fold = folded_integrals(
            integrals, occ_local, vir_local, vir_irrep, occ_irrep[batch], screen_rows
        )
        whole = jnp.zeros((occ_share, vir_total, FOLD), fold.dtype)
        for s in range(4):
            block = move(fold, [(r, r ^ s) for r in range(4)]) if s else fold
            whole = lax.dynamic_update_slice_in_dim(whole, block, jnp.bitwise_xor(row, s) * share, 1)
        total = dense_product(amplitudes, whole, occ_irrep, occ_local, vir_local, vir_irrep)
        quarter = (batch // 2, share, FOLD // 2)
        goals = [jnp.bitwise_xor(col, t) for t in range(4)]
        return [
            lax.dynamic_slice(total, (g // 2 * quarter[0], 0, g % 2 * quarter[2]), quarter) for g in goals
        ]

    branches = [
        sparse(0, lambda m2a, m2b, m3a, m3b: ([m2a], [])),
        sparse(0, lambda m2a, m2b, m3a, m3b: ([m2a, m2b], [])),
        sparse(0, lambda m2a, m2b, m3a, m3b: ([m2a], [m3a[:FEW_WIDE]])),
        sparse(FEW_CAPS[0], lambda m2a, m2b, m3a, m3b: ([], [m3a])),
        sparse(FEW_CAPS[1], lambda m2a, m2b, m3a, m3b: ([], [m3a, m3b])),
        sparse(0, lambda m2a, m2b, m3a, m3b: ([m2a, m2b], [m3a, m3b])),
        dense,
    ]
    quarters = lax.switch(form[0], branches, few, m2a, m2b, m3a, m3b)
    mine = quarters[0]
    for t in (1, 2, 3):
        mine = mine + lax.ppermute(quarters[t], "col", [(q, q ^ t) for q in range(4)])
    places = [(r, q) for r in range(4) for q in range(4)]
    same = lax.ppermute(mine, ("row", "col"), [(r * 4 + q, q * 4 + r) for r, q in places])
    other = lax.ppermute(mine, ("row", "col"), [(r * 4 + q, (q ^ 2) * 4 + r) for r, q in places])
    upper = row // 2 == 1
    low = jnp.where(upper, other, same)
    high = jnp.where(upper, same, other)
    return jnp.concatenate([low, high], axis=0)


def on_any(amplitudes, integrals, occ_irrep, vir_irrep, screen):
    batch, occ_share, share, vir_total = amplitudes.shape
    row = lax.axis_index("row")
    col = lax.axis_index("col")
    occ_local = lax.dynamic_slice_in_dim(occ_irrep, col * occ_share, occ_share)
    vir_local = lax.dynamic_slice_in_dim(vir_irrep, row * share, share)
    screen_rows = lax.dynamic_slice_in_dim(screen, col * occ_share, occ_share, 0)
    fold = folded_integrals(
        integrals, occ_local, vir_local, vir_irrep, occ_irrep[batch], screen_rows
    )
    whole = lax.all_gather(fold, "row", axis=1, tiled=True)
    cycle = dense_product(amplitudes, whole, occ_irrep, occ_local, vir_local, vir_irrep)
    cycle = lax.psum(cycle, "col")
    cycle = jnp.concatenate([cycle] * (vir_total // FOLD), axis=2)
    cycle = lax.all_to_all(cycle, "row", split_axis=2, concat_axis=1, tiled=True)
    a_size = vir_total // lax.axis_size("col")
    return lax.dynamic_slice_in_dim(cycle, col * a_size, a_size, 1)


def on_device(amplitudes, integrals, occ_irrep, vir_irrep, screen, occ_energy, vir_energy):
    batch, _, vir_share, vir_total = amplitudes.shape
    square = lax.axis_size("row") == 4 and lax.axis_size("col") == 4
    form = on_square if square else on_any
    cycle = form(amplitudes, integrals, occ_irrep, vir_irrep, screen)
    a_size = vir_total // lax.axis_size("col")
    return finish(
        cycle, occ_irrep, vir_irrep, occ_energy, vir_energy,
        lax.axis_index("col") * a_size, a_size, lax.axis_index("row") * vir_share, vir_share, batch,
    )


def solution(mesh):
    in_specs = (
        P("parts", "col", "row", None),
        P(("parts", "col"), "row", None),
        P("parts"),
        P("parts"),
        P("parts", None),
        P("parts"),
        P("parts"),
    )
    out_specs = P("row", "parts", "col")
    return jax.shard_map(
        on_device, mesh=mesh, in_specs=in_specs, out_specs=out_specs, check_vma=False
    )
```

```python
import jax
import jax.numpy as jnp
from jax import lax
from jax.experimental import pallas as pl
from jax.experimental.pallas import tpu as pltpu
from jax.sharding import PartitionSpec as P

FOLD = 256
K_STEP = 5


def folded_integrals(integrals, occ_local, vir_local, vir_irrep, pair_label, screen_rows):
    irrep_codes = jnp.arange(8, dtype=jnp.int32)
    screen_local = jnp.sum(
        screen_rows[:, None, :] * (vir_local[None, :, None] == irrep_codes).astype(jnp.int32),
        axis=2,
    )
    target = jnp.bitwise_xor(
        jnp.bitwise_xor(occ_local[:, None], vir_local[None, :]), pair_label
    )
    target = jnp.where(screen_local == 1, target, -1)
    keep = target[:, :, None] == vir_irrep[None, None, :]
    kept = jnp.where(keep, integrals, jnp.zeros_like(integrals))
    return kept[:, :, :FOLD] + kept[:, :, FOLD:]


NARROW = 64
CAPS = (22, 3)
FEW_CAPS = (4, 10)
FEW_WIDE = 5


def largest_irrep(vir_ref):
    return jnp.where(vir_ref[0] == vir_ref[FOLD - 1], vir_ref[0], vir_ref[FOLD])


def label_columns(row_labels):
    return jnp.transpose(jnp.broadcast_to(row_labels, (8, row_labels.shape[1])))


def as_bf16(labels):
    return labels.astype(jnp.float32).astype(jnp.bfloat16)


def label_mix(mix_ref, column_ref, row_ref, row, big, keep_big):
    depth = mix_ref.shape[0]
    column_ref[...] = label_columns(row_ref[...])
    column = column_ref[pl.ds(pl.multiple_of(row * depth, depth), depth), :1]
    is_big = row_ref[...] == big
    wanted = is_big if keep_big else jnp.logical_not(is_big)
    mix_ref[...] = as_bf16(jnp.where(wanted, jnp.bitwise_xor(column, row_ref[...]), 8))


def kept_folded(int_ref, mix_ref, j, x):
    tile = int_ref[j]
    wanted = as_bf16(jnp.full(mix_ref.shape, x))
    kept = jnp.where(mix_ref[...] == wanted, tile, jnp.zeros_like(tile))
    return kept[:, :FOLD] + kept[:, FOLD:]


def narrow_fold(kept, bits, local):
    half = kept.shape[0] // 2
    lane = lax.broadcasted_iota(jnp.int32, (half, 2 * NARROW), 1)
    narrow = (kept[:, : 2 * NARROW] + kept[:, 2 * NARROW:]).astype(jnp.float32)
    narrow = narrow + pltpu.roll(narrow, NARROW, 1)
    on = jnp.bitwise_and(lax.shift_right_logical(jnp.full(local.shape, bits), local), 1) == 1
    narrow = jnp.where(on, narrow, 0.0)
    return jnp.where(lane < NARROW, narrow[:half], narrow[half:]).astype(jnp.bfloat16)


def screen_bits(screen_ref, k):
    bits = screen_ref[0, k]
    for g in range(1, 8):
        bits = bits + screen_ref[g, k] * (1 << g)
    return bits


def copy_of(source_ref, int_ref, sems, group):
    here = pl.ds(group * K_STEP, K_STEP)
    return pltpu.make_async_copy(source_ref.at[here], int_ref.at[here], sems.at[group])


def start_copies(source_ref, int_ref, sems):
    for group in range(int_ref.shape[0] // K_STEP):
        copy_of(source_ref, int_ref, sems, group).start()


def wait_copy(source_ref, int_ref, sems, group):
    copy_of(source_ref, int_ref, sems, group).wait()


def wide_kernel(
    occ_ref, vir_ref, screen_ref, place_ref, source_ref, row_ref,
    few_ref, m2a_ref, m2b_ref, m3a_ref, m3b_ref, pos2_ref, pos3_ref, posx_ref, form_ref, count_ref,
    mix_ref, small_mix_ref, column_ref, counts_ref, int_ref, sems, batch,
):
    start_copies(source_ref, int_ref, sems)
    k_all, depth, total = int_ref.shape
    half = depth // 2
    row, col = place_ref[0], place_ref[1]
    pair_label = occ_ref[batch]
    big = largest_irrep(vir_ref)
    mostly_zero = (occ_ref[col * k_all] == pair_label) | (occ_ref[(col + 1) * k_all - 1] == pair_label)
    most = FEW_CAPS[-1]
    for n in range(3):
        counts_ref[n] = 0
    label_mix(mix_ref, column_ref, row_ref, row, big, True)

    @pl.when(mostly_zero)
    def _():
        label_mix(small_mix_ref, column_ref, row_ref, row, big, False)

    local = column_ref[pl.ds(pl.multiple_of(row * depth, depth), depth), :1]

    @pl.loop(0, k_all)
    def _(k):
        @pl.when(k % K_STEP == 0)
        def _():
            wait_copy(source_ref, int_ref, sems, k // K_STEP)

        k_whole = col * k_all + k
        x = jnp.bitwise_xor(occ_ref[k_whole], pair_label)
        on_big = screen_ref[jnp.bitwise_xor(big, x), k_whole] == 1
        actives = (on_big & (x != 0), on_big & (x == 0), x != 0)
        pos2, pos3, posx = [jnp.where(active, counts_ref[n], -1) for n, active in enumerate(actives)]
        for n, active in enumerate(actives):
            counts_ref[n] = counts_ref[n] + active.astype(jnp.int32)
        pos2_ref[k], pos3_ref[k], posx_ref[k] = pos2, pos3, posx

        @pl.when(pos2 >= 0)
        def _():
            wide = kept_folded(int_ref, mix_ref, k, x)
            short = wide[:half] + wide[half:]

            @pl.when(mostly_zero & (posx < most))
            def _():
                for piece in range(2):
                    few_ref[posx, 1 + piece] = short[:, piece * 2 * NARROW:(piece + 1) * 2 * NARROW]

            @pl.when(pos2 < CAPS[0])
            def _():
                m2a_ref[pos2] = short

            @pl.when(pos2 >= CAPS[0])
            def _():
                m2b_ref[pos2 - CAPS[0]] = short

        @pl.when(mostly_zero & (posx >= 0) & (posx < most))
        def _():
            kept = kept_folded(int_ref, small_mix_ref, k, x)
            few_ref[posx, 0] = narrow_fold(kept, screen_bits(screen_ref, k_whole), local)

            @pl.when(pos2 < 0)
            def _():
                for piece in range(2):
                    few_ref[posx, 1 + piece] = jnp.zeros((half, 2 * NARROW), jnp.bfloat16)

        @pl.when(pos3 >= 0)
        def _():
            wide = kept_folded(int_ref, mix_ref, k, x)

            @pl.when(pos3 < CAPS[0])
            def _():
                m3a_ref[pos3] = wide

            @pl.when(pos3 >= CAPS[0])
            def _():
                m3b_ref[pos3 - CAPS[0]] = wide

    labels = row_ref[...]
    lanes = lax.broadcasted_iota(jnp.int32, labels.shape, 1)
    ahead = pltpu.roll(labels, total - NARROW, 1)
    long = (labels == ahead) & (lanes < total - NARROW) & (labels != big)
    too_long = jnp.max(long.astype(jnp.int32)) == 1
    n2, n3, nx = counts_ref[0], counts_ref[1], counts_ref[2]
    count_ref[0] = nx
    one_label = occ_ref[0] == pair_label
    form = jnp.where((nx <= FEW_CAPS[0]) & (n3 <= CAPS[0]), 3, jnp.where(nx <= FEW_CAPS[1], 4, 5))
    form = jnp.where(mostly_zero, form, 5)
    form = jnp.where((n3 <= FEW_WIDE) & (n2 <= CAPS[0]), 2, form)
    form = jnp.where(one_label, form, 6)
    form = jnp.where(n3 == 0, jnp.where(n2 <= CAPS[0], 0, 1), form)
    form_ref[0] = jnp.where(too_long, 6, form)


def wide_blocks(integrals, occ_irrep, vir_irrep, screen, place, batch):
    occ_share, depth, total = integrals.shape
    shapes = [(n, depth // 2, FOLD) for n in CAPS] + [(n, depth, FOLD) for n in CAPS]
    few = (FEW_CAPS[-1], 3, depth // 2, 2 * NARROW)
    smem = pl.BlockSpec(memory_space=pltpu.SMEM)

    def kernel(*refs):
        wide_kernel(*refs, batch)

    vmem = pl.BlockSpec(memory_space=pltpu.VMEM)
    return pl.pallas_call(
        kernel,
        in_specs=[smem] * 4 + [pl.BlockSpec(memory_space=pltpu.HBM), vmem],
        out_specs=[vmem] * (1 + len(shapes)) + [smem] * 5,
        scratch_shapes=[
            pltpu.VMEM((depth, total), jnp.bfloat16),
            pltpu.VMEM((depth, total), jnp.bfloat16),
            pltpu.VMEM((total, 8), jnp.int32),
            pltpu.SMEM((3,), jnp.int32),
            pltpu.VMEM(integrals.shape, jnp.bfloat16),
            pltpu.SemaphoreType.DMA((occ_share // K_STEP,)),
        ],
        out_shape=[jax.ShapeDtypeStruct(v, jnp.bfloat16) for v in [few] + shapes]
        + [jax.ShapeDtypeStruct((n,), jnp.int32) for n in (occ_share, occ_share, occ_share, 1, 1)],
        cost_estimate=cost(5),
        compiler_params=pltpu.CompilerParams(vmem_limit_bytes=24 * 1024 * 1024),
    )(occ_irrep, vir_irrep, screen.T, place, integrals, vir_irrep[None, :])


def narrow_kernel(
    occ_ref, vir_ref, screen_ref, place_ref, source_ref, row_ref, few_ref, narrow_ref,
    mix_ref, column_ref, int_ref, sems, batch,
):
    start_copies(source_ref, int_ref, sems)
    k_all, depth, total = int_ref.shape
    row, col = place_ref[0], place_ref[1]
    label_mix(mix_ref, column_ref, row_ref, row, largest_irrep(vir_ref), False)
    if few_ref is not None:
        for n in range(few_ref.shape[0]):
            for piece in range(2):
                narrow_ref[k_all + 2 * n + piece] = few_ref[n, 1 + piece]
    local = column_ref[pl.ds(pl.multiple_of(row * depth, depth), depth), :1]

    @pl.loop(0, k_all // K_STEP)
    def _(group):
        wait_copy(source_ref, int_ref, sems, group)
        for j in range(K_STEP):
            k = group * K_STEP + j
            k_whole = col * k_all + k
            x = jnp.bitwise_xor(occ_ref[k_whole], occ_ref[batch])
            kept = kept_folded(int_ref, mix_ref, k, x)
            narrow_ref[k] = narrow_fold(kept, screen_bits(screen_ref, k_whole), local)


def narrow_blocks(integrals, occ_irrep, vir_irrep, screen, place, few, batch):
    occ_share, depth, total = integrals.shape
    extra = [] if few is None else [few]
    count = occ_share + sum(2 * v.shape[0] for v in extra)
    smem = pl.BlockSpec(memory_space=pltpu.SMEM)
    vmem = pl.BlockSpec(memory_space=pltpu.VMEM)

    def kernel(*refs):
        narrow_kernel(*(refs if extra else refs[:6] + (None,) + refs[6:]), batch)

    return pl.pallas_call(
        kernel,
        in_specs=[smem] * 4 + [pl.BlockSpec(memory_space=pltpu.HBM), vmem] + [vmem] * len(extra),
        out_specs=vmem,
        out_shape=jax.ShapeDtypeStruct((count, depth // 2, 2 * NARROW), jnp.bfloat16),
        scratch_shapes=[
            pltpu.VMEM((depth, total), jnp.bfloat16),
            pltpu.VMEM((total, 8), jnp.int32),
            pltpu.VMEM(integrals.shape, jnp.bfloat16),
            pltpu.SemaphoreType.DMA((occ_share // K_STEP,)),
        ],
        cost_estimate=cost(4),
        compiler_params=pltpu.CompilerParams(vmem_limit_bytes=16 * 1024 * 1024),
    )(occ_irrep, vir_irrep, screen.T, place, integrals, vir_irrep[None, :], *extra)


def cost(micros):
    return pl.CostEstimate(flops=int(micros * 1e9), bytes_accessed=int(micros * 3e6), transcendentals=0)


SLOTS = (0, 1, 3, 2)
NEAR = 3


def amplitude_rows(column_ref, row_ref, occ_ref, row, batch, share):
    column_ref[...] = label_columns(row_ref[...])
    column = column_ref[pl.ds(pl.multiple_of(row * share, share), share), :1]
    return jnp.concatenate([jnp.bitwise_xor(column, occ_ref[i]) for i in range(batch)], axis=0)


def write_quarters(total_ref, col, outs):
    rows, fold = total_ref.shape
    width, height = fold // 2, rows // 2
    for t, out_ref in enumerate(outs):
        goal = jnp.bitwise_xor(col, t)
        lanes = pl.ds(pl.multiple_of((goal % 2) * width, width), width)
        lines = pl.ds(pl.multiple_of((goal // 2) * height, height), height)
        out_ref[...] = total_ref[lines, lanes].reshape(out_ref.shape)


def chosen(refs, starts, pos, pick):
    block = None
    for n, group in enumerate(refs):
        inside = (pos >= starts[n]) & (pos < starts[n + 1])
        at = jnp.clip(pos - starts[n], 0, starts[n + 1] - starts[n] - 1)
        found = pick(group, at)
        found = jnp.where(inside, found, jnp.zeros_like(found))
        block = found if block is None else block + found
    return block


def starts_of(arrays):
    starts = [0]
    for v in arrays:
        starts.append(starts[-1] + v.shape[0])
    return starts


def mask_kernel(
    occ_ref, place_ref, posx_ref, amp_ref, row_ref, lhs_ref, far_ref, fold_ref, few_lhs_ref,
    mix_ref, column_ref, amp_buffer, sems,
):
    batch, k_all, share, total = amp_ref.shape
    rows, groups = batch * share, k_all // K_STEP
    row, col = place_ref[0], place_ref[1]

    def fetch(group):
        slot = group % 2
        source = amp_ref.at[:, pl.ds(group * K_STEP, K_STEP)]
        return pltpu.make_async_copy(source, amp_buffer.at[slot], sems.at[slot])

    fetch(0).start()
    column = amplitude_rows(column_ref, row_ref, occ_ref, row, batch, share)
    mix_ref[...] = as_bf16(jnp.bitwise_xor(column, row_ref[...]))
    if few_lhs_ref is not None:
        few_lhs_ref[...] = jnp.zeros(few_lhs_ref.shape, jnp.bfloat16)

    @pl.loop(0, groups)
    def _(group):
        slot = group % 2

        @pl.when(group + 1 < groups)
        def _():
            fetch(group + 1).start()

        fetch(group).wait()

        @pl.loop(0, K_STEP)
        def _(j):
            wanted = as_bf16(jnp.full((rows, share), occ_ref[col * k_all + group * K_STEP + j]))
            folded = None
            for n, s in enumerate(SLOTS):
                place = pl.ds(pl.multiple_of(jnp.bitwise_xor(row, s) * share, share), share)
                tile = amp_buffer[slot, :, j, :, place].reshape(rows, share)
                piece = jnp.where(mix_ref[:, place] == wanted, tile, jnp.zeros_like(tile))
                if n < NEAR:
                    lhs_ref[group, :, pl.ds(pl.multiple_of((n * K_STEP + j) * share, share), share)] = piece
                else:
                    far_ref[group, :, pl.ds(pl.multiple_of(j * share, share), share)] = piece
                folded = piece if folded is None else folded + piece
            if fold_ref is not None:
                fold_ref[group, :, pl.ds(pl.multiple_of(j * share, share), share)] = folded
            else:
                posx = posx_ref[group * K_STEP + j]

                @pl.when((posx >= 0) & (posx < few_lhs_ref.shape[0]))
                def _():
                    third = lhs_ref[group, :, pl.ds(pl.multiple_of((2 * K_STEP + j) * share, share), share)]
                    few_lhs_ref[posx, 0] = third
                    few_lhs_ref[posx, 1] = far_ref[group, :, pl.ds(pl.multiple_of(j * share, share), share)]
                    few_lhs_ref[posx, 2] = folded


def masked_amplitudes(amplitudes, occ_irrep, vir_irrep, place, posx, few):
    batch, k_all, share, total = amplitudes.shape
    rows, groups = batch * share, k_all // K_STEP
    smem = pl.BlockSpec(memory_space=pltpu.SMEM)
    vmem = pl.BlockSpec(memory_space=pltpu.VMEM)
    hbm = pl.BlockSpec(memory_space=pltpu.HBM)
    shapes = [(groups, rows, w) for w in (NEAR * K_STEP * share, K_STEP * share)]
    shapes += [(few, 3, rows, share)] if few else [(groups, rows, K_STEP * share)]

    def kernel(*refs):
        mask_kernel(*(refs[:7] + (None,) + refs[7:] if few else refs[:8] + (None,) + refs[8:]))

    return pl.pallas_call(
        kernel,
        in_specs=[smem, smem, smem, hbm, vmem],
        out_specs=[vmem] * len(shapes),
        out_shape=[jax.ShapeDtypeStruct(v, jnp.bfloat16) for v in shapes],
        scratch_shapes=[
            pltpu.VMEM((rows, total), jnp.bfloat16),
            pltpu.VMEM((total, 8), jnp.int32),
            pltpu.VMEM((2, batch, K_STEP, share, total), jnp.bfloat16),
            pltpu.SemaphoreType.DMA((2,)),
        ],
        cost_estimate=cost(7),
        compiler_params=pltpu.CompilerParams(vmem_limit_bytes=28 * 1024 * 1024),
    )(occ_irrep, place, posx, amplitudes, vir_irrep[None, :])


def make_first_kernel(few, n3, starts3):
    def kernel(pos3_ref, posx_ref, place_ref, lhs_ref, far_ref, *refs):
        sources = 3 if few else 6
        narrow_refs, refs = refs[:sources], refs[sources:]
        m3_refs = [refs[3 * n:3 * n + 3] for n in range(n3)]
        narrow_sum, wide_sum, narrow_rhs, wide_rhs = refs[3 * n3:]
        row = place_ref[0]
        at_end = (row == 0) | (row == 3)
        groups, _, depth = lhs_ref.shape
        share = depth // (NEAR * K_STEP)
        half = share // 2
        lane = lax.broadcasted_iota(jnp.int32, (half, 2 * NARROW), 1)

        narrow_sum[...] = jnp.zeros(narrow_sum.shape, jnp.float32)
        wide_sum[...] = jnp.zeros(wide_sum.shape, jnp.float32)

        @pl.loop(0, groups)
        def _(group):
            @pl.loop(0, K_STEP)
            def _(j):
                k = group * K_STEP + j
                if few:
                    blocks = [ref[k] for ref in narrow_refs]
                else:
                    own, e1, o1, e2, o2, e3 = [ref[k] for ref in narrow_refs]
                    blocks = (own, e1, jnp.where(at_end, e3, o1), jnp.where(at_end, e2, o2))
                for n, block in enumerate(blocks):
                    zero = jnp.zeros_like(block)
                    first = pl.multiple_of((n * K_STEP + j) * share, share)
                    narrow_rhs[pl.ds(first, half)] = jnp.where(lane < NARROW, block, zero)
                    narrow_rhs[pl.ds(first + half, half)] = jnp.where(lane < NARROW, zero, block)
                for n in range(3 if n3 else 0):
                    block = chosen(m3_refs, starts3, pos3_ref[k], lambda group, at, n=n: group[n][at])
                    if n == 2:
                        block = jnp.where(at_end, jnp.zeros_like(block), block)
                    wide_rhs[pl.ds(pl.multiple_of((n * K_STEP + j) * share, share), share)] = block

            narrow = jnp.dot(lhs_ref[group], narrow_rhs[:depth], preferred_element_type=jnp.float32)
            if not few:
                narrow += jnp.dot(far_ref[group], narrow_rhs[depth:], preferred_element_type=jnp.float32)
            narrow_sum[...] += narrow
            if n3:
                wide_sum[...] += jnp.dot(lhs_ref[group], wide_rhs[...], preferred_element_type=jnp.float32)

    return kernel


def first_product(lhs, far_lhs, pos3, posx, place, narrow, few, m3):
    groups, rows, depth = lhs.shape
    vmem = pl.BlockSpec(memory_space=pltpu.VMEM)
    smem = pl.BlockSpec(memory_space=pltpu.SMEM)
    arrays = list(narrow) + [v for group in m3 for v in group]
    wide = (rows, FOLD) if m3 else (16, FOLD)
    wide_depth = depth if m3 else 16
    return pl.pallas_call(
        make_first_kernel(few, len(m3), starts_of([v[0] for v in m3])),
        in_specs=[smem] * 3 + [vmem] * (2 + len(arrays)),
        out_specs=[vmem] * 2,
        out_shape=[jax.ShapeDtypeStruct(v, jnp.float32) for v in ((rows, 2 * NARROW), wide)],
        scratch_shapes=[
            pltpu.VMEM((depth // NEAR * len(SLOTS), 2 * NARROW), jnp.bfloat16),
            pltpu.VMEM((wide_depth, FOLD), jnp.bfloat16),
        ],
        cost_estimate=cost(9 if m3 else 6),
        compiler_params=pltpu.CompilerParams(vmem_limit_bytes=32 * 1024 * 1024),
    )(pos3, posx, place, lhs, far_lhs, *arrays)


def make_last_kernel(few, n2, starts2, n3, starts3):
    def kernel(
        occ_ref, vir_ref, pos2_ref, pos3_ref, count_ref, place_ref, fold_ref, far_ref, row_ref, narrow_ref, wide_ref,
        *refs,
    ):
        m2_refs, refs = refs[:n2], refs[n2:]
        m3_refs = [refs[2 * n:2 * n + 2] for n in range(n3)]
        refs = refs[2 * n3:]
        outs = refs[:4]
        column_ref, total_ref, narrow_sum, short_rhs, far_rhs = refs[4:]
        row, col = place_ref[0], place_ref[1]
        at_end = (row == 0) | (row == 3)
        groups, rows, width = far_ref.shape if few else fold_ref.shape
        share = width // K_STEP
        batch = rows // share
        @pl.loop(0, groups * K_STEP)
        def _(k):
            here = pl.ds(pl.multiple_of(k * share, share), share)
            if not few:
                short = chosen(m2_refs, starts2, pos2_ref[k], lambda ref, at: ref[at])
                short_rhs[here] = jnp.concatenate([short, short], axis=0)
            if n3:
                far_rhs[here] = chosen(
                    m3_refs, starts3, pos3_ref[k], lambda pair, at: jnp.where(at_end, pair[0][at], pair[1][at])
                )

        column = amplitude_rows(column_ref, row_ref, occ_ref, row, batch, share)
        target = jnp.bitwise_xor(column, occ_ref[batch])
        if few:
            own, e1, o1, two, three = m2_refs
            half = share // 2
            lane = lax.broadcasted_iota(jnp.int32, (half, 2 * NARROW), 1)
            total_ref[...] = wide_ref[...]
            narrow_sum[...] = narrow_ref[...]

            @pl.loop(0, count_ref[0])
            def _(n):
                for slot, wanted, ref in ((0, at_end, three), (1, True, two)):
                    block = ref[n, 0]
                    zero = jnp.zeros_like(block)
                    block = jnp.where(wanted, block, zero)
                    rhs = jnp.concatenate(
                        [jnp.where(lane < NARROW, block, zero), jnp.where(lane < NARROW, zero, block)], axis=0
                    )
                    narrow_sum[...] += jnp.dot(fold_ref[n, slot], rhs, preferred_element_type=jnp.float32)
                pieces = []
                for piece in range(2):
                    close = groups * K_STEP + 2 * n + piece
                    block = own[n, 1 + piece] + e1[close] + two[n, 1 + piece]
                    pieces.append(block + jnp.where(at_end, three[n, 1 + piece], o1[close]))
                short = jnp.concatenate(pieces, axis=1)
                rhs = jnp.concatenate([short, short], axis=0)
                total_ref[...] += jnp.dot(fold_ref[n, 2], rhs, preferred_element_type=jnp.float32)

            part, both = total_ref[...], narrow_sum[...]
        else:
            part, both = wide_ref[...] if n3 else 0.0, narrow_ref[...]
        both = both + pltpu.roll(both, NARROW, 1)
        both = jnp.concatenate([both] * (FOLD // (2 * NARROW)), axis=1)
        for group in range(groups):
            here = pl.ds(group * width, width)
            if not few:
                part += jnp.dot(fold_ref[group], short_rhs[here], preferred_element_type=jnp.float32)
            if n3:
                part += jnp.dot(far_ref[group], far_rhs[here], preferred_element_type=jnp.float32)
        total_ref[...] = jnp.where(target == largest_irrep(vir_ref), part, both)
        write_quarters(total_ref, col, outs)

    return kernel


def last_product(far_lhs, fold, occ_irrep, vir_irrep, pos2, pos3, count, place, narrow_sum, wide_sum, few, m2, m3, batch):
    groups, rows, width = far_lhs.shape
    share = rows // batch
    vmem = pl.BlockSpec(memory_space=pltpu.VMEM)
    smem = pl.BlockSpec(memory_space=pltpu.SMEM)
    arrays = [narrow_sum, wide_sum] + list(m2) + [v for group in m3 for v in group]
    quarter = (batch // 2, share, FOLD // 2)
    whole = groups * width
    far_lhs = far_lhs if m3 else jnp.zeros((8, 128), jnp.bfloat16)
    return pl.pallas_call(
        make_last_kernel(few, len(m2), starts_of(m2), len(m3), starts_of([v[0] for v in m3])),
        in_specs=[smem] * 6 + [vmem] * (3 + len(arrays)),
        out_specs=[vmem] * 4,
        out_shape=[jax.ShapeDtypeStruct(quarter, jnp.float32)] * 4,
        scratch_shapes=[
            pltpu.VMEM((vir_irrep.shape[0], 8), jnp.int32),
            pltpu.VMEM((rows, FOLD), jnp.float32),
            pltpu.VMEM((rows, 2 * NARROW), jnp.float32),
            pltpu.VMEM((16 if few else whole, FOLD), jnp.bfloat16),
            pltpu.VMEM((whole if m3 else 16, FOLD), jnp.bfloat16),
        ],
        cost_estimate=cost(4 if m3 else 2),
        compiler_params=pltpu.CompilerParams(vmem_limit_bytes=32 * 1024 * 1024),
    )(occ_irrep, vir_irrep, pos2, pos3, count, place, fold, far_lhs, vir_irrep[None, :], *arrays)


def dense_product(amplitudes, whole, occ_irrep, occ_local, vir_local, vir_irrep):
    batch = amplitudes.shape[0]
    keep = (
        jnp.bitwise_xor(occ_irrep[:batch, None], occ_local[None, :])[:, :, None, None]
        == jnp.bitwise_xor(vir_local[:, None], vir_irrep[None, :])[None, None]
    )
    kept = jnp.where(keep, amplitudes, jnp.zeros_like(amplitudes))
    return lax.dot_general(
        kept, whole, (((1, 3), (0, 1)), ((), ())), preferred_element_type=jnp.float32
    )


def finish(cycle, occ_irrep, vir_irrep, occ_energy, vir_energy, a_start, a_size, b_start, b_size, batch):
    label_a = lax.dynamic_slice_in_dim(vir_irrep, a_start, a_size)
    label_b = lax.dynamic_slice_in_dim(vir_irrep, b_start, b_size)
    energy_a = lax.dynamic_slice_in_dim(vir_energy, a_start, a_size)
    energy_b = lax.dynamic_slice_in_dim(vir_energy, b_start, b_size)
    target = jnp.bitwise_xor(
        jnp.bitwise_xor(occ_irrep[:batch, None], occ_irrep[batch]), label_a[None, :]
    )
    keep = label_b[:, None, None] == target[None, :, :]
    denominator = (
        occ_energy[:batch][None, :, None]
        + occ_energy[batch]
        - energy_a[None, None, :]
        - energy_b[:, None, None]
    )
    swapped = jnp.transpose(cycle, (2, 0, 1))
    return jnp.where(keep, swapped, 0.0) / denominator


def on_square(amplitudes, integrals, occ_irrep, vir_irrep, screen):
    batch, occ_share, share, vir_total = amplitudes.shape
    row = lax.axis_index("row")
    col = lax.axis_index("col")
    place = jnp.stack([row, col]).astype(jnp.int32)
    few, m2a, m2b, m3a, m3b, pos2, pos3, posx, form, count = wide_blocks(
        integrals, occ_irrep, vir_irrep, screen, place, batch
    )
    outer = [(0, 1), (1, 0), (2, 3), (3, 2)]
    inner = [(1, 2), (2, 1)]
    inward = [(0, 1), (3, 2)]
    outward = [(1, 0), (2, 3)]
    ends = [(0, 3), (3, 0)]
    second = [(r, r ^ 2) for r in range(4)]

    def move(v, pairs):
        return lax.ppermute(v, "row", pairs)

    def sparse(use_few, choose):
        def run(few, m2a, m2b, m3a, m3b):
            shorts, wides = choose(m2a, m2b, m3a, m3b)
            near = [(own, move(own, outer), move(own, inner)) for own in wides]
            few = few[:use_few] if use_few else None
            narrow = narrow_blocks(integrals, occ_irrep, vir_irrep, screen, place, few, batch)
            if use_few:
                e1, o1 = move(narrow, outer), move(narrow, inner)
                lhs, far_lhs, fold = masked_amplitudes(
                    amplitudes, occ_irrep, vir_irrep, place, posx, use_few
                )
                near, e1, o1, few, _ = lax.optimization_barrier((near, e1, o1, few, fold))
                two, three = move(few, second), move(few, ends)
                blocks = (narrow, e1, o1)
                sums = (few, e1, o1, two, three)
            else:
                h1 = [move(v, inward) for v in shorts]
                o1, e1 = move(narrow, inner), move(narrow, outward)
                lhs, far_lhs, fold = masked_amplitudes(amplitudes, occ_irrep, vir_irrep, place, posx, 0)
                near, h1, o1, e1, _ = lax.optimization_barrier((near, h1, o1, e1, fold))
                h2 = [move(own + v, inner) for own, v in zip(shorts, h1)]
                e1 = e1 + move(narrow, inward)
                e2 = move(o1, outward)
                h2, e1, e2 = lax.optimization_barrier((h2, e1, e2))
                h3 = [move(own + v, outward) for own, v in zip(shorts, h2)]
                o2 = move(e1, inner)
                blocks = (narrow, e1, o1, e2, o2, move(o2, outward))
                sums = [a + b + c + d for a, b, c, d in zip(shorts, h1, h2, h3)]
            far = [(move(o, outward), move(e, inner)) for _, e, o in near]
            narrow_sum, wide_sum = first_product(
                lhs, far_lhs, pos3, posx, place, blocks, bool(use_few), near
            )
            return list(last_product(
                far_lhs, fold, occ_irrep, vir_irrep, pos2, pos3, count, place, narrow_sum, wide_sum, bool(use_few), sums,
                far, batch
            ))

        return run

    def dense(*_):
        occ_local = lax.dynamic_slice_in_dim(occ_irrep, col * occ_share, occ_share)
        vir_local = lax.dynamic_slice_in_dim(vir_irrep, row * share, share)
        screen_rows = lax.dynamic_slice_in_dim(screen, col * occ_share, occ_share, 0)
        fold = folded_integrals(
            integrals, occ_local, vir_local, vir_irrep, occ_irrep[batch], screen_rows
        )
        whole = jnp.zeros((occ_share, vir_total, FOLD), fold.dtype)
        for s in range(4):
            block = move(fold, [(r, r ^ s) for r in range(4)]) if s else fold
            whole = lax.dynamic_update_slice_in_dim(whole, block, jnp.bitwise_xor(row, s) * share, 1)
        total = dense_product(amplitudes, whole, occ_irrep, occ_local, vir_local, vir_irrep)
        quarter = (batch // 2, share, FOLD // 2)
        goals = [jnp.bitwise_xor(col, t) for t in range(4)]
        return [
            lax.dynamic_slice(total, (g // 2 * quarter[0], 0, g % 2 * quarter[2]), quarter) for g in goals
        ]

    branches = [
        sparse(0, lambda m2a, m2b, m3a, m3b: ([m2a], [])),
        sparse(0, lambda m2a, m2b, m3a, m3b: ([m2a, m2b], [])),
        sparse(0, lambda m2a, m2b, m3a, m3b: ([m2a], [m3a[:FEW_WIDE]])),
        sparse(FEW_CAPS[0], lambda m2a, m2b, m3a, m3b: ([], [m3a])),
        sparse(FEW_CAPS[1], lambda m2a, m2b, m3a, m3b: ([], [m3a, m3b])),
        sparse(0, lambda m2a, m2b, m3a, m3b: ([m2a, m2b], [m3a, m3b])),
        dense,
    ]
    quarters = lax.switch(form[0], branches, few, m2a, m2b, m3a, m3b)
    mine = quarters[0]
    for t in (1, 2, 3):
        mine = mine + lax.ppermute(quarters[t], "col", [(q, q ^ t) for q in range(4)])
    places = [(r, q) for r in range(4) for q in range(4)]
    same = lax.ppermute(mine, ("row", "col"), [(r * 4 + q, q * 4 + r) for r, q in places])
    other = lax.ppermute(mine, ("row", "col"), [(r * 4 + q, (q ^ 2) * 4 + r) for r, q in places])
    upper = row // 2 == 1
    low = jnp.where(upper, other, same)
    high = jnp.where(upper, same, other)
    return jnp.concatenate([low, high], axis=0)


def on_any(amplitudes, integrals, occ_irrep, vir_irrep, screen):
    batch, occ_share, share, vir_total = amplitudes.shape
    row = lax.axis_index("row")
    col = lax.axis_index("col")
    occ_local = lax.dynamic_slice_in_dim(occ_irrep, col * occ_share, occ_share)
    vir_local = lax.dynamic_slice_in_dim(vir_irrep, row * share, share)
    screen_rows = lax.dynamic_slice_in_dim(screen, col * occ_share, occ_share, 0)
    fold = folded_integrals(
        integrals, occ_local, vir_local, vir_irrep, occ_irrep[batch], screen_rows
    )
    whole = lax.all_gather(fold, "row", axis=1, tiled=True)
    cycle = dense_product(amplitudes, whole, occ_irrep, occ_local, vir_local, vir_irrep)
    cycle = lax.psum(cycle, "col")
    cycle = jnp.concatenate([cycle] * (vir_total // FOLD), axis=2)
    cycle = lax.all_to_all(cycle, "row", split_axis=2, concat_axis=1, tiled=True)
    a_size = vir_total // lax.axis_size("col")
    return lax.dynamic_slice_in_dim(cycle, col * a_size, a_size, 1)


def on_device(amplitudes, integrals, occ_irrep, vir_irrep, screen, occ_energy, vir_energy):
    batch, _, vir_share, vir_total = amplitudes.shape
    square = lax.axis_size("row") == 4 and lax.axis_size("col") == 4
    form = on_square if square else on_any
    cycle = form(amplitudes, integrals, occ_irrep, vir_irrep, screen)
    a_size = vir_total // lax.axis_size("col")
    return finish(
        cycle, occ_irrep, vir_irrep, occ_energy, vir_energy,
        lax.axis_index("col") * a_size, a_size, lax.axis_index("row") * vir_share, vir_share, batch,
    )


def solution(mesh):
    in_specs = (
        P("parts", "col", "row", None),
        P(("parts", "col"), "row", None),
        P("parts"),
        P("parts"),
        P("parts", None),
        P("parts"),
        P("parts"),
    )
    out_specs = P("row", "parts", "col")
    return jax.shard_map(
        on_device, mesh=mesh, in_specs=in_specs, out_specs=out_specs, check_vma=False
    )
```

```python
import jax
import jax.numpy as jnp
from jax import lax
from jax.experimental import pallas as pl
from jax.experimental.pallas import tpu as pltpu
from jax.sharding import PartitionSpec as P

FOLD = 256
K_STEP = 5


def folded_integrals(integrals, occ_local, vir_local, vir_irrep, pair_label, screen_rows):
    irrep_codes = jnp.arange(8, dtype=jnp.int32)
    screen_local = jnp.sum(
        screen_rows[:, None, :] * (vir_local[None, :, None] == irrep_codes).astype(jnp.int32),
        axis=2,
    )
    target = jnp.bitwise_xor(
        jnp.bitwise_xor(occ_local[:, None], vir_local[None, :]), pair_label
    )
    target = jnp.where(screen_local == 1, target, -1)
    keep = target[:, :, None] == vir_irrep[None, None, :]
    kept = jnp.where(keep, integrals, jnp.zeros_like(integrals))
    return kept[:, :, :FOLD] + kept[:, :, FOLD:]


NARROW = 64
CAPS = (22, 3)
FEW_CAPS = (4, 10)
FEW_WIDE = 5


def largest_irrep(vir_ref):
    return jnp.where(vir_ref[0] == vir_ref[FOLD - 1], vir_ref[0], vir_ref[FOLD])


def label_columns(row_labels):
    return jnp.transpose(jnp.broadcast_to(row_labels, (8, row_labels.shape[1])))


def as_bf16(labels):
    return labels.astype(jnp.float32).astype(jnp.bfloat16)


def label_mix(mix_ref, column_ref, row_ref, row, big, keep_big):
    depth = mix_ref.shape[0]
    column_ref[...] = label_columns(row_ref[...])
    column = column_ref[pl.ds(pl.multiple_of(row * depth, depth), depth), :1]
    is_big = row_ref[...] == big
    wanted = is_big if keep_big else jnp.logical_not(is_big)
    mix_ref[...] = as_bf16(jnp.where(wanted, jnp.bitwise_xor(column, row_ref[...]), 8))


def kept_folded(int_ref, mix_ref, j, x):
    tile = int_ref[j]
    wanted = as_bf16(jnp.full(mix_ref.shape, x))
    kept = jnp.where(mix_ref[...] == wanted, tile, jnp.zeros_like(tile))
    return kept[:, :FOLD] + kept[:, FOLD:]


def narrow_fold(kept, bits, local):
    half = kept.shape[0] // 2
    lane = lax.broadcasted_iota(jnp.int32, (half, 2 * NARROW), 1)
    narrow = (kept[:, : 2 * NARROW] + kept[:, 2 * NARROW:]).astype(jnp.float32)
    narrow = narrow + pltpu.roll(narrow, NARROW, 1)
    on = jnp.bitwise_and(lax.shift_right_logical(jnp.full(local.shape, bits), local), 1) == 1
    narrow = jnp.where(on, narrow, 0.0)
    return jnp.where(lane < NARROW, narrow[:half], narrow[half:]).astype(jnp.bfloat16)


def screen_bits(screen_ref, k):
    bits = screen_ref[0, k]
    for g in range(1, 8):
        bits = bits + screen_ref[g, k] * (1 << g)
    return bits


def copy_of(source_ref, int_ref, sems, group):
    here = pl.ds(group * K_STEP, K_STEP)
    return pltpu.make_async_copy(source_ref.at[here], int_ref.at[here], sems.at[group])


def start_copies(source_ref, int_ref, sems):
    for group in range(int_ref.shape[0] // K_STEP):
        copy_of(source_ref, int_ref, sems, group).start()


def wait_copy(source_ref, int_ref, sems, group):
    copy_of(source_ref, int_ref, sems, group).wait()


def wide_kernel(
    occ_ref, vir_ref, screen_ref, place_ref, source_ref, row_ref,
    few_ref, m2a_ref, m2b_ref, m3a_ref, m3b_ref, pos2_ref, pos3_ref, posx_ref, form_ref, count_ref,
    mix_ref, small_mix_ref, column_ref, counts_ref, int_ref, sems, batch,
):
    start_copies(source_ref, int_ref, sems)
    k_all, depth, total = int_ref.shape
    half = depth // 2
    row, col = place_ref[0], place_ref[1]
    pair_label = occ_ref[batch]
    big = largest_irrep(vir_ref)
    mostly_zero = (occ_ref[col * k_all] == pair_label) | (occ_ref[(col + 1) * k_all - 1] == pair_label)
    most = FEW_CAPS[-1]
    for n in range(3):
        counts_ref[n] = 0
    label_mix(mix_ref, column_ref, row_ref, row, big, True)

    @pl.when(mostly_zero)
    def _():
        label_mix(small_mix_ref, column_ref, row_ref, row, big, False)

    local = column_ref[pl.ds(pl.multiple_of(row * depth, depth), depth), :1]

    @pl.loop(0, k_all)
    def _(k):
        @pl.when(k % K_STEP == 0)
        def _():
            wait_copy(source_ref, int_ref, sems, k // K_STEP)

        k_whole = col * k_all + k
        x = jnp.bitwise_xor(occ_ref[k_whole], pair_label)
        on_big = screen_ref[jnp.bitwise_xor(big, x), k_whole] == 1
        actives = (on_big & (x != 0), on_big & (x == 0), x != 0)
        pos2, pos3, posx = [jnp.where(active, counts_ref[n], -1) for n, active in enumerate(actives)]
        for n, active in enumerate(actives):
            counts_ref[n] = counts_ref[n] + active.astype(jnp.int32)
        pos2_ref[k], pos3_ref[k], posx_ref[k] = pos2, pos3, posx

        @pl.when(pos2 >= 0)
        def _():
            wide = kept_folded(int_ref, mix_ref, k, x)
            short = wide[:half] + wide[half:]

            @pl.when(mostly_zero & (posx < most))
            def _():
                for piece in range(2):
                    few_ref[posx, 1 + piece] = short[:, piece * 2 * NARROW:(piece + 1) * 2 * NARROW]

            @pl.when(pos2 < CAPS[0])
            def _():
                m2a_ref[pos2] = short

            @pl.when(pos2 >= CAPS[0])
            def _():
                m2b_ref[pos2 - CAPS[0]] = short

        @pl.when(mostly_zero & (posx >= 0) & (posx < most))
        def _():
            kept = kept_folded(int_ref, small_mix_ref, k, x)
            few_ref[posx, 0] = narrow_fold(kept, screen_bits(screen_ref, k_whole), local)

            @pl.when(pos2 < 0)
            def _():
                for piece in range(2):
                    few_ref[posx, 1 + piece] = jnp.zeros((half, 2 * NARROW), jnp.bfloat16)

        @pl.when(pos3 >= 0)
        def _():
            wide = kept_folded(int_ref, mix_ref, k, x)

            @pl.when(pos3 < CAPS[0])
            def _():
                m3a_ref[pos3] = wide

            @pl.when(pos3 >= CAPS[0])
            def _():
                m3b_ref[pos3 - CAPS[0]] = wide

    labels = row_ref[...]
    lanes = lax.broadcasted_iota(jnp.int32, labels.shape, 1)
    ahead = pltpu.roll(labels, total - NARROW, 1)
    long = (labels == ahead) & (lanes < total - NARROW) & (labels != big)
    too_long = jnp.max(long.astype(jnp.int32)) == 1
    n2, n3, nx = counts_ref[0], counts_ref[1], counts_ref[2]
    count_ref[0] = nx
    one_label = occ_ref[0] == pair_label
    form = jnp.where((nx <= FEW_CAPS[0]) & (n3 <= CAPS[0]), 3, jnp.where(nx <= FEW_CAPS[1], 4, 5))
    form = jnp.where(mostly_zero, form, 5)
    form = jnp.where((n3 <= FEW_WIDE) & (n2 <= CAPS[0]), 2, form)
    form = jnp.where(one_label, form, 6)
    form = jnp.where(n3 == 0, jnp.where(n2 <= CAPS[0], 0, 1), form)
    form_ref[0] = jnp.where(too_long, 6, form)


def wide_blocks(integrals, occ_irrep, vir_irrep, screen, place, batch):
    occ_share, depth, total = integrals.shape
    shapes = [(n, depth // 2, FOLD) for n in CAPS] + [(n, depth, FOLD) for n in CAPS]
    few = (FEW_CAPS[-1], 3, depth // 2, 2 * NARROW)
    smem = pl.BlockSpec(memory_space=pltpu.SMEM)

    def kernel(*refs):
        wide_kernel(*refs, batch)

    vmem = pl.BlockSpec(memory_space=pltpu.VMEM)
    return pl.pallas_call(
        kernel,
        in_specs=[smem] * 4 + [pl.BlockSpec(memory_space=pltpu.HBM), vmem],
        out_specs=[vmem] * (1 + len(shapes)) + [smem] * 5,
        scratch_shapes=[
            pltpu.VMEM((depth, total), jnp.bfloat16),
            pltpu.VMEM((depth, total), jnp.bfloat16),
            pltpu.VMEM((total, 8), jnp.int32),
            pltpu.SMEM((3,), jnp.int32),
            pltpu.VMEM(integrals.shape, jnp.bfloat16),
            pltpu.SemaphoreType.DMA((occ_share // K_STEP,)),
        ],
        out_shape=[jax.ShapeDtypeStruct(v, jnp.bfloat16) for v in [few] + shapes]
        + [jax.ShapeDtypeStruct((n,), jnp.int32) for n in (occ_share, occ_share, occ_share, 1, 1)],
        cost_estimate=cost(5),
        compiler_params=pltpu.CompilerParams(vmem_limit_bytes=24 * 1024 * 1024),
    )(occ_irrep, vir_irrep, screen.T, place, integrals, vir_irrep[None, :])


def narrow_kernel(
    occ_ref, vir_ref, screen_ref, place_ref, source_ref, row_ref, few_ref, narrow_ref,
    mix_ref, column_ref, int_ref, sems, batch,
):
    start_copies(source_ref, int_ref, sems)
    k_all, depth, total = int_ref.shape
    row, col = place_ref[0], place_ref[1]
    label_mix(mix_ref, column_ref, row_ref, row, largest_irrep(vir_ref), False)
    if few_ref is not None:
        for n in range(few_ref.shape[0]):
            for piece in range(2):
                narrow_ref[k_all + 2 * n + piece] = few_ref[n, 1 + piece]
    local = column_ref[pl.ds(pl.multiple_of(row * depth, depth), depth), :1]

    @pl.loop(0, k_all // K_STEP)
    def _(group):
        wait_copy(source_ref, int_ref, sems, group)
        for j in range(K_STEP):
            k = group * K_STEP + j
            k_whole = col * k_all + k
            x = jnp.bitwise_xor(occ_ref[k_whole], occ_ref[batch])
            kept = kept_folded(int_ref, mix_ref, k, x)
            narrow_ref[k] = narrow_fold(kept, screen_bits(screen_ref, k_whole), local)


def narrow_blocks(integrals, occ_irrep, vir_irrep, screen, place, few, batch):
    occ_share, depth, total = integrals.shape
    extra = [] if few is None else [few]
    count = occ_share + sum(2 * v.shape[0] for v in extra)
    smem = pl.BlockSpec(memory_space=pltpu.SMEM)
    vmem = pl.BlockSpec(memory_space=pltpu.VMEM)

    def kernel(*refs):
        narrow_kernel(*(refs if extra else refs[:6] + (None,) + refs[6:]), batch)

    return pl.pallas_call(
        kernel,
        in_specs=[smem] * 4 + [pl.BlockSpec(memory_space=pltpu.HBM), vmem] + [vmem] * len(extra),
        out_specs=vmem,
        out_shape=jax.ShapeDtypeStruct((count, depth // 2, 2 * NARROW), jnp.bfloat16),
        scratch_shapes=[
            pltpu.VMEM((depth, total), jnp.bfloat16),
            pltpu.VMEM((total, 8), jnp.int32),
            pltpu.VMEM(integrals.shape, jnp.bfloat16),
            pltpu.SemaphoreType.DMA((occ_share // K_STEP,)),
        ],
        cost_estimate=cost(4),
        compiler_params=pltpu.CompilerParams(vmem_limit_bytes=16 * 1024 * 1024),
    )(occ_irrep, vir_irrep, screen.T, place, integrals, vir_irrep[None, :], *extra)


def cost(micros):
    return pl.CostEstimate(flops=int(micros * 1e9), bytes_accessed=int(micros * 3e6), transcendentals=0)


SLOTS = (0, 1, 3, 2)
NEAR = 2


def amplitude_rows(column_ref, row_ref, occ_ref, row, batch, share):
    column_ref[...] = label_columns(row_ref[...])
    column = column_ref[pl.ds(pl.multiple_of(row * share, share), share), :1]
    return jnp.concatenate([jnp.bitwise_xor(column, occ_ref[i]) for i in range(batch)], axis=0)


def write_quarters(total_ref, col, outs):
    rows, fold = total_ref.shape
    width, height = fold // 2, rows // 2
    for t, out_ref in enumerate(outs):
        goal = jnp.bitwise_xor(col, t)
        lanes = pl.ds(pl.multiple_of((goal % 2) * width, width), width)
        lines = pl.ds(pl.multiple_of((goal // 2) * height, height), height)
        out_ref[...] = total_ref[lines, lanes].reshape(out_ref.shape)


def chosen(refs, starts, pos, pick):
    block = None
    for n, group in enumerate(refs):
        inside = (pos >= starts[n]) & (pos < starts[n + 1])
        at = jnp.clip(pos - starts[n], 0, starts[n + 1] - starts[n] - 1)
        found = pick(group, at)
        found = jnp.where(inside, found, jnp.zeros_like(found))
        block = found if block is None else block + found
    return block


def starts_of(arrays):
    starts = [0]
    for v in arrays:
        starts.append(starts[-1] + v.shape[0])
    return starts


def mask_kernel(
    occ_ref, place_ref, posx_ref, amp_ref, row_ref, lhs_ref, third_ref, far_ref, fold_ref, few_lhs_ref,
    mix_ref, column_ref, amp_buffer, sems,
):
    batch, k_all, share, total = amp_ref.shape
    rows, groups = batch * share, k_all // K_STEP
    row, col = place_ref[0], place_ref[1]

    def fetch(group):
        slot = group % 2
        source = amp_ref.at[:, pl.ds(group * K_STEP, K_STEP)]
        return pltpu.make_async_copy(source, amp_buffer.at[slot], sems.at[slot])

    fetch(0).start()
    column = amplitude_rows(column_ref, row_ref, occ_ref, row, batch, share)
    mix_ref[...] = as_bf16(jnp.bitwise_xor(column, row_ref[...]))
    if few_lhs_ref is not None:
        few_lhs_ref[...] = jnp.zeros(few_lhs_ref.shape, jnp.bfloat16)

    @pl.loop(0, groups)
    def _(group):
        slot = group % 2

        @pl.when(group + 1 < groups)
        def _():
            fetch(group + 1).start()

        fetch(group).wait()

        @pl.loop(0, K_STEP)
        def _(j):
            wanted = as_bf16(jnp.full((rows, share), occ_ref[col * k_all + group * K_STEP + j]))
            folded = None
            for n, s in enumerate(SLOTS):
                place = pl.ds(pl.multiple_of(jnp.bitwise_xor(row, s) * share, share), share)
                tile = amp_buffer[slot, :, j, :, place].reshape(rows, share)
                piece = jnp.where(mix_ref[:, place] == wanted, tile, jnp.zeros_like(tile))
                if n < NEAR:
                    lhs_ref[group, :, pl.ds(pl.multiple_of((n * K_STEP + j) * share, share), share)] = piece
                else:
                    own_ref = third_ref if n == NEAR else far_ref
                    own_ref[group, :, pl.ds(pl.multiple_of(j * share, share), share)] = piece
                folded = piece if folded is None else folded + piece
            if fold_ref is not None:
                fold_ref[group, :, pl.ds(pl.multiple_of(j * share, share), share)] = folded
            else:
                posx = posx_ref[group * K_STEP + j]

                @pl.when((posx >= 0) & (posx < few_lhs_ref.shape[0]))
                def _():
                    here = pl.ds(pl.multiple_of(j * share, share), share)
                    few_lhs_ref[posx, 0] = third_ref[group, :, here]
                    few_lhs_ref[posx, 1] = far_ref[group, :, here]
                    few_lhs_ref[posx, 2] = folded


def masked_amplitudes(amplitudes, occ_irrep, vir_irrep, place, posx, few):
    batch, k_all, share, total = amplitudes.shape
    rows, groups = batch * share, k_all // K_STEP
    smem = pl.BlockSpec(memory_space=pltpu.SMEM)
    vmem = pl.BlockSpec(memory_space=pltpu.VMEM)
    hbm = pl.BlockSpec(memory_space=pltpu.HBM)
    shapes = [(groups, rows, w) for w in (NEAR * K_STEP * share, K_STEP * share, K_STEP * share)]
    shapes += [(few, 3, rows, share)] if few else [(groups, rows, K_STEP * share)]

    def kernel(*refs):
        mask_kernel(*(refs[:8] + (None,) + refs[8:] if few else refs[:9] + (None,) + refs[9:]))

    return pl.pallas_call(
        kernel,
        in_specs=[smem, smem, smem, hbm, vmem],
        out_specs=[vmem] * len(shapes),
        out_shape=[jax.ShapeDtypeStruct(v, jnp.bfloat16) for v in shapes],
        scratch_shapes=[
            pltpu.VMEM((rows, total), jnp.bfloat16),
            pltpu.VMEM((total, 8), jnp.int32),
            pltpu.VMEM((2, batch, K_STEP, share, total), jnp.bfloat16),
            pltpu.SemaphoreType.DMA((2,)),
        ],
        cost_estimate=cost(7),
        compiler_params=pltpu.CompilerParams(vmem_limit_bytes=28 * 1024 * 1024),
    )(occ_irrep, place, posx, amplitudes, vir_irrep[None, :])


def make_first_kernel(few, n3, starts3):
    def kernel(pos3_ref, place_ref, lhs_ref, third_ref, far_ref, *refs):
        sources = 3 if few else 5
        narrow_refs, refs = refs[:sources], refs[sources:]
        m3_refs = [refs[3 * n:3 * n + 3] for n in range(n3)]
        narrow_sum, wide_sum, narrow_rhs, wide_rhs = refs[3 * n3:]
        row = place_ref[0]
        at_end = (row == 0) | (row == 3)
        groups, _, depth = lhs_ref.shape
        share = depth // (NEAR * K_STEP)
        half = share // 2
        lane = lax.broadcasted_iota(jnp.int32, (half, 2 * NARROW), 1)

        narrow_sum[...] = jnp.zeros(narrow_sum.shape, jnp.float32)
        wide_sum[...] = jnp.zeros(wide_sum.shape, jnp.float32)

        @pl.loop(0, groups)
        def _(group):
            @pl.loop(0, K_STEP)
            def _(j):
                k = group * K_STEP + j
                if few:
                    blocks = [ref[k] for ref in narrow_refs]
                else:
                    own, e1, o1, e2, o2 = [ref[k] for ref in narrow_refs]
                    blocks = (own, e1, o1, jnp.where(at_end, e2, o2))
                for n, block in enumerate(blocks):
                    zero = jnp.zeros_like(block)
                    first = pl.multiple_of((n * K_STEP + j) * share, share)
                    narrow_rhs[pl.ds(first, half)] = jnp.where(lane < NARROW, block, zero)
                    narrow_rhs[pl.ds(first + half, half)] = jnp.where(lane < NARROW, zero, block)
                for n in range(3 if n3 else 0):
                    block = chosen(m3_refs, starts3, pos3_ref[k], lambda group, at, n=n: group[n][at])
                    if n == 2:
                        block = jnp.where(at_end, jnp.zeros_like(block), block)
                    wide_rhs[pl.ds(pl.multiple_of((n * K_STEP + j) * share, share), share)] = block

            one = depth // NEAR
            narrow = jnp.dot(lhs_ref[group], narrow_rhs[:depth], preferred_element_type=jnp.float32)
            narrow += jnp.dot(third_ref[group], narrow_rhs[depth:depth + one], preferred_element_type=jnp.float32)
            if not few:
                narrow += jnp.dot(far_ref[group], narrow_rhs[depth + one:], preferred_element_type=jnp.float32)
            narrow_sum[...] += narrow
            if n3:
                wide = jnp.dot(lhs_ref[group], wide_rhs[:depth], preferred_element_type=jnp.float32)
                wide += jnp.dot(third_ref[group], wide_rhs[depth:], preferred_element_type=jnp.float32)
                wide_sum[...] += wide

    return kernel


def first_product(lhs, third_lhs, far_lhs, pos3, place, narrow, few, m3):
    groups, rows, depth = lhs.shape
    vmem = pl.BlockSpec(memory_space=pltpu.VMEM)
    smem = pl.BlockSpec(memory_space=pltpu.SMEM)
    arrays = list(narrow) + [v for group in m3 for v in group]
    wide = (rows, FOLD) if m3 else (16, FOLD)
    wide_depth = depth // NEAR * 3 if m3 else 16
    return pl.pallas_call(
        make_first_kernel(few, len(m3), starts_of([v[0] for v in m3])),
        in_specs=[smem] * 2 + [vmem] * (3 + len(arrays)),
        out_specs=[vmem] * 2,
        out_shape=[jax.ShapeDtypeStruct(v, jnp.float32) for v in ((rows, 2 * NARROW), wide)],
        scratch_shapes=[
            pltpu.VMEM((depth // NEAR * len(SLOTS), 2 * NARROW), jnp.bfloat16),
            pltpu.VMEM((wide_depth, FOLD), jnp.bfloat16),
        ],
        cost_estimate=cost(9 if m3 else 6),
        compiler_params=pltpu.CompilerParams(vmem_limit_bytes=32 * 1024 * 1024),
    )(pos3, place, lhs, third_lhs, far_lhs, *arrays)


def make_last_kernel(few, n2, starts2, n3, starts3):
    def kernel(
        occ_ref, vir_ref, pos2_ref, pos3_ref, count_ref, place_ref, fold_ref, third_ref, far_ref, row_ref, narrow_ref, wide_ref,
        *refs,
    ):
        m2_refs, refs = refs[:n2], refs[n2:]
        m3_refs = [refs[2 * n:2 * n + 2] for n in range(n3)]
        refs = refs[2 * n3:]
        e3_ref, refs = (None, refs) if few else (refs[0], refs[1:])
        outs = refs[:4]
        column_ref, total_ref, narrow_sum, short_rhs, far_rhs, third_rhs = refs[4:]
        row, col = place_ref[0], place_ref[1]
        at_end = (row == 0) | (row == 3)
        groups, rows, width = far_ref.shape if few else fold_ref.shape
        share = width // K_STEP
        batch = rows // share
        @pl.loop(0, groups * K_STEP)
        def _(k):
            here = pl.ds(pl.multiple_of(k * share, share), share)
            if not few:
                short = chosen(m2_refs, starts2, pos2_ref[k], lambda ref, at: ref[at])
                short_rhs[here] = jnp.concatenate([short, short], axis=0)
            if n3:
                far_rhs[here] = chosen(
                    m3_refs, starts3, pos3_ref[k], lambda pair, at: jnp.where(at_end, pair[0][at], pair[1][at])
                )

        column = amplitude_rows(column_ref, row_ref, occ_ref, row, batch, share)
        target = jnp.bitwise_xor(column, occ_ref[batch])
        if few:
            own, e1, o1, two, three = m2_refs
            half = share // 2
            lane = lax.broadcasted_iota(jnp.int32, (half, 2 * NARROW), 1)
            total_ref[...] = wide_ref[...]
            narrow_sum[...] = narrow_ref[...]

            @pl.loop(0, count_ref[0])
            def _(n):
                for slot, wanted, ref in ((0, at_end, three), (1, True, two)):
                    block = ref[n, 0]
                    zero = jnp.zeros_like(block)
                    block = jnp.where(wanted, block, zero)
                    rhs = jnp.concatenate(
                        [jnp.where(lane < NARROW, block, zero), jnp.where(lane < NARROW, zero, block)], axis=0
                    )
                    narrow_sum[...] += jnp.dot(fold_ref[n, slot], rhs, preferred_element_type=jnp.float32)
                pieces = []
                for piece in range(2):
                    close = groups * K_STEP + 2 * n + piece
                    block = own[n, 1 + piece] + e1[close] + two[n, 1 + piece]
                    pieces.append(block + jnp.where(at_end, three[n, 1 + piece], o1[close]))
                short = jnp.concatenate(pieces, axis=1)
                rhs = jnp.concatenate([short, short], axis=0)
                total_ref[...] += jnp.dot(fold_ref[n, 2], rhs, preferred_element_type=jnp.float32)

        else:
            narrow_sum[...] = narrow_ref[...]

            @pl.when(at_end)
            def _():
                half = share // 2
                lane = lax.broadcasted_iota(jnp.int32, (half, 2 * NARROW), 1)

                @pl.loop(0, groups * K_STEP)
                def _(k):
                    block = e3_ref[k]
                    zero = jnp.zeros_like(block)
                    first = pl.multiple_of(k * share, share)
                    third_rhs[pl.ds(first, half)] = jnp.where(lane < NARROW, block, zero)
                    third_rhs[pl.ds(first + half, half)] = jnp.where(lane < NARROW, zero, block)

                @pl.loop(0, groups)
                def _(group):
                    rhs = third_rhs[pl.ds(pl.multiple_of(group * width, width), width)]
                    narrow_sum[...] += jnp.dot(third_ref[group], rhs, preferred_element_type=jnp.float32)

            total_ref[...] = wide_ref[...] if n3 else jnp.zeros(total_ref.shape, jnp.float32)
        @pl.loop(0, groups)
        def _(group):
            here = pl.ds(pl.multiple_of(group * width, width), width)
            if not few:
                total_ref[...] += jnp.dot(fold_ref[group], short_rhs[here], preferred_element_type=jnp.float32)
            if n3:
                total_ref[...] += jnp.dot(far_ref[group], far_rhs[here], preferred_element_type=jnp.float32)

        both = narrow_sum[...]
        both = both + pltpu.roll(both, NARROW, 1)
        both = jnp.concatenate([both] * (FOLD // (2 * NARROW)), axis=1)
        total_ref[...] = jnp.where(target == largest_irrep(vir_ref), total_ref[...], both)
        write_quarters(total_ref, col, outs)

    return kernel


def last_product(third_lhs, far_lhs, fold, occ_irrep, vir_irrep, pos2, pos3, count, place, narrow_sum, wide_sum, few, m2, m3, e3, batch):
    groups, rows, width = far_lhs.shape
    share = rows // batch
    vmem = pl.BlockSpec(memory_space=pltpu.VMEM)
    smem = pl.BlockSpec(memory_space=pltpu.SMEM)
    arrays = [narrow_sum, wide_sum] + list(m2) + [v for group in m3 for v in group] + list(e3)
    quarter = (batch // 2, share, FOLD // 2)
    whole = groups * width
    unused = jnp.zeros((16, 128), jnp.bfloat16)
    return pl.pallas_call(
        make_last_kernel(few, len(m2), starts_of(m2), len(m3), starts_of([v[0] for v in m3])),
        in_specs=[smem] * 6 + [vmem] * (4 + len(arrays)),
        out_specs=[vmem] * 4,
        out_shape=[jax.ShapeDtypeStruct(quarter, jnp.float32)] * 4,
        scratch_shapes=[
            pltpu.VMEM((vir_irrep.shape[0], 8), jnp.int32),
            pltpu.VMEM((rows, FOLD), jnp.float32),
            pltpu.VMEM((rows, 2 * NARROW), jnp.float32),
            pltpu.VMEM((16 if few else whole, FOLD), jnp.bfloat16),
            pltpu.VMEM((whole if m3 else 16, FOLD), jnp.bfloat16),
            pltpu.VMEM((16 if few else whole, 2 * NARROW), jnp.bfloat16),
        ],
        cost_estimate=cost(4 if m3 else 3),
        compiler_params=pltpu.CompilerParams(vmem_limit_bytes=32 * 1024 * 1024),
    )(occ_irrep, vir_irrep, pos2, pos3, count, place, fold, unused if few else third_lhs,
      far_lhs if m3 else unused, vir_irrep[None, :], *arrays)


def dense_product(amplitudes, whole, occ_irrep, occ_local, vir_local, vir_irrep):
    batch = amplitudes.shape[0]
    keep = (
        jnp.bitwise_xor(occ_irrep[:batch, None], occ_local[None, :])[:, :, None, None]
        == jnp.bitwise_xor(vir_local[:, None], vir_irrep[None, :])[None, None]
    )
    kept = jnp.where(keep, amplitudes, jnp.zeros_like(amplitudes))
    return lax.dot_general(
        kept, whole, (((1, 3), (0, 1)), ((), ())), preferred_element_type=jnp.float32
    )


def finish(cycle, occ_irrep, vir_irrep, occ_energy, vir_energy, a_start, a_size, b_start, b_size, batch):
    label_a = lax.dynamic_slice_in_dim(vir_irrep, a_start, a_size)
    label_b = lax.dynamic_slice_in_dim(vir_irrep, b_start, b_size)
    energy_a = lax.dynamic_slice_in_dim(vir_energy, a_start, a_size)
    energy_b = lax.dynamic_slice_in_dim(vir_energy, b_start, b_size)
    target = jnp.bitwise_xor(
        jnp.bitwise_xor(occ_irrep[:batch, None], occ_irrep[batch]), label_a[None, :]
    )
    keep = label_b[:, None, None] == target[None, :, :]
    denominator = (
        occ_energy[:batch][None, :, None]
        + occ_energy[batch]
        - energy_a[None, None, :]
        - energy_b[:, None, None]
    )
    swapped = jnp.transpose(cycle, (2, 0, 1))
    return jnp.where(keep, swapped, 0.0) / denominator


def on_square(amplitudes, integrals, occ_irrep, vir_irrep, screen):
    batch, occ_share, share, vir_total = amplitudes.shape
    row = lax.axis_index("row")
    col = lax.axis_index("col")
    place = jnp.stack([row, col]).astype(jnp.int32)
    few, m2a, m2b, m3a, m3b, pos2, pos3, posx, form, count = wide_blocks(
        integrals, occ_irrep, vir_irrep, screen, place, batch
    )
    outer = [(0, 1), (1, 0), (2, 3), (3, 2)]
    inner = [(1, 2), (2, 1)]
    inward = [(0, 1), (3, 2)]
    outward = [(1, 0), (2, 3)]
    ends = [(0, 3), (3, 0)]
    second = [(r, r ^ 2) for r in range(4)]

    def move(v, pairs):
        return lax.ppermute(v, "row", pairs)

    def sparse(use_few, choose):
        def run(few, m2a, m2b, m3a, m3b):
            shorts, wides = choose(m2a, m2b, m3a, m3b)
            near = [(own, move(own, outer), move(own, inner)) for own in wides]
            few = few[:use_few] if use_few else None
            narrow = narrow_blocks(integrals, occ_irrep, vir_irrep, screen, place, few, batch)
            if use_few:
                e1, o1 = move(narrow, outer), move(narrow, inner)
                lhs, third_lhs, far_lhs, fold = masked_amplitudes(
                    amplitudes, occ_irrep, vir_irrep, place, posx, use_few
                )
                near, e1, o1, few, _ = lax.optimization_barrier((near, e1, o1, few, fold))
                two, three = move(few, second), move(few, ends)
                blocks, e3 = (narrow, e1, o1), []
                sums = (few, e1, o1, two, three)
            else:
                h1 = [move(v, inward) for v in shorts]
                o1, e1 = move(narrow, inner), move(narrow, outward)
                lhs, third_lhs, far_lhs, fold = masked_amplitudes(
                    amplitudes, occ_irrep, vir_irrep, place, posx, 0
                )
                near, h1, o1, e1, _ = lax.optimization_barrier((near, h1, o1, e1, fold))
                h2 = [move(own + v, inner) for own, v in zip(shorts, h1)]
                e1 = e1 + move(narrow, inward)
                e2 = move(o1, outward)
                h2, e1, e2 = lax.optimization_barrier((h2, e1, e2))
                h3 = [move(own + v, outward) for own, v in zip(shorts, h2)]
                o2 = move(e1, inner)
                blocks, e3 = (narrow, e1, o1, e2, o2), [move(o2, outward)]
                sums = [a + b + c + d for a, b, c, d in zip(shorts, h1, h2, h3)]
            far = [(move(o, outward), move(e, inner)) for _, e, o in near]
            narrow_sum, wide_sum = first_product(
                lhs, third_lhs, far_lhs, pos3, place, blocks, bool(use_few), near
            )
            return list(last_product(
                third_lhs, far_lhs, fold, occ_irrep, vir_irrep, pos2, pos3, count, place, narrow_sum, wide_sum,
                bool(use_few), sums, far, e3, batch
            ))

        return run

    def dense(*_):
        occ_local = lax.dynamic_slice_in_dim(occ_irrep, col * occ_share, occ_share)
        vir_local = lax.dynamic_slice_in_dim(vir_irrep, row * share, share)
        screen_rows = lax.dynamic_slice_in_dim(screen, col * occ_share, occ_share, 0)
        fold = folded_integrals(
            integrals, occ_local, vir_local, vir_irrep, occ_irrep[batch], screen_rows
        )
        whole = jnp.zeros((occ_share, vir_total, FOLD), fold.dtype)
        for s in range(4):
            block = move(fold, [(r, r ^ s) for r in range(4)]) if s else fold
            whole = lax.dynamic_update_slice_in_dim(whole, block, jnp.bitwise_xor(row, s) * share, 1)
        total = dense_product(amplitudes, whole, occ_irrep, occ_local, vir_local, vir_irrep)
        quarter = (batch // 2, share, FOLD // 2)
        goals = [jnp.bitwise_xor(col, t) for t in range(4)]
        return [
            lax.dynamic_slice(total, (g // 2 * quarter[0], 0, g % 2 * quarter[2]), quarter) for g in goals
        ]

    branches = [
        sparse(0, lambda m2a, m2b, m3a, m3b: ([m2a], [])),
        sparse(0, lambda m2a, m2b, m3a, m3b: ([m2a, m2b], [])),
        sparse(0, lambda m2a, m2b, m3a, m3b: ([m2a], [m3a[:FEW_WIDE]])),
        sparse(FEW_CAPS[0], lambda m2a, m2b, m3a, m3b: ([], [m3a])),
        sparse(FEW_CAPS[1], lambda m2a, m2b, m3a, m3b: ([], [m3a, m3b])),
        sparse(0, lambda m2a, m2b, m3a, m3b: ([m2a, m2b], [m3a, m3b])),
        dense,
    ]
    quarters = lax.switch(form[0], branches, few, m2a, m2b, m3a, m3b)
    mine = quarters[0]
    for t in (1, 2, 3):
        mine = mine + lax.ppermute(quarters[t], "col", [(q, q ^ t) for q in range(4)])
    places = [(r, q) for r in range(4) for q in range(4)]
    same = lax.ppermute(mine, ("row", "col"), [(r * 4 + q, q * 4 + r) for r, q in places])
    other = lax.ppermute(mine, ("row", "col"), [(r * 4 + q, (q ^ 2) * 4 + r) for r, q in places])
    upper = row // 2 == 1
    low = jnp.where(upper, other, same)
    high = jnp.where(upper, same, other)
    return jnp.concatenate([low, high], axis=0)


def on_any(amplitudes, integrals, occ_irrep, vir_irrep, screen):
    batch, occ_share, share, vir_total = amplitudes.shape
    row = lax.axis_index("row")
    col = lax.axis_index("col")
    occ_local = lax.dynamic_slice_in_dim(occ_irrep, col * occ_share, occ_share)
    vir_local = lax.dynamic_slice_in_dim(vir_irrep, row * share, share)
    screen_rows = lax.dynamic_slice_in_dim(screen, col * occ_share, occ_share, 0)
    fold = folded_integrals(
        integrals, occ_local, vir_local, vir_irrep, occ_irrep[batch], screen_rows
    )
    whole = lax.all_gather(fold, "row", axis=1, tiled=True)
    cycle = dense_product(amplitudes, whole, occ_irrep, occ_local, vir_local, vir_irrep)
    cycle = lax.psum(cycle, "col")
    cycle = jnp.concatenate([cycle] * (vir_total // FOLD), axis=2)
    cycle = lax.all_to_all(cycle, "row", split_axis=2, concat_axis=1, tiled=True)
    a_size = vir_total // lax.axis_size("col")
    return lax.dynamic_slice_in_dim(cycle, col * a_size, a_size, 1)


def on_device(amplitudes, integrals, occ_irrep, vir_irrep, screen, occ_energy, vir_energy):
    batch, _, vir_share, vir_total = amplitudes.shape
    square = lax.axis_size("row") == 4 and lax.axis_size("col") == 4
    form = on_square if square else on_any
    cycle = form(amplitudes, integrals, occ_irrep, vir_irrep, screen)
    a_size = vir_total // lax.axis_size("col")
    return finish(
        cycle, occ_irrep, vir_irrep, occ_energy, vir_energy,
        lax.axis_index("col") * a_size, a_size, lax.axis_index("row") * vir_share, vir_share, batch,
    )


def solution(mesh):
    in_specs = (
        P("parts", "col", "row", None),
        P(("parts", "col"), "row", None),
        P("parts"),
        P("parts"),
        P("parts", None),
        P("parts"),
        P("parts"),
    )
    out_specs = P("row", "parts", "col")
    return jax.shard_map(
        on_device, mesh=mesh, in_specs=in_specs, out_specs=out_specs, check_vma=False
    )
```

```python
import jax
import jax.numpy as jnp
from jax import lax
from jax.experimental import pallas as pl
from jax.experimental.pallas import tpu as pltpu
from jax.sharding import PartitionSpec as P

FOLD = 256
K_STEP = 5


def folded_integrals(integrals, occ_local, vir_local, vir_irrep, pair_label, screen_rows):
    irrep_codes = jnp.arange(8, dtype=jnp.int32)
    screen_local = jnp.sum(
        screen_rows[:, None, :] * (vir_local[None, :, None] == irrep_codes).astype(jnp.int32),
        axis=2,
    )
    target = jnp.bitwise_xor(
        jnp.bitwise_xor(occ_local[:, None], vir_local[None, :]), pair_label
    )
    target = jnp.where(screen_local == 1, target, -1)
    keep = target[:, :, None] == vir_irrep[None, None, :]
    kept = jnp.where(keep, integrals, jnp.zeros_like(integrals))
    return kept[:, :, :FOLD] + kept[:, :, FOLD:]


NARROW = 64
CAPS = (22, 3)
FEW_CAPS = (4, 10)
FEW_WIDE = 5


def largest_irrep(vir_ref):
    return jnp.where(vir_ref[0] == vir_ref[FOLD - 1], vir_ref[0], vir_ref[FOLD])


def label_columns(row_labels):
    return jnp.transpose(jnp.broadcast_to(row_labels, (8, row_labels.shape[1])))


def as_bf16(labels):
    return labels.astype(jnp.float32).astype(jnp.bfloat16)


def label_mix(mix_ref, column_ref, row_ref, row, big, keep_big):
    depth = mix_ref.shape[0]
    column_ref[...] = label_columns(row_ref[...])
    column = column_ref[pl.ds(pl.multiple_of(row * depth, depth), depth), :1]
    is_big = row_ref[...] == big
    wanted = is_big if keep_big else jnp.logical_not(is_big)
    mix_ref[...] = as_bf16(jnp.where(wanted, jnp.bitwise_xor(column, row_ref[...]), 8))


def kept_folded(int_ref, mix_ref, j, x):
    tile = int_ref[j]
    wanted = as_bf16(jnp.full(mix_ref.shape, x))
    kept = jnp.where(mix_ref[...] == wanted, tile, jnp.zeros_like(tile))
    return kept[:, :FOLD] + kept[:, FOLD:]


def narrow_fold(kept, bits, local):
    half = kept.shape[0] // 2
    lane = lax.broadcasted_iota(jnp.int32, (half, 2 * NARROW), 1)
    narrow = (kept[:, : 2 * NARROW] + kept[:, 2 * NARROW:]).astype(jnp.float32)
    narrow = narrow + pltpu.roll(narrow, NARROW, 1)
    on = jnp.bitwise_and(lax.shift_right_logical(jnp.full(local.shape, bits), local), 1) == 1
    narrow = jnp.where(on, narrow, 0.0)
    return jnp.where(lane < NARROW, narrow[:half], narrow[half:]).astype(jnp.bfloat16)


def screen_bits(screen_ref, k):
    bits = screen_ref[0, k]
    for g in range(1, 8):
        bits = bits + screen_ref[g, k] * (1 << g)
    return bits


def copy_of(source_ref, int_ref, sems, group):
    here = pl.ds(group * K_STEP, K_STEP)
    return pltpu.make_async_copy(source_ref.at[here], int_ref.at[here], sems.at[group])


def start_copies(source_ref, int_ref, sems):
    for group in range(int_ref.shape[0] // K_STEP):
        copy_of(source_ref, int_ref, sems, group).start()


def wait_copy(source_ref, int_ref, sems, group):
    copy_of(source_ref, int_ref, sems, group).wait()


def wide_kernel(
    occ_ref, vir_ref, screen_ref, place_ref, source_ref, row_ref,
    few_ref, m2a_ref, m2b_ref, m3a_ref, m3b_ref, pos2_ref, pos3_ref, posx_ref, form_ref, count_ref,
    mix_ref, small_mix_ref, column_ref, counts_ref, int_ref, sems, batch,
):
    start_copies(source_ref, int_ref, sems)
    k_all, depth, total = int_ref.shape
    half = depth // 2
    row, col = place_ref[0], place_ref[1]
    pair_label = occ_ref[batch]
    big = largest_irrep(vir_ref)
    mostly_zero = (occ_ref[col * k_all] == pair_label) | (occ_ref[(col + 1) * k_all - 1] == pair_label)
    most = FEW_CAPS[-1]
    for n in range(3):
        counts_ref[n] = 0
    label_mix(mix_ref, column_ref, row_ref, row, big, True)

    @pl.when(mostly_zero)
    def _():
        label_mix(small_mix_ref, column_ref, row_ref, row, big, False)

    local = column_ref[pl.ds(pl.multiple_of(row * depth, depth), depth), :1]

    @pl.loop(0, k_all)
    def _(k):
        @pl.when(k % K_STEP == 0)
        def _():
            wait_copy(source_ref, int_ref, sems, k // K_STEP)

        k_whole = col * k_all + k
        x = jnp.bitwise_xor(occ_ref[k_whole], pair_label)
        on_big = screen_ref[jnp.bitwise_xor(big, x), k_whole] == 1
        actives = (on_big & (x != 0), on_big & (x == 0), x != 0)
        pos2, pos3, posx = [jnp.where(active, counts_ref[n], -1) for n, active in enumerate(actives)]
        for n, active in enumerate(actives):
            counts_ref[n] = counts_ref[n] + active.astype(jnp.int32)
        pos2_ref[k], pos3_ref[k], posx_ref[k] = pos2, pos3, posx

        @pl.when(pos2 >= 0)
        def _():
            wide = kept_folded(int_ref, mix_ref, k, x)
            short = wide[:half] + wide[half:]

            @pl.when(mostly_zero & (posx < most))
            def _():
                for piece in range(2):
                    few_ref[posx, 1 + piece] = short[:, piece * 2 * NARROW:(piece + 1) * 2 * NARROW]

            @pl.when(pos2 < CAPS[0])
            def _():
                m2a_ref[pos2] = short

            @pl.when(pos2 >= CAPS[0])
            def _():
                m2b_ref[pos2 - CAPS[0]] = short

        @pl.when(mostly_zero & (posx >= 0) & (posx < most))
        def _():
            kept = kept_folded(int_ref, small_mix_ref, k, x)
            few_ref[posx, 0] = narrow_fold(kept, screen_bits(screen_ref, k_whole), local)

            @pl.when(pos2 < 0)
            def _():
                for piece in range(2):
                    few_ref[posx, 1 + piece] = jnp.zeros((half, 2 * NARROW), jnp.bfloat16)

        @pl.when(pos3 >= 0)
        def _():
            wide = kept_folded(int_ref, mix_ref, k, x)

            @pl.when(pos3 < CAPS[0])
            def _():
                m3a_ref[pos3] = wide

            @pl.when(pos3 >= CAPS[0])
            def _():
                m3b_ref[pos3 - CAPS[0]] = wide

    labels = row_ref[...]
    lanes = lax.broadcasted_iota(jnp.int32, labels.shape, 1)
    ahead = pltpu.roll(labels, total - NARROW, 1)
    long = (labels == ahead) & (lanes < total - NARROW) & (labels != big)
    too_long = jnp.max(long.astype(jnp.int32)) == 1
    n2, n3, nx = counts_ref[0], counts_ref[1], counts_ref[2]
    count_ref[0] = nx
    one_label = occ_ref[0] == pair_label
    form = jnp.where(nx <= FEW_CAPS[0], 3, jnp.where(nx <= FEW_CAPS[1], 4, 5))
    form = jnp.where(mostly_zero & (n3 <= CAPS[0]), form, 5)
    form = jnp.where((n3 <= FEW_WIDE) & (n2 <= CAPS[0]), 2, form)
    form = jnp.where(one_label, form, 6)
    form = jnp.where(n3 == 0, jnp.where(n2 <= CAPS[0], 0, 1), form)
    form_ref[0] = jnp.where(too_long, 6, form)


def wide_blocks(integrals, occ_irrep, vir_irrep, screen, place, batch):
    occ_share, depth, total = integrals.shape
    shapes = [(n, depth // 2, FOLD) for n in CAPS] + [(n, depth, FOLD) for n in CAPS]
    few = (FEW_CAPS[-1], 3, depth // 2, 2 * NARROW)
    smem = pl.BlockSpec(memory_space=pltpu.SMEM)

    def kernel(*refs):
        wide_kernel(*refs, batch)

    vmem = pl.BlockSpec(memory_space=pltpu.VMEM)
    return pl.pallas_call(
        kernel,
        in_specs=[smem] * 4 + [pl.BlockSpec(memory_space=pltpu.HBM), vmem],
        out_specs=[vmem] * (1 + len(shapes)) + [smem] * 5,
        scratch_shapes=[
            pltpu.VMEM((depth, total), jnp.bfloat16),
            pltpu.VMEM((depth, total), jnp.bfloat16),
            pltpu.VMEM((total, 8), jnp.int32),
            pltpu.SMEM((3,), jnp.int32),
            pltpu.VMEM(integrals.shape, jnp.bfloat16),
            pltpu.SemaphoreType.DMA((occ_share // K_STEP,)),
        ],
        out_shape=[jax.ShapeDtypeStruct(v, jnp.bfloat16) for v in [few] + shapes]
        + [jax.ShapeDtypeStruct((n,), jnp.int32) for n in (occ_share, occ_share, occ_share, 1, 1)],
        cost_estimate=cost(5),
        compiler_params=pltpu.CompilerParams(vmem_limit_bytes=24 * 1024 * 1024),
    )(occ_irrep, vir_irrep, screen.T, place, integrals, vir_irrep[None, :])


def narrow_kernel(
    occ_ref, vir_ref, screen_ref, place_ref, source_ref, row_ref, few_ref, narrow_ref,
    mix_ref, column_ref, int_ref, sems, batch,
):
    start_copies(source_ref, int_ref, sems)
    k_all, depth, total = int_ref.shape
    row, col = place_ref[0], place_ref[1]
    label_mix(mix_ref, column_ref, row_ref, row, largest_irrep(vir_ref), False)
    if few_ref is not None:
        for n in range(few_ref.shape[0]):
            for piece in range(2):
                narrow_ref[k_all + 2 * n + piece] = few_ref[n, 1 + piece]
    local = column_ref[pl.ds(pl.multiple_of(row * depth, depth), depth), :1]

    @pl.loop(0, k_all // K_STEP)
    def _(group):
        wait_copy(source_ref, int_ref, sems, group)
        for j in range(K_STEP):
            k = group * K_STEP + j
            k_whole = col * k_all + k
            x = jnp.bitwise_xor(occ_ref[k_whole], occ_ref[batch])
            kept = kept_folded(int_ref, mix_ref, k, x)
            narrow_ref[k] = narrow_fold(kept, screen_bits(screen_ref, k_whole), local)


def narrow_blocks(integrals, occ_irrep, vir_irrep, screen, place, few, batch):
    occ_share, depth, total = integrals.shape
    extra = [] if few is None else [few]
    count = occ_share + sum(2 * v.shape[0] for v in extra)
    smem = pl.BlockSpec(memory_space=pltpu.SMEM)
    vmem = pl.BlockSpec(memory_space=pltpu.VMEM)

    def kernel(*refs):
        narrow_kernel(*(refs if extra else refs[:6] + (None,) + refs[6:]), batch)

    return pl.pallas_call(
        kernel,
        in_specs=[smem] * 4 + [pl.BlockSpec(memory_space=pltpu.HBM), vmem] + [vmem] * len(extra),
        out_specs=vmem,
        out_shape=jax.ShapeDtypeStruct((count, depth // 2, 2 * NARROW), jnp.bfloat16),
        scratch_shapes=[
            pltpu.VMEM((depth, total), jnp.bfloat16),
            pltpu.VMEM((total, 8), jnp.int32),
            pltpu.VMEM(integrals.shape, jnp.bfloat16),
            pltpu.SemaphoreType.DMA((occ_share // K_STEP,)),
        ],
        cost_estimate=cost(4),
        compiler_params=pltpu.CompilerParams(vmem_limit_bytes=16 * 1024 * 1024),
    )(occ_irrep, vir_irrep, screen.T, place, integrals, vir_irrep[None, :], *extra)


def cost(micros):
    return pl.CostEstimate(flops=int(micros * 1e9), bytes_accessed=int(micros * 3e6), transcendentals=0)


SLOTS = (0, 1, 3, 2)
NEAR = 2


def amplitude_rows(column_ref, row_ref, occ_ref, row, batch, share):
    column_ref[...] = label_columns(row_ref[...])
    column = column_ref[pl.ds(pl.multiple_of(row * share, share), share), :1]
    return jnp.concatenate([jnp.bitwise_xor(column, occ_ref[i]) for i in range(batch)], axis=0)


def write_quarters(total_ref, col, outs):
    rows, fold = total_ref.shape
    width, height = fold // 2, rows // 2
    for t, out_ref in enumerate(outs):
        goal = jnp.bitwise_xor(col, t)
        lanes = pl.ds(pl.multiple_of((goal % 2) * width, width), width)
        lines = pl.ds(pl.multiple_of((goal // 2) * height, height), height)
        out_ref[...] = total_ref[lines, lanes].reshape(out_ref.shape)


def chosen(refs, starts, pos, pick):
    block = None
    for n, group in enumerate(refs):
        inside = (pos >= starts[n]) & (pos < starts[n + 1])
        at = jnp.clip(pos - starts[n], 0, starts[n + 1] - starts[n] - 1)
        found = pick(group, at)
        found = jnp.where(inside, found, jnp.zeros_like(found))
        block = found if block is None else block + found
    return block


def starts_of(arrays):
    starts = [0]
    for v in arrays:
        starts.append(starts[-1] + v.shape[0])
    return starts


def mask_kernel(
    occ_ref, place_ref, posx_ref, amp_ref, row_ref, lhs_ref, third_ref, far_ref, fold_ref, few_lhs_ref,
    mix_ref, column_ref, amp_buffer, sems,
):
    batch, k_all, share, total = amp_ref.shape
    rows, groups = batch * share, k_all // K_STEP
    row, col = place_ref[0], place_ref[1]

    def fetch(group):
        slot = group % 2
        source = amp_ref.at[:, pl.ds(group * K_STEP, K_STEP)]
        return pltpu.make_async_copy(source, amp_buffer.at[slot], sems.at[slot])

    fetch(0).start()
    column = amplitude_rows(column_ref, row_ref, occ_ref, row, batch, share)
    mix_ref[...] = as_bf16(jnp.bitwise_xor(column, row_ref[...]))
    if few_lhs_ref is not None:
        few_lhs_ref[...] = jnp.zeros(few_lhs_ref.shape, jnp.bfloat16)

    @pl.loop(0, groups)
    def _(group):
        slot = group % 2

        @pl.when(group + 1 < groups)
        def _():
            fetch(group + 1).start()

        fetch(group).wait()

        @pl.loop(0, K_STEP)
        def _(j):
            wanted = as_bf16(jnp.full((rows, share), occ_ref[col * k_all + group * K_STEP + j]))
            folded = None
            for n, s in enumerate(SLOTS):
                place = pl.ds(pl.multiple_of(jnp.bitwise_xor(row, s) * share, share), share)
                tile = amp_buffer[slot, :, j, :, place].reshape(rows, share)
                piece = jnp.where(mix_ref[:, place] == wanted, tile, jnp.zeros_like(tile))
                if n < NEAR:
                    lhs_ref[group, :, pl.ds(pl.multiple_of((n * K_STEP + j) * share, share), share)] = piece
                else:
                    own_ref = third_ref if n == NEAR else far_ref
                    own_ref[group, :, pl.ds(pl.multiple_of(j * share, share), share)] = piece
                folded = piece if folded is None else folded + piece
            if fold_ref is not None:
                fold_ref[group, :, pl.ds(pl.multiple_of(j * share, share), share)] = folded
            else:
                posx = posx_ref[group * K_STEP + j]

                @pl.when((posx >= 0) & (posx < few_lhs_ref.shape[0]))
                def _():
                    here = pl.ds(pl.multiple_of(j * share, share), share)
                    few_lhs_ref[posx, 0] = third_ref[group, :, here]
                    few_lhs_ref[posx, 1] = far_ref[group, :, here]
                    few_lhs_ref[posx, 2] = folded


def masked_amplitudes(amplitudes, occ_irrep, vir_irrep, place, posx, few):
    batch, k_all, share, total = amplitudes.shape
    rows, groups = batch * share, k_all // K_STEP
    smem = pl.BlockSpec(memory_space=pltpu.SMEM)
    vmem = pl.BlockSpec(memory_space=pltpu.VMEM)
    hbm = pl.BlockSpec(memory_space=pltpu.HBM)
    shapes = [(groups, rows, w) for w in (NEAR * K_STEP * share, K_STEP * share, K_STEP * share)]
    shapes += [(few, 3, rows, share)] if few else [(groups, rows, K_STEP * share)]

    def kernel(*refs):
        mask_kernel(*(refs[:8] + (None,) + refs[8:] if few else refs[:9] + (None,) + refs[9:]))

    return pl.pallas_call(
        kernel,
        in_specs=[smem, smem, smem, hbm, vmem],
        out_specs=[vmem] * len(shapes),
        out_shape=[jax.ShapeDtypeStruct(v, jnp.bfloat16) for v in shapes],
        scratch_shapes=[
            pltpu.VMEM((rows, total), jnp.bfloat16),
            pltpu.VMEM((total, 8), jnp.int32),
            pltpu.VMEM((2, batch, K_STEP, share, total), jnp.bfloat16),
            pltpu.SemaphoreType.DMA((2,)),
        ],
        cost_estimate=cost(7),
        compiler_params=pltpu.CompilerParams(vmem_limit_bytes=28 * 1024 * 1024),
    )(occ_irrep, place, posx, amplitudes, vir_irrep[None, :])


def make_first_kernel(few, n3, starts3):
    def kernel(pos3_ref, place_ref, lhs_ref, third_ref, far_ref, *refs):
        sources = 3 if few else 5
        narrow_refs, refs = refs[:sources], refs[sources:]
        m3_refs = [refs[3 * n:3 * n + 3] for n in range(n3)]
        narrow_sum, wide_sum, narrow_rhs, wide_rhs = refs[3 * n3:]
        row = place_ref[0]
        at_end = (row == 0) | (row == 3)
        groups, _, depth = lhs_ref.shape
        share = depth // (NEAR * K_STEP)
        half = share // 2
        lane = lax.broadcasted_iota(jnp.int32, (half, 2 * NARROW), 1)

        narrow_sum[...] = jnp.zeros(narrow_sum.shape, jnp.float32)
        wide_sum[...] = jnp.zeros(wide_sum.shape, jnp.float32)

        @pl.loop(0, groups)
        def _(group):
            @pl.loop(0, K_STEP)
            def _(j):
                k = group * K_STEP + j
                if few:
                    blocks = [ref[k] for ref in narrow_refs]
                else:
                    own, e1, o1, e2, o2 = [ref[k] for ref in narrow_refs]
                    blocks = (own, e1, o1, jnp.where(at_end, e2, o2))
                for n, block in enumerate(blocks):
                    zero = jnp.zeros_like(block)
                    first = pl.multiple_of((n * K_STEP + j) * share, share)
                    narrow_rhs[pl.ds(first, half)] = jnp.where(lane < NARROW, block, zero)
                    narrow_rhs[pl.ds(first + half, half)] = jnp.where(lane < NARROW, zero, block)
                for n in range(3 if n3 else 0):
                    block = chosen(m3_refs, starts3, pos3_ref[k], lambda group, at, n=n: group[n][at])
                    if n == 2:
                        block = jnp.where(at_end, jnp.zeros_like(block), block)
                    wide_rhs[pl.ds(pl.multiple_of((n * K_STEP + j) * share, share), share)] = block

            one = depth // NEAR
            narrow = jnp.dot(lhs_ref[group], narrow_rhs[:depth], preferred_element_type=jnp.float32)
            narrow += jnp.dot(third_ref[group], narrow_rhs[depth:depth + one], preferred_element_type=jnp.float32)
            if not few:
                narrow += jnp.dot(far_ref[group], narrow_rhs[depth + one:], preferred_element_type=jnp.float32)
            narrow_sum[...] += narrow
            if n3:
                wide = jnp.dot(lhs_ref[group], wide_rhs[:depth], preferred_element_type=jnp.float32)
                wide += jnp.dot(third_ref[group], wide_rhs[depth:], preferred_element_type=jnp.float32)
                wide_sum[...] += wide

    return kernel


def first_product(lhs, third_lhs, far_lhs, pos3, place, narrow, few, m3):
    groups, rows, depth = lhs.shape
    vmem = pl.BlockSpec(memory_space=pltpu.VMEM)
    smem = pl.BlockSpec(memory_space=pltpu.SMEM)
    arrays = list(narrow) + [v for group in m3 for v in group]
    wide = (rows, FOLD) if m3 else (16, FOLD)
    wide_depth = depth // NEAR * 3 if m3 else 16
    return pl.pallas_call(
        make_first_kernel(few, len(m3), starts_of([v[0] for v in m3])),
        in_specs=[smem] * 2 + [vmem] * (3 + len(arrays)),
        out_specs=[vmem] * 2,
        out_shape=[jax.ShapeDtypeStruct(v, jnp.float32) for v in ((rows, 2 * NARROW), wide)],
        scratch_shapes=[
            pltpu.VMEM((depth // NEAR * len(SLOTS), 2 * NARROW), jnp.bfloat16),
            pltpu.VMEM((wide_depth, FOLD), jnp.bfloat16),
        ],
        cost_estimate=cost(9 if m3 else 6),
        compiler_params=pltpu.CompilerParams(vmem_limit_bytes=32 * 1024 * 1024),
    )(pos3, place, lhs, third_lhs, far_lhs, *arrays)


def make_last_kernel(few, n2, starts2, n3, starts3):
    def kernel(
        occ_ref, vir_ref, pos2_ref, pos3_ref, count_ref, place_ref, fold_ref, third_ref, far_ref, row_ref, narrow_ref, wide_ref,
        *refs,
    ):
        m2_refs, refs = refs[:n2], refs[n2:]
        m3_refs = [refs[2 * n:2 * n + 2] for n in range(n3)]
        refs = refs[2 * n3:]
        e3_ref, refs = (None, refs) if few else (refs[0], refs[1:])
        outs = refs[:4]
        column_ref, total_ref, narrow_sum, short_rhs, far_rhs, third_rhs = refs[4:]
        row, col = place_ref[0], place_ref[1]
        at_end = (row == 0) | (row == 3)
        groups, rows, width = far_ref.shape if few else fold_ref.shape
        share = width // K_STEP
        batch = rows // share
        @pl.loop(0, groups * K_STEP)
        def _(k):
            here = pl.ds(pl.multiple_of(k * share, share), share)
            if not few:
                short = chosen(m2_refs, starts2, pos2_ref[k], lambda ref, at: ref[at])
                short_rhs[here] = jnp.concatenate([short, short], axis=0)
            if n3:
                far_rhs[here] = chosen(
                    m3_refs, starts3, pos3_ref[k], lambda pair, at: jnp.where(at_end, pair[0][at], pair[1][at])
                )

        column = amplitude_rows(column_ref, row_ref, occ_ref, row, batch, share)
        target = jnp.bitwise_xor(column, occ_ref[batch])
        if few:
            own, e1, o1, two, three = m2_refs
            half = share // 2
            lane = lax.broadcasted_iota(jnp.int32, (half, 2 * NARROW), 1)
            total_ref[...] = wide_ref[...]
            narrow_sum[...] = narrow_ref[...]

            @pl.loop(0, count_ref[0])
            def _(n):
                for slot, wanted, ref in ((0, at_end, three), (1, True, two)):
                    block = ref[n, 0]
                    zero = jnp.zeros_like(block)
                    block = jnp.where(wanted, block, zero)
                    rhs = jnp.concatenate(
                        [jnp.where(lane < NARROW, block, zero), jnp.where(lane < NARROW, zero, block)], axis=0
                    )
                    narrow_sum[...] += jnp.dot(fold_ref[n, slot], rhs, preferred_element_type=jnp.float32)
                pieces = []
                for piece in range(2):
                    close = groups * K_STEP + 2 * n + piece
                    block = own[n, 1 + piece] + e1[close] + two[n, 1 + piece]
                    pieces.append(block + jnp.where(at_end, three[n, 1 + piece], o1[close]))
                short = jnp.concatenate(pieces, axis=1)
                rhs = jnp.concatenate([short, short], axis=0)
                total_ref[...] += jnp.dot(fold_ref[n, 2], rhs, preferred_element_type=jnp.float32)

        else:
            narrow_sum[...] = narrow_ref[...]

            @pl.when(at_end)
            def _():
                half = share // 2
                lane = lax.broadcasted_iota(jnp.int32, (half, 2 * NARROW), 1)

                @pl.loop(0, groups * K_STEP)
                def _(k):
                    block = e3_ref[k]
                    zero = jnp.zeros_like(block)
                    first = pl.multiple_of(k * share, share)
                    third_rhs[pl.ds(first, half)] = jnp.where(lane < NARROW, block, zero)
                    third_rhs[pl.ds(first + half, half)] = jnp.where(lane < NARROW, zero, block)

                @pl.loop(0, groups)
                def _(group):
                    rhs = third_rhs[pl.ds(pl.multiple_of(group * width, width), width)]
                    narrow_sum[...] += jnp.dot(third_ref[group], rhs, preferred_element_type=jnp.float32)

            total_ref[...] = wide_ref[...] if n3 else jnp.zeros(total_ref.shape, jnp.float32)
        @pl.loop(0, groups)
        def _(group):
            here = pl.ds(pl.multiple_of(group * width, width), width)
            if not few:
                total_ref[...] += jnp.dot(fold_ref[group], short_rhs[here], preferred_element_type=jnp.float32)
            if n3:
                total_ref[...] += jnp.dot(far_ref[group], far_rhs[here], preferred_element_type=jnp.float32)

        both = narrow_sum[...]
        both = both + pltpu.roll(both, NARROW, 1)
        both = jnp.concatenate([both] * (FOLD // (2 * NARROW)), axis=1)
        total_ref[...] = jnp.where(target == largest_irrep(vir_ref), total_ref[...], both)
        write_quarters(total_ref, col, outs)

    return kernel


def last_product(third_lhs, far_lhs, fold, occ_irrep, vir_irrep, pos2, pos3, count, place, narrow_sum, wide_sum, few, m2, m3, e3, batch):
    groups, rows, width = far_lhs.shape
    share = rows // batch
    vmem = pl.BlockSpec(memory_space=pltpu.VMEM)
    smem = pl.BlockSpec(memory_space=pltpu.SMEM)
    arrays = [narrow_sum, wide_sum] + list(m2) + [v for group in m3 for v in group] + list(e3)
    quarter = (batch // 2, share, FOLD // 2)
    whole = groups * width
    unused = jnp.zeros((16, 128), jnp.bfloat16)
    return pl.pallas_call(
        make_last_kernel(few, len(m2), starts_of(m2), len(m3), starts_of([v[0] for v in m3])),
        in_specs=[smem] * 6 + [vmem] * (4 + len(arrays)),
        out_specs=[vmem] * 4,
        out_shape=[jax.ShapeDtypeStruct(quarter, jnp.float32)] * 4,
        scratch_shapes=[
            pltpu.VMEM((vir_irrep.shape[0], 8), jnp.int32),
            pltpu.VMEM((rows, FOLD), jnp.float32),
            pltpu.VMEM((rows, 2 * NARROW), jnp.float32),
            pltpu.VMEM((16 if few else whole, FOLD), jnp.bfloat16),
            pltpu.VMEM((whole if m3 else 16, FOLD), jnp.bfloat16),
            pltpu.VMEM((16 if few else whole, 2 * NARROW), jnp.bfloat16),
        ],
        cost_estimate=cost(4 if m3 else 3),
        compiler_params=pltpu.CompilerParams(vmem_limit_bytes=32 * 1024 * 1024),
    )(occ_irrep, vir_irrep, pos2, pos3, count, place, fold, unused if few else third_lhs,
      far_lhs if m3 else unused, vir_irrep[None, :], *arrays)


def dense_product(amplitudes, whole, occ_irrep, occ_local, vir_local, vir_irrep):
    batch = amplitudes.shape[0]
    keep = (
        jnp.bitwise_xor(occ_irrep[:batch, None], occ_local[None, :])[:, :, None, None]
        == jnp.bitwise_xor(vir_local[:, None], vir_irrep[None, :])[None, None]
    )
    kept = jnp.where(keep, amplitudes, jnp.zeros_like(amplitudes))
    return lax.dot_general(
        kept, whole, (((1, 3), (0, 1)), ((), ())), preferred_element_type=jnp.float32
    )


def finish(cycle, occ_irrep, vir_irrep, occ_energy, vir_energy, a_start, a_size, b_start, b_size, batch):
    label_a = lax.dynamic_slice_in_dim(vir_irrep, a_start, a_size)
    label_b = lax.dynamic_slice_in_dim(vir_irrep, b_start, b_size)
    energy_a = lax.dynamic_slice_in_dim(vir_energy, a_start, a_size)
    energy_b = lax.dynamic_slice_in_dim(vir_energy, b_start, b_size)
    target = jnp.bitwise_xor(
        jnp.bitwise_xor(occ_irrep[:batch, None], occ_irrep[batch]), label_a[None, :]
    )
    keep = label_b[:, None, None] == target[None, :, :]
    denominator = (
        occ_energy[:batch][None, :, None]
        + occ_energy[batch]
        - energy_a[None, None, :]
        - energy_b[:, None, None]
    )
    swapped = jnp.transpose(cycle, (2, 0, 1))
    return jnp.where(keep, swapped, 0.0) / denominator


def on_square(amplitudes, integrals, occ_irrep, vir_irrep, screen):
    batch, occ_share, share, vir_total = amplitudes.shape
    row = lax.axis_index("row")
    col = lax.axis_index("col")
    place = jnp.stack([row, col]).astype(jnp.int32)
    few, m2a, m2b, m3a, m3b, pos2, pos3, posx, form, count = wide_blocks(
        integrals, occ_irrep, vir_irrep, screen, place, batch
    )
    outer = [(0, 1), (1, 0), (2, 3), (3, 2)]
    inner = [(1, 2), (2, 1)]
    inward = [(0, 1), (3, 2)]
    outward = [(1, 0), (2, 3)]
    ends = [(0, 3), (3, 0)]
    second = [(r, r ^ 2) for r in range(4)]

    def move(v, pairs):
        return lax.ppermute(v, "row", pairs)

    def sparse(use_few, choose):
        def run(few, m2a, m2b, m3a, m3b):
            shorts, wides = choose(m2a, m2b, m3a, m3b)
            near = [(own, move(own, outer), move(own, inner)) for own in wides]
            few = few[:use_few] if use_few else None
            narrow = narrow_blocks(integrals, occ_irrep, vir_irrep, screen, place, few, batch)
            if use_few:
                e1, o1 = move(narrow, outer), move(narrow, inner)
                lhs, third_lhs, far_lhs, fold = masked_amplitudes(
                    amplitudes, occ_irrep, vir_irrep, place, posx, use_few
                )
                near, e1, o1, few, _ = lax.optimization_barrier((near, e1, o1, few, fold))
                two, three = move(few, second), move(few, ends)
                blocks, e3 = (narrow, e1, o1), []
                sums = (few, e1, o1, two, three)
            else:
                h1 = [move(v, inward) for v in shorts]
                o1, e1 = move(narrow, inner), move(narrow, outward)
                lhs, third_lhs, far_lhs, fold = masked_amplitudes(
                    amplitudes, occ_irrep, vir_irrep, place, posx, 0
                )
                near, h1, o1, e1, _ = lax.optimization_barrier((near, h1, o1, e1, fold))
                h2 = [move(own + v, inner) for own, v in zip(shorts, h1)]
                e1 = e1 + move(narrow, inward)
                e2 = move(o1, outward)
                h2, e1, e2 = lax.optimization_barrier((h2, e1, e2))
                h3 = [move(own + v, outward) for own, v in zip(shorts, h2)]
                o2 = move(e1, inner)
                blocks, e3 = (narrow, e1, o1, e2, o2), [move(o2, outward)]
                sums = [a + b + c + d for a, b, c, d in zip(shorts, h1, h2, h3)]
            far = [(move(o, outward), move(e, inner)) for _, e, o in near]
            narrow_sum, wide_sum = first_product(
                lhs, third_lhs, far_lhs, pos3, place, blocks, bool(use_few), near
            )
            return list(last_product(
                third_lhs, far_lhs, fold, occ_irrep, vir_irrep, pos2, pos3, count, place, narrow_sum, wide_sum,
                bool(use_few), sums, far, e3, batch
            ))

        return run

    def dense(*_):
        occ_local = lax.dynamic_slice_in_dim(occ_irrep, col * occ_share, occ_share)
        vir_local = lax.dynamic_slice_in_dim(vir_irrep, row * share, share)
        screen_rows = lax.dynamic_slice_in_dim(screen, col * occ_share, occ_share, 0)
        fold = folded_integrals(
            integrals, occ_local, vir_local, vir_irrep, occ_irrep[batch], screen_rows
        )
        whole = jnp.zeros((occ_share, vir_total, FOLD), fold.dtype)
        for s in range(4):
            block = move(fold, [(r, r ^ s) for r in range(4)]) if s else fold
            whole = lax.dynamic_update_slice_in_dim(whole, block, jnp.bitwise_xor(row, s) * share, 1)
        total = dense_product(amplitudes, whole, occ_irrep, occ_local, vir_local, vir_irrep)
        quarter = (batch // 2, share, FOLD // 2)
        goals = [jnp.bitwise_xor(col, t) for t in range(4)]
        return [
            lax.dynamic_slice(total, (g // 2 * quarter[0], 0, g % 2 * quarter[2]), quarter) for g in goals
        ]

    branches = [
        sparse(0, lambda m2a, m2b, m3a, m3b: ([m2a], [])),
        sparse(0, lambda m2a, m2b, m3a, m3b: ([m2a, m2b], [])),
        sparse(0, lambda m2a, m2b, m3a, m3b: ([m2a], [m3a[:FEW_WIDE]])),
        sparse(FEW_CAPS[0], lambda m2a, m2b, m3a, m3b: ([], [m3a])),
        sparse(FEW_CAPS[1], lambda m2a, m2b, m3a, m3b: ([], [m3a])),
        sparse(0, lambda m2a, m2b, m3a, m3b: ([m2a, m2b], [m3a, m3b])),
        dense,
    ]
    quarters = lax.switch(form[0], branches, few, m2a, m2b, m3a, m3b)
    mine = quarters[0]
    for t in (1, 2, 3):
        mine = mine + lax.ppermute(quarters[t], "col", [(q, q ^ t) for q in range(4)])
    places = [(r, q) for r in range(4) for q in range(4)]
    same = lax.ppermute(mine, ("row", "col"), [(r * 4 + q, q * 4 + r) for r, q in places])
    other = lax.ppermute(mine, ("row", "col"), [(r * 4 + q, (q ^ 2) * 4 + r) for r, q in places])
    upper = row // 2 == 1
    low = jnp.where(upper, other, same)
    high = jnp.where(upper, same, other)
    return jnp.concatenate([low, high], axis=0)


def on_any(amplitudes, integrals, occ_irrep, vir_irrep, screen):
    batch, occ_share, share, vir_total = amplitudes.shape
    row = lax.axis_index("row")
    col = lax.axis_index("col")
    occ_local = lax.dynamic_slice_in_dim(occ_irrep, col * occ_share, occ_share)
    vir_local = lax.dynamic_slice_in_dim(vir_irrep, row * share, share)
    screen_rows = lax.dynamic_slice_in_dim(screen, col * occ_share, occ_share, 0)
    fold = folded_integrals(
        integrals, occ_local, vir_local, vir_irrep, occ_irrep[batch], screen_rows
    )
    whole = lax.all_gather(fold, "row", axis=1, tiled=True)
    cycle = dense_product(amplitudes, whole, occ_irrep, occ_local, vir_local, vir_irrep)
    cycle = lax.psum(cycle, "col")
    cycle = jnp.concatenate([cycle] * (vir_total // FOLD), axis=2)
    cycle = lax.all_to_all(cycle, "row", split_axis=2, concat_axis=1, tiled=True)
    a_size = vir_total // lax.axis_size("col")
    return lax.dynamic_slice_in_dim(cycle, col * a_size, a_size, 1)


def on_device(amplitudes, integrals, occ_irrep, vir_irrep, screen, occ_energy, vir_energy):
    batch, _, vir_share, vir_total = amplitudes.shape
    square = lax.axis_size("row") == 4 and lax.axis_size("col") == 4
    form = on_square if square else on_any
    cycle = form(amplitudes, integrals, occ_irrep, vir_irrep, screen)
    a_size = vir_total // lax.axis_size("col")
    return finish(
        cycle, occ_irrep, vir_irrep, occ_energy, vir_energy,
        lax.axis_index("col") * a_size, a_size, lax.axis_index("row") * vir_share, vir_share, batch,
    )


def solution(mesh):
    in_specs = (
        P("parts", "col", "row", None),
        P(("parts", "col"), "row", None),
        P("parts"),
        P("parts"),
        P("parts", None),
        P("parts"),
        P("parts"),
    )
    out_specs = P("row", "parts", "col")
    return jax.shard_map(
        on_device, mesh=mesh, in_specs=in_specs, out_specs=out_specs, check_vma=False
    )
```

```python
import jax
import jax.numpy as jnp
from jax import lax
from jax.experimental import pallas as pl
from jax.experimental.pallas import tpu as pltpu
from jax.sharding import PartitionSpec as P

FOLD = 256
K_STEP = 5


def folded_integrals(integrals, occ_local, vir_local, vir_irrep, pair_label, screen_rows):
    irrep_codes = jnp.arange(8, dtype=jnp.int32)
    screen_local = jnp.sum(
        screen_rows[:, None, :] * (vir_local[None, :, None] == irrep_codes).astype(jnp.int32),
        axis=2,
    )
    target = jnp.bitwise_xor(
        jnp.bitwise_xor(occ_local[:, None], vir_local[None, :]), pair_label
    )
    target = jnp.where(screen_local == 1, target, -1)
    keep = target[:, :, None] == vir_irrep[None, None, :]
    kept = jnp.where(keep, integrals, jnp.zeros_like(integrals))
    return kept[:, :, :FOLD] + kept[:, :, FOLD:]


NARROW = 64
CAPS = (22, 3)
FEW_CAPS = (4, 10)
FEW_WIDE = 5


def largest_irrep(vir_ref):
    return jnp.where(vir_ref[0] == vir_ref[FOLD - 1], vir_ref[0], vir_ref[FOLD])


def label_columns(row_labels):
    return jnp.transpose(jnp.broadcast_to(row_labels, (8, row_labels.shape[1])))


def as_bf16(labels):
    return labels.astype(jnp.float32).astype(jnp.bfloat16)


def label_mix(mix_ref, column_ref, row_ref, row, big, keep_big):
    depth = mix_ref.shape[0]
    column_ref[...] = label_columns(row_ref[...])
    column = column_ref[pl.ds(pl.multiple_of(row * depth, depth), depth), :1]
    is_big = row_ref[...] == big
    wanted = is_big if keep_big else jnp.logical_not(is_big)
    mix_ref[...] = as_bf16(jnp.where(wanted, jnp.bitwise_xor(column, row_ref[...]), 8))


def kept_folded(int_ref, mix_ref, j, x):
    tile = int_ref[j]
    wanted = as_bf16(jnp.full(mix_ref.shape, x))
    kept = jnp.where(mix_ref[...] == wanted, tile, jnp.zeros_like(tile))
    return kept[:, :FOLD] + kept[:, FOLD:]


def narrow_fold(kept, bits, local):
    half = kept.shape[0] // 2
    lane = lax.broadcasted_iota(jnp.int32, (half, 2 * NARROW), 1)
    narrow = (kept[:, : 2 * NARROW] + kept[:, 2 * NARROW:]).astype(jnp.float32)
    narrow = narrow + pltpu.roll(narrow, NARROW, 1)
    on = jnp.bitwise_and(lax.shift_right_logical(jnp.full(local.shape, bits), local), 1) == 1
    narrow = jnp.where(on, narrow, 0.0)
    return jnp.where(lane < NARROW, narrow[:half], narrow[half:]).astype(jnp.bfloat16)


def screen_bits(screen_ref, k):
    bits = screen_ref[0, k]
    for g in range(1, 8):
        bits = bits + screen_ref[g, k] * (1 << g)
    return bits


def copy_of(source_ref, int_ref, sems, group):
    here = pl.ds(group * K_STEP, K_STEP)
    return pltpu.make_async_copy(source_ref.at[here], int_ref.at[here], sems.at[group])


def start_copies(source_ref, int_ref, sems):
    for group in range(int_ref.shape[0] // K_STEP):
        copy_of(source_ref, int_ref, sems, group).start()


def wait_copy(source_ref, int_ref, sems, group):
    copy_of(source_ref, int_ref, sems, group).wait()


def wide_kernel(
    occ_ref, vir_ref, screen_ref, place_ref, source_ref, row_ref,
    few_ref, m2a_ref, m2b_ref, m3a_ref, m3b_ref, pos2_ref, pos3_ref, posx_ref, form_ref, count_ref,
    mix_ref, small_mix_ref, column_ref, counts_ref, int_ref, sems, batch,
):
    start_copies(source_ref, int_ref, sems)
    k_all, depth, total = int_ref.shape
    half = depth // 2
    row, col = place_ref[0], place_ref[1]
    pair_label = occ_ref[batch]
    big = largest_irrep(vir_ref)
    mostly_zero = (occ_ref[col * k_all] == pair_label) | (occ_ref[(col + 1) * k_all - 1] == pair_label)
    most = FEW_CAPS[-1]
    for n in range(3):
        counts_ref[n] = 0
    label_mix(mix_ref, column_ref, row_ref, row, big, True)

    @pl.when(mostly_zero)
    def _():
        label_mix(small_mix_ref, column_ref, row_ref, row, big, False)

    local = column_ref[pl.ds(pl.multiple_of(row * depth, depth), depth), :1]

    @pl.loop(0, k_all)
    def _(k):
        @pl.when(k % K_STEP == 0)
        def _():
            wait_copy(source_ref, int_ref, sems, k // K_STEP)

        k_whole = col * k_all + k
        x = jnp.bitwise_xor(occ_ref[k_whole], pair_label)
        on_big = screen_ref[jnp.bitwise_xor(big, x), k_whole] == 1
        actives = (on_big & (x != 0), on_big & (x == 0), x != 0)
        pos2, pos3, posx = [jnp.where(active, counts_ref[n], -1) for n, active in enumerate(actives)]
        for n, active in enumerate(actives):
            counts_ref[n] = counts_ref[n] + active.astype(jnp.int32)
        pos2_ref[k], pos3_ref[k], posx_ref[k] = pos2, pos3, posx

        @pl.when(pos2 >= 0)
        def _():
            wide = kept_folded(int_ref, mix_ref, k, x)
            short = wide[:half] + wide[half:]

            @pl.when(mostly_zero & (posx < most))
            def _():
                for piece in range(2):
                    few_ref[posx, 1 + piece] = short[:, piece * 2 * NARROW:(piece + 1) * 2 * NARROW]

            @pl.when(pos2 < CAPS[0])
            def _():
                m2a_ref[pos2] = short

            @pl.when(pos2 >= CAPS[0])
            def _():
                m2b_ref[pos2 - CAPS[0]] = short

        @pl.when(mostly_zero & (posx >= 0) & (posx < most))
        def _():
            kept = kept_folded(int_ref, small_mix_ref, k, x)
            few_ref[posx, 0] = narrow_fold(kept, screen_bits(screen_ref, k_whole), local)

            @pl.when(pos2 < 0)
            def _():
                for piece in range(2):
                    few_ref[posx, 1 + piece] = jnp.zeros((half, 2 * NARROW), jnp.bfloat16)

        @pl.when(pos3 >= 0)
        def _():
            wide = kept_folded(int_ref, mix_ref, k, x)

            @pl.when(pos3 < CAPS[0])
            def _():
                m3a_ref[pos3] = wide

            @pl.when(pos3 >= CAPS[0])
            def _():
                m3b_ref[pos3 - CAPS[0]] = wide

    labels = row_ref[...]
    lanes = lax.broadcasted_iota(jnp.int32, labels.shape, 1)
    ahead = pltpu.roll(labels, total - NARROW, 1)
    long = (labels == ahead) & (lanes < total - NARROW) & (labels != big)
    too_long = jnp.max(long.astype(jnp.int32)) == 1
    n2, n3, nx = counts_ref[0], counts_ref[1], counts_ref[2]
    count_ref[0] = nx
    one_label = occ_ref[0] == pair_label
    form = jnp.where(nx <= FEW_CAPS[0], 3, jnp.where(nx <= FEW_CAPS[1], 4, 5))
    form = jnp.where(mostly_zero & (n3 <= CAPS[0]), form, 5)
    form = jnp.where((n3 <= FEW_WIDE) & (n2 <= CAPS[0]), 2, form)
    form = jnp.where(one_label, form, 6)
    form = jnp.where(n3 == 0, jnp.where(n2 <= CAPS[0], 0, 1), form)
    form_ref[0] = jnp.where(too_long, 6, form)


def wide_blocks(integrals, occ_irrep, vir_irrep, screen, place, batch):
    occ_share, depth, total = integrals.shape
    shapes = [(n, depth // 2, FOLD) for n in CAPS] + [(n, depth, FOLD) for n in CAPS]
    few = (FEW_CAPS[-1], 3, depth // 2, 2 * NARROW)
    smem = pl.BlockSpec(memory_space=pltpu.SMEM)

    def kernel(*refs):
        wide_kernel(*refs, batch)

    vmem = pl.BlockSpec(memory_space=pltpu.VMEM)
    return pl.pallas_call(
        kernel,
        in_specs=[smem] * 4 + [pl.BlockSpec(memory_space=pltpu.HBM), vmem],
        out_specs=[vmem] * (1 + len(shapes)) + [smem] * 5,
        scratch_shapes=[
            pltpu.VMEM((depth, total), jnp.bfloat16),
            pltpu.VMEM((depth, total), jnp.bfloat16),
            pltpu.VMEM((total, 8), jnp.int32),
            pltpu.SMEM((3,), jnp.int32),
            pltpu.VMEM(integrals.shape, jnp.bfloat16),
            pltpu.SemaphoreType.DMA((occ_share // K_STEP,)),
        ],
        out_shape=[jax.ShapeDtypeStruct(v, jnp.bfloat16) for v in [few] + shapes]
        + [jax.ShapeDtypeStruct((n,), jnp.int32) for n in (occ_share, occ_share, occ_share, 1, 1)],
        cost_estimate=cost(5),
        compiler_params=pltpu.CompilerParams(vmem_limit_bytes=24 * 1024 * 1024),
    )(occ_irrep, vir_irrep, screen.T, place, integrals, vir_irrep[None, :])


def narrow_kernel(
    occ_ref, vir_ref, screen_ref, place_ref, source_ref, row_ref, few_ref, narrow_ref,
    mix_ref, column_ref, int_ref, sems, batch,
):
    start_copies(source_ref, int_ref, sems)
    k_all, depth, total = int_ref.shape
    row, col = place_ref[0], place_ref[1]
    label_mix(mix_ref, column_ref, row_ref, row, largest_irrep(vir_ref), False)
    if few_ref is not None:
        for n in range(few_ref.shape[0]):
            for piece in range(2):
                narrow_ref[k_all + 2 * n + piece] = few_ref[n, 1 + piece]
    local = column_ref[pl.ds(pl.multiple_of(row * depth, depth), depth), :1]

    @pl.loop(0, k_all // K_STEP)
    def _(group):
        wait_copy(source_ref, int_ref, sems, group)
        for j in range(K_STEP):
            k = group * K_STEP + j
            k_whole = col * k_all + k
            x = jnp.bitwise_xor(occ_ref[k_whole], occ_ref[batch])
            kept = kept_folded(int_ref, mix_ref, k, x)
            narrow_ref[k] = narrow_fold(kept, screen_bits(screen_ref, k_whole), local)


def narrow_blocks(integrals, occ_irrep, vir_irrep, screen, place, few, batch):
    occ_share, depth, total = integrals.shape
    extra = [] if few is None else [few]
    count = occ_share + sum(2 * v.shape[0] for v in extra)
    smem = pl.BlockSpec(memory_space=pltpu.SMEM)
    vmem = pl.BlockSpec(memory_space=pltpu.VMEM)

    def kernel(*refs):
        narrow_kernel(*(refs if extra else refs[:6] + (None,) + refs[6:]), batch)

    return pl.pallas_call(
        kernel,
        in_specs=[smem] * 4 + [pl.BlockSpec(memory_space=pltpu.HBM), vmem] + [vmem] * len(extra),
        out_specs=vmem,
        out_shape=jax.ShapeDtypeStruct((count, depth // 2, 2 * NARROW), jnp.bfloat16),
        scratch_shapes=[
            pltpu.VMEM((depth, total), jnp.bfloat16),
            pltpu.VMEM((total, 8), jnp.int32),
            pltpu.VMEM(integrals.shape, jnp.bfloat16),
            pltpu.SemaphoreType.DMA((occ_share // K_STEP,)),
        ],
        cost_estimate=cost(4),
        compiler_params=pltpu.CompilerParams(vmem_limit_bytes=16 * 1024 * 1024),
    )(occ_irrep, vir_irrep, screen.T, place, integrals, vir_irrep[None, :], *extra)


def cost(micros):
    return pl.CostEstimate(flops=int(micros * 1e9), bytes_accessed=int(micros * 3e6), transcendentals=0)


SLOTS = (0, 1, 3, 2)
NEAR = 2


def amplitude_rows(column_ref, row_ref, occ_ref, row, batch, share):
    column_ref[...] = label_columns(row_ref[...])
    column = column_ref[pl.ds(pl.multiple_of(row * share, share), share), :1]
    return jnp.concatenate([jnp.bitwise_xor(column, occ_ref[i]) for i in range(batch)], axis=0)


def write_quarters(total_ref, col, outs):
    rows, fold = total_ref.shape
    width, height = fold // 2, rows // 2
    for t, out_ref in enumerate(outs):
        goal = jnp.bitwise_xor(col, t)
        lanes = pl.ds(pl.multiple_of((goal % 2) * width, width), width)
        lines = pl.ds(pl.multiple_of((goal // 2) * height, height), height)
        out_ref[...] = total_ref[lines, lanes].reshape(out_ref.shape)


def chosen(refs, starts, pos, pick):
    block = None
    for n, group in enumerate(refs):
        inside = (pos >= starts[n]) & (pos < starts[n + 1])
        at = jnp.clip(pos - starts[n], 0, starts[n + 1] - starts[n] - 1)
        found = pick(group, at)
        found = jnp.where(inside, found, jnp.zeros_like(found))
        block = found if block is None else block + found
    return block


def starts_of(arrays):
    starts = [0]
    for v in arrays:
        starts.append(starts[-1] + v.shape[0])
    return starts


def mask_kernel(
    occ_ref, place_ref, posx_ref, amp_ref, row_ref, lhs_ref, third_ref, far_ref, fold_ref, few_lhs_ref,
    mix_ref, column_ref, amp_buffer, sems,
):
    batch, k_all, share, total = amp_ref.shape
    rows, groups = batch * share, k_all // K_STEP
    row, col = place_ref[0], place_ref[1]

    def fetch(group):
        slot = group % 2
        source = amp_ref.at[:, pl.ds(group * K_STEP, K_STEP)]
        return pltpu.make_async_copy(source, amp_buffer.at[slot], sems.at[slot])

    fetch(0).start()
    column = amplitude_rows(column_ref, row_ref, occ_ref, row, batch, share)
    mix_ref[...] = as_bf16(jnp.bitwise_xor(column, row_ref[...]))
    if few_lhs_ref is not None:
        few_lhs_ref[...] = jnp.zeros(few_lhs_ref.shape, jnp.bfloat16)

    @pl.loop(0, groups)
    def _(group):
        slot = group % 2

        @pl.when(group + 1 < groups)
        def _():
            fetch(group + 1).start()

        fetch(group).wait()

        @pl.loop(0, K_STEP)
        def _(j):
            wanted = as_bf16(jnp.full((rows, share), occ_ref[col * k_all + group * K_STEP + j]))
            folded = None
            for n, s in enumerate(SLOTS):
                place = pl.ds(pl.multiple_of(jnp.bitwise_xor(row, s) * share, share), share)
                tile = amp_buffer[slot, :, j, :, place].reshape(rows, share)
                piece = jnp.where(mix_ref[:, place] == wanted, tile, jnp.zeros_like(tile))
                if n < NEAR:
                    lhs_ref[group, :, pl.ds(pl.multiple_of((n * K_STEP + j) * share, share), share)] = piece
                else:
                    own_ref = third_ref if n == NEAR else far_ref
                    own_ref[group, :, pl.ds(pl.multiple_of(j * share, share), share)] = piece
                folded = piece if folded is None else folded + piece
            if fold_ref is not None:
                fold_ref[group, :, pl.ds(pl.multiple_of(j * share, share), share)] = folded
            else:
                posx = posx_ref[group * K_STEP + j]

                @pl.when((posx >= 0) & (posx < few_lhs_ref.shape[2] // share))
                def _():
                    here = pl.ds(pl.multiple_of(j * share, share), share)
                    there = pl.ds(pl.multiple_of(posx * share, share), share)
                    few_lhs_ref[0, :, there] = third_ref[group, :, here]
                    few_lhs_ref[1, :, there] = far_ref[group, :, here]
                    few_lhs_ref[2, :, there] = folded


def masked_amplitudes(amplitudes, occ_irrep, vir_irrep, place, posx, few):
    batch, k_all, share, total = amplitudes.shape
    rows, groups = batch * share, k_all // K_STEP
    smem = pl.BlockSpec(memory_space=pltpu.SMEM)
    vmem = pl.BlockSpec(memory_space=pltpu.VMEM)
    hbm = pl.BlockSpec(memory_space=pltpu.HBM)
    shapes = [(groups, rows, w) for w in (NEAR * K_STEP * share, K_STEP * share, K_STEP * share)]
    shapes += [(3, rows, few * share)] if few else [(groups, rows, K_STEP * share)]

    def kernel(*refs):
        mask_kernel(*(refs[:8] + (None,) + refs[8:] if few else refs[:9] + (None,) + refs[9:]))

    return pl.pallas_call(
        kernel,
        in_specs=[smem, smem, smem, hbm, vmem],
        out_specs=[vmem] * len(shapes),
        out_shape=[jax.ShapeDtypeStruct(v, jnp.bfloat16) for v in shapes],
        scratch_shapes=[
            pltpu.VMEM((rows, total), jnp.bfloat16),
            pltpu.VMEM((total, 8), jnp.int32),
            pltpu.VMEM((2, batch, K_STEP, share, total), jnp.bfloat16),
            pltpu.SemaphoreType.DMA((2,)),
        ],
        cost_estimate=cost(7),
        compiler_params=pltpu.CompilerParams(vmem_limit_bytes=28 * 1024 * 1024),
    )(occ_irrep, place, posx, amplitudes, vir_irrep[None, :])


def make_first_kernel(few, n3, starts3):
    def kernel(pos3_ref, place_ref, lhs_ref, third_ref, far_ref, *refs):
        sources = 3 if few else 5
        narrow_refs, refs = refs[:sources], refs[sources:]
        m3_refs = [refs[3 * n:3 * n + 3] for n in range(n3)]
        narrow_sum, wide_sum, narrow_rhs, wide_rhs = refs[3 * n3:]
        row = place_ref[0]
        at_end = (row == 0) | (row == 3)
        groups, _, depth = lhs_ref.shape
        share = depth // (NEAR * K_STEP)
        half = share // 2
        lane = lax.broadcasted_iota(jnp.int32, (half, 2 * NARROW), 1)

        narrow_sum[...] = jnp.zeros(narrow_sum.shape, jnp.float32)
        wide_sum[...] = jnp.zeros(wide_sum.shape, jnp.float32)

        @pl.loop(0, groups)
        def _(group):
            @pl.loop(0, K_STEP)
            def _(j):
                k = group * K_STEP + j
                if few:
                    blocks = [ref[k] for ref in narrow_refs]
                else:
                    own, e1, o1, e2, o2 = [ref[k] for ref in narrow_refs]
                    blocks = (own, e1, o1, jnp.where(at_end, e2, o2))
                for n, block in enumerate(blocks):
                    zero = jnp.zeros_like(block)
                    first = pl.multiple_of((n * K_STEP + j) * share, share)
                    narrow_rhs[pl.ds(first, half)] = jnp.where(lane < NARROW, block, zero)
                    narrow_rhs[pl.ds(first + half, half)] = jnp.where(lane < NARROW, zero, block)
                for n in range(3 if n3 else 0):
                    block = chosen(m3_refs, starts3, pos3_ref[k], lambda group, at, n=n: group[n][at])
                    if n == 2:
                        block = jnp.where(at_end, jnp.zeros_like(block), block)
                    wide_rhs[pl.ds(pl.multiple_of((n * K_STEP + j) * share, share), share)] = block

            one = depth // NEAR
            narrow = jnp.dot(lhs_ref[group], narrow_rhs[:depth], preferred_element_type=jnp.float32)
            narrow += jnp.dot(third_ref[group], narrow_rhs[depth:depth + one], preferred_element_type=jnp.float32)
            if not few:
                narrow += jnp.dot(far_ref[group], narrow_rhs[depth + one:], preferred_element_type=jnp.float32)
            narrow_sum[...] += narrow
            if n3:
                wide = jnp.dot(lhs_ref[group], wide_rhs[:depth], preferred_element_type=jnp.float32)
                wide += jnp.dot(third_ref[group], wide_rhs[depth:], preferred_element_type=jnp.float32)
                wide_sum[...] += wide

    return kernel


def first_product(lhs, third_lhs, far_lhs, pos3, place, narrow, few, m3):
    groups, rows, depth = lhs.shape
    vmem = pl.BlockSpec(memory_space=pltpu.VMEM)
    smem = pl.BlockSpec(memory_space=pltpu.SMEM)
    arrays = list(narrow) + [v for group in m3 for v in group]
    wide = (rows, FOLD) if m3 else (16, FOLD)
    wide_depth = depth // NEAR * 3 if m3 else 16
    return pl.pallas_call(
        make_first_kernel(few, len(m3), starts_of([v[0] for v in m3])),
        in_specs=[smem] * 2 + [vmem] * (3 + len(arrays)),
        out_specs=[vmem] * 2,
        out_shape=[jax.ShapeDtypeStruct(v, jnp.float32) for v in ((rows, 2 * NARROW), wide)],
        scratch_shapes=[
            pltpu.VMEM((depth // NEAR * len(SLOTS), 2 * NARROW), jnp.bfloat16),
            pltpu.VMEM((wide_depth, FOLD), jnp.bfloat16),
        ],
        cost_estimate=cost(9 if m3 else 6),
        compiler_params=pltpu.CompilerParams(vmem_limit_bytes=32 * 1024 * 1024),
    )(pos3, place, lhs, third_lhs, far_lhs, *arrays)


def make_last_kernel(few, n2, starts2, n3, starts3):
    def kernel(
        occ_ref, vir_ref, pos2_ref, pos3_ref, count_ref, place_ref, fold_ref, third_ref, far_ref, row_ref, narrow_ref, wide_ref,
        *refs,
    ):
        m2_refs, refs = refs[:n2], refs[n2:]
        m3_refs = [refs[2 * n:2 * n + 2] for n in range(n3)]
        refs = refs[2 * n3:]
        e3_ref, refs = (None, refs) if few else (refs[0], refs[1:])
        outs = refs[:4]
        column_ref, total_ref, narrow_sum, short_rhs, far_rhs, third_rhs = refs[4:]
        row, col = place_ref[0], place_ref[1]
        at_end = (row == 0) | (row == 3)
        groups, rows, width = far_ref.shape if few else fold_ref.shape
        share = width // K_STEP
        batch = rows // share
        @pl.loop(0, groups * K_STEP)
        def _(k):
            here = pl.ds(pl.multiple_of(k * share, share), share)
            if not few:
                short = chosen(m2_refs, starts2, pos2_ref[k], lambda ref, at: ref[at])
                short_rhs[here] = jnp.concatenate([short, short], axis=0)
            if n3:
                far_rhs[here] = chosen(
                    m3_refs, starts3, pos3_ref[k], lambda pair, at: jnp.where(at_end, pair[0][at], pair[1][at])
                )

        column = amplitude_rows(column_ref, row_ref, occ_ref, row, batch, share)
        target = jnp.bitwise_xor(column, occ_ref[batch])
        if few:
            own, e1, o1, two, three = m2_refs
            half = share // 2
            lane = lax.broadcasted_iota(jnp.int32, (half, 2 * NARROW), 1)

            @pl.loop(0, fold_ref.shape[2] // share)
            def _(n):
                used = n < count_ref[0]
                first = pl.multiple_of(n * share, share)
                for slot, wanted, ref in ((0, used & at_end, three), (1, used, two)):
                    block = ref[n, 0]
                    zero = jnp.zeros_like(block)
                    block = jnp.where(wanted, block, zero)
                    third_rhs[slot, pl.ds(first, half)] = jnp.where(lane < NARROW, block, zero)
                    third_rhs[slot, pl.ds(first + half, half)] = jnp.where(lane < NARROW, zero, block)
                pieces = []
                for piece in range(2):
                    close = groups * K_STEP + 2 * n + piece
                    block = own[n, 1 + piece] + e1[close] + two[n, 1 + piece]
                    block = block + jnp.where(at_end, three[n, 1 + piece], o1[close])
                    pieces.append(jnp.where(used, block, jnp.zeros_like(block)))
                short = jnp.concatenate(pieces, axis=1)
                short_rhs[pl.ds(first, share)] = jnp.concatenate([short, short], axis=0)

            narrow = jnp.dot(fold_ref[0], third_rhs[0], preferred_element_type=jnp.float32)
            narrow += jnp.dot(fold_ref[1], third_rhs[1], preferred_element_type=jnp.float32)
            narrow_sum[...] = narrow_ref[...] + narrow
            total_ref[...] = wide_ref[...] + jnp.dot(
                fold_ref[2], short_rhs[...], preferred_element_type=jnp.float32
            )
        else:
            narrow_sum[...] = narrow_ref[...]

            @pl.when(at_end)
            def _():
                half = share // 2
                lane = lax.broadcasted_iota(jnp.int32, (half, 2 * NARROW), 1)

                @pl.loop(0, groups * K_STEP)
                def _(k):
                    block = e3_ref[k]
                    zero = jnp.zeros_like(block)
                    first = pl.multiple_of(k * share, share)
                    third_rhs[0, pl.ds(first, half)] = jnp.where(lane < NARROW, block, zero)
                    third_rhs[0, pl.ds(first + half, half)] = jnp.where(lane < NARROW, zero, block)

                @pl.loop(0, groups)
                def _(group):
                    rhs = third_rhs[0, pl.ds(pl.multiple_of(group * width, width), width)]
                    narrow_sum[...] += jnp.dot(third_ref[group], rhs, preferred_element_type=jnp.float32)

            total_ref[...] = wide_ref[...] if n3 else jnp.zeros(total_ref.shape, jnp.float32)
        @pl.loop(0, groups)
        def _(group):
            here = pl.ds(pl.multiple_of(group * width, width), width)
            if not few:
                total_ref[...] += jnp.dot(fold_ref[group], short_rhs[here], preferred_element_type=jnp.float32)
            if n3:
                total_ref[...] += jnp.dot(far_ref[group], far_rhs[here], preferred_element_type=jnp.float32)

        both = narrow_sum[...]
        both = both + pltpu.roll(both, NARROW, 1)
        both = jnp.concatenate([both] * (FOLD // (2 * NARROW)), axis=1)
        total_ref[...] = jnp.where(target == largest_irrep(vir_ref), total_ref[...], both)
        write_quarters(total_ref, col, outs)

    return kernel


def last_product(third_lhs, far_lhs, fold, occ_irrep, vir_irrep, pos2, pos3, count, place, narrow_sum, wide_sum, few, m2, m3, e3, batch):
    groups, rows, width = far_lhs.shape
    share = rows // batch
    vmem = pl.BlockSpec(memory_space=pltpu.VMEM)
    smem = pl.BlockSpec(memory_space=pltpu.SMEM)
    arrays = [narrow_sum, wide_sum] + list(m2) + [v for group in m3 for v in group] + list(e3)
    quarter = (batch // 2, share, FOLD // 2)
    whole = groups * width
    unused = jnp.zeros((16, 128), jnp.bfloat16)
    return pl.pallas_call(
        make_last_kernel(few, len(m2), starts_of(m2), len(m3), starts_of([v[0] for v in m3])),
        in_specs=[smem] * 6 + [vmem] * (4 + len(arrays)),
        out_specs=[vmem] * 4,
        out_shape=[jax.ShapeDtypeStruct(quarter, jnp.float32)] * 4,
        scratch_shapes=[
            pltpu.VMEM((vir_irrep.shape[0], 8), jnp.int32),
            pltpu.VMEM((rows, FOLD), jnp.float32),
            pltpu.VMEM((rows, 2 * NARROW), jnp.float32),
            pltpu.VMEM((fold.shape[2] if few else whole, FOLD), jnp.bfloat16),
            pltpu.VMEM((whole if m3 else 16, FOLD), jnp.bfloat16),
            pltpu.VMEM((2, fold.shape[2]) + (2 * NARROW,) if few else (1, whole, 2 * NARROW), jnp.bfloat16),
        ],
        cost_estimate=cost(4 if m3 else 3),
        compiler_params=pltpu.CompilerParams(vmem_limit_bytes=32 * 1024 * 1024),
    )(occ_irrep, vir_irrep, pos2, pos3, count, place, fold, unused if few else third_lhs,
      far_lhs if m3 else unused, vir_irrep[None, :], *arrays)


def dense_product(amplitudes, whole, occ_irrep, occ_local, vir_local, vir_irrep):
    batch = amplitudes.shape[0]
    keep = (
        jnp.bitwise_xor(occ_irrep[:batch, None], occ_local[None, :])[:, :, None, None]
        == jnp.bitwise_xor(vir_local[:, None], vir_irrep[None, :])[None, None]
    )
    kept = jnp.where(keep, amplitudes, jnp.zeros_like(amplitudes))
    return lax.dot_general(
        kept, whole, (((1, 3), (0, 1)), ((), ())), preferred_element_type=jnp.float32
    )


def finish(cycle, occ_irrep, vir_irrep, occ_energy, vir_energy, a_start, a_size, b_start, b_size, batch):
    label_a = lax.dynamic_slice_in_dim(vir_irrep, a_start, a_size)
    label_b = lax.dynamic_slice_in_dim(vir_irrep, b_start, b_size)
    energy_a = lax.dynamic_slice_in_dim(vir_energy, a_start, a_size)
    energy_b = lax.dynamic_slice_in_dim(vir_energy, b_start, b_size)
    target = jnp.bitwise_xor(
        jnp.bitwise_xor(occ_irrep[:batch, None], occ_irrep[batch]), label_a[None, :]
    )
    keep = label_b[:, None, None] == target[None, :, :]
    denominator = (
        occ_energy[:batch][None, :, None]
        + occ_energy[batch]
        - energy_a[None, None, :]
        - energy_b[:, None, None]
    )
    swapped = jnp.transpose(cycle, (2, 0, 1))
    return jnp.where(keep, swapped, 0.0) / denominator


def on_square(amplitudes, integrals, occ_irrep, vir_irrep, screen):
    batch, occ_share, share, vir_total = amplitudes.shape
    row = lax.axis_index("row")
    col = lax.axis_index("col")
    place = jnp.stack([row, col]).astype(jnp.int32)
    few, m2a, m2b, m3a, m3b, pos2, pos3, posx, form, count = wide_blocks(
        integrals, occ_irrep, vir_irrep, screen, place, batch
    )
    outer = [(0, 1), (1, 0), (2, 3), (3, 2)]
    inner = [(1, 2), (2, 1)]
    inward = [(0, 1), (3, 2)]
    outward = [(1, 0), (2, 3)]
    ends = [(0, 3), (3, 0)]
    second = [(r, r ^ 2) for r in range(4)]

    def move(v, pairs):
        return lax.ppermute(v, "row", pairs)

    def sparse(use_few, choose):
        def run(few, m2a, m2b, m3a, m3b):
            shorts, wides = choose(m2a, m2b, m3a, m3b)
            near = [(own, move(own, outer), move(own, inner)) for own in wides]
            few = few[:use_few] if use_few else None
            narrow = narrow_blocks(integrals, occ_irrep, vir_irrep, screen, place, few, batch)
            if use_few:
                e1, o1 = move(narrow, outer), move(narrow, inner)
                lhs, third_lhs, far_lhs, fold = masked_amplitudes(
                    amplitudes, occ_irrep, vir_irrep, place, posx, use_few
                )
                near, e1, o1, few, _ = lax.optimization_barrier((near, e1, o1, few, fold))
                two, three = move(few, second), move(few, ends)
                blocks, e3 = (narrow, e1, o1), []
                sums = (few, e1, o1, two, three)
            else:
                h1 = [move(v, inward) for v in shorts]
                o1, e1 = move(narrow, inner), move(narrow, outward)
                lhs, third_lhs, far_lhs, fold = masked_amplitudes(
                    amplitudes, occ_irrep, vir_irrep, place, posx, 0
                )
                near, h1, o1, e1, _ = lax.optimization_barrier((near, h1, o1, e1, fold))
                h2 = [move(own + v, inner) for own, v in zip(shorts, h1)]
                e1 = e1 + move(narrow, inward)
                e2 = move(o1, outward)
                h2, e1, e2 = lax.optimization_barrier((h2, e1, e2))
                h3 = [move(own + v, outward) for own, v in zip(shorts, h2)]
                o2 = move(e1, inner)
                blocks, e3 = (narrow, e1, o1, e2, o2), [move(o2, outward)]
                sums = [a + b + c + d for a, b, c, d in zip(shorts, h1, h2, h3)]
            far = [(move(o, outward), move(e, inner)) for _, e, o in near]
            narrow_sum, wide_sum = first_product(
                lhs, third_lhs, far_lhs, pos3, place, blocks, bool(use_few), near
            )
            return list(last_product(
                third_lhs, far_lhs, fold, occ_irrep, vir_irrep, pos2, pos3, count, place, narrow_sum, wide_sum,
                bool(use_few), sums, far, e3, batch
            ))

        return run

    def dense(*_):
        occ_local = lax.dynamic_slice_in_dim(occ_irrep, col * occ_share, occ_share)
        vir_local = lax.dynamic_slice_in_dim(vir_irrep, row * share, share)
        screen_rows = lax.dynamic_slice_in_dim(screen, col * occ_share, occ_share, 0)
        fold = folded_integrals(
            integrals, occ_local, vir_local, vir_irrep, occ_irrep[batch], screen_rows
        )
        whole = jnp.zeros((occ_share, vir_total, FOLD), fold.dtype)
        for s in range(4):
            block = move(fold, [(r, r ^ s) for r in range(4)]) if s else fold
            whole = lax.dynamic_update_slice_in_dim(whole, block, jnp.bitwise_xor(row, s) * share, 1)
        total = dense_product(amplitudes, whole, occ_irrep, occ_local, vir_local, vir_irrep)
        quarter = (batch // 2, share, FOLD // 2)
        goals = [jnp.bitwise_xor(col, t) for t in range(4)]
        return [
            lax.dynamic_slice(total, (g // 2 * quarter[0], 0, g % 2 * quarter[2]), quarter) for g in goals
        ]

    branches = [
        sparse(0, lambda m2a, m2b, m3a, m3b: ([m2a], [])),
        sparse(0, lambda m2a, m2b, m3a, m3b: ([m2a, m2b], [])),
        sparse(0, lambda m2a, m2b, m3a, m3b: ([m2a], [m3a[:FEW_WIDE]])),
        sparse(FEW_CAPS[0], lambda m2a, m2b, m3a, m3b: ([], [m3a])),
        sparse(FEW_CAPS[1], lambda m2a, m2b, m3a, m3b: ([], [m3a])),
        sparse(0, lambda m2a, m2b, m3a, m3b: ([m2a, m2b], [m3a, m3b])),
        dense,
    ]
    quarters = lax.switch(form[0], branches, few, m2a, m2b, m3a, m3b)
    mine = quarters[0]
    for t in (1, 2, 3):
        mine = mine + lax.ppermute(quarters[t], "col", [(q, q ^ t) for q in range(4)])
    places = [(r, q) for r in range(4) for q in range(4)]
    same = lax.ppermute(mine, ("row", "col"), [(r * 4 + q, q * 4 + r) for r, q in places])
    other = lax.ppermute(mine, ("row", "col"), [(r * 4 + q, (q ^ 2) * 4 + r) for r, q in places])
    upper = row // 2 == 1
    low = jnp.where(upper, other, same)
    high = jnp.where(upper, same, other)
    return jnp.concatenate([low, high], axis=0)


def on_any(amplitudes, integrals, occ_irrep, vir_irrep, screen):
    batch, occ_share, share, vir_total = amplitudes.shape
    row = lax.axis_index("row")
    col = lax.axis_index("col")
    occ_local = lax.dynamic_slice_in_dim(occ_irrep, col * occ_share, occ_share)
    vir_local = lax.dynamic_slice_in_dim(vir_irrep, row * share, share)
    screen_rows = lax.dynamic_slice_in_dim(screen, col * occ_share, occ_share, 0)
    fold = folded_integrals(
        integrals, occ_local, vir_local, vir_irrep, occ_irrep[batch], screen_rows
    )
    whole = lax.all_gather(fold, "row", axis=1, tiled=True)
    cycle = dense_product(amplitudes, whole, occ_irrep, occ_local, vir_local, vir_irrep)
    cycle = lax.psum(cycle, "col")
    cycle = jnp.concatenate([cycle] * (vir_total // FOLD), axis=2)
    cycle = lax.all_to_all(cycle, "row", split_axis=2, concat_axis=1, tiled=True)
    a_size = vir_total // lax.axis_size("col")
    return lax.dynamic_slice_in_dim(cycle, col * a_size, a_size, 1)


def on_device(amplitudes, integrals, occ_irrep, vir_irrep, screen, occ_energy, vir_energy):
    batch, _, vir_share, vir_total = amplitudes.shape
    square = lax.axis_size("row") == 4 and lax.axis_size("col") == 4
    form = on_square if square else on_any
    cycle = form(amplitudes, integrals, occ_irrep, vir_irrep, screen)
    a_size = vir_total // lax.axis_size("col")
    return finish(
        cycle, occ_irrep, vir_irrep, occ_energy, vir_energy,
        lax.axis_index("col") * a_size, a_size, lax.axis_index("row") * vir_share, vir_share, batch,
    )


def solution(mesh):
    in_specs = (
        P("parts", "col", "row", None),
        P(("parts", "col"), "row", None),
        P("parts"),
        P("parts"),
        P("parts", None),
        P("parts"),
        P("parts"),
    )
    out_specs = P("row", "parts", "col")
    return jax.shard_map(
        on_device, mesh=mesh, in_specs=in_specs, out_specs=out_specs, check_vma=False
    )
```

```python
import jax
import jax.numpy as jnp
from jax import lax
from jax.experimental import pallas as pl
from jax.experimental.pallas import tpu as pltpu
from jax.sharding import PartitionSpec as P

FOLD = 256
K_STEP = 5


def folded_integrals(integrals, occ_local, vir_local, vir_irrep, pair_label, screen_rows):
    irrep_codes = jnp.arange(8, dtype=jnp.int32)
    screen_local = jnp.sum(
        screen_rows[:, None, :] * (vir_local[None, :, None] == irrep_codes).astype(jnp.int32),
        axis=2,
    )
    target = jnp.bitwise_xor(
        jnp.bitwise_xor(occ_local[:, None], vir_local[None, :]), pair_label
    )
    target = jnp.where(screen_local == 1, target, -1)
    keep = target[:, :, None] == vir_irrep[None, None, :]
    kept = jnp.where(keep, integrals, jnp.zeros_like(integrals))
    return kept[:, :, :FOLD] + kept[:, :, FOLD:]


NARROW = 64
CAPS = (22, 3)
FEW_CAPS = (4, 10)
FEW_WIDE = 7


def largest_irrep(vir_ref):
    return jnp.where(vir_ref[0] == vir_ref[FOLD - 1], vir_ref[0], vir_ref[FOLD])


def label_columns(row_labels):
    return jnp.transpose(jnp.broadcast_to(row_labels, (8, row_labels.shape[1])))


def as_bf16(labels):
    return labels.astype(jnp.float32).astype(jnp.bfloat16)


def label_mix(mix_ref, column_ref, row_ref, row, big, keep_big):
    depth = mix_ref.shape[0]
    column_ref[...] = label_columns(row_ref[...])
    column = column_ref[pl.ds(pl.multiple_of(row * depth, depth), depth), :1]
    is_big = row_ref[...] == big
    wanted = is_big if keep_big else jnp.logical_not(is_big)
    mix_ref[...] = as_bf16(jnp.where(wanted, jnp.bitwise_xor(column, row_ref[...]), 8))


def kept_folded(int_ref, mix_ref, j, x):
    tile = int_ref[j]
    wanted = as_bf16(jnp.full(mix_ref.shape, x))
    kept = jnp.where(mix_ref[...] == wanted, tile, jnp.zeros_like(tile))
    return kept[:, :FOLD] + kept[:, FOLD:]


def narrow_fold(kept, bits, local):
    half = kept.shape[0] // 2
    lane = lax.broadcasted_iota(jnp.int32, (half, 2 * NARROW), 1)
    narrow = (kept[:, : 2 * NARROW] + kept[:, 2 * NARROW:]).astype(jnp.float32)
    narrow = narrow + pltpu.roll(narrow, NARROW, 1)
    on = jnp.bitwise_and(lax.shift_right_logical(jnp.full(local.shape, bits), local), 1) == 1
    narrow = jnp.where(on, narrow, 0.0)
    return jnp.where(lane < NARROW, narrow[:half], narrow[half:]).astype(jnp.bfloat16)


def screen_bits(screen_ref, k):
    bits = screen_ref[0, k]
    for g in range(1, 8):
        bits = bits + screen_ref[g, k] * (1 << g)
    return bits


def copy_of(source_ref, int_ref, sems, group):
    here = pl.ds(group * K_STEP, K_STEP)
    return pltpu.make_async_copy(source_ref.at[here], int_ref.at[here], sems.at[group])


def start_copies(source_ref, int_ref, sems):
    for group in range(int_ref.shape[0] // K_STEP):
        copy_of(source_ref, int_ref, sems, group).start()


def wait_copy(source_ref, int_ref, sems, group):
    copy_of(source_ref, int_ref, sems, group).wait()


def wide_kernel(
    occ_ref, vir_ref, screen_ref, place_ref, source_ref, row_ref,
    few_ref, m2a_ref, m2b_ref, m3a_ref, m3b_ref, pos2_ref, pos3_ref, posx_ref, form_ref, count_ref,
    mix_ref, small_mix_ref, column_ref, counts_ref, int_ref, sems, batch,
):
    start_copies(source_ref, int_ref, sems)
    k_all, depth, total = int_ref.shape
    half = depth // 2
    row, col = place_ref[0], place_ref[1]
    pair_label = occ_ref[batch]
    big = largest_irrep(vir_ref)
    mostly_zero = (occ_ref[col * k_all] == pair_label) | (occ_ref[(col + 1) * k_all - 1] == pair_label)
    most = FEW_CAPS[-1]
    for n in range(3):
        counts_ref[n] = 0
    label_mix(mix_ref, column_ref, row_ref, row, big, True)

    @pl.when(mostly_zero)
    def _():
        label_mix(small_mix_ref, column_ref, row_ref, row, big, False)

    local = column_ref[pl.ds(pl.multiple_of(row * depth, depth), depth), :1]

    @pl.loop(0, k_all)
    def _(k):
        @pl.when(k % K_STEP == 0)
        def _():
            wait_copy(source_ref, int_ref, sems, k // K_STEP)

        k_whole = col * k_all + k
        x = jnp.bitwise_xor(occ_ref[k_whole], pair_label)
        on_big = screen_ref[jnp.bitwise_xor(big, x), k_whole] == 1
        actives = (on_big & (x != 0), on_big & (x == 0), x != 0)
        pos2, pos3, posx = [jnp.where(active, counts_ref[n], -1) for n, active in enumerate(actives)]
        for n, active in enumerate(actives):
            counts_ref[n] = counts_ref[n] + active.astype(jnp.int32)
        pos2_ref[k], pos3_ref[k], posx_ref[k] = pos2, pos3, posx

        @pl.when(pos2 >= 0)
        def _():
            wide = kept_folded(int_ref, mix_ref, k, x)
            short = wide[:half] + wide[half:]

            @pl.when(mostly_zero & (posx < most))
            def _():
                for piece in range(2):
                    few_ref[posx, 1 + piece] = short[:, piece * 2 * NARROW:(piece + 1) * 2 * NARROW]

            @pl.when(pos2 < CAPS[0])
            def _():
                m2a_ref[pos2] = short

            @pl.when(pos2 >= CAPS[0])
            def _():
                m2b_ref[pos2 - CAPS[0]] = short

        @pl.when(mostly_zero & (posx >= 0) & (posx < most))
        def _():
            kept = kept_folded(int_ref, small_mix_ref, k, x)
            few_ref[posx, 0] = narrow_fold(kept, screen_bits(screen_ref, k_whole), local)

            @pl.when(pos2 < 0)
            def _():
                for piece in range(2):
                    few_ref[posx, 1 + piece] = jnp.zeros((half, 2 * NARROW), jnp.bfloat16)

        @pl.when(pos3 >= 0)
        def _():
            wide = kept_folded(int_ref, mix_ref, k, x)

            @pl.when(pos3 < CAPS[0])
            def _():
                m3a_ref[pos3] = wide

            @pl.when(pos3 >= CAPS[0])
            def _():
                m3b_ref[pos3 - CAPS[0]] = wide

    labels = row_ref[...]
    lanes = lax.broadcasted_iota(jnp.int32, labels.shape, 1)
    ahead = pltpu.roll(labels, total - NARROW, 1)
    long = (labels == ahead) & (lanes < total - NARROW) & (labels != big)
    too_long = jnp.max(long.astype(jnp.int32)) == 1
    n2, n3, nx = counts_ref[0], counts_ref[1], counts_ref[2]
    count_ref[0] = nx
    one_label = occ_ref[0] == pair_label
    form = jnp.where(nx <= FEW_CAPS[0], 3, jnp.where(nx <= FEW_CAPS[1], 4, 5))
    form = jnp.where(mostly_zero & (n3 <= CAPS[0]), form, 5)
    form = jnp.where((n3 <= FEW_WIDE) & (n2 <= CAPS[0]), 2, form)
    form = jnp.where(one_label, form, 6)
    form = jnp.where(n3 == 0, jnp.where(n2 <= CAPS[0], 0, 1), form)
    form_ref[0] = jnp.where(too_long, 6, form)


def wide_blocks(integrals, occ_irrep, vir_irrep, screen, place, batch):
    occ_share, depth, total = integrals.shape
    shapes = [(n, depth // 2, FOLD) for n in CAPS] + [(n, depth, FOLD) for n in CAPS]
    few = (FEW_CAPS[-1], 3, depth // 2, 2 * NARROW)
    smem = pl.BlockSpec(memory_space=pltpu.SMEM)

    def kernel(*refs):
        wide_kernel(*refs, batch)

    vmem = pl.BlockSpec(memory_space=pltpu.VMEM)
    return pl.pallas_call(
        kernel,
        in_specs=[smem] * 4 + [pl.BlockSpec(memory_space=pltpu.HBM), vmem],
        out_specs=[vmem] * (1 + len(shapes)) + [smem] * 5,
        scratch_shapes=[
            pltpu.VMEM((depth, total), jnp.bfloat16),
            pltpu.VMEM((depth, total), jnp.bfloat16),
            pltpu.VMEM((total, 8), jnp.int32),
            pltpu.SMEM((3,), jnp.int32),
            pltpu.VMEM(integrals.shape, jnp.bfloat16),
            pltpu.SemaphoreType.DMA((occ_share // K_STEP,)),
        ],
        out_shape=[jax.ShapeDtypeStruct(v, jnp.bfloat16) for v in [few] + shapes]
        + [jax.ShapeDtypeStruct((n,), jnp.int32) for n in (occ_share, occ_share, occ_share, 1, 1)],
        cost_estimate=cost(5),
        compiler_params=pltpu.CompilerParams(vmem_limit_bytes=24 * 1024 * 1024),
    )(occ_irrep, vir_irrep, screen.T, place, integrals, vir_irrep[None, :])


def narrow_kernel(
    occ_ref, vir_ref, screen_ref, place_ref, source_ref, row_ref, few_ref, narrow_ref,
    mix_ref, column_ref, int_ref, sems, batch,
):
    start_copies(source_ref, int_ref, sems)
    k_all, depth, total = int_ref.shape
    row, col = place_ref[0], place_ref[1]
    label_mix(mix_ref, column_ref, row_ref, row, largest_irrep(vir_ref), False)
    if few_ref is not None:
        for n in range(few_ref.shape[0]):
            for piece in range(2):
                narrow_ref[k_all + 2 * n + piece] = few_ref[n, 1 + piece]
    local = column_ref[pl.ds(pl.multiple_of(row * depth, depth), depth), :1]

    @pl.loop(0, k_all // K_STEP)
    def _(group):
        wait_copy(source_ref, int_ref, sems, group)
        for j in range(K_STEP):
            k = group * K_STEP + j
            k_whole = col * k_all + k
            x = jnp.bitwise_xor(occ_ref[k_whole], occ_ref[batch])
            kept = kept_folded(int_ref, mix_ref, k, x)
            narrow_ref[k] = narrow_fold(kept, screen_bits(screen_ref, k_whole), local)


def narrow_blocks(integrals, occ_irrep, vir_irrep, screen, place, few, batch):
    occ_share, depth, total = integrals.shape
    extra = [] if few is None else [few]
    count = occ_share + sum(2 * v.shape[0] for v in extra)
    smem = pl.BlockSpec(memory_space=pltpu.SMEM)
    vmem = pl.BlockSpec(memory_space=pltpu.VMEM)

    def kernel(*refs):
        narrow_kernel(*(refs if extra else refs[:6] + (None,) + refs[6:]), batch)

    return pl.pallas_call(
        kernel,
        in_specs=[smem] * 4 + [pl.BlockSpec(memory_space=pltpu.HBM), vmem] + [vmem] * len(extra),
        out_specs=vmem,
        out_shape=jax.ShapeDtypeStruct((count, depth // 2, 2 * NARROW), jnp.bfloat16),
        scratch_shapes=[
            pltpu.VMEM((depth, total), jnp.bfloat16),
            pltpu.VMEM((total, 8), jnp.int32),
            pltpu.VMEM(integrals.shape, jnp.bfloat16),
            pltpu.SemaphoreType.DMA((occ_share // K_STEP,)),
        ],
        cost_estimate=cost(4),
        compiler_params=pltpu.CompilerParams(vmem_limit_bytes=16 * 1024 * 1024),
    )(occ_irrep, vir_irrep, screen.T, place, integrals, vir_irrep[None, :], *extra)


def cost(micros):
    return pl.CostEstimate(flops=int(micros * 1e9), bytes_accessed=int(micros * 3e6), transcendentals=0)


SLOTS = (0, 1, 3, 2)
NEAR = 2


def amplitude_rows(column_ref, row_ref, occ_ref, row, batch, share):
    column_ref[...] = label_columns(row_ref[...])
    column = column_ref[pl.ds(pl.multiple_of(row * share, share), share), :1]
    return jnp.concatenate([jnp.bitwise_xor(column, occ_ref[i]) for i in range(batch)], axis=0)


def write_quarters(total_ref, col, outs):
    rows, fold = total_ref.shape
    width, height = fold // 2, rows // 2
    for t, out_ref in enumerate(outs):
        goal = jnp.bitwise_xor(col, t)
        lanes = pl.ds(pl.multiple_of((goal % 2) * width, width), width)
        lines = pl.ds(pl.multiple_of((goal // 2) * height, height), height)
        out_ref[...] = total_ref[lines, lanes].reshape(out_ref.shape)


def chosen(refs, starts, pos, pick):
    block = None
    for n, group in enumerate(refs):
        inside = (pos >= starts[n]) & (pos < starts[n + 1])
        at = jnp.clip(pos - starts[n], 0, starts[n + 1] - starts[n] - 1)
        found = pick(group, at)
        found = jnp.where(inside, found, jnp.zeros_like(found))
        block = found if block is None else block + found
    return block


def starts_of(arrays):
    starts = [0]
    for v in arrays:
        starts.append(starts[-1] + v.shape[0])
    return starts


def mask_kernel(
    occ_ref, place_ref, posx_ref, amp_ref, row_ref, lhs_ref, third_ref, far_ref, fold_ref, few_lhs_ref,
    mix_ref, column_ref, amp_buffer, sems,
):
    batch, k_all, share, total = amp_ref.shape
    rows, groups = batch * share, k_all // K_STEP
    row, col = place_ref[0], place_ref[1]

    def fetch(group):
        slot = group % 2
        source = amp_ref.at[:, pl.ds(group * K_STEP, K_STEP)]
        return pltpu.make_async_copy(source, amp_buffer.at[slot], sems.at[slot])

    fetch(0).start()
    column = amplitude_rows(column_ref, row_ref, occ_ref, row, batch, share)
    mix_ref[...] = as_bf16(jnp.bitwise_xor(column, row_ref[...]))
    if few_lhs_ref is not None:
        few_lhs_ref[...] = jnp.zeros(few_lhs_ref.shape, jnp.bfloat16)

    @pl.loop(0, groups)
    def _(group):
        slot = group % 2

        @pl.when(group + 1 < groups)
        def _():
            fetch(group + 1).start()

        fetch(group).wait()

        @pl.loop(0, K_STEP)
        def _(j):
            wanted = as_bf16(jnp.full((rows, share), occ_ref[col * k_all + group * K_STEP + j]))
            folded = None
            for n, s in enumerate(SLOTS):
                place = pl.ds(pl.multiple_of(jnp.bitwise_xor(row, s) * share, share), share)
                tile = amp_buffer[slot, :, j, :, place].reshape(rows, share)
                piece = jnp.where(mix_ref[:, place] == wanted, tile, jnp.zeros_like(tile))
                if n < NEAR:
                    lhs_ref[group, :, pl.ds(pl.multiple_of((n * K_STEP + j) * share, share), share)] = piece
                else:
                    own_ref = third_ref if n == NEAR else far_ref
                    own_ref[group, :, pl.ds(pl.multiple_of(j * share, share), share)] = piece
                folded = piece if folded is None else folded + piece
            if fold_ref is not None:
                fold_ref[group, :, pl.ds(pl.multiple_of(j * share, share), share)] = folded
            else:
                posx = posx_ref[group * K_STEP + j]

                @pl.when((posx >= 0) & (posx < few_lhs_ref.shape[2] // share))
                def _():
                    here = pl.ds(pl.multiple_of(j * share, share), share)
                    there = pl.ds(pl.multiple_of(posx * share, share), share)
                    few_lhs_ref[0, :, there] = third_ref[group, :, here]
                    few_lhs_ref[1, :, there] = far_ref[group, :, here]
                    few_lhs_ref[2, :, there] = folded


def masked_amplitudes(amplitudes, occ_irrep, vir_irrep, place, posx, few):
    batch, k_all, share, total = amplitudes.shape
    rows, groups = batch * share, k_all // K_STEP
    smem = pl.BlockSpec(memory_space=pltpu.SMEM)
    vmem = pl.BlockSpec(memory_space=pltpu.VMEM)
    hbm = pl.BlockSpec(memory_space=pltpu.HBM)
    shapes = [(groups, rows, w) for w in (NEAR * K_STEP * share, K_STEP * share, K_STEP * share)]
    shapes += [(3, rows, few * share)] if few else [(groups, rows, K_STEP * share)]

    def kernel(*refs):
        mask_kernel(*(refs[:8] + (None,) + refs[8:] if few else refs[:9] + (None,) + refs[9:]))

    return pl.pallas_call(
        kernel,
        in_specs=[smem, smem, smem, hbm, vmem],
        out_specs=[vmem] * len(shapes),
        out_shape=[jax.ShapeDtypeStruct(v, jnp.bfloat16) for v in shapes],
        scratch_shapes=[
            pltpu.VMEM((rows, total), jnp.bfloat16),
            pltpu.VMEM((total, 8), jnp.int32),
            pltpu.VMEM((2, batch, K_STEP, share, total), jnp.bfloat16),
            pltpu.SemaphoreType.DMA((2,)),
        ],
        cost_estimate=cost(7),
        compiler_params=pltpu.CompilerParams(vmem_limit_bytes=28 * 1024 * 1024),
    )(occ_irrep, place, posx, amplitudes, vir_irrep[None, :])


def make_first_kernel(few, n3, starts3):
    def kernel(pos3_ref, place_ref, lhs_ref, third_ref, far_ref, *refs):
        sources = 3 if few else 5
        narrow_refs, refs = refs[:sources], refs[sources:]
        m3_refs = [refs[3 * n:3 * n + 3] for n in range(n3)]
        narrow_sum, wide_sum, narrow_rhs, wide_rhs = refs[3 * n3:]
        row = place_ref[0]
        at_end = (row == 0) | (row == 3)
        groups, _, depth = lhs_ref.shape
        share = depth // (NEAR * K_STEP)
        half = share // 2
        lane = lax.broadcasted_iota(jnp.int32, (half, 2 * NARROW), 1)

        narrow_sum[...] = jnp.zeros(narrow_sum.shape, jnp.float32)
        wide_sum[...] = jnp.zeros(wide_sum.shape, jnp.float32)

        @pl.loop(0, groups)
        def _(group):
            @pl.loop(0, K_STEP)
            def _(j):
                k = group * K_STEP + j
                if few:
                    blocks = [ref[k] for ref in narrow_refs]
                else:
                    own, e1, o1, e2, o2 = [ref[k] for ref in narrow_refs]
                    blocks = (own, e1, o1, jnp.where(at_end, e2, o2))
                for n, block in enumerate(blocks):
                    zero = jnp.zeros_like(block)
                    first = pl.multiple_of((n * K_STEP + j) * share, share)
                    narrow_rhs[pl.ds(first, half)] = jnp.where(lane < NARROW, block, zero)
                    narrow_rhs[pl.ds(first + half, half)] = jnp.where(lane < NARROW, zero, block)
                for n in range(3 if n3 else 0):
                    block = chosen(m3_refs, starts3, pos3_ref[k], lambda group, at, n=n: group[n][at])
                    if n == 2:
                        block = jnp.where(at_end, jnp.zeros_like(block), block)
                    wide_rhs[pl.ds(pl.multiple_of((n * K_STEP + j) * share, share), share)] = block

            one = depth // NEAR
            narrow = jnp.dot(lhs_ref[group], narrow_rhs[:depth], preferred_element_type=jnp.float32)
            narrow += jnp.dot(third_ref[group], narrow_rhs[depth:depth + one], preferred_element_type=jnp.float32)
            if not few:
                narrow += jnp.dot(far_ref[group], narrow_rhs[depth + one:], preferred_element_type=jnp.float32)
            narrow_sum[...] += narrow
            if n3:
                wide = jnp.dot(lhs_ref[group], wide_rhs[:depth], preferred_element_type=jnp.float32)
                wide += jnp.dot(third_ref[group], wide_rhs[depth:], preferred_element_type=jnp.float32)
                wide_sum[...] += wide

    return kernel


def first_product(lhs, third_lhs, far_lhs, pos3, place, narrow, few, m3):
    groups, rows, depth = lhs.shape
    vmem = pl.BlockSpec(memory_space=pltpu.VMEM)
    smem = pl.BlockSpec(memory_space=pltpu.SMEM)
    arrays = list(narrow) + [v for group in m3 for v in group]
    wide = (rows, FOLD) if m3 else (16, FOLD)
    wide_depth = depth // NEAR * 3 if m3 else 16
    return pl.pallas_call(
        make_first_kernel(few, len(m3), starts_of([v[0] for v in m3])),
        in_specs=[smem] * 2 + [vmem] * (3 + len(arrays)),
        out_specs=[vmem] * 2,
        out_shape=[jax.ShapeDtypeStruct(v, jnp.float32) for v in ((rows, 2 * NARROW), wide)],
        scratch_shapes=[
            pltpu.VMEM((depth // NEAR * len(SLOTS), 2 * NARROW), jnp.bfloat16),
            pltpu.VMEM((wide_depth, FOLD), jnp.bfloat16),
        ],
        cost_estimate=cost(9 if m3 else 6),
        compiler_params=pltpu.CompilerParams(vmem_limit_bytes=32 * 1024 * 1024),
    )(pos3, place, lhs, third_lhs, far_lhs, *arrays)


def make_last_kernel(few, n2, starts2, n3, starts3):
    def kernel(
        occ_ref, vir_ref, pos2_ref, pos3_ref, count_ref, place_ref, fold_ref, third_ref, far_ref, row_ref, narrow_ref, wide_ref,
        *refs,
    ):
        m2_refs, refs = refs[:n2], refs[n2:]
        m3_refs = [refs[2 * n:2 * n + 2] for n in range(n3)]
        refs = refs[2 * n3:]
        e3_ref, refs = (None, refs) if few else (refs[0], refs[1:])
        outs = refs[:4]
        column_ref, total_ref, narrow_sum, short_rhs, far_rhs, third_rhs = refs[4:]
        row, col = place_ref[0], place_ref[1]
        at_end = (row == 0) | (row == 3)
        groups, rows, width = far_ref.shape if few else fold_ref.shape
        share = width // K_STEP
        batch = rows // share
        @pl.loop(0, groups * K_STEP)
        def _(k):
            here = pl.ds(pl.multiple_of(k * share, share), share)
            if not few:
                short = chosen(m2_refs, starts2, pos2_ref[k], lambda ref, at: ref[at])
                short_rhs[here] = jnp.concatenate([short, short], axis=0)
            if n3:
                far_rhs[here] = chosen(
                    m3_refs, starts3, pos3_ref[k], lambda pair, at: jnp.where(at_end, pair[0][at], pair[1][at])
                )

        column = amplitude_rows(column_ref, row_ref, occ_ref, row, batch, share)
        target = jnp.bitwise_xor(column, occ_ref[batch])
        if few:
            own, e1, o1, two, three = m2_refs
            half = share // 2
            lane = lax.broadcasted_iota(jnp.int32, (half, 2 * NARROW), 1)

            @pl.loop(0, fold_ref.shape[2] // share)
            def _(n):
                used = n < count_ref[0]
                first = pl.multiple_of(n * share, share)
                for slot, wanted, ref in ((0, used & at_end, three), (1, used, two)):
                    block = ref[n, 0]
                    zero = jnp.zeros_like(block)
                    block = jnp.where(wanted, block, zero)
                    third_rhs[slot, pl.ds(first, half)] = jnp.where(lane < NARROW, block, zero)
                    third_rhs[slot, pl.ds(first + half, half)] = jnp.where(lane < NARROW, zero, block)
                pieces = []
                for piece in range(2):
                    close = groups * K_STEP + 2 * n + piece
                    block = own[n, 1 + piece] + e1[close] + two[n, 1 + piece]
                    block = block + jnp.where(at_end, three[n, 1 + piece], o1[close])
                    pieces.append(jnp.where(used, block, jnp.zeros_like(block)))
                short = jnp.concatenate(pieces, axis=1)
                short_rhs[pl.ds(first, share)] = jnp.concatenate([short, short], axis=0)

            narrow = jnp.dot(fold_ref[0], third_rhs[0], preferred_element_type=jnp.float32)
            narrow += jnp.dot(fold_ref[1], third_rhs[1], preferred_element_type=jnp.float32)
            narrow_sum[...] = narrow_ref[...] + narrow
            total_ref[...] = wide_ref[...] + jnp.dot(
                fold_ref[2], short_rhs[...], preferred_element_type=jnp.float32
            )
        else:
            narrow_sum[...] = narrow_ref[...]

            @pl.when(at_end)
            def _():
                half = share // 2
                lane = lax.broadcasted_iota(jnp.int32, (half, 2 * NARROW), 1)

                @pl.loop(0, groups * K_STEP)
                def _(k):
                    block = e3_ref[k]
                    zero = jnp.zeros_like(block)
                    first = pl.multiple_of(k * share, share)
                    third_rhs[0, pl.ds(first, half)] = jnp.where(lane < NARROW, block, zero)
                    third_rhs[0, pl.ds(first + half, half)] = jnp.where(lane < NARROW, zero, block)

                @pl.loop(0, groups)
                def _(group):
                    rhs = third_rhs[0, pl.ds(pl.multiple_of(group * width, width), width)]
                    narrow_sum[...] += jnp.dot(third_ref[group], rhs, preferred_element_type=jnp.float32)

            total_ref[...] = wide_ref[...] if n3 else jnp.zeros(total_ref.shape, jnp.float32)
        @pl.loop(0, groups)
        def _(group):
            here = pl.ds(pl.multiple_of(group * width, width), width)
            if not few:
                total_ref[...] += jnp.dot(fold_ref[group], short_rhs[here], preferred_element_type=jnp.float32)
            if n3:
                total_ref[...] += jnp.dot(far_ref[group], far_rhs[here], preferred_element_type=jnp.float32)

        both = narrow_sum[...]
        both = both + pltpu.roll(both, NARROW, 1)
        both = jnp.concatenate([both] * (FOLD // (2 * NARROW)), axis=1)
        total_ref[...] = jnp.where(target == largest_irrep(vir_ref), total_ref[...], both)
        write_quarters(total_ref, col, outs)

    return kernel


def last_product(third_lhs, far_lhs, fold, occ_irrep, vir_irrep, pos2, pos3, count, place, narrow_sum, wide_sum, few, m2, m3, e3, batch):
    groups, rows, width = far_lhs.shape
    share = rows // batch
    vmem = pl.BlockSpec(memory_space=pltpu.VMEM)
    smem = pl.BlockSpec(memory_space=pltpu.SMEM)
    arrays = [narrow_sum, wide_sum] + list(m2) + [v for group in m3 for v in group] + list(e3)
    quarter = (batch // 2, share, FOLD // 2)
    whole = groups * width
    unused = jnp.zeros((16, 128), jnp.bfloat16)
    return pl.pallas_call(
        make_last_kernel(few, len(m2), starts_of(m2), len(m3), starts_of([v[0] for v in m3])),
        in_specs=[smem] * 6 + [vmem] * (4 + len(arrays)),
        out_specs=[vmem] * 4,
        out_shape=[jax.ShapeDtypeStruct(quarter, jnp.float32)] * 4,
        scratch_shapes=[
            pltpu.VMEM((vir_irrep.shape[0], 8), jnp.int32),
            pltpu.VMEM((rows, FOLD), jnp.float32),
            pltpu.VMEM((rows, 2 * NARROW), jnp.float32),
            pltpu.VMEM((fold.shape[2] if few else whole, FOLD), jnp.bfloat16),
            pltpu.VMEM((whole if m3 else 16, FOLD), jnp.bfloat16),
            pltpu.VMEM((2, fold.shape[2]) + (2 * NARROW,) if few else (1, whole, 2 * NARROW), jnp.bfloat16),
        ],
        cost_estimate=cost(4 if m3 else 3),
        compiler_params=pltpu.CompilerParams(vmem_limit_bytes=32 * 1024 * 1024),
    )(occ_irrep, vir_irrep, pos2, pos3, count, place, fold, unused if few else third_lhs,
      far_lhs if m3 else unused, vir_irrep[None, :], *arrays)


def dense_product(amplitudes, whole, occ_irrep, occ_local, vir_local, vir_irrep):
    batch = amplitudes.shape[0]
    keep = (
        jnp.bitwise_xor(occ_irrep[:batch, None], occ_local[None, :])[:, :, None, None]
        == jnp.bitwise_xor(vir_local[:, None], vir_irrep[None, :])[None, None]
    )
    kept = jnp.where(keep, amplitudes, jnp.zeros_like(amplitudes))
    return lax.dot_general(
        kept, whole, (((1, 3), (0, 1)), ((), ())), preferred_element_type=jnp.float32
    )


def finish(cycle, occ_irrep, vir_irrep, occ_energy, vir_energy, a_start, a_size, b_start, b_size, batch):
    label_a = lax.dynamic_slice_in_dim(vir_irrep, a_start, a_size)
    label_b = lax.dynamic_slice_in_dim(vir_irrep, b_start, b_size)
    energy_a = lax.dynamic_slice_in_dim(vir_energy, a_start, a_size)
    energy_b = lax.dynamic_slice_in_dim(vir_energy, b_start, b_size)
    target = jnp.bitwise_xor(
        jnp.bitwise_xor(occ_irrep[:batch, None], occ_irrep[batch]), label_a[None, :]
    )
    keep = label_b[:, None, None] == target[None, :, :]
    denominator = (
        occ_energy[:batch][None, :, None]
        + occ_energy[batch]
        - energy_a[None, None, :]
        - energy_b[:, None, None]
    )
    swapped = jnp.transpose(cycle, (2, 0, 1))
    return jnp.where(keep, swapped, 0.0) / denominator


def on_square(amplitudes, integrals, occ_irrep, vir_irrep, screen):
    batch, occ_share, share, vir_total = amplitudes.shape
    row = lax.axis_index("row")
    col = lax.axis_index("col")
    place = jnp.stack([row, col]).astype(jnp.int32)
    few, m2a, m2b, m3a, m3b, pos2, pos3, posx, form, count = wide_blocks(
        integrals, occ_irrep, vir_irrep, screen, place, batch
    )
    outer = [(0, 1), (1, 0), (2, 3), (3, 2)]
    inner = [(1, 2), (2, 1)]
    inward = [(0, 1), (3, 2)]
    outward = [(1, 0), (2, 3)]
    ends = [(0, 3), (3, 0)]
    second = [(r, r ^ 2) for r in range(4)]

    def move(v, pairs):
        return lax.ppermute(v, "row", pairs)

    def sparse(use_few, choose):
        def run(few, m2a, m2b, m3a, m3b):
            shorts, wides = choose(m2a, m2b, m3a, m3b)
            near = [(own, move(own, outer), move(own, inner)) for own in wides]
            few = few[:use_few] if use_few else None
            narrow = narrow_blocks(integrals, occ_irrep, vir_irrep, screen, place, few, batch)
            if use_few:
                e1, o1 = move(narrow, outer), move(narrow, inner)
                lhs, third_lhs, far_lhs, fold = masked_amplitudes(
                    amplitudes, occ_irrep, vir_irrep, place, posx, use_few
                )
                near, e1, o1, few, _ = lax.optimization_barrier((near, e1, o1, few, fold))
                two, three = move(few, second), move(few, ends)
                blocks, e3 = (narrow, e1, o1), []
                sums = (few, e1, o1, two, three)
            else:
                h1 = [move(v, inward) for v in shorts]
                o1, e1 = move(narrow, inner), move(narrow, outward)
                lhs, third_lhs, far_lhs, fold = masked_amplitudes(
                    amplitudes, occ_irrep, vir_irrep, place, posx, 0
                )
                near, h1, o1, e1, _ = lax.optimization_barrier((near, h1, o1, e1, fold))
                h2 = [move(own + v, inner) for own, v in zip(shorts, h1)]
                e1 = e1 + move(narrow, inward)
                e2 = move(o1, outward)
                h2, e1, e2 = lax.optimization_barrier((h2, e1, e2))
                h3 = [move(own + v, outward) for own, v in zip(shorts, h2)]
                o2 = move(e1, inner)
                blocks, e3 = (narrow, e1, o1, e2, o2), [move(o2, outward)]
                sums = [a + b + c + d for a, b, c, d in zip(shorts, h1, h2, h3)]
            far = [(move(o, outward), move(e, inner)) for _, e, o in near]
            narrow_sum, wide_sum = first_product(
                lhs, third_lhs, far_lhs, pos3, place, blocks, bool(use_few), near
            )
            return list(last_product(
                third_lhs, far_lhs, fold, occ_irrep, vir_irrep, pos2, pos3, count, place, narrow_sum, wide_sum,
                bool(use_few), sums, far, e3, batch
            ))

        return run

    def dense(*_):
        occ_local = lax.dynamic_slice_in_dim(occ_irrep, col * occ_share, occ_share)
        vir_local = lax.dynamic_slice_in_dim(vir_irrep, row * share, share)
        screen_rows = lax.dynamic_slice_in_dim(screen, col * occ_share, occ_share, 0)
        fold = folded_integrals(
            integrals, occ_local, vir_local, vir_irrep, occ_irrep[batch], screen_rows
        )
        whole = jnp.zeros((occ_share, vir_total, FOLD), fold.dtype)
        for s in range(4):
            block = move(fold, [(r, r ^ s) for r in range(4)]) if s else fold
            whole = lax.dynamic_update_slice_in_dim(whole, block, jnp.bitwise_xor(row, s) * share, 1)
        total = dense_product(amplitudes, whole, occ_irrep, occ_local, vir_local, vir_irrep)
        quarter = (batch // 2, share, FOLD // 2)
        goals = [jnp.bitwise_xor(col, t) for t in range(4)]
        return [
            lax.dynamic_slice(total, (g // 2 * quarter[0], 0, g % 2 * quarter[2]), quarter) for g in goals
        ]

    branches = [
        sparse(0, lambda m2a, m2b, m3a, m3b: ([m2a], [])),
        sparse(0, lambda m2a, m2b, m3a, m3b: ([m2a, m2b], [])),
        sparse(0, lambda m2a, m2b, m3a, m3b: ([m2a], [m3a[:FEW_WIDE]])),
        sparse(FEW_CAPS[0], lambda m2a, m2b, m3a, m3b: ([], [m3a])),
        sparse(FEW_CAPS[1], lambda m2a, m2b, m3a, m3b: ([], [m3a])),
        sparse(0, lambda m2a, m2b, m3a, m3b: ([m2a, m2b], [m3a, m3b])),
        dense,
    ]
    quarters = lax.switch(form[0], branches, few, m2a, m2b, m3a, m3b)
    mine = quarters[0]
    for t in (1, 2, 3):
        mine = mine + lax.ppermute(quarters[t], "col", [(q, q ^ t) for q in range(4)])
    places = [(r, q) for r in range(4) for q in range(4)]
    same = lax.ppermute(mine, ("row", "col"), [(r * 4 + q, q * 4 + r) for r, q in places])
    other = lax.ppermute(mine, ("row", "col"), [(r * 4 + q, (q ^ 2) * 4 + r) for r, q in places])
    upper = row // 2 == 1
    low = jnp.where(upper, other, same)
    high = jnp.where(upper, same, other)
    return jnp.concatenate([low, high], axis=0)


def on_any(amplitudes, integrals, occ_irrep, vir_irrep, screen):
    batch, occ_share, share, vir_total = amplitudes.shape
    row = lax.axis_index("row")
    col = lax.axis_index("col")
    occ_local = lax.dynamic_slice_in_dim(occ_irrep, col * occ_share, occ_share)
    vir_local = lax.dynamic_slice_in_dim(vir_irrep, row * share, share)
    screen_rows = lax.dynamic_slice_in_dim(screen, col * occ_share, occ_share, 0)
    fold = folded_integrals(
        integrals, occ_local, vir_local, vir_irrep, occ_irrep[batch], screen_rows
    )
    whole = lax.all_gather(fold, "row", axis=1, tiled=True)
    cycle = dense_product(amplitudes, whole, occ_irrep, occ_local, vir_local, vir_irrep)
    cycle = lax.psum(cycle, "col")
    cycle = jnp.concatenate([cycle] * (vir_total // FOLD), axis=2)
    cycle = lax.all_to_all(cycle, "row", split_axis=2, concat_axis=1, tiled=True)
    a_size = vir_total // lax.axis_size("col")
    return lax.dynamic_slice_in_dim(cycle, col * a_size, a_size, 1)


def on_device(amplitudes, integrals, occ_irrep, vir_irrep, screen, occ_energy, vir_energy):
    batch, _, vir_share, vir_total = amplitudes.shape
    square = lax.axis_size("row") == 4 and lax.axis_size("col") == 4
    form = on_square if square else on_any
    cycle = form(amplitudes, integrals, occ_irrep, vir_irrep, screen)
    a_size = vir_total // lax.axis_size("col")
    return finish(
        cycle, occ_irrep, vir_irrep, occ_energy, vir_energy,
        lax.axis_index("col") * a_size, a_size, lax.axis_index("row") * vir_share, vir_share, batch,
    )


def solution(mesh):
    in_specs = (
        P("parts", "col", "row", None),
        P(("parts", "col"), "row", None),
        P("parts"),
        P("parts"),
        P("parts", None),
        P("parts"),
        P("parts"),
    )
    out_specs = P("row", "parts", "col")
    return jax.shard_map(
        on_device, mesh=mesh, in_specs=in_specs, out_specs=out_specs, check_vma=False
    )
```

```python
import jax
import jax.numpy as jnp
from jax import lax
from jax.experimental import pallas as pl
from jax.experimental.pallas import tpu as pltpu
from jax.sharding import PartitionSpec as P

FOLD = 256
K_STEP = 5


def folded_integrals(integrals, occ_local, vir_local, vir_irrep, pair_label, screen_rows):
    irrep_codes = jnp.arange(8, dtype=jnp.int32)
    screen_local = jnp.sum(
        screen_rows[:, None, :] * (vir_local[None, :, None] == irrep_codes).astype(jnp.int32),
        axis=2,
    )
    target = jnp.bitwise_xor(
        jnp.bitwise_xor(occ_local[:, None], vir_local[None, :]), pair_label
    )
    target = jnp.where(screen_local == 1, target, -1)
    keep = target[:, :, None] == vir_irrep[None, None, :]
    kept = jnp.where(keep, integrals, jnp.zeros_like(integrals))
    return kept[:, :, :FOLD] + kept[:, :, FOLD:]


NARROW = 64
CAPS = (22, 3)
FEW_CAPS = (4, 10)
FEW_WIDE = 7


def largest_irrep(vir_ref):
    return jnp.where(vir_ref[0] == vir_ref[FOLD - 1], vir_ref[0], vir_ref[FOLD])


def label_columns(row_labels):
    return jnp.transpose(jnp.broadcast_to(row_labels, (8, row_labels.shape[1])))


def as_bf16(labels):
    return labels.astype(jnp.float32).astype(jnp.bfloat16)


def label_mix(mix_ref, column_ref, row_ref, row, big, keep_big):
    depth = mix_ref.shape[0]
    column_ref[...] = label_columns(row_ref[...])
    column = column_ref[pl.ds(pl.multiple_of(row * depth, depth), depth), :1]
    is_big = row_ref[...] == big
    wanted = is_big if keep_big else jnp.logical_not(is_big)
    mix_ref[...] = as_bf16(jnp.where(wanted, jnp.bitwise_xor(column, row_ref[...]), 8))


def kept_folded(int_ref, mix_ref, j, x):
    tile = int_ref[j]
    wanted = as_bf16(jnp.full(mix_ref.shape, x))
    kept = jnp.where(mix_ref[...] == wanted, tile, jnp.zeros_like(tile))
    return kept[:, :FOLD] + kept[:, FOLD:]


def narrow_fold(kept, bits, local):
    half = kept.shape[0] // 2
    lane = lax.broadcasted_iota(jnp.int32, (half, 2 * NARROW), 1)
    narrow = (kept[:, : 2 * NARROW] + kept[:, 2 * NARROW:]).astype(jnp.float32)
    narrow = narrow + pltpu.roll(narrow, NARROW, 1)
    on = jnp.bitwise_and(lax.shift_right_logical(jnp.full(local.shape, bits), local), 1) == 1
    narrow = jnp.where(on, narrow, 0.0)
    return jnp.where(lane < NARROW, narrow[:half], narrow[half:]).astype(jnp.bfloat16)


def screen_bits(screen_ref, k):
    bits = screen_ref[0, k]
    for g in range(1, 8):
        bits = bits + screen_ref[g, k] * (1 << g)
    return bits


def copy_of(source_ref, int_ref, sems, group):
    here = pl.ds(group * K_STEP, K_STEP)
    return pltpu.make_async_copy(source_ref.at[here], int_ref.at[here], sems.at[group])


def start_copies(source_ref, int_ref, sems):
    for group in range(int_ref.shape[0] // K_STEP):
        copy_of(source_ref, int_ref, sems, group).start()


def wait_copy(source_ref, int_ref, sems, group):
    copy_of(source_ref, int_ref, sems, group).wait()


def wide_kernel(
    occ_ref, vir_ref, screen_ref, place_ref, source_ref, row_ref,
    few_ref, m2a_ref, m2b_ref, m3a_ref, m3b_ref, pos2_ref, pos3_ref, posx_ref, form_ref, count_ref,
    mix_ref, small_mix_ref, column_ref, counts_ref, int_ref, sems, batch,
):
    start_copies(source_ref, int_ref, sems)
    k_all, depth, total = int_ref.shape
    half = depth // 2
    row, col = place_ref[0], place_ref[1]
    pair_label = occ_ref[batch]
    big = largest_irrep(vir_ref)
    mostly_zero = (occ_ref[col * k_all] == pair_label) | (occ_ref[(col + 1) * k_all - 1] == pair_label)
    most = FEW_CAPS[-1]
    for n in range(3):
        counts_ref[n] = 0
    label_mix(mix_ref, column_ref, row_ref, row, big, True)

    @pl.when(mostly_zero)
    def _():
        label_mix(small_mix_ref, column_ref, row_ref, row, big, False)

    local = column_ref[pl.ds(pl.multiple_of(row * depth, depth), depth), :1]

    @pl.loop(0, k_all)
    def _(k):
        @pl.when(k % K_STEP == 0)
        def _():
            wait_copy(source_ref, int_ref, sems, k // K_STEP)

        k_whole = col * k_all + k
        x = jnp.bitwise_xor(occ_ref[k_whole], pair_label)
        on_big = screen_ref[jnp.bitwise_xor(big, x), k_whole] == 1
        actives = (on_big & (x != 0), on_big & (x == 0), x != 0)
        pos2, pos3, posx = [jnp.where(active, counts_ref[n], -1) for n, active in enumerate(actives)]
        for n, active in enumerate(actives):
            counts_ref[n] = counts_ref[n] + active.astype(jnp.int32)
        pos2_ref[k], pos3_ref[k], posx_ref[k] = pos2, pos3, posx

        @pl.when(pos2 >= 0)
        def _():
            wide = kept_folded(int_ref, mix_ref, k, x)
            short = wide[:half] + wide[half:]

            @pl.when(mostly_zero & (posx < most))
            def _():
                for piece in range(2):
                    few_ref[posx, 1 + piece] = short[:, piece * 2 * NARROW:(piece + 1) * 2 * NARROW]

            @pl.when(pos2 < CAPS[0])
            def _():
                m2a_ref[pos2] = short

            @pl.when(pos2 >= CAPS[0])
            def _():
                m2b_ref[pos2 - CAPS[0]] = short

        @pl.when(mostly_zero & (posx >= 0) & (posx < most))
        def _():
            kept = kept_folded(int_ref, small_mix_ref, k, x)
            few_ref[posx, 0] = narrow_fold(kept, screen_bits(screen_ref, k_whole), local)

            @pl.when(pos2 < 0)
            def _():
                for piece in range(2):
                    few_ref[posx, 1 + piece] = jnp.zeros((half, 2 * NARROW), jnp.bfloat16)

        @pl.when(pos3 >= 0)
        def _():
            wide = kept_folded(int_ref, mix_ref, k, x)

            @pl.when(pos3 < CAPS[0])
            def _():
                m3a_ref[pos3] = wide

            @pl.when(pos3 >= CAPS[0])
            def _():
                m3b_ref[pos3 - CAPS[0]] = wide

    labels = row_ref[...]
    lanes = lax.broadcasted_iota(jnp.int32, labels.shape, 1)
    ahead = pltpu.roll(labels, total - NARROW, 1)
    long = (labels == ahead) & (lanes < total - NARROW) & (labels != big)
    too_long = jnp.max(long.astype(jnp.int32)) == 1
    n2, n3, nx = counts_ref[0], counts_ref[1], counts_ref[2]
    count_ref[0] = nx
    one_label = occ_ref[0] == pair_label
    form = jnp.where(nx <= FEW_CAPS[0], 3, jnp.where(nx <= FEW_CAPS[1], 4, 5))
    form = jnp.where(mostly_zero & (n3 <= CAPS[0]), form, 5)
    form = jnp.where((n3 <= FEW_WIDE) & (n2 <= CAPS[0]), 2, form)
    form = jnp.where(one_label, form, 6)
    form = jnp.where(n3 == 0, jnp.where(n2 <= CAPS[0], 0, 1), form)
    form_ref[0] = jnp.where(too_long, 6, form)


def wide_blocks(integrals, occ_irrep, vir_irrep, screen, place, batch):
    occ_share, depth, total = integrals.shape
    shapes = [(n, depth // 2, FOLD) for n in CAPS] + [(n, depth, FOLD) for n in CAPS]
    few = (FEW_CAPS[-1], 3, depth // 2, 2 * NARROW)
    smem = pl.BlockSpec(memory_space=pltpu.SMEM)

    def kernel(*refs):
        wide_kernel(*refs, batch)

    vmem = pl.BlockSpec(memory_space=pltpu.VMEM)
    return pl.pallas_call(
        kernel,
        in_specs=[smem] * 4 + [pl.BlockSpec(memory_space=pltpu.HBM), vmem],
        out_specs=[vmem] * (1 + len(shapes)) + [smem] * 5,
        scratch_shapes=[
            pltpu.VMEM((depth, total), jnp.bfloat16),
            pltpu.VMEM((depth, total), jnp.bfloat16),
            pltpu.VMEM((total, 8), jnp.int32),
            pltpu.SMEM((3,), jnp.int32),
            pltpu.VMEM(integrals.shape, jnp.bfloat16),
            pltpu.SemaphoreType.DMA((occ_share // K_STEP,)),
        ],
        out_shape=[jax.ShapeDtypeStruct(v, jnp.bfloat16) for v in [few] + shapes]
        + [jax.ShapeDtypeStruct((n,), jnp.int32) for n in (occ_share, occ_share, occ_share, 1, 1)],
        cost_estimate=cost(5),
        compiler_params=pltpu.CompilerParams(vmem_limit_bytes=24 * 1024 * 1024),
    )(occ_irrep, vir_irrep, screen.T, place, integrals, vir_irrep[None, :])


def narrow_kernel(
    occ_ref, vir_ref, screen_ref, place_ref, source_ref, row_ref, few_ref, narrow_ref,
    mix_ref, column_ref, int_ref, sems, batch,
):
    start_copies(source_ref, int_ref, sems)
    k_all, depth, total = int_ref.shape
    row, col = place_ref[0], place_ref[1]
    label_mix(mix_ref, column_ref, row_ref, row, largest_irrep(vir_ref), False)
    if few_ref is not None:
        for n in range(few_ref.shape[0]):
            for piece in range(2):
                narrow_ref[k_all + 2 * n + piece] = few_ref[n, 1 + piece]
    local = column_ref[pl.ds(pl.multiple_of(row * depth, depth), depth), :1]

    @pl.loop(0, k_all // K_STEP)
    def _(group):
        wait_copy(source_ref, int_ref, sems, group)
        for j in range(K_STEP):
            k = group * K_STEP + j
            k_whole = col * k_all + k
            x = jnp.bitwise_xor(occ_ref[k_whole], occ_ref[batch])
            kept = kept_folded(int_ref, mix_ref, k, x)
            narrow_ref[k] = narrow_fold(kept, screen_bits(screen_ref, k_whole), local)


def narrow_blocks(integrals, occ_irrep, vir_irrep, screen, place, few, batch):
    occ_share, depth, total = integrals.shape
    extra = [] if few is None else [few]
    count = occ_share + sum(2 * v.shape[0] for v in extra)
    smem = pl.BlockSpec(memory_space=pltpu.SMEM)
    vmem = pl.BlockSpec(memory_space=pltpu.VMEM)

    def kernel(*refs):
        narrow_kernel(*(refs if extra else refs[:6] + (None,) + refs[6:]), batch)

    return pl.pallas_call(
        kernel,
        in_specs=[smem] * 4 + [pl.BlockSpec(memory_space=pltpu.HBM), vmem] + [vmem] * len(extra),
        out_specs=vmem,
        out_shape=jax.ShapeDtypeStruct((count, depth // 2, 2 * NARROW), jnp.bfloat16),
        scratch_shapes=[
            pltpu.VMEM((depth, total), jnp.bfloat16),
            pltpu.VMEM((total, 8), jnp.int32),
            pltpu.VMEM(integrals.shape, jnp.bfloat16),
            pltpu.SemaphoreType.DMA((occ_share // K_STEP,)),
        ],
        cost_estimate=cost(4),
        compiler_params=pltpu.CompilerParams(vmem_limit_bytes=16 * 1024 * 1024),
    )(occ_irrep, vir_irrep, screen.T, place, integrals, vir_irrep[None, :], *extra)


def cost(micros):
    return pl.CostEstimate(flops=int(micros * 1e9), bytes_accessed=int(micros * 3e6), transcendentals=0)


SLOTS = (0, 1, 3, 2)
NEAR = 2


def amplitude_rows(column_ref, row_ref, occ_ref, row, batch, share):
    column_ref[...] = label_columns(row_ref[...])
    column = column_ref[pl.ds(pl.multiple_of(row * share, share), share), :1]
    return jnp.concatenate([jnp.bitwise_xor(column, occ_ref[i]) for i in range(batch)], axis=0)


def write_quarters(total_ref, col, outs):
    rows, fold = total_ref.shape
    width, height = fold // 2, rows // 2
    for t, out_ref in enumerate(outs):
        goal = jnp.bitwise_xor(col, t)
        lanes = pl.ds(pl.multiple_of((goal % 2) * width, width), width)
        lines = pl.ds(pl.multiple_of((goal // 2) * height, height), height)
        out_ref[...] = total_ref[lines, lanes].reshape(out_ref.shape)


def chosen(refs, starts, pos, pick):
    block = None
    for n, group in enumerate(refs):
        inside = (pos >= starts[n]) & (pos < starts[n + 1])
        at = jnp.clip(pos - starts[n], 0, starts[n + 1] - starts[n] - 1)
        found = pick(group, at)
        found = jnp.where(inside, found, jnp.zeros_like(found))
        block = found if block is None else block + found
    return block


def starts_of(arrays):
    starts = [0]
    for v in arrays:
        starts.append(starts[-1] + v.shape[0])
    return starts


def mask_kernel(
    occ_ref, place_ref, posx_ref, amp_ref, row_ref, lhs_ref, third_ref, far_ref, fold_ref, few_lhs_ref,
    mix_ref, column_ref, amp_buffer, sems,
):
    batch, k_all, share, total = amp_ref.shape
    rows, groups = batch * share, k_all // K_STEP
    row, col = place_ref[0], place_ref[1]

    def fetch(group):
        slot = group % 2
        source = amp_ref.at[:, pl.ds(group * K_STEP, K_STEP)]
        return pltpu.make_async_copy(source, amp_buffer.at[slot], sems.at[slot])

    fetch(0).start()
    column = amplitude_rows(column_ref, row_ref, occ_ref, row, batch, share)
    mix_ref[...] = as_bf16(jnp.bitwise_xor(column, row_ref[...]))
    if few_lhs_ref is not None:
        few_lhs_ref[...] = jnp.zeros(few_lhs_ref.shape, jnp.bfloat16)

    @pl.loop(0, groups)
    def _(group):
        slot = group % 2

        @pl.when(group + 1 < groups)
        def _():
            fetch(group + 1).start()

        fetch(group).wait()

        @pl.loop(0, K_STEP)
        def _(j):
            wanted = as_bf16(jnp.full((rows, share), occ_ref[col * k_all + group * K_STEP + j]))
            folded = None
            for n, s in enumerate(SLOTS):
                place = pl.ds(pl.multiple_of(jnp.bitwise_xor(row, s) * share, share), share)
                tile = amp_buffer[slot, :, j, :, place].reshape(rows, share)
                piece = jnp.where(mix_ref[:, place] == wanted, tile, jnp.zeros_like(tile))
                if n < NEAR:
                    lhs_ref[group, :, pl.ds(pl.multiple_of((n * K_STEP + j) * share, share), share)] = piece
                else:
                    own_ref = third_ref if n == NEAR else far_ref
                    own_ref[group, :, pl.ds(pl.multiple_of(j * share, share), share)] = piece
                folded = piece if folded is None else folded + piece
            if fold_ref is not None:
                fold_ref[group, :, pl.ds(pl.multiple_of(j * share, share), share)] = folded
            else:
                posx = posx_ref[group * K_STEP + j]

                @pl.when((posx >= 0) & (posx < few_lhs_ref.shape[2] // share))
                def _():
                    here = pl.ds(pl.multiple_of(j * share, share), share)
                    there = pl.ds(pl.multiple_of(posx * share, share), share)
                    few_lhs_ref[0, :, there] = third_ref[group, :, here]
                    few_lhs_ref[1, :, there] = far_ref[group, :, here]
                    few_lhs_ref[2, :, there] = folded


def masked_amplitudes(amplitudes, occ_irrep, vir_irrep, place, posx, few):
    batch, k_all, share, total = amplitudes.shape
    rows, groups = batch * share, k_all // K_STEP
    smem = pl.BlockSpec(memory_space=pltpu.SMEM)
    vmem = pl.BlockSpec(memory_space=pltpu.VMEM)
    hbm = pl.BlockSpec(memory_space=pltpu.HBM)
    shapes = [(groups, rows, w) for w in (NEAR * K_STEP * share, K_STEP * share, K_STEP * share)]
    shapes += [(3, rows, few * share)] if few else [(groups, rows, K_STEP * share)]

    def kernel(*refs):
        mask_kernel(*(refs[:8] + (None,) + refs[8:] if few else refs[:9] + (None,) + refs[9:]))

    return pl.pallas_call(
        kernel,
        in_specs=[smem, smem, smem, hbm, vmem],
        out_specs=[vmem] * len(shapes),
        out_shape=[jax.ShapeDtypeStruct(v, jnp.bfloat16) for v in shapes],
        scratch_shapes=[
            pltpu.VMEM((rows, total), jnp.bfloat16),
            pltpu.VMEM((total, 8), jnp.int32),
            pltpu.VMEM((2, batch, K_STEP, share, total), jnp.bfloat16),
            pltpu.SemaphoreType.DMA((2,)),
        ],
        cost_estimate=cost(7),
        compiler_params=pltpu.CompilerParams(vmem_limit_bytes=28 * 1024 * 1024),
    )(occ_irrep, place, posx, amplitudes, vir_irrep[None, :])


def make_first_kernel(few, n3, starts3):
    def kernel(pos3_ref, place_ref, lhs_ref, third_ref, far_ref, *refs):
        sources = 3 if few else 5
        narrow_refs, refs = refs[:sources], refs[sources:]
        m3_refs = [refs[3 * n:3 * n + 3] for n in range(n3)]
        narrow_sum, wide_sum, narrow_rhs, wide_rhs = refs[3 * n3:]
        row = place_ref[0]
        at_end = (row == 0) | (row == 3)
        groups, _, depth = lhs_ref.shape
        share = depth // (NEAR * K_STEP)
        half = share // 2
        lane = lax.broadcasted_iota(jnp.int32, (half, 2 * NARROW), 1)

        narrow_sum[...] = jnp.zeros(narrow_sum.shape, jnp.float32)
        wide_sum[...] = jnp.zeros(wide_sum.shape, jnp.float32)

        @pl.loop(0, groups)
        def _(group):
            @pl.loop(0, K_STEP)
            def _(j):
                k = group * K_STEP + j
                if few:
                    blocks = [ref[k] for ref in narrow_refs]
                else:
                    own, e1, o1, e2, o2 = [ref[k] for ref in narrow_refs]
                    blocks = (own, e1, o1, jnp.where(at_end, e2, o2))
                for n, block in enumerate(blocks):
                    zero = jnp.zeros_like(block)
                    first = pl.multiple_of((n * K_STEP + j) * share, share)
                    narrow_rhs[pl.ds(first, half)] = jnp.where(lane < NARROW, block, zero)
                    narrow_rhs[pl.ds(first + half, half)] = jnp.where(lane < NARROW, zero, block)
                for n in range(3 if n3 else 0):
                    block = chosen(m3_refs, starts3, pos3_ref[k], lambda group, at, n=n: group[n][at])
                    if n == 2:
                        block = jnp.where(at_end, jnp.zeros_like(block), block)
                    wide_rhs[pl.ds(pl.multiple_of((n * K_STEP + j) * share, share), share)] = block

            one = depth // NEAR
            narrow = jnp.dot(lhs_ref[group], narrow_rhs[:depth], preferred_element_type=jnp.float32)
            narrow += jnp.dot(third_ref[group], narrow_rhs[depth:depth + one], preferred_element_type=jnp.float32)
            if not few:
                narrow += jnp.dot(far_ref[group], narrow_rhs[depth + one:], preferred_element_type=jnp.float32)
            narrow_sum[...] += narrow
            if n3:
                wide = jnp.dot(lhs_ref[group], wide_rhs[:depth], preferred_element_type=jnp.float32)
                wide += jnp.dot(third_ref[group], wide_rhs[depth:], preferred_element_type=jnp.float32)
                wide_sum[...] += wide

    return kernel


def first_product(lhs, third_lhs, far_lhs, pos3, place, narrow, few, m3):
    groups, rows, depth = lhs.shape
    vmem = pl.BlockSpec(memory_space=pltpu.VMEM)
    smem = pl.BlockSpec(memory_space=pltpu.SMEM)
    arrays = list(narrow) + [v for group in m3 for v in group]
    wide = (rows, FOLD) if m3 else (16, FOLD)
    wide_depth = depth // NEAR * 3 if m3 else 16
    return pl.pallas_call(
        make_first_kernel(few, len(m3), starts_of([v[0] for v in m3])),
        in_specs=[smem] * 2 + [vmem] * (3 + len(arrays)),
        out_specs=[vmem] * 2,
        out_shape=[jax.ShapeDtypeStruct(v, jnp.float32) for v in ((rows, 2 * NARROW), wide)],
        scratch_shapes=[
            pltpu.VMEM((depth // NEAR * len(SLOTS), 2 * NARROW), jnp.bfloat16),
            pltpu.VMEM((wide_depth, FOLD), jnp.bfloat16),
        ],
        cost_estimate=cost(9 if m3 else 6),
        compiler_params=pltpu.CompilerParams(vmem_limit_bytes=32 * 1024 * 1024),
    )(pos3, place, lhs, third_lhs, far_lhs, *arrays)


def make_last_kernel(few, n2, starts2, n3, starts3):
    def kernel(
        occ_ref, vir_ref, pos2_ref, pos3_ref, count_ref, place_ref, fold_ref, third_ref, far_ref, row_ref, narrow_ref, wide_ref,
        *refs,
    ):
        m2_refs, refs = refs[:n2], refs[n2:]
        m3_refs = [refs[2 * n:2 * n + 2] for n in range(n3)]
        refs = refs[2 * n3:]
        e3_ref, refs = (None, refs) if few else (refs[0], refs[1:])
        outs = refs[:4]
        column_ref, total_ref, narrow_sum, short_rhs, far_rhs, third_rhs = refs[4:]
        row, col = place_ref[0], place_ref[1]
        at_end = (row == 0) | (row == 3)
        groups, rows, width = far_ref.shape if few else fold_ref.shape
        share = width // K_STEP
        batch = rows // share
        @pl.loop(0, groups * K_STEP)
        def _(k):
            here = pl.ds(pl.multiple_of(k * share, share), share)
            if not few:
                short = chosen(m2_refs, starts2, pos2_ref[k], lambda ref, at: ref[at])
                short_rhs[here] = jnp.concatenate([short, short], axis=0)
            if n3:
                far_rhs[here] = chosen(
                    m3_refs, starts3, pos3_ref[k], lambda pair, at: jnp.where(at_end, pair[0][at], pair[1][at])
                )

        column = amplitude_rows(column_ref, row_ref, occ_ref, row, batch, share)
        target = jnp.bitwise_xor(column, occ_ref[batch])
        if few:
            own, e1, o1, two, three = m2_refs
            half = share // 2
            lane = lax.broadcasted_iota(jnp.int32, (half, 2 * NARROW), 1)

            @pl.loop(0, fold_ref.shape[2] // share)
            def _(n):
                used = n < count_ref[0]
                first = pl.multiple_of(n * share, share)
                for slot, wanted, ref in ((0, used & at_end, three), (1, used, two)):
                    block = ref[n, 0]
                    zero = jnp.zeros_like(block)
                    block = jnp.where(wanted, block, zero)
                    third_rhs[slot, pl.ds(first, half)] = jnp.where(lane < NARROW, block, zero)
                    third_rhs[slot, pl.ds(first + half, half)] = jnp.where(lane < NARROW, zero, block)
                pieces = []
                for piece in range(2):
                    close = groups * K_STEP + 2 * n + piece
                    block = own[n, 1 + piece] + e1[close] + two[n, 1 + piece]
                    block = block + jnp.where(at_end, three[n, 1 + piece], o1[close])
                    pieces.append(jnp.where(used, block, jnp.zeros_like(block)))
                short = jnp.concatenate(pieces, axis=1)
                short_rhs[pl.ds(first, share)] = jnp.concatenate([short, short], axis=0)

            narrow = jnp.dot(fold_ref[0], third_rhs[0], preferred_element_type=jnp.float32)
            narrow += jnp.dot(fold_ref[1], third_rhs[1], preferred_element_type=jnp.float32)
            narrow_sum[...] = narrow_ref[...] + narrow
            total_ref[...] = wide_ref[...] + jnp.dot(
                fold_ref[2], short_rhs[...], preferred_element_type=jnp.float32
            )
        else:
            narrow_sum[...] = narrow_ref[...]

            @pl.when(at_end)
            def _():
                half = share // 2
                lane = lax.broadcasted_iota(jnp.int32, (half, 2 * NARROW), 1)

                @pl.loop(0, groups * K_STEP)
                def _(k):
                    block = e3_ref[k]
                    zero = jnp.zeros_like(block)
                    first = pl.multiple_of(k * share, share)
                    third_rhs[0, pl.ds(first, half)] = jnp.where(lane < NARROW, block, zero)
                    third_rhs[0, pl.ds(first + half, half)] = jnp.where(lane < NARROW, zero, block)

                @pl.loop(0, groups)
                def _(group):
                    rhs = third_rhs[0, pl.ds(pl.multiple_of(group * width, width), width)]
                    narrow_sum[...] += jnp.dot(third_ref[group], rhs, preferred_element_type=jnp.float32)

            total_ref[...] = wide_ref[...] if n3 else jnp.zeros(total_ref.shape, jnp.float32)
        @pl.loop(0, groups)
        def _(group):
            here = pl.ds(pl.multiple_of(group * width, width), width)
            if not few:
                total_ref[...] += jnp.dot(fold_ref[group], short_rhs[here], preferred_element_type=jnp.float32)
            if n3:
                total_ref[...] += jnp.dot(far_ref[group], far_rhs[here], preferred_element_type=jnp.float32)

        both = narrow_sum[...]
        both = both + pltpu.roll(both, NARROW, 1)
        both = jnp.concatenate([both] * (FOLD // (2 * NARROW)), axis=1)
        total_ref[...] = jnp.where(target == largest_irrep(vir_ref), total_ref[...], both)
        write_quarters(total_ref, col, outs)

    return kernel


def last_product(third_lhs, far_lhs, fold, occ_irrep, vir_irrep, pos2, pos3, count, place, narrow_sum, wide_sum, few, m2, m3, e3, batch):
    groups, rows, width = far_lhs.shape
    share = rows // batch
    vmem = pl.BlockSpec(memory_space=pltpu.VMEM)
    smem = pl.BlockSpec(memory_space=pltpu.SMEM)
    arrays = [narrow_sum, wide_sum] + list(m2) + [v for group in m3 for v in group] + list(e3)
    quarter = (batch // 2, share, FOLD // 2)
    whole = groups * width
    unused = jnp.zeros((16, 128), jnp.bfloat16)
    return pl.pallas_call(
        make_last_kernel(few, len(m2), starts_of(m2), len(m3), starts_of([v[0] for v in m3])),
        in_specs=[smem] * 6 + [vmem] * (4 + len(arrays)),
        out_specs=[vmem] * 4,
        out_shape=[jax.ShapeDtypeStruct(quarter, jnp.float32)] * 4,
        scratch_shapes=[
            pltpu.VMEM((vir_irrep.shape[0], 8), jnp.int32),
            pltpu.VMEM((rows, FOLD), jnp.float32),
            pltpu.VMEM((rows, 2 * NARROW), jnp.float32),
            pltpu.VMEM((fold.shape[2] if few else whole, FOLD), jnp.bfloat16),
            pltpu.VMEM((whole if m3 else 16, FOLD), jnp.bfloat16),
            pltpu.VMEM((2, fold.shape[2]) + (2 * NARROW,) if few else (1, whole, 2 * NARROW), jnp.bfloat16),
        ],
        cost_estimate=cost(4 if m3 else 3),
        compiler_params=pltpu.CompilerParams(vmem_limit_bytes=32 * 1024 * 1024),
    )(occ_irrep, vir_irrep, pos2, pos3, count, place, fold, unused if few else third_lhs,
      far_lhs if m3 else unused, vir_irrep[None, :], *arrays)


def dense_product(amplitudes, whole, occ_irrep, occ_local, vir_local, vir_irrep):
    batch = amplitudes.shape[0]
    keep = (
        jnp.bitwise_xor(occ_irrep[:batch, None], occ_local[None, :])[:, :, None, None]
        == jnp.bitwise_xor(vir_local[:, None], vir_irrep[None, :])[None, None]
    )
    kept = jnp.where(keep, amplitudes, jnp.zeros_like(amplitudes))
    return lax.dot_general(
        kept, whole, (((1, 3), (0, 1)), ((), ())), preferred_element_type=jnp.float32
    )


def finish(cycle, occ_irrep, vir_irrep, occ_energy, vir_energy, a_start, a_size, b_start, b_size, batch):
    label_a = lax.dynamic_slice_in_dim(vir_irrep, a_start, a_size)
    label_b = lax.dynamic_slice_in_dim(vir_irrep, b_start, b_size)
    energy_a = lax.dynamic_slice_in_dim(vir_energy, a_start, a_size)
    energy_b = lax.dynamic_slice_in_dim(vir_energy, b_start, b_size)
    target = jnp.bitwise_xor(
        jnp.bitwise_xor(occ_irrep[:batch, None], occ_irrep[batch]), label_a[None, :]
    )
    keep = label_b[:, None, None] == target[None, :, :]
    denominator = (
        occ_energy[:batch][None, :, None]
        + occ_energy[batch]
        - energy_a[None, None, :]
        - energy_b[:, None, None]
    )
    swapped = jnp.transpose(cycle, (2, 0, 1))
    return jnp.where(keep, swapped, 0.0) / denominator


def on_square(amplitudes, integrals, occ_irrep, vir_irrep, screen):
    batch, occ_share, share, vir_total = amplitudes.shape
    row = lax.axis_index("row")
    col = lax.axis_index("col")
    place = jnp.stack([row, col]).astype(jnp.int32)
    few, m2a, m2b, m3a, m3b, pos2, pos3, posx, form, count = wide_blocks(
        integrals, occ_irrep, vir_irrep, screen, place, batch
    )
    outer = [(0, 1), (1, 0), (2, 3), (3, 2)]
    inner = [(1, 2), (2, 1)]
    inward = [(0, 1), (3, 2)]
    outward = [(1, 0), (2, 3)]
    ends = [(0, 3), (3, 0)]
    second = [(r, r ^ 2) for r in range(4)]

    def move(v, pairs):
        return lax.ppermute(v, "row", pairs)

    def sparse(use_few, choose):
        def run(few, m2a, m2b, m3a, m3b):
            shorts, wides = choose(m2a, m2b, m3a, m3b)
            near = [(own, move(own, outer), move(own, inner)) for own in wides]
            few = few[:use_few] if use_few else None
            narrow = narrow_blocks(integrals, occ_irrep, vir_irrep, screen, place, few, batch)
            if use_few:
                e1, o1 = move(narrow, outer), move(narrow, inner)
                lhs, third_lhs, far_lhs, fold = masked_amplitudes(
                    amplitudes, occ_irrep, vir_irrep, place, posx, use_few
                )
                near, few, _ = lax.optimization_barrier((near, few, fold))
                two, three = move(few, second), move(few, ends)
                blocks, e3 = (narrow, e1, o1), []
                sums = (few, e1, o1, two, three)
            else:
                h1 = [move(v, inward) for v in shorts]
                o1, e1 = move(narrow, inner), move(narrow, outward)
                lhs, third_lhs, far_lhs, fold = masked_amplitudes(
                    amplitudes, occ_irrep, vir_irrep, place, posx, 0
                )
                near, h1, o1, e1, _ = lax.optimization_barrier((near, h1, o1, e1, fold))
                h2 = [move(own + v, inner) for own, v in zip(shorts, h1)]
                e1 = e1 + move(narrow, inward)
                e2 = move(o1, outward)
                h2, e1, e2 = lax.optimization_barrier((h2, e1, e2))
                h3 = [move(own + v, outward) for own, v in zip(shorts, h2)]
                o2 = move(e1, inner)
                blocks, e3 = (narrow, e1, o1, e2, o2), [move(o2, outward)]
                sums = [a + b + c + d for a, b, c, d in zip(shorts, h1, h2, h3)]
            far = [(move(o, outward), move(e, inner)) for _, e, o in near]
            narrow_sum, wide_sum = first_product(
                lhs, third_lhs, far_lhs, pos3, place, blocks, bool(use_few), near
            )
            return list(last_product(
                third_lhs, far_lhs, fold, occ_irrep, vir_irrep, pos2, pos3, count, place, narrow_sum, wide_sum,
                bool(use_few), sums, far, e3, batch
            ))

        return run

    def dense(*_):
        occ_local = lax.dynamic_slice_in_dim(occ_irrep, col * occ_share, occ_share)
        vir_local = lax.dynamic_slice_in_dim(vir_irrep, row * share, share)
        screen_rows = lax.dynamic_slice_in_dim(screen, col * occ_share, occ_share, 0)
        fold = folded_integrals(
            integrals, occ_local, vir_local, vir_irrep, occ_irrep[batch], screen_rows
        )
        whole = jnp.zeros((occ_share, vir_total, FOLD), fold.dtype)
        for s in range(4):
            block = move(fold, [(r, r ^ s) for r in range(4)]) if s else fold
            whole = lax.dynamic_update_slice_in_dim(whole, block, jnp.bitwise_xor(row, s) * share, 1)
        total = dense_product(amplitudes, whole, occ_irrep, occ_local, vir_local, vir_irrep)
        quarter = (batch // 2, share, FOLD // 2)
        goals = [jnp.bitwise_xor(col, t) for t in range(4)]
        return [
            lax.dynamic_slice(total, (g // 2 * quarter[0], 0, g % 2 * quarter[2]), quarter) for g in goals
        ]

    branches = [
        sparse(0, lambda m2a, m2b, m3a, m3b: ([m2a], [])),
        sparse(0, lambda m2a, m2b, m3a, m3b: ([m2a, m2b], [])),
        sparse(0, lambda m2a, m2b, m3a, m3b: ([m2a], [m3a[:FEW_WIDE]])),
        sparse(FEW_CAPS[0], lambda m2a, m2b, m3a, m3b: ([], [m3a])),
        sparse(FEW_CAPS[1], lambda m2a, m2b, m3a, m3b: ([], [m3a])),
        sparse(0, lambda m2a, m2b, m3a, m3b: ([m2a, m2b], [m3a, m3b])),
        dense,
    ]
    quarters = lax.switch(form[0], branches, few, m2a, m2b, m3a, m3b)
    mine = quarters[0]
    for t in (1, 2, 3):
        mine = mine + lax.ppermute(quarters[t], "col", [(q, q ^ t) for q in range(4)])
    places = [(r, q) for r in range(4) for q in range(4)]
    same = lax.ppermute(mine, ("row", "col"), [(r * 4 + q, q * 4 + r) for r, q in places])
    other = lax.ppermute(mine, ("row", "col"), [(r * 4 + q, (q ^ 2) * 4 + r) for r, q in places])
    upper = row // 2 == 1
    low = jnp.where(upper, other, same)
    high = jnp.where(upper, same, other)
    return jnp.concatenate([low, high], axis=0)


def on_any(amplitudes, integrals, occ_irrep, vir_irrep, screen):
    batch, occ_share, share, vir_total = amplitudes.shape
    row = lax.axis_index("row")
    col = lax.axis_index("col")
    occ_local = lax.dynamic_slice_in_dim(occ_irrep, col * occ_share, occ_share)
    vir_local = lax.dynamic_slice_in_dim(vir_irrep, row * share, share)
    screen_rows = lax.dynamic_slice_in_dim(screen, col * occ_share, occ_share, 0)
    fold = folded_integrals(
        integrals, occ_local, vir_local, vir_irrep, occ_irrep[batch], screen_rows
    )
    whole = lax.all_gather(fold, "row", axis=1, tiled=True)
    cycle = dense_product(amplitudes, whole, occ_irrep, occ_local, vir_local, vir_irrep)
    cycle = lax.psum(cycle, "col")
    cycle = jnp.concatenate([cycle] * (vir_total // FOLD), axis=2)
    cycle = lax.all_to_all(cycle, "row", split_axis=2, concat_axis=1, tiled=True)
    a_size = vir_total // lax.axis_size("col")
    return lax.dynamic_slice_in_dim(cycle, col * a_size, a_size, 1)


def on_device(amplitudes, integrals, occ_irrep, vir_irrep, screen, occ_energy, vir_energy):
    batch, _, vir_share, vir_total = amplitudes.shape
    square = lax.axis_size("row") == 4 and lax.axis_size("col") == 4
    form = on_square if square else on_any
    cycle = form(amplitudes, integrals, occ_irrep, vir_irrep, screen)
    a_size = vir_total // lax.axis_size("col")
    return finish(
        cycle, occ_irrep, vir_irrep, occ_energy, vir_energy,
        lax.axis_index("col") * a_size, a_size, lax.axis_index("row") * vir_share, vir_share, batch,
    )


def solution(mesh):
    in_specs = (
        P("parts", "col", "row", None),
        P(("parts", "col"), "row", None),
        P("parts"),
        P("parts"),
        P("parts", None),
        P("parts"),
        P("parts"),
    )
    out_specs = P("row", "parts", "col")
    return jax.shard_map(
        on_device, mesh=mesh, in_specs=in_specs, out_specs=out_specs, check_vma=False
    )
```
